32 devices in a mesh: seq: 8 (over z, x), head: 4 (over y, core).
Axes of the slice: x: 2, y: 2, z: 4, core: 2. Of those that a mesh axis runs over, the one named last changes fastest.
Arguments:
- projections: bfloat16 [4096, 3, 4096], P('seq', None, 'head'), may hold values from -53 to 53
- output_gradient: bfloat16 [4096, 5120], P('seq', 'head'), may hold values from -0.75 to 0.75
- output_projection_weight: bfloat16 [5120, 4096], P(None, 'head'), may hold values from -0.625 to 0.625
- kept_token_indices: int32 [8, 192], P('seq'), may hold values from -1 to 511, as said below
- surviving_token_count: int32 [8], replicated, may hold values from 64 to 192, as said below
Outputs:
- projection_grad: bfloat16 [4096, 3, 4096], P('seq', None, 'head')
- weight_grad: float32 [5120, 4096], P('seq', 'head')
The draws below stay inside these ranges and needn't reach their ends.
Inputs may be any that keep to these rules, and one draw needn't show every extreme that they name: `kept_token_indices`: row s holds, in its first surviving_token_count[s] entries, distinct indices 0 to 511 in ascending order; its other entries are -1. Every shard that keeps 192 tokens keeps its last token. `surviving_token_count`: some shard keeps exactly 192 tokens and some other keeps exactly 64.
All inputs are finite; a program needn't handle non-finite values.
Results may differ from the reference program's by a relative error of at most 0.0099.
Values may be sent and summed in bfloat16 or wider, within the bound.
No kernel may reach another device: no remote copies, remote signals or barrier semaphores. Data moves between devices by JAX's collectives and lax.ppermute only.
A program may use at most 128 MiB of HBM per device.

```python
import math
import jax
import jax.numpy as jnp
from jax import lax

D = 5120
DH = 128
HEADS = 32
TOK_DEV = 512
TOKENS = 4096
CAP = 192
N_SEQ = 8


def shared_counts(key):
    inner_key = jax.random.fold_in(key, 101)
    first_key, second_key, third_key = jax.random.split(inner_key, 3)
    floor_count = CAP // 3
    drawn_counts = jax.random.randint(first_key, (N_SEQ,), floor_count, CAP + 1)
    full_shard = jax.random.randint(second_key, (), 0, N_SEQ)
    low_shard = (full_shard + 1 + jax.random.randint(third_key, (), 0, N_SEQ - 1)) % N_SEQ
    drawn_counts = drawn_counts.at[full_shard].set(CAP).at[low_shard].set(floor_count)
    return drawn_counts.astype(jnp.int32)


def draw_surviving_token_count(key, part):
    return shared_counts(key)


def draw_kept_token_indices(key, part):
    live_counts = shared_counts(key)
    key = jax.random.fold_in(key, 3)
    shard_keys = jax.random.split(key, N_SEQ)
    orders = jax.vmap(lambda single: jax.random.permutation(single, TOK_DEV))(shard_keys)
    chosen = orders[:, :CAP].astype(jnp.int32)
    last_index = jnp.int32(TOK_DEV - 1)
    holds_last = jnp.any(chosen == last_index, axis=1)
    needs_last = (live_counts == CAP) & jnp.logical_not(holds_last)
    chosen = chosen.at[:, 0].set(jnp.where(needs_last, last_index, chosen[:, 0]))
    slot_ids = jnp.arange(CAP, dtype=jnp.int32)[None, :]
    marked = jnp.where(slot_ids < live_counts[:, None], chosen, TOK_DEV)
    ordered = jnp.sort(marked, axis=1)
    return jnp.where(ordered == TOK_DEV, -1, ordered).astype(jnp.int32)


def draw_projections(key, part):
    key = jax.random.fold_in(key, 7)
    base_key = jax.random.fold_in(key, 0)
    full_shape = (TOKENS, 3, HEADS * DH)
    return jax.random.normal(base_key, full_shape, jnp.float32).astype(jnp.bfloat16)


def with_spikes(values, rng, source, target, shards_of, factor):
    owner, partner = [(jnp.arange(values.shape[dim]) // (values.shape[dim] // shards_of)).reshape([-1 if axis == dim else 1 for axis in range(values.ndim)]) for dim in (source, target)]
    chosen = jax.random.permutation(rng, shards_of)[partner]
    strong = (owner == chosen) | (owner == (partner + shards_of // 2) % shards_of)
    return jnp.where(strong, factor * values, values)


def levels(rng, extent, cuts, least, top_value):
    level = 1.0
    for axis_at, blocks in cuts:
        steps = jax.random.uniform(jax.random.fold_in(jax.random.fold_in(rng, 6), axis_at), (blocks,), jnp.float32, least / len(cuts), top_value / len(cuts))
        level = level * jnp.repeat(jnp.exp(steps), extent[axis_at] // blocks).reshape((-1,) + (1,) * (len(extent) - 1 - axis_at))
    return level


def scatter_about(own_key, shape, scale, limit, cuts=(), held_as=jnp.bfloat16):
    level = levels(own_key, shape, cuts, -0.22, 0.18) if cuts else 1.0
    drawn = jax.random.normal(own_key, shape, jnp.float32) * scale * level
    return jnp.minimum(jnp.maximum(drawn, -limit), limit).astype(held_as)


def bell_draw_with(rng, extent, scale, reach, cuts, heavy, held_as=jnp.bfloat16):
    entries = scale * jax.random.normal(rng, extent, jnp.float32)
    if cuts:
        entries = entries * levels(rng, extent, cuts, -0.22, 0.18)
    return jnp.clip(with_spikes(entries, jax.random.fold_in(rng, 3), *heavy), -reach, reach).astype(held_as)


def setup_inputs(seed: int = 0) -> dict:
    seeds = jax.random.split(jax.random.key(seed), 6)
    return {
        "projections": draw_projections(jax.random.fold_in(seeds[5], 71), 0),
        "output_gradient": bell_draw_with(seeds[1], (TOKENS, D), 0.125, 0.75, ((0, 8), (1, 4)), (0, 1, 8, 2.0)),
        "output_projection_weight": scatter_about(seeds[2], (D, HEADS * DH), (D // 64) ** -0.5, 0.625, ((1, 4),)),
        "kept_token_indices": draw_kept_token_indices(jax.random.fold_in(seeds[5], 71), 0),
        "surviving_token_count": draw_surviving_token_count(jax.random.fold_in(seeds[5], 71), 0),
    }


def head_major(matrix):
    return matrix.reshape(matrix.shape[0], HEADS, DH).transpose(1, 0, 2)

def reference(projections, output_gradient, output_projection_weight, kept_token_indices, surviving_token_count):
    slot_total = N_SEQ * CAP
    slot_index = jnp.arange(slot_total, dtype=jnp.int32)
    owning_shard = slot_index // CAP
    inside_shard_index = slot_index % CAP
    slot_is_alive = inside_shard_index < surviving_token_count[owning_shard]
    local_index = kept_token_indices.reshape(slot_total).astype(jnp.int32)
    token_row = owning_shard * TOK_DEV + jnp.maximum(local_index, 0)
    packed = jnp.where(slot_is_alive[:, None, None], projections[token_row], jnp.zeros((), jnp.bfloat16))
    grad_rows = jnp.where(slot_is_alive[:, None], output_gradient[token_row], jnp.zeros((), jnp.bfloat16))
    grad_attn = jnp.dot(grad_rows, output_projection_weight, preferred_element_type=jnp.float32).astype(jnp.bfloat16)
    allowed = slot_is_alive[None, :] & (slot_index[None, :] <= slot_index[:, None])
    score_scale = 1.0 / math.sqrt(DH)

    def per_head(operands):
        query, key_mat, value_mat, grad_head = operands
        scores = jnp.dot(query, key_mat.T, preferred_element_type=jnp.float32) * score_scale
        scores = jnp.where(allowed, scores, -1e+30)
        row_peak = lax.optimization_barrier(jnp.max(scores, axis=1, keepdims=True))
        weights = jnp.where(allowed, jnp.exp(scores - row_peak), 0.0)
        probabilities = weights / lax.optimization_barrier(jnp.sum(weights, axis=1, keepdims=True))
        probs_low = probabilities.astype(jnp.bfloat16)
        attended = jnp.dot(probs_low, value_mat, preferred_element_type=jnp.float32)
        grad_probs = jnp.dot(grad_head, value_mat.T, preferred_element_type=jnp.float32)
        row_dot = lax.optimization_barrier(jnp.sum(grad_head.astype(jnp.float32) * attended, axis=1, keepdims=True))
        grad_scores = (probabilities * (grad_probs - row_dot)).astype(jnp.bfloat16)
        grad_query = (jnp.dot(grad_scores, key_mat, preferred_element_type=jnp.float32) * score_scale).astype(jnp.bfloat16)
        grad_key = (jnp.dot(grad_scores.T, query, preferred_element_type=jnp.float32) * score_scale).astype(jnp.bfloat16)
        grad_value = jnp.dot(probs_low.T, grad_head, preferred_element_type=jnp.float32).astype(jnp.bfloat16)
        return (grad_query, grad_key, grad_value, attended.astype(jnp.bfloat16))
    results = lax.map(per_head, (head_major(packed[:, 0]), head_major(packed[:, 1]), head_major(packed[:, 2]), head_major(grad_attn)))

    def to_rows_layout(stacked):
        return stacked.transpose(1, 0, 2).reshape(slot_total, HEADS * DH)
    grad_query = to_rows_layout(results[0])
    grad_key = to_rows_layout(results[1])
    grad_value = to_rows_layout(results[2])
    attended_low = to_rows_layout(results[3])
    weight_grad = jnp.dot(grad_rows.T, attended_low, preferred_element_type=jnp.float32)
    grad_packed = jnp.stack([grad_query, grad_key, grad_value], axis=1)
    target = jnp.where(slot_is_alive, token_row, N_SEQ * TOK_DEV).astype(jnp.int32)
    projection_grad = jnp.zeros((N_SEQ * TOK_DEV, 3, HEADS * DH), jnp.bfloat16).at[target].set(grad_packed, mode='drop')
    return (projection_grad, weight_grad)
```

```python
import functools
import math

import jax
import jax.numpy as jnp
from jax import lax
from jax.experimental import pallas as pl
from jax.experimental.pallas import tpu as pltpu
from jax.sharding import PartitionSpec as P

DH = 128
QUERY_BLOCK = 256
VMEM_BYTES = 48 * 1024 * 1024
F32 = jnp.float32
BF16 = jnp.bfloat16


def params():
    return pltpu.CompilerParams(vmem_limit_bytes=VMEM_BYTES)


def dot(left, right):
    return jnp.dot(left, right, preferred_element_type=F32)


def dot_rows(left, right):
    return lax.dot_general(left, right, (((0,), (0,)), ((), ())), preferred_element_type=F32)


def dot_cols(left, right):
    return lax.dot_general(left, right, (((1,), (1,)), ((), ())), preferred_element_type=F32)


def token_selector(index_ref, tokens):
    slots = index_ref.shape[1]
    token = lax.broadcasted_iota(jnp.int32, (tokens, slots), 0)
    return jnp.where(token == index_ref[...], 1.0, 0.0).astype(BF16)


def pack_grad_kernel(index_ref, grad_ref, out_ref):
    selector = token_selector(index_ref, grad_ref.shape[0])
    out_ref[...] = dot_rows(selector, grad_ref[...]).astype(BF16)


def pack_grad(index, grad):
    slots = index.shape[1]
    return pl.pallas_call(
        pack_grad_kernel,
        out_shape=jax.ShapeDtypeStruct((slots, grad.shape[1]), BF16),
        compiler_params=params(),
    )(index, grad)


def pack_heads_kernel(index_ref, proj_ref, out_ref):
    selector = token_selector(index_ref, proj_ref.shape[1])
    for which in range(3):
        rows = dot_rows(selector, proj_ref[which]).astype(BF16)
        for head in range(out_ref.shape[0]):
            out_ref[head, :, which * DH : (which + 1) * DH] = rows[:, head * DH : (head + 1) * DH]


def pack_heads(index, proj):
    slots = index.shape[1]
    _, tokens, width = proj.shape
    heads = width // DH
    step = 2
    return pl.pallas_call(
        pack_heads_kernel,
        grid=(heads // step,),
        in_specs=[
            pl.BlockSpec((1, slots), lambda i: (0, 0)),
            pl.BlockSpec((3, tokens, step * DH), lambda i: (0, 0, i)),
        ],
        out_specs=pl.BlockSpec((step, slots, 3 * DH), lambda i: (i, 0, 0)),
        out_shape=jax.ShapeDtypeStruct((heads, slots, 3 * DH), BF16),
        compiler_params=params(),
    )(index, proj)


def unpack_heads_kernel(index_ref, rows_ref, out_ref):
    selector = token_selector(index_ref, out_ref.shape[1])
    for head in range(rows_ref.shape[0]):
        tokens = dot(selector, rows_ref[head]).astype(BF16)
        for which in range(3):
            out_ref[which, :, head * DH : (head + 1) * DH] = tokens[
                :, which * DH : (which + 1) * DH
            ]


def unpack_heads(index, rows, tokens):
    heads, slots, _ = rows.shape
    step = 2
    return pl.pallas_call(
        unpack_heads_kernel,
        grid=(heads // step,),
        in_specs=[
            pl.BlockSpec((1, slots), lambda i: (0, 0)),
            pl.BlockSpec((step, slots, 3 * DH), lambda i: (i, 0, 0)),
        ],
        out_specs=pl.BlockSpec((3, tokens, step * DH), lambda i: (0, 0, i)),
        out_shape=jax.ShapeDtypeStruct((3, tokens, heads * DH), BF16),
        compiler_params=params(),
    )(index, rows)


def grad_attn_kernel(rows_ref, weight_ref, out_ref):
    product = dot(rows_ref[...], weight_ref[...]).astype(BF16)
    for head in range(out_ref.shape[0]):
        out_ref[head] = product[:, head * DH : (head + 1) * DH]


def grad_attn_heads(rows, weight):
    slots, depth = rows.shape
    heads = weight.shape[1] // DH
    step = 2
    return pl.pallas_call(
        grad_attn_kernel,
        grid=(heads // step,),
        in_specs=[
            pl.BlockSpec((slots, depth), lambda i: (0, 0)),
            pl.BlockSpec((depth, step * DH), lambda i: (0, i)),
        ],
        out_specs=pl.BlockSpec((step, slots, DH), lambda i: (i, 0, 0)),
        out_shape=jax.ShapeDtypeStruct((heads, slots, DH), BF16),
        compiler_params=params(),
    )(rows, weight)


def weight_grad_kernel(rows_ref, attended_ref, out_ref):
    attended = jnp.concatenate([attended_ref[head] for head in range(attended_ref.shape[0])], axis=1)
    out_ref[...] = dot_rows(rows_ref[...], attended)


def weight_grad_heads(rows, attended):
    total, width = rows.shape
    heads = attended.shape[0]
    step = 2
    return pl.pallas_call(
        weight_grad_kernel,
        grid=(heads // step,),
        in_specs=[
            pl.BlockSpec((total, width), lambda i: (0, 0)),
            pl.BlockSpec((step, total, DH), lambda i: (i, 0, 0)),
        ],
        out_specs=pl.BlockSpec((width, step * DH), lambda i: (0, i)),
        out_shape=jax.ShapeDtypeStruct((width, heads * DH), F32),
        compiler_params=params(),
    )(rows, attended)


def attention_kernel(
    slots,
    part_rows,
    part_ref,
    live_ref,
    query_ref,
    grad_ref,
    key_ref,
    value_ref,
    attended_ref,
    query_grad_ref,
    key_grad_ref,
    value_grad_ref,
    key_total,
    value_total,
):
    scale = 1.0 / math.sqrt(DH)
    rows_total = query_ref.shape[0]
    keys_total = key_ref.shape[0]
    quarters = slots // part_rows
    key_flip = key_ref[...].T
    value_flip = value_ref[...].T
    for start in range(0, rows_total, QUERY_BLOCK):
        rows = slice(start, start + QUERY_BLOCK)
        last = start + QUERY_BLOCK - 1
        last_pos = last // part_rows * slots + (quarters - 1) * part_rows + last % part_rows
        first_pos = start // part_rows * slots + start % part_rows
        keys = min(-(-(last_pos + 1) // 128) * 128, keys_total)
        clear = first_pos // 128 * 128
        query = query_ref[rows]
        grad = grad_ref[rows]
        row = start + lax.broadcasted_iota(jnp.int32, (1, QUERY_BLOCK), 1)
        if quarters > 1:
            shard = row // part_rows
            row = shard * slots + part_ref[0] * part_rows + row - shard * part_rows
        scores = dot_cols(key_ref[:keys], query) * scale + live_ref[:keys, :1]
        key_pos = clear + lax.broadcasted_iota(jnp.int32, (keys - clear, 1), 0)
        edge = jnp.where(key_pos <= row, scores[clear:], -1e30)
        scores = jnp.concatenate([scores[:clear], edge], axis=0) if clear else edge
        peak = jnp.max(scores, axis=0, keepdims=True)
        weights = jnp.exp(scores - peak)
        probs = weights * (1.0 / jnp.sum(weights, axis=0, keepdims=True))
        probs_low = probs.astype(BF16)
        attended = dot(value_flip[:, :keys], probs_low)
        attended_ref[rows] = attended.T.astype(BF16)
        row_dot = jnp.sum(grad.T.astype(F32) * attended, axis=0, keepdims=True)
        grad_probs = dot_cols(value_ref[:keys], grad)
        grad_scores = (probs * (grad_probs - row_dot)).astype(BF16)
        query_grad = dot(key_flip[:, :keys], grad_scores) * scale
        query_grad_ref[rows] = query_grad.T.astype(BF16)
        key_part = dot(grad_scores, query)
        value_part = dot(probs_low, grad)
        prev = start - 1
        reached = 0
        if start:
            prev_pos = prev // part_rows * slots + (quarters - 1) * part_rows + prev % part_rows
            reached = min(-(-(prev_pos + 1) // 128) * 128, keys_total)
        if reached:
            key_total[:reached] += key_part[:reached]
            value_total[:reached] += value_part[:reached]
        if keys > reached:
            key_total[reached:keys] = key_part[reached:]
            value_total[reached:keys] = value_part[reached:]
    key_grad_ref[...] = (key_total[...] * scale).astype(key_grad_ref.dtype)
    value_grad_ref[...] = value_total[...].astype(value_grad_ref.dtype)


def attention(part, live, query, grad, key, value, slots, part_rows, key_type):
    rows, keys = query.shape[0], key.shape[0]
    vmem = pl.BlockSpec(memory_space=pltpu.VMEM)
    return pl.pallas_call(
        functools.partial(attention_kernel, slots, part_rows),
        in_specs=[pl.BlockSpec(memory_space=pltpu.SMEM)] + [vmem] * 5,
        out_specs=[vmem] * 4,
        out_shape=[
            jax.ShapeDtypeStruct((rows, DH), BF16),
            jax.ShapeDtypeStruct((rows, DH), BF16),
            jax.ShapeDtypeStruct((keys, DH), key_type),
            jax.ShapeDtypeStruct((keys, DH), key_type),
        ],
        scratch_shapes=[pltpu.VMEM((keys, DH), F32)] * 2,
        compiler_params=params(),
    )(part, live, query, grad, key, value)


def on_device(
    projections,
    output_gradient,
    output_projection_weight,
    kept_token_indices,
    surviving_token_count,
):
    tok_dev = projections.shape[0]
    group_width = projections.shape[2]
    slots = kept_token_indices.shape[1]
    heads = group_width // DH
    seq_count = lax.axis_size("seq")
    head_count = lax.axis_size("head")
    quarters = seq_count // heads
    part_rows = slots // quarters
    part = (lax.axis_index("seq") % quarters).astype(jnp.int32).reshape(1)
    index = kept_token_indices
    keys = seq_count * slots

    grad_local = pack_grad(index, output_gradient)
    grad_rows = lax.all_gather(grad_local, "head", axis=1, tiled=True)
    packed = pack_heads(index, projections.transpose(1, 0, 2))

    position = jnp.arange(slots, dtype=jnp.int32)
    live = position[None, :] < surviving_token_count[:, None]
    live = jnp.where(live, 0.0, -1e30).astype(F32).reshape(keys, 1)
    live = jnp.broadcast_to(live, (keys, DH))

    def swap(blocks):
        return lax.all_to_all(blocks, "seq", split_axis=0, concat_axis=0, tiled=True)

    if quarters == 1:
        arrived = swap(packed).reshape(keys, 3 * DH)
        query, key, value = (arrived[:, n * DH : (n + 1) * DH] for n in range(3))
    else:
        query = swap(packed[:, :, :DH].reshape(seq_count, part_rows, DH))
        query = query.reshape(seq_count * part_rows, DH)
        sides = jnp.broadcast_to(packed[:, None, :, DH:], (heads, quarters, slots, 2 * DH))
        sides = swap(sides.reshape(seq_count, slots, 2 * DH)).reshape(keys, 2 * DH)
        key, value = sides[:, :DH], sides[:, DH:]

    grad_heads = grad_attn_heads(grad_rows, output_projection_weight)
    grad_in = swap(grad_heads.reshape(seq_count, part_rows, DH)).reshape(-1, DH)

    width = grad_rows.shape[1] // seq_count
    piece = slots // head_count
    mine = lax.dynamic_slice_in_dim(grad_rows, lax.axis_index("head") * piece, piece, 0)
    mine = swap(mine.reshape(piece, seq_count, width).transpose(1, 0, 2))
    all_rows = lax.all_gather(mine, "head", axis=1, tiled=True)

    key_type = BF16 if quarters == 1 else F32
    attended, query_grad, key_grad, value_grad = attention(
        part, live, query, grad_in, key, value, slots, part_rows, key_type
    )

    gathered = lax.all_gather(attended, "seq", axis=0).reshape(heads, keys, DH)
    all_rows = all_rows.reshape(seq_count, quarters, part_rows, width).transpose(1, 0, 2, 3)
    weight_grad = weight_grad_heads(all_rows.reshape(keys, width), gathered)

    if quarters == 1:
        back = jnp.concatenate([query_grad, key_grad, value_grad], axis=1)
        home = swap(back.reshape(seq_count, slots, 3 * DH))
    else:
        query_home = swap(query_grad.reshape(seq_count, part_rows, DH)).reshape(heads, slots, DH)
        back = jnp.concatenate([key_grad, value_grad], axis=1)
        key_home = swap(back.reshape(seq_count, slots, 2 * DH))
        key_home = jnp.sum(key_home.reshape(heads, quarters, slots, 2 * DH), axis=1)
        home = jnp.concatenate([query_home, key_home.astype(BF16)], axis=2)
    projection_grad = unpack_heads(index, home, tok_dev).transpose(1, 0, 2)
    return (projection_grad, weight_grad)


def solution(mesh):
    return jax.shard_map(
        on_device,
        mesh=mesh,
        in_specs=(P("seq", None, "head"), P("seq", "head"), P(None, "head"), P("seq", None), P()),
        out_specs=(P("seq", None, "head"), P("seq", "head")),
        check_vma=False,
    )
```

```python
import functools
import math

import jax
import jax.numpy as jnp
from jax import lax
from jax.experimental import pallas as pl
from jax.experimental.pallas import tpu as pltpu
from jax.sharding import PartitionSpec as P

DH = 128
QUERY_BLOCK = 256
VMEM_BYTES = 48 * 1024 * 1024
F32 = jnp.float32
BF16 = jnp.bfloat16


def params():
    return pltpu.CompilerParams(vmem_limit_bytes=VMEM_BYTES)


def dot(left, right):
    return jnp.dot(left, right, preferred_element_type=F32)


def dot_rows(left, right):
    return lax.dot_general(left, right, (((0,), (0,)), ((), ())), preferred_element_type=F32)


def dot_cols(left, right):
    return lax.dot_general(left, right, (((1,), (1,)), ((), ())), preferred_element_type=F32)


def token_selector(index_ref, tokens):
    slots = index_ref.shape[1]
    token = lax.broadcasted_iota(jnp.int32, (tokens, slots), 0)
    return jnp.where(token == index_ref[...], 1.0, 0.0).astype(BF16)


def pack_grad_kernel(index_ref, grad_ref, out_ref):
    selector = token_selector(index_ref, grad_ref.shape[0])
    out_ref[...] = dot_rows(selector, grad_ref[...]).astype(BF16)


def pack_grad(index, grad):
    slots = index.shape[1]
    return pl.pallas_call(
        pack_grad_kernel,
        out_shape=jax.ShapeDtypeStruct((slots, grad.shape[1]), BF16),
        compiler_params=params(),
    )(index, grad)


def pack_heads_kernel(index_ref, proj_ref, out_ref):
    selector = token_selector(index_ref, proj_ref.shape[1])
    for which in range(3):
        rows = dot_rows(selector, proj_ref[which]).astype(BF16)
        for head in range(out_ref.shape[0]):
            out_ref[head, :, which * DH : (which + 1) * DH] = rows[:, head * DH : (head + 1) * DH]


def pack_heads(index, proj):
    slots = index.shape[1]
    _, tokens, width = proj.shape
    heads = width // DH
    step = 2
    return pl.pallas_call(
        pack_heads_kernel,
        grid=(heads // step,),
        in_specs=[
            pl.BlockSpec((1, slots), lambda i: (0, 0)),
            pl.BlockSpec((3, tokens, step * DH), lambda i: (0, 0, i)),
        ],
        out_specs=pl.BlockSpec((step, slots, 3 * DH), lambda i: (i, 0, 0)),
        out_shape=jax.ShapeDtypeStruct((heads, slots, 3 * DH), BF16),
        compiler_params=params(),
    )(index, proj)


def unpack_heads_kernel(index_ref, rows_ref, out_ref):
    selector = token_selector(index_ref, out_ref.shape[1])
    for head in range(rows_ref.shape[0]):
        tokens = dot(selector, rows_ref[head]).astype(BF16)
        for which in range(3):
            out_ref[which, :, head * DH : (head + 1) * DH] = tokens[
                :, which * DH : (which + 1) * DH
            ]


def unpack_heads(index, rows, tokens):
    heads, slots, _ = rows.shape
    step = 2
    return pl.pallas_call(
        unpack_heads_kernel,
        grid=(heads // step,),
        in_specs=[
            pl.BlockSpec((1, slots), lambda i: (0, 0)),
            pl.BlockSpec((step, slots, 3 * DH), lambda i: (i, 0, 0)),
        ],
        out_specs=pl.BlockSpec((3, tokens, step * DH), lambda i: (0, 0, i)),
        out_shape=jax.ShapeDtypeStruct((3, tokens, heads * DH), BF16),
        compiler_params=params(),
    )(index, rows)


def grad_attn_kernel(rows_ref, weight_ref, out_ref):
    product = dot(rows_ref[...], weight_ref[...]).astype(BF16)
    for head in range(out_ref.shape[0]):
        out_ref[head] = product[:, head * DH : (head + 1) * DH]


def grad_attn_heads(rows, weight):
    slots, depth = rows.shape
    heads = weight.shape[1] // DH
    step = 2
    return pl.pallas_call(
        grad_attn_kernel,
        grid=(heads // step,),
        in_specs=[
            pl.BlockSpec((slots, depth), lambda i: (0, 0)),
            pl.BlockSpec((depth, step * DH), lambda i: (0, i)),
        ],
        out_specs=pl.BlockSpec((step, slots, DH), lambda i: (i, 0, 0)),
        out_shape=jax.ShapeDtypeStruct((heads, slots, DH), BF16),
        compiler_params=params(),
    )(rows, weight)


def weight_grad_kernel(rows_ref, attended_ref, out_ref):
    attended = jnp.concatenate([attended_ref[head] for head in range(attended_ref.shape[0])], axis=1)
    out_ref[...] = dot_rows(rows_ref[...], attended)


def weight_grad_heads(rows, attended):
    total, width = rows.shape
    heads = attended.shape[0]
    step = 2
    return pl.pallas_call(
        weight_grad_kernel,
        grid=(heads // step,),
        in_specs=[
            pl.BlockSpec((total, width), lambda i: (0, 0)),
            pl.BlockSpec((step, total, DH), lambda i: (i, 0, 0)),
        ],
        out_specs=pl.BlockSpec((width, step * DH), lambda i: (0, i)),
        out_shape=jax.ShapeDtypeStruct((width, heads * DH), F32),
        compiler_params=params(),
    )(rows, attended)


def attention_kernel(
    slots,
    part_rows,
    part_ref,
    live_ref,
    query_ref,
    grad_ref,
    key_ref,
    value_ref,
    attended_ref,
    query_grad_ref,
    key_grad_ref,
    value_grad_ref,
    key_total,
    value_total,
):
    scale = 1.0 / math.sqrt(DH)
    rows_total = query_ref.shape[0]
    keys_total = key_ref.shape[0]
    quarters = slots // part_rows
    key_flip = key_ref[...].T
    value_flip = value_ref[...].T
    for start in range(0, rows_total, QUERY_BLOCK):
        rows = slice(start, start + QUERY_BLOCK)
        last = start + QUERY_BLOCK - 1
        last_pos = last // part_rows * slots + (quarters - 1) * part_rows + last % part_rows
        first_pos = start // part_rows * slots + start % part_rows
        keys = min(-(-(last_pos + 1) // 128) * 128, keys_total)
        clear = first_pos // 128 * 128
        query = query_ref[rows]
        grad = grad_ref[rows]
        row = start + lax.broadcasted_iota(jnp.int32, (1, QUERY_BLOCK), 1)
        if quarters > 1:
            shard = row // part_rows
            row = shard * slots + part_ref[0] * part_rows + row - shard * part_rows
        scores = dot_cols(key_ref[:keys], query) * scale + live_ref[:keys, :1]
        key_pos = clear + lax.broadcasted_iota(jnp.int32, (keys - clear, 1), 0)
        edge = jnp.where(key_pos <= row, scores[clear:], -1e30)
        scores = jnp.concatenate([scores[:clear], edge], axis=0) if clear else edge
        peak = jnp.max(scores, axis=0, keepdims=True)
        weights = jnp.exp(scores - peak)
        probs = weights * (1.0 / jnp.sum(weights, axis=0, keepdims=True))
        probs_low = probs.astype(BF16)
        attended = dot(value_flip[:, :keys], probs_low)
        attended_ref[rows] = attended.T.astype(BF16)
        row_dot = jnp.sum(grad.T.astype(F32) * attended, axis=0, keepdims=True)
        grad_probs = dot_cols(value_ref[:keys], grad)
        grad_scores = (probs * (grad_probs - row_dot)).astype(BF16)
        query_grad = dot(key_flip[:, :keys], grad_scores) * scale
        query_grad_ref[rows] = query_grad.T.astype(BF16)
        key_part = dot(grad_scores, query)
        value_part = dot(probs_low, grad)
        prev = start - 1
        reached = 0
        if start:
            prev_pos = prev // part_rows * slots + (quarters - 1) * part_rows + prev % part_rows
            reached = min(-(-(prev_pos + 1) // 128) * 128, keys_total)
        if reached:
            key_total[:reached] += key_part[:reached]
            value_total[:reached] += value_part[:reached]
        if keys > reached:
            key_total[reached:keys] = key_part[reached:]
            value_total[reached:keys] = value_part[reached:]
    key_grad_ref[...] = (key_total[...] * scale).astype(key_grad_ref.dtype)
    value_grad_ref[...] = value_total[...].astype(value_grad_ref.dtype)


def attention(part, live, query, grad, key, value, slots, part_rows, key_type):
    rows, keys = query.shape[0], key.shape[0]
    vmem = pl.BlockSpec(memory_space=pltpu.VMEM)
    return pl.pallas_call(
        functools.partial(attention_kernel, slots, part_rows),
        in_specs=[pl.BlockSpec(memory_space=pltpu.SMEM)] + [vmem] * 5,
        out_specs=[vmem] * 4,
        out_shape=[
            jax.ShapeDtypeStruct((rows, DH), BF16),
            jax.ShapeDtypeStruct((rows, DH), BF16),
            jax.ShapeDtypeStruct((keys, DH), key_type),
            jax.ShapeDtypeStruct((keys, DH), key_type),
        ],
        scratch_shapes=[pltpu.VMEM((keys, DH), F32)] * 2,
        compiler_params=params(),
    )(part, live, query, grad, key, value)


def on_device_split_heads(
    projections,
    output_gradient,
    output_projection_weight,
    kept_token_indices,
    surviving_token_count,
):
    tok_dev = projections.shape[0]
    group_width = projections.shape[2]
    slots = kept_token_indices.shape[1]
    heads = group_width // DH
    seq_count = lax.axis_size("seq")
    head_count = lax.axis_size("head")
    quarters = seq_count // heads
    part_rows = slots // quarters
    part = (lax.axis_index("seq") % quarters).astype(jnp.int32).reshape(1)
    index = kept_token_indices
    keys = seq_count * slots

    grad_local = pack_grad(index, output_gradient)
    grad_rows = lax.all_gather(grad_local, "head", axis=1, tiled=True)
    packed = pack_heads(index, projections.transpose(1, 0, 2))

    position = jnp.arange(slots, dtype=jnp.int32)
    live = position[None, :] < surviving_token_count[:, None]
    live = jnp.where(live, 0.0, -1e30).astype(F32).reshape(keys, 1)
    live = jnp.broadcast_to(live, (keys, DH))

    def swap(blocks):
        return lax.all_to_all(blocks, "seq", split_axis=0, concat_axis=0, tiled=True)

    if quarters == 1:
        arrived = swap(packed).reshape(keys, 3 * DH)
        query, key, value = (arrived[:, n * DH : (n + 1) * DH] for n in range(3))
    else:
        query = swap(packed[:, :, :DH].reshape(seq_count, part_rows, DH))
        query = query.reshape(seq_count * part_rows, DH)
        sides = jnp.broadcast_to(packed[:, None, :, DH:], (heads, quarters, slots, 2 * DH))
        sides = swap(sides.reshape(seq_count, slots, 2 * DH)).reshape(keys, 2 * DH)
        key, value = sides[:, :DH], sides[:, DH:]

    grad_heads = grad_attn_heads(grad_rows, output_projection_weight)
    grad_in = swap(grad_heads.reshape(seq_count, part_rows, DH)).reshape(-1, DH)

    width = grad_rows.shape[1] // seq_count
    piece = slots // head_count
    mine = lax.dynamic_slice_in_dim(grad_rows, lax.axis_index("head") * piece, piece, 0)
    mine = swap(mine.reshape(piece, seq_count, width).transpose(1, 0, 2))
    all_rows = lax.all_gather(mine, "head", axis=1, tiled=True)

    key_type = BF16 if quarters == 1 else F32
    attended, query_grad, key_grad, value_grad = attention(
        part, live, query, grad_in, key, value, slots, part_rows, key_type
    )

    gathered = lax.all_gather(attended, "seq", axis=0).reshape(heads, keys, DH)
    all_rows = all_rows.reshape(seq_count, quarters, part_rows, width).transpose(1, 0, 2, 3)
    weight_grad = weight_grad_heads(all_rows.reshape(keys, width), gathered)

    if quarters == 1:
        back = jnp.concatenate([query_grad, key_grad, value_grad], axis=1)
        home = swap(back.reshape(seq_count, slots, 3 * DH))
    else:
        query_home = swap(query_grad.reshape(seq_count, part_rows, DH)).reshape(heads, slots, DH)
        back = jnp.concatenate([key_grad, value_grad], axis=1)
        key_home = swap(back.reshape(seq_count, slots, 2 * DH))
        key_home = jnp.sum(key_home.reshape(heads, quarters, slots, 2 * DH), axis=1)
        home = jnp.concatenate([query_home, key_home.astype(BF16)], axis=2)
    projection_grad = unpack_heads(index, home, tok_dev).transpose(1, 0, 2)
    return (projection_grad, weight_grad)


def swap_blocks(blocks, axis):
    count = len(blocks)
    return [blocks[0]] + [
        lax.ppermute(blocks[step], axis, [(i, i ^ step) for i in range(count)])
        for step in range(1, count)
    ]


def gather_blocks(block, axis, bits):
    count = lax.axis_size(axis)
    held = {0: block}
    for bit in bits:
        pairs = [(i, i ^ bit) for i in range(count)]
        held.update({step ^ bit: lax.ppermute(held[step], axis, pairs) for step in list(held)})
    return [held[step] for step in range(count)]


def pack_swap_kernel(place_ref, index_ref, proj_ref, *out_refs):
    selector = token_selector(index_ref, proj_ref.shape[1])
    for step, out_ref in enumerate(out_refs):
        head = pl.multiple_of((place_ref[0] ^ step) * DH, DH)
        for which in range(3):
            rows = dot_rows(selector, proj_ref[which, :, pl.ds(head, DH)])
            out_ref[:, which * DH : (which + 1) * DH] = rows.astype(BF16)


SMEM_SPEC = pl.BlockSpec(memory_space=pltpu.SMEM)
VMEM_SPEC = pl.BlockSpec(memory_space=pltpu.VMEM)


def pack_swap(place, index, proj):
    slots = index.shape[1]
    _, tokens, width = proj.shape
    heads = width // DH
    block = jax.ShapeDtypeStruct((slots, 3 * DH), BF16)
    return pl.pallas_call(
        pack_swap_kernel,
        in_specs=[SMEM_SPEC, VMEM_SPEC, VMEM_SPEC],
        out_specs=[VMEM_SPEC] * heads,
        out_shape=[block] * heads,
        compiler_params=params(),
        cost_estimate=pl.CostEstimate(
            flops=2 * slots * tokens * 3 * width, bytes_accessed=8 * tokens * width, transcendentals=0
        ),
    )(place, index, proj)


def unpack_swap_kernel(place_ref, index_ref, *refs):
    block_refs, out_ref = refs[:-1], refs[-1]
    selector = token_selector(index_ref, out_ref.shape[1])
    for step, block_ref in enumerate(block_refs):
        head = pl.multiple_of((place_ref[0] ^ step) * DH, DH)
        tokens = dot(selector, block_ref[...]).astype(BF16)
        for which in range(3):
            out_ref[which, :, pl.ds(head, DH)] = tokens[:, which * DH : (which + 1) * DH]


def unpack_swap(place, index, blocks, tokens):
    heads = len(blocks)
    slots = index.shape[1]
    return pl.pallas_call(
        unpack_swap_kernel,
        in_specs=[SMEM_SPEC] + [VMEM_SPEC] * (1 + heads),
        out_specs=VMEM_SPEC,
        out_shape=jax.ShapeDtypeStruct((3, tokens, heads * DH), BF16),
        compiler_params=params(),
        cost_estimate=pl.CostEstimate(
            flops=2 * slots * tokens * 3 * heads * DH,
            bytes_accessed=8 * tokens * heads * DH,
            transcendentals=0,
        ),
    )(place, index, *blocks)


def grad_swap_kernel(count, seq_count, place_ref, *refs):
    row_refs, weight_ref = refs[:count], refs[count]
    out_refs = refs[count + 1 : count + 1 + seq_count]
    piece_refs = refs[count + 1 + seq_count : count + 1 + 2 * seq_count]
    total, staged = refs[-2:]
    me, mine = place_ref[0], place_ref[1]
    piece, width = piece_refs[0].shape
    per_block = row_refs[0].shape[1] // width
    for step in range(count):

        @pl.when(pl.program_id(0) == step)
        def _(step=step):
            part = dot(row_refs[step][...], weight_ref[...])
            total[...] = part if step == 0 else total[...] + part
            start = pl.multiple_of(mine * piece, piece)
            staged[mine ^ step] = row_refs[step][pl.ds(start, piece), :]

    @pl.when(pl.program_id(0) == count - 1)
    def _():
        for step in range(seq_count):
            partner = me ^ step
            out_refs[step][...] = total[:, pl.ds(pl.multiple_of(partner * DH, DH), DH)].astype(BF16)
            column = pl.multiple_of(partner % per_block * width, DH)
            piece_refs[step][...] = staged[partner // per_block, :, pl.ds(column, width)]


def grad_swap(place, blocks, weight, seq_count):
    count = len(blocks)
    slots, depth = blocks[0].shape
    width = count * depth // seq_count
    piece = slots // count
    columns = weight.shape[1]
    whole = pl.BlockSpec((slots, depth), lambda i, place: (0, 0))
    return pl.pallas_call(
        functools.partial(grad_swap_kernel, count, seq_count),
        grid_spec=pltpu.PrefetchScalarGridSpec(
            num_scalar_prefetch=1,
            grid=(count,),
            in_specs=[whole] * count
            + [pl.BlockSpec((depth, columns), lambda i, place: (place[1] ^ i, 0))],
            out_specs=[pl.BlockSpec((slots, DH), lambda i, place: (0, 0))] * seq_count
            + [pl.BlockSpec((piece, width), lambda i, place: (0, 0))] * seq_count,
            scratch_shapes=[
                pltpu.VMEM((slots, columns), F32),
                pltpu.VMEM((count, piece, depth), BF16),
            ],
        ),
        out_shape=[jax.ShapeDtypeStruct((slots, DH), BF16)] * seq_count
        + [jax.ShapeDtypeStruct((piece, width), BF16)] * seq_count,
        compiler_params=params(),
        cost_estimate=pl.CostEstimate(
            flops=2 * slots * count * depth * columns,
            bytes_accessed=2 * count * depth * columns,
            transcendentals=0,
        ),
    )(place, *blocks, weight)


def weight_grad_swap_kernel(head_count, seq_count, place_ref, *refs):
    row_refs = refs[:head_count]
    attended_refs = refs[head_count : head_count + seq_count]
    out_ref, rows = refs[-2:]
    me, mine = place_ref[0], place_ref[1]
    _, piece, _ = row_refs[0].shape
    slots = piece * head_count
    for part in range(head_count):
        for step in range(seq_count):
            start = pl.multiple_of((me ^ step) * slots + (mine ^ part) * piece, piece)
            rows[pl.ds(start, piece), :] = row_refs[part][step]
    for step in range(0, seq_count, 2):
        pair = jnp.concatenate([attended_refs[step][...], attended_refs[step + 1][...]], axis=1)
        product = dot_rows(rows[...], pair)
        for side in range(2):
            column = pl.multiple_of((me ^ (step + side)) * DH, DH)
            out_ref[:, pl.ds(column, DH)] = product[:, side * DH : (side + 1) * DH]


def weight_grad_swap(place, row_blocks, attended):
    head_count, seq_count = len(row_blocks), len(attended)
    _, _, width = row_blocks[0].shape
    keys = attended[0].shape[0]
    return pl.pallas_call(
        functools.partial(weight_grad_swap_kernel, head_count, seq_count),
        in_specs=[SMEM_SPEC] + [VMEM_SPEC] * (head_count + seq_count),
        out_specs=VMEM_SPEC,
        out_shape=jax.ShapeDtypeStruct((width, seq_count * DH), F32),
        scratch_shapes=[pltpu.VMEM((keys, width), BF16)],
        compiler_params=params(),
        cost_estimate=pl.CostEstimate(
            flops=2 * keys * width * seq_count * DH,
            bytes_accessed=8 * keys * DH * seq_count,
            transcendentals=0,
        ),
    )(place, *row_blocks, *attended)


def masked_scores(start, keys, key_ref, query, live_ref):
    scores = dot_cols(key_ref[:keys], query) * (1.0 / math.sqrt(DH)) + live_ref[:keys, :1]
    row = start + lax.broadcasted_iota(jnp.int32, (1, QUERY_BLOCK), 1)
    key_pos = start + lax.broadcasted_iota(jnp.int32, (QUERY_BLOCK, 1), 0)
    edge = jnp.where(key_pos <= row, scores[start:], -1e30)
    return jnp.concatenate([scores[:start], edge], axis=0) if start else edge


def forward_kernel(seq_count, place_ref, live_ref, *refs):
    block_refs = refs[:seq_count]
    attended_ref, query_ref, key_ref, value_ref, flip_ref, stat_ref = refs[seq_count:]
    slots = block_refs[0].shape[0]
    for step in range(seq_count):
        here = pl.ds(pl.multiple_of((place_ref[0] ^ step) * slots, slots), slots)
        for which, ref in enumerate((query_ref, key_ref, value_ref)):
            ref[here, :] = block_refs[step][:, which * DH : (which + 1) * DH]
    value_flip = value_ref[...].T
    for start in range(0, query_ref.shape[0], QUERY_BLOCK):
        rows = slice(start, start + QUERY_BLOCK)
        keys = start + QUERY_BLOCK
        scores = masked_scores(start, keys, key_ref, query_ref[rows], live_ref)
        peak = jnp.max(scores, axis=0, keepdims=True)
        weights = jnp.exp(scores - peak)
        inverse = 1.0 / jnp.sum(weights, axis=0, keepdims=True)
        attended = dot(value_flip[:, :keys], (weights * inverse).astype(BF16))
        attended_ref[rows] = attended.T.astype(BF16)
        flip_ref[:, rows] = attended
        stat_ref[0:1, rows] = peak
        stat_ref[1:2, rows] = inverse


def attention_cost(keys, dots):
    return pl.CostEstimate(
        flops=dots * keys * keys * DH, bytes_accessed=16 * keys * DH, transcendentals=keys * keys // 2
    )


def forward(place, live, blocks):
    seq_count = len(blocks)
    keys = seq_count * blocks[0].shape[0]
    rows = jax.ShapeDtypeStruct((keys, DH), BF16)
    return pl.pallas_call(
        functools.partial(forward_kernel, seq_count),
        in_specs=[SMEM_SPEC] + [VMEM_SPEC] * (1 + seq_count),
        out_specs=[VMEM_SPEC] * 6,
        out_shape=[rows] * 4
        + [jax.ShapeDtypeStruct((DH, keys), F32), jax.ShapeDtypeStruct((8, keys), F32)],
        compiler_params=params(),
        cost_estimate=attention_cost(keys, 2),
    )(place, live, *blocks)


def backward_kernel(seq_count, place_ref, live_ref, query_ref, key_ref, value_ref, flip_ref, stat_ref, *refs):
    grad_refs, out_refs = refs[:seq_count], refs[seq_count : 2 * seq_count]
    grad_ref, query_total, key_total, value_total = refs[2 * seq_count :]
    slots = grad_refs[0].shape[0]
    scale = 1.0 / math.sqrt(DH)
    for step in range(seq_count):
        here = pl.ds(pl.multiple_of((place_ref[0] ^ step) * slots, slots), slots)
        grad_ref[here, :] = grad_refs[step][...]
    key_flip = key_ref[...].T
    for start in range(0, query_ref.shape[0], QUERY_BLOCK):
        rows = slice(start, start + QUERY_BLOCK)
        keys = start + QUERY_BLOCK
        query = query_ref[rows]
        grad = grad_ref[rows]
        scores = masked_scores(start, keys, key_ref, query, live_ref)
        probs = jnp.exp(scores - stat_ref[0:1, rows]) * stat_ref[1:2, rows]
        probs_low = probs.astype(BF16)
        row_dot = jnp.sum(grad.T.astype(F32) * flip_ref[:, rows], axis=0, keepdims=True)
        grad_probs = dot_cols(value_ref[:keys], grad)
        grad_scores = (probs * (grad_probs - row_dot)).astype(BF16)
        query_total[rows] = (dot(key_flip[:, :keys], grad_scores) * scale).T.astype(BF16)
        key_part = dot(grad_scores, query)
        value_part = dot(probs_low, grad)
        if start:
            key_total[:start] += key_part[:start]
            value_total[:start] += value_part[:start]
        key_total[rows] = key_part[start:]
        value_total[rows] = value_part[start:]
    for step in range(seq_count):
        here = pl.ds(pl.multiple_of((place_ref[0] ^ step) * slots, slots), slots)
        out_refs[step][:, :DH] = query_total[here, :]
        out_refs[step][:, DH : 2 * DH] = (key_total[here, :] * scale).astype(BF16)
        out_refs[step][:, 2 * DH :] = value_total[here, :].astype(BF16)


def backward(place, live, query, key, value, flip, stats, grads):
    seq_count = len(grads)
    keys = query.shape[0]
    return pl.pallas_call(
        functools.partial(backward_kernel, seq_count),
        in_specs=[SMEM_SPEC] + [VMEM_SPEC] * (6 + seq_count),
        out_specs=[VMEM_SPEC] * seq_count,
        out_shape=[jax.ShapeDtypeStruct((keys // seq_count, 3 * DH), BF16)] * seq_count,
        scratch_shapes=[pltpu.VMEM((keys, DH), BF16)] * 2 + [pltpu.VMEM((keys, DH), F32)] * 2,
        compiler_params=params(),
        cost_estimate=attention_cost(keys, 5),
    )(place, live, query, key, value, flip, stats, *grads)


def live_bias(counts, slots):
    position = jnp.arange(slots, dtype=jnp.int32)
    live = position[None, :] < counts[:, None]
    live = jnp.where(live, 0.0, -1e30).astype(F32).reshape(-1, 1)
    return jnp.broadcast_to(live, (live.shape[0], DH))


def on_device_whole_heads(
    projections,
    output_gradient,
    output_projection_weight,
    kept_token_indices,
    surviving_token_count,
):
    tok_dev = projections.shape[0]
    slots = kept_token_indices.shape[1]
    seq_count = lax.axis_size("seq")
    head_count = lax.axis_size("head")
    index = kept_token_indices
    place = jnp.stack([lax.axis_index("seq"), lax.axis_index("head")]).astype(jnp.int32)
    seq_bits = [1 << bit for bit in reversed(range(seq_count.bit_length() - 1))]
    head_bits = [1 << bit for bit in reversed(range(head_count.bit_length() - 1))]

    grad_local = pack_grad(index, output_gradient)
    grad_blocks = gather_blocks(grad_local, "head", head_bits)
    packed = pack_swap(place, index, projections.transpose(1, 0, 2))
    arrived = swap_blocks(packed, "seq")
    sent = grad_swap(place, grad_blocks, output_projection_weight, seq_count)
    grads_in = swap_blocks(sent[:seq_count], "seq")
    pieces = swap_blocks(sent[seq_count:], "seq")

    live = live_bias(surviving_token_count, slots)
    attended, query, key, value, flip, stats = forward(place, live, arrived)
    gathered = gather_blocks(attended, "seq", seq_bits)
    back = backward(place, live, query, key, value, flip, stats, grads_in)
    home = swap_blocks(back, "seq")

    row_blocks = gather_blocks(jnp.stack(pieces), "head", head_bits)
    weight_grad = weight_grad_swap(place, row_blocks, gathered)
    projection_grad = unpack_swap(place, index, home, tok_dev).transpose(1, 0, 2)
    return (projection_grad, weight_grad)


def on_device(projections, output_gradient, weight, index, counts):
    heads = projections.shape[2] // DH
    seq_count, head_count = lax.axis_size("seq"), lax.axis_size("head")
    width = output_gradient.shape[1] * head_count // seq_count
    whole = seq_count == heads and seq_count % 2 == 0 and width % DH == 0
    powers = seq_count & (seq_count - 1) == 0 and head_count & (head_count - 1) == 0
    body = on_device_whole_heads if whole and powers else on_device_split_heads
    return body(projections, output_gradient, weight, index, counts)


def solution(mesh):
    return jax.shard_map(
        on_device,
        mesh=mesh,
        in_specs=(P("seq", None, "head"), P("seq", "head"), P(None, "head"), P("seq", None), P()),
        out_specs=(P("seq", None, "head"), P("seq", "head")),
        check_vma=False,
    )
```

```python
import functools
import math

import jax
import jax.numpy as jnp
from jax import lax
from jax.experimental import pallas as pl
from jax.experimental.pallas import tpu as pltpu
from jax.sharding import PartitionSpec as P

DH = 128
QUERY_BLOCK = 256
VMEM_BYTES = 48 * 1024 * 1024
F32 = jnp.float32
BF16 = jnp.bfloat16


def params():
    return pltpu.CompilerParams(vmem_limit_bytes=VMEM_BYTES)


def dot(left, right):
    return jnp.dot(left, right, preferred_element_type=F32)


def dot_rows(left, right):
    return lax.dot_general(left, right, (((0,), (0,)), ((), ())), preferred_element_type=F32)


def dot_cols(left, right):
    return lax.dot_general(left, right, (((1,), (1,)), ((), ())), preferred_element_type=F32)


def token_selector(index_ref, tokens):
    slots = index_ref.shape[1]
    token = lax.broadcasted_iota(jnp.int32, (tokens, slots), 0)
    return jnp.where(token == index_ref[...], 1.0, 0.0).astype(BF16)


def pack_grad_kernel(index_ref, grad_ref, out_ref):
    selector = token_selector(index_ref, grad_ref.shape[0])
    out_ref[...] = dot_rows(selector, grad_ref[...]).astype(BF16)


def pack_grad(index, grad):
    slots = index.shape[1]
    return pl.pallas_call(
        pack_grad_kernel,
        out_shape=jax.ShapeDtypeStruct((slots, grad.shape[1]), BF16),
        compiler_params=params(),
    )(index, grad)


def pack_heads_kernel(index_ref, proj_ref, out_ref):
    selector = token_selector(index_ref, proj_ref.shape[1])
    for which in range(3):
        rows = dot_rows(selector, proj_ref[which]).astype(BF16)
        for head in range(out_ref.shape[0]):
            out_ref[head, :, which * DH : (which + 1) * DH] = rows[:, head * DH : (head + 1) * DH]


def pack_heads(index, proj):
    slots = index.shape[1]
    _, tokens, width = proj.shape
    heads = width // DH
    step = 2
    return pl.pallas_call(
        pack_heads_kernel,
        grid=(heads // step,),
        in_specs=[
            pl.BlockSpec((1, slots), lambda i: (0, 0)),
            pl.BlockSpec((3, tokens, step * DH), lambda i: (0, 0, i)),
        ],
        out_specs=pl.BlockSpec((step, slots, 3 * DH), lambda i: (i, 0, 0)),
        out_shape=jax.ShapeDtypeStruct((heads, slots, 3 * DH), BF16),
        compiler_params=params(),
    )(index, proj)


def unpack_heads_kernel(index_ref, rows_ref, out_ref):
    selector = token_selector(index_ref, out_ref.shape[1])
    for head in range(rows_ref.shape[0]):
        tokens = dot(selector, rows_ref[head]).astype(BF16)
        for which in range(3):
            out_ref[which, :, head * DH : (head + 1) * DH] = tokens[
                :, which * DH : (which + 1) * DH
            ]


def unpack_heads(index, rows, tokens):
    heads, slots, _ = rows.shape
    step = 2
    return pl.pallas_call(
        unpack_heads_kernel,
        grid=(heads // step,),
        in_specs=[
            pl.BlockSpec((1, slots), lambda i: (0, 0)),
            pl.BlockSpec((step, slots, 3 * DH), lambda i: (i, 0, 0)),
        ],
        out_specs=pl.BlockSpec((3, tokens, step * DH), lambda i: (0, 0, i)),
        out_shape=jax.ShapeDtypeStruct((3, tokens, heads * DH), BF16),
        compiler_params=params(),
    )(index, rows)


def grad_attn_kernel(rows_ref, weight_ref, out_ref):
    product = dot(rows_ref[...], weight_ref[...]).astype(BF16)
    for head in range(out_ref.shape[0]):
        out_ref[head] = product[:, head * DH : (head + 1) * DH]


def grad_attn_heads(rows, weight):
    slots, depth = rows.shape
    heads = weight.shape[1] // DH
    step = 2
    return pl.pallas_call(
        grad_attn_kernel,
        grid=(heads // step,),
        in_specs=[
            pl.BlockSpec((slots, depth), lambda i: (0, 0)),
            pl.BlockSpec((depth, step * DH), lambda i: (0, i)),
        ],
        out_specs=pl.BlockSpec((step, slots, DH), lambda i: (i, 0, 0)),
        out_shape=jax.ShapeDtypeStruct((heads, slots, DH), BF16),
        compiler_params=params(),
    )(rows, weight)


def weight_grad_kernel(rows_ref, attended_ref, out_ref):
    attended = jnp.concatenate([attended_ref[head] for head in range(attended_ref.shape[0])], axis=1)
    out_ref[...] = dot_rows(rows_ref[...], attended)


def weight_grad_heads(rows, attended):
    total, width = rows.shape
    heads = attended.shape[0]
    step = 2
    return pl.pallas_call(
        weight_grad_kernel,
        grid=(heads // step,),
        in_specs=[
            pl.BlockSpec((total, width), lambda i: (0, 0)),
            pl.BlockSpec((step, total, DH), lambda i: (i, 0, 0)),
        ],
        out_specs=pl.BlockSpec((width, step * DH), lambda i: (0, i)),
        out_shape=jax.ShapeDtypeStruct((width, heads * DH), F32),
        compiler_params=params(),
    )(rows, attended)


def attention_kernel(
    slots,
    part_rows,
    part_ref,
    live_ref,
    query_ref,
    grad_ref,
    key_ref,
    value_ref,
    attended_ref,
    query_grad_ref,
    key_grad_ref,
    value_grad_ref,
    key_total,
    value_total,
):
    scale = 1.0 / math.sqrt(DH)
    rows_total = query_ref.shape[0]
    keys_total = key_ref.shape[0]
    quarters = slots // part_rows
    key_flip = key_ref[...].T
    value_flip = value_ref[...].T
    for start in range(0, rows_total, QUERY_BLOCK):
        rows = slice(start, start + QUERY_BLOCK)
        last = start + QUERY_BLOCK - 1
        last_pos = last // part_rows * slots + (quarters - 1) * part_rows + last % part_rows
        first_pos = start // part_rows * slots + start % part_rows
        keys = min(-(-(last_pos + 1) // 128) * 128, keys_total)
        clear = first_pos // 128 * 128
        query = query_ref[rows]
        grad = grad_ref[rows]
        row = start + lax.broadcasted_iota(jnp.int32, (1, QUERY_BLOCK), 1)
        if quarters > 1:
            shard = row // part_rows
            row = shard * slots + part_ref[0] * part_rows + row - shard * part_rows
        scores = dot_cols(key_ref[:keys], query) * scale + live_ref[:keys, :1]
        key_pos = clear + lax.broadcasted_iota(jnp.int32, (keys - clear, 1), 0)
        edge = jnp.where(key_pos <= row, scores[clear:], -1e30)
        scores = jnp.concatenate([scores[:clear], edge], axis=0) if clear else edge
        peak = jnp.max(scores, axis=0, keepdims=True)
        weights = jnp.exp(scores - peak)
        probs = weights * (1.0 / jnp.sum(weights, axis=0, keepdims=True))
        probs_low = probs.astype(BF16)
        attended = dot(value_flip[:, :keys], probs_low)
        attended_ref[rows] = attended.T.astype(BF16)
        row_dot = jnp.sum(grad.T.astype(F32) * attended, axis=0, keepdims=True)
        grad_probs = dot_cols(value_ref[:keys], grad)
        grad_scores = (probs * (grad_probs - row_dot)).astype(BF16)
        query_grad = dot(key_flip[:, :keys], grad_scores) * scale
        query_grad_ref[rows] = query_grad.T.astype(BF16)
        key_part = dot(grad_scores, query)
        value_part = dot(probs_low, grad)
        prev = start - 1
        reached = 0
        if start:
            prev_pos = prev // part_rows * slots + (quarters - 1) * part_rows + prev % part_rows
            reached = min(-(-(prev_pos + 1) // 128) * 128, keys_total)
        if reached:
            key_total[:reached] += key_part[:reached]
            value_total[:reached] += value_part[:reached]
        if keys > reached:
            key_total[reached:keys] = key_part[reached:]
            value_total[reached:keys] = value_part[reached:]
    key_grad_ref[...] = (key_total[...] * scale).astype(key_grad_ref.dtype)
    value_grad_ref[...] = value_total[...].astype(value_grad_ref.dtype)


def attention(part, live, query, grad, key, value, slots, part_rows, key_type):
    rows, keys = query.shape[0], key.shape[0]
    vmem = pl.BlockSpec(memory_space=pltpu.VMEM)
    return pl.pallas_call(
        functools.partial(attention_kernel, slots, part_rows),
        in_specs=[pl.BlockSpec(memory_space=pltpu.SMEM)] + [vmem] * 5,
        out_specs=[vmem] * 4,
        out_shape=[
            jax.ShapeDtypeStruct((rows, DH), BF16),
            jax.ShapeDtypeStruct((rows, DH), BF16),
            jax.ShapeDtypeStruct((keys, DH), key_type),
            jax.ShapeDtypeStruct((keys, DH), key_type),
        ],
        scratch_shapes=[pltpu.VMEM((keys, DH), F32)] * 2,
        compiler_params=params(),
    )(part, live, query, grad, key, value)


def on_device_split_heads(
    projections,
    output_gradient,
    output_projection_weight,
    kept_token_indices,
    surviving_token_count,
):
    tok_dev = projections.shape[0]
    group_width = projections.shape[2]
    slots = kept_token_indices.shape[1]
    heads = group_width // DH
    seq_count = lax.axis_size("seq")
    head_count = lax.axis_size("head")
    quarters = seq_count // heads
    part_rows = slots // quarters
    part = (lax.axis_index("seq") % quarters).astype(jnp.int32).reshape(1)
    index = kept_token_indices
    keys = seq_count * slots

    grad_local = pack_grad(index, output_gradient)
    grad_rows = lax.all_gather(grad_local, "head", axis=1, tiled=True)
    packed = pack_heads(index, projections.transpose(1, 0, 2))

    position = jnp.arange(slots, dtype=jnp.int32)
    live = position[None, :] < surviving_token_count[:, None]
    live = jnp.where(live, 0.0, -1e30).astype(F32).reshape(keys, 1)
    live = jnp.broadcast_to(live, (keys, DH))

    def swap(blocks):
        return lax.all_to_all(blocks, "seq", split_axis=0, concat_axis=0, tiled=True)

    if quarters == 1:
        arrived = swap(packed).reshape(keys, 3 * DH)
        query, key, value = (arrived[:, n * DH : (n + 1) * DH] for n in range(3))
    else:
        query = swap(packed[:, :, :DH].reshape(seq_count, part_rows, DH))
        query = query.reshape(seq_count * part_rows, DH)
        sides = jnp.broadcast_to(packed[:, None, :, DH:], (heads, quarters, slots, 2 * DH))
        sides = swap(sides.reshape(seq_count, slots, 2 * DH)).reshape(keys, 2 * DH)
        key, value = sides[:, :DH], sides[:, DH:]

    grad_heads = grad_attn_heads(grad_rows, output_projection_weight)
    grad_in = swap(grad_heads.reshape(seq_count, part_rows, DH)).reshape(-1, DH)

    width = grad_rows.shape[1] // seq_count
    piece = slots // head_count
    mine = lax.dynamic_slice_in_dim(grad_rows, lax.axis_index("head") * piece, piece, 0)
    mine = swap(mine.reshape(piece, seq_count, width).transpose(1, 0, 2))
    all_rows = lax.all_gather(mine, "head", axis=1, tiled=True)

    key_type = BF16 if quarters == 1 else F32
    attended, query_grad, key_grad, value_grad = attention(
        part, live, query, grad_in, key, value, slots, part_rows, key_type
    )

    gathered = lax.all_gather(attended, "seq", axis=0).reshape(heads, keys, DH)
    all_rows = all_rows.reshape(seq_count, quarters, part_rows, width).transpose(1, 0, 2, 3)
    weight_grad = weight_grad_heads(all_rows.reshape(keys, width), gathered)

    if quarters == 1:
        back = jnp.concatenate([query_grad, key_grad, value_grad], axis=1)
        home = swap(back.reshape(seq_count, slots, 3 * DH))
    else:
        query_home = swap(query_grad.reshape(seq_count, part_rows, DH)).reshape(heads, slots, DH)
        back = jnp.concatenate([key_grad, value_grad], axis=1)
        key_home = swap(back.reshape(seq_count, slots, 2 * DH))
        key_home = jnp.sum(key_home.reshape(heads, quarters, slots, 2 * DH), axis=1)
        home = jnp.concatenate([query_home, key_home.astype(BF16)], axis=2)
    projection_grad = unpack_heads(index, home, tok_dev).transpose(1, 0, 2)
    return (projection_grad, weight_grad)


def gather_blocks(block, axis, bits):
    count = lax.axis_size(axis)
    held = {0: block}
    for bit in bits:
        pairs = [(i, i ^ bit) for i in range(count)]
        held.update({step ^ bit: lax.ppermute(held[step], axis, pairs) for step in list(held)})
    return [held[step] for step in range(count)]


SMEM_SPEC = pl.BlockSpec(memory_space=pltpu.SMEM)
VMEM_SPEC = pl.BlockSpec(memory_space=pltpu.VMEM)


def grad_swap_kernel(count, place_ref, *refs):
    row_refs, weight_ref, out_ref, total = refs[:count], refs[count], refs[count + 1], refs[count + 2]
    mine = place_ref[1]
    seq_count, height, _ = out_ref.shape
    slots, depth = row_refs[0].shape
    piece = slots // count
    chunks = (height - slots) // piece
    per_block = depth // (chunks * DH)
    for step in range(count):

        @pl.when(pl.program_id(0) == step)
        def _(step=step):
            part = dot(row_refs[step][...], weight_ref[...])
            total[...] = part if step == 0 else total[...] + part
            share = row_refs[step][pl.ds(pl.multiple_of(mine * piece, piece), piece), :]
            for chunk in range(per_block * chunks):
                partner = (mine ^ step) * per_block + chunk // chunks
                start = slots + chunk % chunks * piece
                out_ref[partner, start : start + piece, :] = share[:, chunk * DH : (chunk + 1) * DH]

    @pl.when(pl.program_id(0) == count - 1)
    def _():
        for head in range(seq_count):
            out_ref[head, :slots, :] = total[:, head * DH : (head + 1) * DH].astype(BF16)


def grad_swap(place, blocks, weight, seq_count):
    count = len(blocks)
    slots, depth = blocks[0].shape
    columns = weight.shape[1]
    height = slots + slots // count * (count * depth // seq_count // DH)
    return pl.pallas_call(
        functools.partial(grad_swap_kernel, count),
        grid_spec=pltpu.PrefetchScalarGridSpec(
            num_scalar_prefetch=1,
            grid=(count,),
            in_specs=[pl.BlockSpec((slots, depth), lambda i, place: (0, 0))] * count
            + [pl.BlockSpec((depth, columns), lambda i, place: (place[1] ^ i, 0))],
            out_specs=pl.BlockSpec((seq_count, height, DH), lambda i, place: (0, 0, 0)),
            scratch_shapes=[pltpu.VMEM((slots, columns), F32)],
        ),
        out_shape=jax.ShapeDtypeStruct((seq_count, height, DH), BF16),
        compiler_params=params(),
        cost_estimate=pl.CostEstimate(
            flops=2 * slots * count * depth * columns,
            bytes_accessed=2 * count * depth * columns,
            transcendentals=0,
        ),
    )(place, *blocks, weight)


def weight_grad_swap_kernel(head_count, seq_count, place_ref, *refs):
    piece_refs = refs[:head_count]
    attended_refs = refs[head_count : head_count + seq_count]
    out_ref, rows = refs[-2:]
    me, mine = place_ref[0], place_ref[1]
    chunks = rows.shape[1] // DH
    piece = piece_refs[0].shape[1] // chunks
    slots = piece * head_count
    for part in range(head_count):
        for shard in range(seq_count):
            here = pl.ds(pl.multiple_of(shard * slots + (mine ^ part) * piece, piece), piece)
            for chunk in range(chunks):
                rows[here, chunk * DH : (chunk + 1) * DH] = piece_refs[part][
                    shard, chunk * piece : (chunk + 1) * piece, :
                ]
    for step in range(0, seq_count, 2):
        pair = jnp.concatenate([attended_refs[step][...], attended_refs[step + 1][...]], axis=1)
        product = dot_rows(rows[...], pair)
        for side in range(2):
            column = pl.multiple_of((me ^ (step + side)) * DH, DH)
            out_ref[:, pl.ds(column, DH)] = product[:, side * DH : (side + 1) * DH]


def weight_grad_swap(place, pieces, attended):
    head_count, seq_count = len(pieces), len(attended)
    keys = attended[0].shape[0]
    width = pieces[0].shape[1] // (keys // seq_count // head_count) * DH
    return pl.pallas_call(
        functools.partial(weight_grad_swap_kernel, head_count, seq_count),
        in_specs=[SMEM_SPEC] + [VMEM_SPEC] * (head_count + seq_count),
        out_specs=VMEM_SPEC,
        out_shape=jax.ShapeDtypeStruct((width, seq_count * DH), F32),
        scratch_shapes=[pltpu.VMEM((keys, width), BF16)],
        compiler_params=params(),
        cost_estimate=pl.CostEstimate(
            flops=2 * keys * width * seq_count * DH,
            bytes_accessed=8 * keys * DH * seq_count,
            transcendentals=0,
        ),
    )(place, *pieces, *attended)


def masked_scores(start, keys, key_ref, query, live_ref):
    scores = dot_cols(key_ref[:keys], query) * (1.0 / math.sqrt(DH)) + live_ref[:keys, :1]
    row = start + lax.broadcasted_iota(jnp.int32, (1, QUERY_BLOCK), 1)
    key_pos = start + lax.broadcasted_iota(jnp.int32, (QUERY_BLOCK, 1), 0)
    edge = jnp.where(key_pos <= row, scores[start:], -1e30)
    return jnp.concatenate([scores[:start], edge], axis=0) if start else edge


def forward_kernel(
    live_ref, block_ref, attended_ref, query_ref, key_ref, value_ref, flip_ref, stat_ref
):
    seq_count, slots, _ = block_ref.shape
    for shard in range(seq_count):
        here = slice(shard * slots, (shard + 1) * slots)
        for which, ref in enumerate((query_ref, key_ref, value_ref)):
            ref[here] = block_ref[shard, :, which * DH : (which + 1) * DH]
    value_flip = value_ref[...].T
    for start in range(0, query_ref.shape[0], QUERY_BLOCK):
        rows = slice(start, start + QUERY_BLOCK)
        keys = start + QUERY_BLOCK
        scores = masked_scores(start, keys, key_ref, query_ref[rows], live_ref)
        peak = jnp.max(scores, axis=0, keepdims=True)
        weights = jnp.exp(scores - peak)
        inverse = 1.0 / jnp.sum(weights, axis=0, keepdims=True)
        attended = dot(value_flip[:, :keys], (weights * inverse).astype(BF16))
        attended_ref[rows] = attended.T.astype(BF16)
        flip_ref[:, rows] = attended
        stat_ref[0:1, rows] = peak
        stat_ref[1:2, rows] = inverse


def attention_cost(keys, dots):
    return pl.CostEstimate(
        flops=dots * keys * keys * DH, bytes_accessed=16 * keys * DH, transcendentals=keys * keys // 2
    )


def forward(live, blocks):
    keys = blocks.shape[0] * blocks.shape[1]
    rows = jax.ShapeDtypeStruct((keys, DH), BF16)
    return pl.pallas_call(
        forward_kernel,
        in_specs=[VMEM_SPEC] * 2,
        out_specs=[VMEM_SPEC] * 6,
        out_shape=[rows] * 4
        + [jax.ShapeDtypeStruct((DH, keys), F32), jax.ShapeDtypeStruct((8, keys), F32)],
        compiler_params=params(),
        cost_estimate=attention_cost(keys, 2),
    )(live, blocks)


def backward_kernel(
    live_ref,
    query_ref,
    key_ref,
    value_ref,
    flip_ref,
    stat_ref,
    grads_ref,
    out_ref,
    grad_ref,
    query_total,
    key_total,
    value_total,
):
    seq_count, slots, _ = out_ref.shape
    scale = 1.0 / math.sqrt(DH)
    for shard in range(seq_count):
        grad_ref[shard * slots : (shard + 1) * slots] = grads_ref[shard, :slots]
    key_flip = key_ref[...].T
    for start in range(0, query_ref.shape[0], QUERY_BLOCK):
        rows = slice(start, start + QUERY_BLOCK)
        keys = start + QUERY_BLOCK
        query = query_ref[rows]
        grad = grad_ref[rows]
        scores = masked_scores(start, keys, key_ref, query, live_ref)
        probs = jnp.exp(scores - stat_ref[0:1, rows]) * stat_ref[1:2, rows]
        probs_low = probs.astype(BF16)
        row_dot = jnp.sum(grad.T.astype(F32) * flip_ref[:, rows], axis=0, keepdims=True)
        grad_probs = dot_cols(value_ref[:keys], grad)
        grad_scores = (probs * (grad_probs - row_dot)).astype(BF16)
        query_total[rows] = (dot(key_flip[:, :keys], grad_scores) * scale).T.astype(BF16)
        key_part = dot(grad_scores, query)
        value_part = dot(probs_low, grad)
        if start:
            key_total[:start] += key_part[:start]
            value_total[:start] += value_part[:start]
        key_total[rows] = key_part[start:]
        value_total[rows] = value_part[start:]
    for shard in range(seq_count):
        here = slice(shard * slots, (shard + 1) * slots)
        out_ref[shard, :, :DH] = query_total[here]
        out_ref[shard, :, DH : 2 * DH] = (key_total[here] * scale).astype(BF16)
        out_ref[shard, :, 2 * DH :] = value_total[here].astype(BF16)


def backward(live, query, key, value, flip, stats, grads):
    seq_count = grads.shape[0]
    keys = query.shape[0]
    return pl.pallas_call(
        backward_kernel,
        in_specs=[VMEM_SPEC] * 7,
        out_specs=VMEM_SPEC,
        out_shape=jax.ShapeDtypeStruct((seq_count, keys // seq_count, 3 * DH), BF16),
        scratch_shapes=[pltpu.VMEM((keys, DH), BF16)] * 2 + [pltpu.VMEM((keys, DH), F32)] * 2,
        compiler_params=params(),
        cost_estimate=attention_cost(keys, 5),
    )(live, query, key, value, flip, stats, grads)


def live_bias(counts, slots):
    position = jnp.arange(slots, dtype=jnp.int32)
    live = position[None, :] < counts[:, None]
    live = jnp.where(live, 0.0, -1e30).astype(F32).reshape(-1, 1)
    return jnp.broadcast_to(live, (live.shape[0], DH))


def on_device_whole_heads(
    projections,
    output_gradient,
    output_projection_weight,
    kept_token_indices,
    surviving_token_count,
):
    tok_dev = projections.shape[0]
    slots = kept_token_indices.shape[1]
    seq_count = lax.axis_size("seq")
    head_count = lax.axis_size("head")
    index = kept_token_indices
    place = jnp.stack([lax.axis_index("seq"), lax.axis_index("head")]).astype(jnp.int32)
    seq_bits = [1 << bit for bit in reversed(range(seq_count.bit_length() - 1))]
    head_bits = [1 << bit for bit in reversed(range(head_count.bit_length() - 1))]

    grad_local = pack_grad(index, output_gradient)
    grad_blocks = gather_blocks(grad_local, "head", head_bits)
    packed = pack_heads(index, projections.transpose(1, 0, 2))
    live = live_bias(surviving_token_count, slots)

    def swap(blocks):
        return lax.all_to_all(blocks, "seq", split_axis=0, concat_axis=0, tiled=True)

    arrived = swap(packed)
    grads = swap(grad_swap(place, grad_blocks, output_projection_weight, seq_count))
    attended, query, key, value, flip, stats = forward(live, arrived)
    gathered = gather_blocks(attended, "seq", seq_bits)
    pieces = gather_blocks(grads[:, slots:], "head", head_bits)
    home = swap(backward(live, query, key, value, flip, stats, grads))
    weight_grad = weight_grad_swap(place, pieces, gathered)
    projection_grad = unpack_heads(index, home, tok_dev).transpose(1, 0, 2)
    return (projection_grad, weight_grad)


def on_device(projections, output_gradient, weight, index, counts):
    heads = projections.shape[2] // DH
    seq_count, head_count = lax.axis_size("seq"), lax.axis_size("head")
    width = output_gradient.shape[1] * head_count // seq_count
    whole = seq_count == heads and seq_count % 2 == 0 and width % DH == 0
    powers = seq_count & (seq_count - 1) == 0 and head_count & (head_count - 1) == 0
    body = on_device_whole_heads if whole and powers else on_device_split_heads
    return body(projections, output_gradient, weight, index, counts)


def solution(mesh):
    return jax.shard_map(
        on_device,
        mesh=mesh,
        in_specs=(P("seq", None, "head"), P("seq", "head"), P(None, "head"), P("seq", None), P()),
        out_specs=(P("seq", None, "head"), P("seq", "head")),
        check_vma=False,
    )
```

```python
import functools
import math

import jax
import jax.numpy as jnp
from jax import lax
from jax.experimental import pallas as pl
from jax.experimental.pallas import tpu as pltpu
from jax.sharding import PartitionSpec as P

DH = 128
QUERY_BLOCK = 256
VMEM_BYTES = 20 * 1024 * 1024
F32 = jnp.float32
BF16 = jnp.bfloat16


def params():
    return pltpu.CompilerParams(vmem_limit_bytes=VMEM_BYTES)


def dot(left, right):
    return jnp.dot(left, right, preferred_element_type=F32)


def dot_rows(left, right):
    return lax.dot_general(left, right, (((0,), (0,)), ((), ())), preferred_element_type=F32)


def dot_cols(left, right):
    return lax.dot_general(left, right, (((1,), (1,)), ((), ())), preferred_element_type=F32)


def token_selector(index_ref, tokens):
    slots = index_ref.shape[1]
    token = lax.broadcasted_iota(jnp.int32, (tokens, slots), 0)
    return jnp.where(token == index_ref[...], 1.0, 0.0).astype(BF16)


def pack_grad_kernel(index_ref, grad_ref, out_ref):
    selector = token_selector(index_ref, grad_ref.shape[0])
    out_ref[...] = dot_rows(selector, grad_ref[...]).astype(BF16)


def pack_grad(index, grad):
    slots = index.shape[1]
    return pl.pallas_call(
        pack_grad_kernel,
        out_shape=jax.ShapeDtypeStruct((slots, grad.shape[1]), BF16),
        compiler_params=params(),
    )(index, grad)


def pack_heads_kernel(index_ref, proj_ref, out_ref):
    selector = token_selector(index_ref, proj_ref.shape[1])
    for which in range(3):
        rows = dot_rows(selector, proj_ref[which]).astype(BF16)
        for head in range(out_ref.shape[0]):
            out_ref[head, :, which * DH : (which + 1) * DH] = rows[:, head * DH : (head + 1) * DH]


def pack_heads(index, proj):
    slots = index.shape[1]
    _, tokens, width = proj.shape
    heads = width // DH
    step = 2
    return pl.pallas_call(
        pack_heads_kernel,
        grid=(heads // step,),
        in_specs=[
            pl.BlockSpec((1, slots), lambda i: (0, 0)),
            pl.BlockSpec((3, tokens, step * DH), lambda i: (0, 0, i)),
        ],
        out_specs=pl.BlockSpec((step, slots, 3 * DH), lambda i: (i, 0, 0)),
        out_shape=jax.ShapeDtypeStruct((heads, slots, 3 * DH), BF16),
        compiler_params=params(),
    )(index, proj)


def unpack_heads_kernel(index_ref, rows_ref, out_ref):
    selector = token_selector(index_ref, out_ref.shape[1])
    for head in range(rows_ref.shape[0]):
        tokens = dot(selector, rows_ref[head]).astype(BF16)
        for which in range(3):
            out_ref[which, :, head * DH : (head + 1) * DH] = tokens[
                :, which * DH : (which + 1) * DH
            ]


def unpack_heads(index, rows, tokens):
    heads, slots, _ = rows.shape
    step = 2
    return pl.pallas_call(
        unpack_heads_kernel,
        grid=(heads // step,),
        in_specs=[
            pl.BlockSpec((1, slots), lambda i: (0, 0)),
            pl.BlockSpec((step, slots, 3 * DH), lambda i: (i, 0, 0)),
        ],
        out_specs=pl.BlockSpec((3, tokens, step * DH), lambda i: (0, 0, i)),
        out_shape=jax.ShapeDtypeStruct((3, tokens, heads * DH), BF16),
        compiler_params=params(),
    )(index, rows)


def grad_attn_kernel(rows_ref, weight_ref, out_ref):
    product = dot(rows_ref[...], weight_ref[...]).astype(BF16)
    for head in range(out_ref.shape[0]):
        out_ref[head] = product[:, head * DH : (head + 1) * DH]


def grad_attn_heads(rows, weight):
    slots, depth = rows.shape
    heads = weight.shape[1] // DH
    step = 2
    return pl.pallas_call(
        grad_attn_kernel,
        grid=(heads // step,),
        in_specs=[
            pl.BlockSpec((slots, depth), lambda i: (0, 0)),
            pl.BlockSpec((depth, step * DH), lambda i: (0, i)),
        ],
        out_specs=pl.BlockSpec((step, slots, DH), lambda i: (i, 0, 0)),
        out_shape=jax.ShapeDtypeStruct((heads, slots, DH), BF16),
        compiler_params=params(),
    )(rows, weight)


def weight_grad_kernel(rows_ref, attended_ref, out_ref):
    attended = jnp.concatenate([attended_ref[head] for head in range(attended_ref.shape[0])], axis=1)
    out_ref[...] = dot_rows(rows_ref[...], attended)


def weight_grad_heads(rows, attended):
    total, width = rows.shape
    heads = attended.shape[0]
    step = 2
    return pl.pallas_call(
        weight_grad_kernel,
        grid=(heads // step,),
        in_specs=[
            pl.BlockSpec((total, width), lambda i: (0, 0)),
            pl.BlockSpec((step, total, DH), lambda i: (i, 0, 0)),
        ],
        out_specs=pl.BlockSpec((width, step * DH), lambda i: (0, i)),
        out_shape=jax.ShapeDtypeStruct((width, heads * DH), F32),
        compiler_params=params(),
    )(rows, attended)


def attention_kernel(
    slots,
    part_rows,
    part_ref,
    live_ref,
    query_ref,
    grad_ref,
    key_ref,
    value_ref,
    attended_ref,
    query_grad_ref,
    key_grad_ref,
    value_grad_ref,
    key_total,
    value_total,
):
    scale = 1.0 / math.sqrt(DH)
    rows_total = query_ref.shape[0]
    keys_total = key_ref.shape[0]
    quarters = slots // part_rows
    key_flip = key_ref[...].T
    value_flip = value_ref[...].T
    for start in range(0, rows_total, QUERY_BLOCK):
        rows = slice(start, start + QUERY_BLOCK)
        last = start + QUERY_BLOCK - 1
        last_pos = last // part_rows * slots + (quarters - 1) * part_rows + last % part_rows
        first_pos = start // part_rows * slots + start % part_rows
        keys = min(-(-(last_pos + 1) // 128) * 128, keys_total)
        clear = first_pos // 128 * 128
        query = query_ref[rows]
        grad = grad_ref[rows]
        row = start + lax.broadcasted_iota(jnp.int32, (1, QUERY_BLOCK), 1)
        if quarters > 1:
            shard = row // part_rows
            row = shard * slots + part_ref[0] * part_rows + row - shard * part_rows
        scores = dot_cols(key_ref[:keys], query) * scale + live_ref[:keys, :1]
        key_pos = clear + lax.broadcasted_iota(jnp.int32, (keys - clear, 1), 0)
        edge = jnp.where(key_pos <= row, scores[clear:], -1e30)
        scores = jnp.concatenate([scores[:clear], edge], axis=0) if clear else edge
        peak = jnp.max(scores, axis=0, keepdims=True)
        weights = jnp.exp(scores - peak)
        probs = weights * (1.0 / jnp.sum(weights, axis=0, keepdims=True))
        probs_low = probs.astype(BF16)
        attended = dot(value_flip[:, :keys], probs_low)
        attended_ref[rows] = attended.T.astype(BF16)
        row_dot = jnp.sum(grad.T.astype(F32) * attended, axis=0, keepdims=True)
        grad_probs = dot_cols(value_ref[:keys], grad)
        grad_scores = (probs * (grad_probs - row_dot)).astype(BF16)
        query_grad = dot(key_flip[:, :keys], grad_scores) * scale
        query_grad_ref[rows] = query_grad.T.astype(BF16)
        key_part = dot(grad_scores, query)
        value_part = dot(probs_low, grad)
        prev = start - 1
        reached = 0
        if start:
            prev_pos = prev // part_rows * slots + (quarters - 1) * part_rows + prev % part_rows
            reached = min(-(-(prev_pos + 1) // 128) * 128, keys_total)
        if reached:
            key_total[:reached] += key_part[:reached]
            value_total[:reached] += value_part[:reached]
        if keys > reached:
            key_total[reached:keys] = key_part[reached:]
            value_total[reached:keys] = value_part[reached:]
    key_grad_ref[...] = (key_total[...] * scale).astype(key_grad_ref.dtype)
    value_grad_ref[...] = value_total[...].astype(value_grad_ref.dtype)


def attention(part, live, query, grad, key, value, slots, part_rows, key_type):
    rows, keys = query.shape[0], key.shape[0]
    vmem = pl.BlockSpec(memory_space=pltpu.VMEM)
    return pl.pallas_call(
        functools.partial(attention_kernel, slots, part_rows),
        in_specs=[pl.BlockSpec(memory_space=pltpu.SMEM)] + [vmem] * 5,
        out_specs=[vmem] * 4,
        out_shape=[
            jax.ShapeDtypeStruct((rows, DH), BF16),
            jax.ShapeDtypeStruct((rows, DH), BF16),
            jax.ShapeDtypeStruct((keys, DH), key_type),
            jax.ShapeDtypeStruct((keys, DH), key_type),
        ],
        scratch_shapes=[pltpu.VMEM((keys, DH), F32)] * 2,
        compiler_params=params(),
    )(part, live, query, grad, key, value)


def on_device_split_heads(
    projections,
    output_gradient,
    output_projection_weight,
    kept_token_indices,
    surviving_token_count,
):
    tok_dev = projections.shape[0]
    group_width = projections.shape[2]
    slots = kept_token_indices.shape[1]
    heads = group_width // DH
    seq_count = lax.axis_size("seq")
    head_count = lax.axis_size("head")
    quarters = seq_count // heads
    part_rows = slots // quarters
    part = (lax.axis_index("seq") % quarters).astype(jnp.int32).reshape(1)
    index = kept_token_indices
    keys = seq_count * slots

    grad_local = pack_grad(index, output_gradient)
    grad_rows = lax.all_gather(grad_local, "head", axis=1, tiled=True)
    packed = pack_heads(index, projections.transpose(1, 0, 2))

    position = jnp.arange(slots, dtype=jnp.int32)
    live = position[None, :] < surviving_token_count[:, None]
    live = jnp.where(live, 0.0, -1e30).astype(F32).reshape(keys, 1)
    live = jnp.broadcast_to(live, (keys, DH))

    def swap(blocks):
        return lax.all_to_all(blocks, "seq", split_axis=0, concat_axis=0, tiled=True)

    if quarters == 1:
        arrived = swap(packed).reshape(keys, 3 * DH)
        query, key, value = (arrived[:, n * DH : (n + 1) * DH] for n in range(3))
    else:
        query = swap(packed[:, :, :DH].reshape(seq_count, part_rows, DH))
        query = query.reshape(seq_count * part_rows, DH)
        sides = jnp.broadcast_to(packed[:, None, :, DH:], (heads, quarters, slots, 2 * DH))
        sides = swap(sides.reshape(seq_count, slots, 2 * DH)).reshape(keys, 2 * DH)
        key, value = sides[:, :DH], sides[:, DH:]

    grad_heads = grad_attn_heads(grad_rows, output_projection_weight)
    grad_in = swap(grad_heads.reshape(seq_count, part_rows, DH)).reshape(-1, DH)

    width = grad_rows.shape[1] // seq_count
    piece = slots // head_count
    mine = lax.dynamic_slice_in_dim(grad_rows, lax.axis_index("head") * piece, piece, 0)
    mine = swap(mine.reshape(piece, seq_count, width).transpose(1, 0, 2))
    all_rows = lax.all_gather(mine, "head", axis=1, tiled=True)

    key_type = BF16 if quarters == 1 else F32
    attended, query_grad, key_grad, value_grad = attention(
        part, live, query, grad_in, key, value, slots, part_rows, key_type
    )

    gathered = lax.all_gather(attended, "seq", axis=0).reshape(heads, keys, DH)
    all_rows = all_rows.reshape(seq_count, quarters, part_rows, width).transpose(1, 0, 2, 3)
    weight_grad = weight_grad_heads(all_rows.reshape(keys, width), gathered)

    if quarters == 1:
        back = jnp.concatenate([query_grad, key_grad, value_grad], axis=1)
        home = swap(back.reshape(seq_count, slots, 3 * DH))
    else:
        query_home = swap(query_grad.reshape(seq_count, part_rows, DH)).reshape(heads, slots, DH)
        back = jnp.concatenate([key_grad, value_grad], axis=1)
        key_home = swap(back.reshape(seq_count, slots, 2 * DH))
        key_home = jnp.sum(key_home.reshape(heads, quarters, slots, 2 * DH), axis=1)
        home = jnp.concatenate([query_home, key_home.astype(BF16)], axis=2)
    projection_grad = unpack_heads(index, home, tok_dev).transpose(1, 0, 2)
    return (projection_grad, weight_grad)


def exchange(block, axis, bit):
    return lax.ppermute(block, axis, [(i, i ^ bit) for i in range(lax.axis_size(axis))])


def gather_blocks(block, axis, bits, first=None):
    held = {0: block}
    for bit in bits:
        for step in list(held):
            if first is not None and step == 0:
                held[bit] = first[bit]
            else:
                held[step ^ bit] = exchange(held[step], axis, bit)
    return [held[step] for step in range(lax.axis_size(axis))]


SMEM_SPEC = pl.BlockSpec(memory_space=pltpu.SMEM)
VMEM_SPEC = pl.BlockSpec(memory_space=pltpu.VMEM)


def grad_swap_kernel(count, place_ref, *refs):
    row_refs, weight_ref, out_ref, total = refs[:count], refs[count], refs[count + 1], refs[count + 2]
    mine = place_ref[1]
    seq_count, height, _ = out_ref.shape
    slots, depth = row_refs[0].shape
    piece = slots // count
    chunks = (height - slots) // piece
    per_block = depth // (chunks * DH)
    for step in range(count):

        @pl.when(pl.program_id(0) == step)
        def _(step=step):
            part = dot(row_refs[step][...], weight_ref[...])
            total[...] = part if step == 0 else total[...] + part
            share = row_refs[step][pl.ds(pl.multiple_of(mine * piece, piece), piece), :]
            for chunk in range(per_block * chunks):
                partner = (mine ^ step) * per_block + chunk // chunks
                start = slots + chunk % chunks * piece
                out_ref[partner, start : start + piece, :] = share[:, chunk * DH : (chunk + 1) * DH]

    @pl.when(pl.program_id(0) == count - 1)
    def _():
        for head in range(seq_count):
            out_ref[head, :slots, :] = total[:, head * DH : (head + 1) * DH].astype(BF16)


def grad_swap(place, blocks, weight, seq_count):
    count = len(blocks)
    slots, depth = blocks[0].shape
    columns = weight.shape[1]
    height = slots + slots // count * (count * depth // seq_count // DH)
    return pl.pallas_call(
        functools.partial(grad_swap_kernel, count),
        grid_spec=pltpu.PrefetchScalarGridSpec(
            num_scalar_prefetch=1,
            grid=(count,),
            in_specs=[pl.BlockSpec((slots, depth), lambda i, place: (0, 0))] * count
            + [pl.BlockSpec((depth, columns), lambda i, place: (place[1] ^ i, 0))],
            out_specs=pl.BlockSpec((seq_count, height, DH), lambda i, place: (0, 0, 0)),
            scratch_shapes=[pltpu.VMEM((slots, columns), F32)],
        ),
        out_shape=jax.ShapeDtypeStruct((seq_count, height, DH), BF16),
        compiler_params=params(),
        cost_estimate=pl.CostEstimate(
            flops=2 * slots * count * depth * columns,
            bytes_accessed=2 * count * depth * columns,
            transcendentals=0,
        ),
    )(place, *blocks, weight)


def weight_grad_swap_kernel(head_count, seq_count, place_ref, *refs):
    piece_refs = refs[:head_count]
    attended_refs = refs[head_count : head_count + seq_count]
    out_ref, rows = refs[-2:]
    me, mine = place_ref[0], place_ref[1]
    chunks = rows.shape[1] // DH
    piece = piece_refs[0].shape[1] // chunks
    slots = piece * head_count
    for part in range(head_count):
        for shard in range(seq_count):
            here = pl.ds(pl.multiple_of(shard * slots + (mine ^ part) * piece, piece), piece)
            for chunk in range(chunks):
                rows[here, chunk * DH : (chunk + 1) * DH] = piece_refs[part][
                    shard, chunk * piece : (chunk + 1) * piece, :
                ]
    for step in range(0, seq_count, 2):
        pair = jnp.concatenate([attended_refs[step][...], attended_refs[step + 1][...]], axis=1)
        product = dot_rows(rows[...], pair)
        for side in range(2):
            column = pl.multiple_of((me ^ (step + side)) * DH, DH)
            out_ref[:, pl.ds(column, DH)] = product[:, side * DH : (side + 1) * DH]


def weight_grad_swap(place, pieces, attended):
    head_count, seq_count = len(pieces), len(attended)
    keys = attended[0].shape[0]
    width = pieces[0].shape[1] // (keys // seq_count // head_count) * DH
    return pl.pallas_call(
        functools.partial(weight_grad_swap_kernel, head_count, seq_count),
        in_specs=[SMEM_SPEC] + [VMEM_SPEC] * (head_count + seq_count),
        out_specs=VMEM_SPEC,
        out_shape=jax.ShapeDtypeStruct((width, seq_count * DH), F32),
        scratch_shapes=[pltpu.VMEM((keys, width), BF16)],
        compiler_params=params(),
        cost_estimate=pl.CostEstimate(
            flops=2 * keys * width * seq_count * DH,
            bytes_accessed=8 * keys * DH * seq_count,
            transcendentals=0,
        ),
    )(place, *pieces, *attended)


def masked_scores(start, keys, key_ref, query, live_ref):
    scores = dot_cols(key_ref[:keys], query) * (1.0 / math.sqrt(DH)) + live_ref[:keys, :1]
    row = start + lax.broadcasted_iota(jnp.int32, (1, QUERY_BLOCK), 1)
    key_pos = start + lax.broadcasted_iota(jnp.int32, (QUERY_BLOCK, 1), 0)
    edge = jnp.where(key_pos <= row, scores[start:], -1e30)
    return jnp.concatenate([scores[:start], edge], axis=0) if start else edge


def forward_kernel(
    live_ref, block_ref, attended_ref, query_ref, key_ref, value_ref, flip_ref, stat_ref
):
    seq_count, slots, _ = block_ref.shape
    for shard in range(seq_count):
        here = slice(shard * slots, (shard + 1) * slots)
        for which, ref in enumerate((query_ref, key_ref, value_ref)):
            ref[here] = block_ref[shard, :, which * DH : (which + 1) * DH]
    value_flip = value_ref[...].T
    for start in range(0, query_ref.shape[0], QUERY_BLOCK):
        rows = slice(start, start + QUERY_BLOCK)
        keys = start + QUERY_BLOCK
        scores = masked_scores(start, keys, key_ref, query_ref[rows], live_ref)
        peak = jnp.max(scores, axis=0, keepdims=True)
        weights = jnp.exp(scores - peak)
        inverse = 1.0 / jnp.sum(weights, axis=0, keepdims=True)
        attended = dot(value_flip[:, :keys], (weights * inverse).astype(BF16))
        attended_ref[rows] = attended.T.astype(BF16)
        flip_ref[:, rows] = attended
        stat_ref[0:1, rows] = peak
        stat_ref[1:2, rows] = inverse


def attention_cost(keys, dots):
    return pl.CostEstimate(
        flops=dots * keys * keys * DH, bytes_accessed=16 * keys * DH, transcendentals=keys * keys // 2
    )


def forward(live, blocks):
    keys = blocks.shape[0] * blocks.shape[1]
    rows = jax.ShapeDtypeStruct((keys, DH), BF16)
    return pl.pallas_call(
        forward_kernel,
        in_specs=[VMEM_SPEC] * 2,
        out_specs=[VMEM_SPEC] * 6,
        out_shape=[rows] * 4
        + [jax.ShapeDtypeStruct((DH, keys), F32), jax.ShapeDtypeStruct((8, keys), F32)],
        compiler_params=params(),
        cost_estimate=attention_cost(keys, 2),
    )(live, blocks)


def backward_kernel(
    live_ref,
    query_ref,
    key_ref,
    value_ref,
    flip_ref,
    stat_ref,
    grads_ref,
    out_ref,
    grad_ref,
    query_total,
    key_total,
    value_total,
):
    seq_count, slots, _ = out_ref.shape
    scale = 1.0 / math.sqrt(DH)
    for shard in range(seq_count):
        grad_ref[shard * slots : (shard + 1) * slots] = grads_ref[shard, :slots]
    key_flip = key_ref[...].T
    for start in range(0, query_ref.shape[0], QUERY_BLOCK):
        rows = slice(start, start + QUERY_BLOCK)
        keys = start + QUERY_BLOCK
        query = query_ref[rows]
        grad = grad_ref[rows]
        scores = masked_scores(start, keys, key_ref, query, live_ref)
        probs = jnp.exp(scores - stat_ref[0:1, rows]) * stat_ref[1:2, rows]
        probs_low = probs.astype(BF16)
        row_dot = jnp.sum(grad.T.astype(F32) * flip_ref[:, rows], axis=0, keepdims=True)
        grad_probs = dot_cols(value_ref[:keys], grad)
        grad_scores = (probs * (grad_probs - row_dot)).astype(BF16)
        query_total[rows] = (dot(key_flip[:, :keys], grad_scores) * scale).T.astype(BF16)
        key_part = dot(grad_scores, query)
        value_part = dot(probs_low, grad)
        if start:
            key_total[:start] += key_part[:start]
            value_total[:start] += value_part[:start]
        key_total[rows] = key_part[start:]
        value_total[rows] = value_part[start:]
    for shard in range(seq_count):
        here = slice(shard * slots, (shard + 1) * slots)
        out_ref[shard, :, :DH] = query_total[here]
        out_ref[shard, :, DH : 2 * DH] = (key_total[here] * scale).astype(BF16)
        out_ref[shard, :, 2 * DH :] = value_total[here].astype(BF16)


def backward(live, query, key, value, flip, stats, grads):
    seq_count = grads.shape[0]
    keys = query.shape[0]
    return pl.pallas_call(
        backward_kernel,
        in_specs=[VMEM_SPEC] * 7,
        out_specs=VMEM_SPEC,
        out_shape=jax.ShapeDtypeStruct((seq_count, keys // seq_count, 3 * DH), BF16),
        scratch_shapes=[pltpu.VMEM((keys, DH), BF16)] * 2 + [pltpu.VMEM((keys, DH), F32)] * 2,
        compiler_params=params(),
        cost_estimate=attention_cost(keys, 5),
    )(live, query, key, value, flip, stats, grads)


def live_bias(counts, slots):
    position = jnp.arange(slots, dtype=jnp.int32)
    live = position[None, :] < counts[:, None]
    live = jnp.where(live, 0.0, -1e30).astype(F32).reshape(-1, 1)
    return jnp.broadcast_to(live, (live.shape[0], DH))


def on_device_whole_heads(
    projections,
    output_gradient,
    output_projection_weight,
    kept_token_indices,
    surviving_token_count,
):
    tok_dev = projections.shape[0]
    slots = kept_token_indices.shape[1]
    seq_count = lax.axis_size("seq")
    head_count = lax.axis_size("head")
    index = kept_token_indices
    place = jnp.stack([lax.axis_index("seq"), lax.axis_index("head")]).astype(jnp.int32)
    seq_bits = [1 << bit for bit in reversed(range(seq_count.bit_length() - 1))]
    head_bits = [1 << bit for bit in reversed(range(head_count.bit_length() - 1))]

    grad_local = pack_grad(index, output_gradient)
    grad_blocks = gather_blocks(grad_local, "head", head_bits)
    packed = pack_heads(index, projections.transpose(1, 0, 2))
    live = live_bias(surviving_token_count, slots)

    def swap(blocks):
        return lax.all_to_all(blocks, "seq", split_axis=0, concat_axis=0, tiled=True)

    arrived = swap(packed)
    grads = swap(grad_swap(place, grad_blocks, output_projection_weight, seq_count))
    attended, query, key, value, flip, stats = forward(live, arrived)
    first = {bit: exchange(attended, "seq", bit) for bit in seq_bits}
    pieces = gather_blocks(grads[:, slots:], "head", head_bits)
    back = backward(live, query, key, value, flip, stats, grads)
    back, first = lax.optimization_barrier((back, first))
    home = swap(back)
    gathered = gather_blocks(attended, "seq", seq_bits, first)
    weight_grad = weight_grad_swap(place, pieces, gathered)
    projection_grad = unpack_heads(index, home, tok_dev).transpose(1, 0, 2)
    return (projection_grad, weight_grad)


def on_device(projections, output_gradient, weight, index, counts):
    heads = projections.shape[2] // DH
    seq_count, head_count = lax.axis_size("seq"), lax.axis_size("head")
    width = output_gradient.shape[1] * head_count // seq_count
    whole = seq_count == heads and seq_count % 2 == 0 and width % DH == 0
    powers = seq_count & (seq_count - 1) == 0 and head_count & (head_count - 1) == 0
    body = on_device_whole_heads if whole and powers else on_device_split_heads
    return body(projections, output_gradient, weight, index, counts)


def solution(mesh):
    return jax.shard_map(
        on_device,
        mesh=mesh,
        in_specs=(P("seq", None, "head"), P("seq", "head"), P(None, "head"), P("seq", None), P()),
        out_specs=(P("seq", None, "head"), P("seq", "head")),
        check_vma=False,
    )
```

```python
import functools
import math

import jax
import jax.numpy as jnp
from jax import lax
from jax.experimental import pallas as pl
from jax.experimental.pallas import tpu as pltpu
from jax.sharding import PartitionSpec as P

DH = 128
QUERY_BLOCK = 256
VMEM_BYTES = 20 * 1024 * 1024
VMEM_MOST = 62 * 1024 * 1024
F32 = jnp.float32
BF16 = jnp.bfloat16


def params(limit=VMEM_BYTES):
    return pltpu.CompilerParams(vmem_limit_bytes=limit)


def dot(left, right):
    return jnp.dot(left, right, preferred_element_type=F32)


def dot_rows(left, right):
    return lax.dot_general(left, right, (((0,), (0,)), ((), ())), preferred_element_type=F32)


def dot_cols(left, right):
    return lax.dot_general(left, right, (((1,), (1,)), ((), ())), preferred_element_type=F32)


def token_selector(index_ref, tokens):
    slots = index_ref.shape[1]
    token = lax.broadcasted_iota(jnp.int32, (tokens, slots), 0)
    return jnp.where(token == index_ref[...], 1.0, 0.0).astype(BF16)


def pack_grad_kernel(index_ref, grad_ref, out_ref):
    selector = token_selector(index_ref, grad_ref.shape[0])
    out_ref[...] = dot_rows(selector, grad_ref[...]).astype(BF16)


def pack_grad(index, grad):
    slots = index.shape[1]
    return pl.pallas_call(
        pack_grad_kernel,
        out_shape=jax.ShapeDtypeStruct((slots, grad.shape[1]), BF16),
        compiler_params=params(),
    )(index, grad)


def pack_heads_kernel(index_ref, proj_ref, out_ref):
    selector = token_selector(index_ref, proj_ref.shape[1])
    for which in range(3):
        rows = dot_rows(selector, proj_ref[which]).astype(BF16)
        for head in range(out_ref.shape[0]):
            out_ref[head, :, which * DH : (which + 1) * DH] = rows[:, head * DH : (head + 1) * DH]


def pack_heads(index, proj):
    slots = index.shape[1]
    _, tokens, width = proj.shape
    heads = width // DH
    step = 2
    return pl.pallas_call(
        pack_heads_kernel,
        grid=(heads // step,),
        in_specs=[
            pl.BlockSpec((1, slots), lambda i: (0, 0)),
            pl.BlockSpec((3, tokens, step * DH), lambda i: (0, 0, i)),
        ],
        out_specs=pl.BlockSpec((step, slots, 3 * DH), lambda i: (i, 0, 0)),
        out_shape=jax.ShapeDtypeStruct((heads, slots, 3 * DH), BF16),
        compiler_params=params(),
    )(index, proj)


def unpack_heads_kernel(index_ref, rows_ref, out_ref):
    selector = token_selector(index_ref, out_ref.shape[1])
    for head in range(rows_ref.shape[0]):
        tokens = dot(selector, rows_ref[head]).astype(BF16)
        for which in range(3):
            out_ref[which, :, head * DH : (head + 1) * DH] = tokens[
                :, which * DH : (which + 1) * DH
            ]


def unpack_heads(index, rows, tokens):
    heads, slots, _ = rows.shape
    step = 2
    return pl.pallas_call(
        unpack_heads_kernel,
        grid=(heads // step,),
        in_specs=[
            pl.BlockSpec((1, slots), lambda i: (0, 0)),
            pl.BlockSpec((step, slots, 3 * DH), lambda i: (i, 0, 0)),
        ],
        out_specs=pl.BlockSpec((3, tokens, step * DH), lambda i: (0, 0, i)),
        out_shape=jax.ShapeDtypeStruct((3, tokens, heads * DH), BF16),
        compiler_params=params(),
    )(index, rows)


def grad_attn_kernel(rows_ref, weight_ref, out_ref):
    product = dot(rows_ref[...], weight_ref[...]).astype(BF16)
    for head in range(out_ref.shape[0]):
        out_ref[head] = product[:, head * DH : (head + 1) * DH]


def grad_attn_heads(rows, weight):
    slots, depth = rows.shape
    heads = weight.shape[1] // DH
    step = 2
    return pl.pallas_call(
        grad_attn_kernel,
        grid=(heads // step,),
        in_specs=[
            pl.BlockSpec((slots, depth), lambda i: (0, 0)),
            pl.BlockSpec((depth, step * DH), lambda i: (0, i)),
        ],
        out_specs=pl.BlockSpec((step, slots, DH), lambda i: (i, 0, 0)),
        out_shape=jax.ShapeDtypeStruct((heads, slots, DH), BF16),
        compiler_params=params(),
    )(rows, weight)


def weight_grad_kernel(rows_ref, attended_ref, out_ref):
    attended = jnp.concatenate([attended_ref[head] for head in range(attended_ref.shape[0])], axis=1)
    out_ref[...] = dot_rows(rows_ref[...], attended)


def weight_grad_heads(rows, attended):
    total, width = rows.shape
    heads = attended.shape[0]
    step = 2
    return pl.pallas_call(
        weight_grad_kernel,
        grid=(heads // step,),
        in_specs=[
            pl.BlockSpec((total, width), lambda i: (0, 0)),
            pl.BlockSpec((step, total, DH), lambda i: (i, 0, 0)),
        ],
        out_specs=pl.BlockSpec((width, step * DH), lambda i: (0, i)),
        out_shape=jax.ShapeDtypeStruct((width, heads * DH), F32),
        compiler_params=params(),
    )(rows, attended)


def attention_kernel(
    slots,
    part_rows,
    part_ref,
    live_ref,
    query_ref,
    grad_ref,
    key_ref,
    value_ref,
    attended_ref,
    query_grad_ref,
    key_grad_ref,
    value_grad_ref,
    key_total,
    value_total,
):
    scale = 1.0 / math.sqrt(DH)
    rows_total = query_ref.shape[0]
    keys_total = key_ref.shape[0]
    quarters = slots // part_rows
    key_flip = key_ref[...].T
    value_flip = value_ref[...].T
    for start in range(0, rows_total, QUERY_BLOCK):
        rows = slice(start, start + QUERY_BLOCK)
        last = start + QUERY_BLOCK - 1
        last_pos = last // part_rows * slots + (quarters - 1) * part_rows + last % part_rows
        first_pos = start // part_rows * slots + start % part_rows
        keys = min(-(-(last_pos + 1) // 128) * 128, keys_total)
        clear = first_pos // 128 * 128
        query = query_ref[rows]
        grad = grad_ref[rows]
        row = start + lax.broadcasted_iota(jnp.int32, (1, QUERY_BLOCK), 1)
        if quarters > 1:
            shard = row // part_rows
            row = shard * slots + part_ref[0] * part_rows + row - shard * part_rows
        scores = dot_cols(key_ref[:keys], query) * scale + live_ref[:keys, :1]
        key_pos = clear + lax.broadcasted_iota(jnp.int32, (keys - clear, 1), 0)
        edge = jnp.where(key_pos <= row, scores[clear:], -1e30)
        scores = jnp.concatenate([scores[:clear], edge], axis=0) if clear else edge
        peak = jnp.max(scores, axis=0, keepdims=True)
        weights = jnp.exp(scores - peak)
        probs = weights * (1.0 / jnp.sum(weights, axis=0, keepdims=True))
        probs_low = probs.astype(BF16)
        attended = dot(value_flip[:, :keys], probs_low)
        attended_ref[rows] = attended.T.astype(BF16)
        row_dot = jnp.sum(grad.T.astype(F32) * attended, axis=0, keepdims=True)
        grad_probs = dot_cols(value_ref[:keys], grad)
        grad_scores = (probs * (grad_probs - row_dot)).astype(BF16)
        query_grad = dot(key_flip[:, :keys], grad_scores) * scale
        query_grad_ref[rows] = query_grad.T.astype(BF16)
        key_part = dot(grad_scores, query)
        value_part = dot(probs_low, grad)
        prev = start - 1
        reached = 0
        if start:
            prev_pos = prev // part_rows * slots + (quarters - 1) * part_rows + prev % part_rows
            reached = min(-(-(prev_pos + 1) // 128) * 128, keys_total)
        if reached:
            key_total[:reached] += key_part[:reached]
            value_total[:reached] += value_part[:reached]
        if keys > reached:
            key_total[reached:keys] = key_part[reached:]
            value_total[reached:keys] = value_part[reached:]
    key_grad_ref[...] = (key_total[...] * scale).astype(key_grad_ref.dtype)
    value_grad_ref[...] = value_total[...].astype(value_grad_ref.dtype)


def attention(part, live, query, grad, key, value, slots, part_rows, key_type):
    rows, keys = query.shape[0], key.shape[0]
    vmem = pl.BlockSpec(memory_space=pltpu.VMEM)
    return pl.pallas_call(
        functools.partial(attention_kernel, slots, part_rows),
        in_specs=[pl.BlockSpec(memory_space=pltpu.SMEM)] + [vmem] * 5,
        out_specs=[vmem] * 4,
        out_shape=[
            jax.ShapeDtypeStruct((rows, DH), BF16),
            jax.ShapeDtypeStruct((rows, DH), BF16),
            jax.ShapeDtypeStruct((keys, DH), key_type),
            jax.ShapeDtypeStruct((keys, DH), key_type),
        ],
        scratch_shapes=[pltpu.VMEM((keys, DH), F32)] * 2,
        compiler_params=params(),
    )(part, live, query, grad, key, value)


def on_device_split_heads(
    projections,
    output_gradient,
    output_projection_weight,
    kept_token_indices,
    surviving_token_count,
):
    tok_dev = projections.shape[0]
    group_width = projections.shape[2]
    slots = kept_token_indices.shape[1]
    heads = group_width // DH
    seq_count = lax.axis_size("seq")
    head_count = lax.axis_size("head")
    quarters = seq_count // heads
    part_rows = slots // quarters
    part = (lax.axis_index("seq") % quarters).astype(jnp.int32).reshape(1)
    index = kept_token_indices
    keys = seq_count * slots

    grad_local = pack_grad(index, output_gradient)
    grad_rows = lax.all_gather(grad_local, "head", axis=1, tiled=True)
    packed = pack_heads(index, projections.transpose(1, 0, 2))

    position = jnp.arange(slots, dtype=jnp.int32)
    live = position[None, :] < surviving_token_count[:, None]
    live = jnp.where(live, 0.0, -1e30).astype(F32).reshape(keys, 1)
    live = jnp.broadcast_to(live, (keys, DH))

    def swap(blocks):
        return lax.all_to_all(blocks, "seq", split_axis=0, concat_axis=0, tiled=True)

    if quarters == 1:
        arrived = swap(packed).reshape(keys, 3 * DH)
        query, key, value = (arrived[:, n * DH : (n + 1) * DH] for n in range(3))
    else:
        query = swap(packed[:, :, :DH].reshape(seq_count, part_rows, DH))
        query = query.reshape(seq_count * part_rows, DH)
        sides = jnp.broadcast_to(packed[:, None, :, DH:], (heads, quarters, slots, 2 * DH))
        sides = swap(sides.reshape(seq_count, slots, 2 * DH)).reshape(keys, 2 * DH)
        key, value = sides[:, :DH], sides[:, DH:]

    grad_heads = grad_attn_heads(grad_rows, output_projection_weight)
    grad_in = swap(grad_heads.reshape(seq_count, part_rows, DH)).reshape(-1, DH)

    width = grad_rows.shape[1] // seq_count
    piece = slots // head_count
    mine = lax.dynamic_slice_in_dim(grad_rows, lax.axis_index("head") * piece, piece, 0)
    mine = swap(mine.reshape(piece, seq_count, width).transpose(1, 0, 2))
    all_rows = lax.all_gather(mine, "head", axis=1, tiled=True)

    key_type = BF16 if quarters == 1 else F32
    attended, query_grad, key_grad, value_grad = attention(
        part, live, query, grad_in, key, value, slots, part_rows, key_type
    )

    gathered = lax.all_gather(attended, "seq", axis=0).reshape(heads, keys, DH)
    all_rows = all_rows.reshape(seq_count, quarters, part_rows, width).transpose(1, 0, 2, 3)
    weight_grad = weight_grad_heads(all_rows.reshape(keys, width), gathered)

    if quarters == 1:
        back = jnp.concatenate([query_grad, key_grad, value_grad], axis=1)
        home = swap(back.reshape(seq_count, slots, 3 * DH))
    else:
        query_home = swap(query_grad.reshape(seq_count, part_rows, DH)).reshape(heads, slots, DH)
        back = jnp.concatenate([key_grad, value_grad], axis=1)
        key_home = swap(back.reshape(seq_count, slots, 2 * DH))
        key_home = jnp.sum(key_home.reshape(heads, quarters, slots, 2 * DH), axis=1)
        home = jnp.concatenate([query_home, key_home.astype(BF16)], axis=2)
    projection_grad = unpack_heads(index, home, tok_dev).transpose(1, 0, 2)
    return (projection_grad, weight_grad)


def pack_whole_kernel(index_ref, proj_ref, out_ref, loaded, arrive):
    copies = [
        pltpu.make_async_copy(proj_ref.at[which], loaded.at[which], arrive.at[which])
        for which in range(3)
    ]
    for copy in copies:
        copy.start()
    token = lax.broadcasted_iota(jnp.int32, (loaded.shape[1], index_ref.shape[1]), 0)
    selector = jnp.where(token == index_ref[...], 1.0, 0.0).T.astype(BF16)
    for which, copy in enumerate(copies):
        copy.wait()
        rows = dot(selector, loaded[which]).astype(BF16)
        for head in range(out_ref.shape[0]):
            out_ref[head, :, which * DH : (which + 1) * DH] = rows[:, head * DH : (head + 1) * DH]


def pack_whole(index, proj):
    slots = index.shape[1]
    _, tokens, width = proj.shape
    heads = width // DH
    return pl.pallas_call(
        pack_whole_kernel,
        in_specs=[pl.BlockSpec(), pl.BlockSpec(memory_space=pltpu.HBM)],
        out_shape=jax.ShapeDtypeStruct((heads, slots, 3 * DH), BF16),
        scratch_shapes=[pltpu.VMEM(proj.shape, BF16), pltpu.SemaphoreType.DMA((3,))],
        compiler_params=params(VMEM_MOST),
        cost_estimate=pl.CostEstimate(
            flops=2 * slots * tokens * 3 * width, bytes_accessed=8 * tokens * width, transcendentals=0
        ),
    )(index, proj)


def exchange(block, axis, bit):
    return lax.ppermute(block, axis, [(i, i ^ bit) for i in range(lax.axis_size(axis))])


def gather_blocks(block, axis, bits, held=None):
    held = {0: block} if held is None else dict(held)
    reached = [0]
    for bit in bits:
        for step in list(reached):
            if step ^ bit not in held:
                held[step ^ bit] = exchange(held[step], axis, bit)
            reached.append(step ^ bit)
    return [held[step] for step in range(lax.axis_size(axis))]


SMEM_SPEC = pl.BlockSpec(memory_space=pltpu.SMEM)
VMEM_SPEC = pl.BlockSpec(memory_space=pltpu.VMEM)


def grad_swap_kernel(count, place_ref, *refs):
    row_refs, weight_ref, out_ref, total = refs[:count], refs[count], refs[count + 1], refs[count + 2]
    mine = place_ref[1]
    seq_count, height, _ = out_ref.shape
    slots, depth = row_refs[0].shape
    piece = slots // count
    chunks = (height - slots) // piece
    per_block = depth // (chunks * DH)
    for step in range(count):

        @pl.when(pl.program_id(0) == step)
        def _(step=step):
            part = dot(row_refs[step][...], weight_ref[...])
            total[...] = part if step == 0 else total[...] + part
            share = row_refs[step][pl.ds(pl.multiple_of(mine * piece, piece), piece), :]
            for chunk in range(per_block * chunks):
                partner = (mine ^ step) * per_block + chunk // chunks
                start = slots + chunk % chunks * piece
                out_ref[partner, start : start + piece, :] = share[:, chunk * DH : (chunk + 1) * DH]

    @pl.when(pl.program_id(0) == count - 1)
    def _():
        for head in range(seq_count):
            out_ref[head, :slots, :] = total[:, head * DH : (head + 1) * DH].astype(BF16)


def grad_swap(place, blocks, weight, seq_count):
    count = len(blocks)
    slots, depth = blocks[0].shape
    columns = weight.shape[1]
    height = slots + slots // count * (count * depth // seq_count // DH)
    return pl.pallas_call(
        functools.partial(grad_swap_kernel, count),
        grid_spec=pltpu.PrefetchScalarGridSpec(
            num_scalar_prefetch=1,
            grid=(count,),
            in_specs=[pl.BlockSpec((slots, depth), lambda i, place: (0, 0))] * count
            + [pl.BlockSpec((depth, columns), lambda i, place: (place[1] ^ i, 0))],
            out_specs=pl.BlockSpec((seq_count, height, DH), lambda i, place: (0, 0, 0)),
            scratch_shapes=[pltpu.VMEM((slots, columns), F32)],
        ),
        out_shape=jax.ShapeDtypeStruct((seq_count, height, DH), BF16),
        compiler_params=params(),
        cost_estimate=pl.CostEstimate(
            flops=2 * slots * count * depth * columns,
            bytes_accessed=2 * count * depth * columns,
            transcendentals=0,
        ),
    )(place, *blocks, weight)


def weight_grad_swap_kernel(head_count, seq_count, place_ref, *refs):
    piece_refs = refs[:head_count]
    attended_refs = refs[head_count : head_count + seq_count]
    out_ref, rows = refs[-2:]
    me, mine = place_ref[0], place_ref[1]
    chunks = rows.shape[1] // DH
    piece = piece_refs[0].shape[1] // chunks
    slots = piece * head_count
    for part in range(head_count):
        for shard in range(seq_count):
            here = pl.ds(pl.multiple_of(shard * slots + (mine ^ part) * piece, piece), piece)
            for chunk in range(chunks):
                rows[here, chunk * DH : (chunk + 1) * DH] = piece_refs[part][
                    shard, chunk * piece : (chunk + 1) * piece, :
                ]
    for step in range(0, seq_count, 2):
        pair = jnp.concatenate([attended_refs[step][...], attended_refs[step + 1][...]], axis=1)
        product = dot_rows(rows[...], pair)
        for side in range(2):
            column = pl.multiple_of((me ^ (step + side)) * DH, DH)
            out_ref[:, pl.ds(column, DH)] = product[:, side * DH : (side + 1) * DH]


def weight_grad_swap(place, pieces, attended):
    head_count, seq_count = len(pieces), len(attended)
    keys = attended[0].shape[0]
    width = pieces[0].shape[1] // (keys // seq_count // head_count) * DH
    return pl.pallas_call(
        functools.partial(weight_grad_swap_kernel, head_count, seq_count),
        in_specs=[SMEM_SPEC] + [VMEM_SPEC] * (head_count + seq_count),
        out_specs=VMEM_SPEC,
        out_shape=jax.ShapeDtypeStruct((width, seq_count * DH), F32),
        scratch_shapes=[pltpu.VMEM((keys, width), BF16)],
        compiler_params=params(),
        cost_estimate=pl.CostEstimate(
            flops=2 * keys * width * seq_count * DH,
            bytes_accessed=8 * keys * DH * seq_count,
            transcendentals=0,
        ),
    )(place, *pieces, *attended)


def masked_scores(start, keys, key_ref, query, live_ref):
    scores = dot_cols(key_ref[:keys], query) * (1.0 / math.sqrt(DH)) + live_ref[:keys, :1]
    row = start + lax.broadcasted_iota(jnp.int32, (1, QUERY_BLOCK), 1)
    key_pos = start + lax.broadcasted_iota(jnp.int32, (QUERY_BLOCK, 1), 0)
    edge = jnp.where(key_pos <= row, scores[start:], -1e30)
    return jnp.concatenate([scores[:start], edge], axis=0) if start else edge


def split_blocks(block_ref, *refs):
    shards, slots, _ = block_ref.shape
    for shard in range(shards):
        for which, ref in enumerate(refs):
            ref[shard * slots : (shard + 1) * slots] = block_ref[
                shard, :, which * DH : (which + 1) * DH
            ]


def forward_kernel(live_ref, block_ref, attended_ref, stat_ref, query_ref, key_ref, value_ref):
    split_blocks(block_ref, query_ref, key_ref, value_ref)
    value_flip = value_ref[...].T
    for start in range(0, query_ref.shape[0], QUERY_BLOCK):
        rows = slice(start, start + QUERY_BLOCK)
        keys = start + QUERY_BLOCK
        scores = masked_scores(start, keys, key_ref, query_ref[rows], live_ref)
        peak = jnp.max(scores, axis=0, keepdims=True)
        weights = jnp.exp(scores - peak)
        inverse = 1.0 / jnp.sum(weights, axis=0, keepdims=True)
        attended = dot(value_flip[:, :keys], (weights * inverse).astype(BF16))
        attended_ref[rows] = attended.T.astype(BF16)
        stat_ref[0:1, rows] = peak
        stat_ref[1:2, rows] = inverse


def attention_cost(keys, dots):
    return pl.CostEstimate(
        flops=dots * keys * keys * DH, bytes_accessed=16 * keys * DH, transcendentals=keys * keys // 2
    )


def forward(live, blocks):
    keys = blocks.shape[0] * blocks.shape[1]
    return pl.pallas_call(
        forward_kernel,
        out_shape=[
            jax.ShapeDtypeStruct((keys, DH), BF16),
            jax.ShapeDtypeStruct((8, keys), F32),
        ],
        scratch_shapes=[pltpu.VMEM((keys, DH), BF16)] * 3,
        compiler_params=params(),
        cost_estimate=attention_cost(keys, 2),
    )(live, blocks)


def backward_kernel(
    live_ref,
    block_ref,
    attended_ref,
    stat_ref,
    grads_ref,
    out_ref,
    query_ref,
    key_ref,
    value_ref,
    grad_ref,
    query_total,
    key_total,
    value_total,
):
    seq_count, slots, _ = out_ref.shape
    scale = 1.0 / math.sqrt(DH)
    split_blocks(block_ref, query_ref, key_ref, value_ref)
    for shard in range(seq_count):
        grad_ref[shard * slots : (shard + 1) * slots] = grads_ref[shard, :slots]
    key_flip = key_ref[...].T
    for start in range(0, query_ref.shape[0], QUERY_BLOCK):
        rows = slice(start, start + QUERY_BLOCK)
        keys = start + QUERY_BLOCK
        query = query_ref[rows]
        grad = grad_ref[rows]
        scores = masked_scores(start, keys, key_ref, query, live_ref)
        probs = jnp.exp(scores - stat_ref[0:1, rows]) * stat_ref[1:2, rows]
        probs_low = probs.astype(BF16)
        product = grad.astype(F32) * attended_ref[rows].astype(F32)
        row_dot = jnp.sum(product.T, axis=0, keepdims=True)
        grad_probs = dot_cols(value_ref[:keys], grad)
        grad_scores = (probs * (grad_probs - row_dot)).astype(BF16)
        query_total[rows] = (dot(key_flip[:, :keys], grad_scores) * scale).T.astype(BF16)
        key_part = dot(grad_scores, query)
        value_part = dot(probs_low, grad)
        if start:
            key_total[:start] += key_part[:start]
            value_total[:start] += value_part[:start]
        key_total[rows] = key_part[start:]
        value_total[rows] = value_part[start:]
    for shard in range(seq_count):
        here = slice(shard * slots, (shard + 1) * slots)
        out_ref[shard, :, :DH] = query_total[here]
        out_ref[shard, :, DH : 2 * DH] = (key_total[here] * scale).astype(BF16)
        out_ref[shard, :, 2 * DH :] = value_total[here].astype(BF16)


def backward(live, blocks, attended, stats, grads):
    keys = attended.shape[0]
    return pl.pallas_call(
        backward_kernel,
        out_shape=jax.ShapeDtypeStruct(blocks.shape, BF16),
        scratch_shapes=[pltpu.VMEM((keys, DH), BF16)] * 5 + [pltpu.VMEM((keys, DH), F32)] * 2,
        compiler_params=params(),
        cost_estimate=attention_cost(keys, 5),
    )(live, blocks, attended, stats, grads)


def live_bias(counts, slots):
    position = jnp.arange(slots, dtype=jnp.int32)
    live = position[None, :] < counts[:, None]
    live = jnp.where(live, 0.0, -1e30).astype(F32).reshape(-1, 1)
    return jnp.broadcast_to(live, (live.shape[0], DH))


def on_device_whole_heads(
    projections,
    output_gradient,
    output_projection_weight,
    kept_token_indices,
    surviving_token_count,
):
    tok_dev = projections.shape[0]
    slots = kept_token_indices.shape[1]
    seq_count = lax.axis_size("seq")
    head_count = lax.axis_size("head")
    index = kept_token_indices
    place = jnp.stack([lax.axis_index("seq"), lax.axis_index("head")]).astype(jnp.int32)
    seq_bits = [1 << bit for bit in reversed(range(seq_count.bit_length() - 1))]
    head_bits = [1 << bit for bit in reversed(range(head_count.bit_length() - 1))]

    grad_local = pack_grad(index, output_gradient)
    grad_blocks = gather_blocks(grad_local, "head", head_bits)
    packed = pack_whole(index, projections.transpose(1, 0, 2))
    live = live_bias(surviving_token_count, slots)

    def swap(blocks):
        return lax.all_to_all(blocks, "seq", split_axis=0, concat_axis=0, tiled=True)

    arrived = swap(packed)
    grads = swap(grad_swap(place, grad_blocks, output_projection_weight, seq_count))
    attended, stats = forward(live, arrived)

    held = {bit: exchange(attended, "seq", bit) for bit in seq_bits}
    grads, held = lax.optimization_barrier((grads, held))
    held[0] = attended
    far = [0]
    for bit in seq_bits[:-1]:
        for step in list(far):
            if step ^ bit not in held:
                held[step ^ bit] = exchange(held[step], "seq", bit)
            far.append(step ^ bit)
    back = backward(live, arrived, attended, stats, grads)
    back, held = lax.optimization_barrier((back, held))
    gathered = gather_blocks(attended, "seq", seq_bits, held)
    home = swap(back)

    pieces = gather_blocks(grads[:, slots:], "head", head_bits)
    weight_grad = weight_grad_swap(place, pieces, gathered)
    projection_grad = unpack_heads(index, home, tok_dev).transpose(1, 0, 2)
    return (projection_grad, weight_grad)


def on_device(projections, output_gradient, weight, index, counts):
    heads = projections.shape[2] // DH
    seq_count, head_count = lax.axis_size("seq"), lax.axis_size("head")
    width = output_gradient.shape[1] * head_count // seq_count
    whole = seq_count == heads and seq_count % 2 == 0 and width % DH == 0
    powers = seq_count & (seq_count - 1) == 0 and head_count & (head_count - 1) == 0
    body = on_device_whole_heads if whole and powers else on_device_split_heads
    return body(projections, output_gradient, weight, index, counts)


def solution(mesh):
    return jax.shard_map(
        on_device,
        mesh=mesh,
        in_specs=(P("seq", None, "head"), P("seq", "head"), P(None, "head"), P("seq", None), P()),
        out_specs=(P("seq", None, "head"), P("seq", "head")),
        check_vma=False,
    )
```

```python
import functools
import math

import jax
import jax.numpy as jnp
from jax import lax
from jax.experimental import pallas as pl
from jax.experimental.pallas import tpu as pltpu
from jax.sharding import PartitionSpec as P

DH = 128
QUERY_BLOCK = 256
VMEM_BYTES = 20 * 1024 * 1024
VMEM_MOST = 62 * 1024 * 1024
F32 = jnp.float32
BF16 = jnp.bfloat16


def params(limit=VMEM_BYTES):
    return pltpu.CompilerParams(vmem_limit_bytes=limit)


def dot(left, right):
    return jnp.dot(left, right, preferred_element_type=F32)


def dot_rows(left, right):
    return lax.dot_general(left, right, (((0,), (0,)), ((), ())), preferred_element_type=F32)


def dot_cols(left, right):
    return lax.dot_general(left, right, (((1,), (1,)), ((), ())), preferred_element_type=F32)


def token_selector(index_ref, tokens):
    slots = index_ref.shape[1]
    token = lax.broadcasted_iota(jnp.int32, (tokens, slots), 0)
    return jnp.where(token == index_ref[...], 1.0, 0.0).astype(BF16)


def pack_grad_kernel(index_ref, grad_ref, out_ref):
    selector = token_selector(index_ref, grad_ref.shape[0])
    out_ref[...] = dot_rows(selector, grad_ref[...]).astype(BF16)


def pack_grad(index, grad):
    slots = index.shape[1]
    return pl.pallas_call(
        pack_grad_kernel,
        out_shape=jax.ShapeDtypeStruct((slots, grad.shape[1]), BF16),
        compiler_params=params(),
    )(index, grad)


def pack_heads_kernel(index_ref, proj_ref, out_ref):
    selector = token_selector(index_ref, proj_ref.shape[1])
    for which in range(3):
        rows = dot_rows(selector, proj_ref[which]).astype(BF16)
        for head in range(out_ref.shape[0]):
            out_ref[head, :, which * DH : (which + 1) * DH] = rows[:, head * DH : (head + 1) * DH]


def pack_heads(index, proj):
    slots = index.shape[1]
    _, tokens, width = proj.shape
    heads = width // DH
    step = 2
    return pl.pallas_call(
        pack_heads_kernel,
        grid=(heads // step,),
        in_specs=[
            pl.BlockSpec((1, slots), lambda i: (0, 0)),
            pl.BlockSpec((3, tokens, step * DH), lambda i: (0, 0, i)),
        ],
        out_specs=pl.BlockSpec((step, slots, 3 * DH), lambda i: (i, 0, 0)),
        out_shape=jax.ShapeDtypeStruct((heads, slots, 3 * DH), BF16),
        compiler_params=params(),
    )(index, proj)


def unpack_heads_kernel(index_ref, rows_ref, out_ref):
    selector = token_selector(index_ref, out_ref.shape[1])
    for head in range(rows_ref.shape[0]):
        tokens = dot(selector, rows_ref[head]).astype(BF16)
        for which in range(3):
            out_ref[which, :, head * DH : (head + 1) * DH] = tokens[
                :, which * DH : (which + 1) * DH
            ]


def unpack_heads(index, rows, tokens):
    heads, slots, _ = rows.shape
    step = 2
    return pl.pallas_call(
        unpack_heads_kernel,
        grid=(heads // step,),
        in_specs=[
            pl.BlockSpec((1, slots), lambda i: (0, 0)),
            pl.BlockSpec((step, slots, 3 * DH), lambda i: (i, 0, 0)),
        ],
        out_specs=pl.BlockSpec((3, tokens, step * DH), lambda i: (0, 0, i)),
        out_shape=jax.ShapeDtypeStruct((3, tokens, heads * DH), BF16),
        compiler_params=params(),
    )(index, rows)


def grad_attn_kernel(rows_ref, weight_ref, out_ref):
    product = dot(rows_ref[...], weight_ref[...]).astype(BF16)
    for head in range(out_ref.shape[0]):
        out_ref[head] = product[:, head * DH : (head + 1) * DH]


def grad_attn_heads(rows, weight):
    slots, depth = rows.shape
    heads = weight.shape[1] // DH
    step = 2
    return pl.pallas_call(
        grad_attn_kernel,
        grid=(heads // step,),
        in_specs=[
            pl.BlockSpec((slots, depth), lambda i: (0, 0)),
            pl.BlockSpec((depth, step * DH), lambda i: (0, i)),
        ],
        out_specs=pl.BlockSpec((step, slots, DH), lambda i: (i, 0, 0)),
        out_shape=jax.ShapeDtypeStruct((heads, slots, DH), BF16),
        compiler_params=params(),
    )(rows, weight)


def weight_grad_kernel(rows_ref, attended_ref, out_ref):
    attended = jnp.concatenate([attended_ref[head] for head in range(attended_ref.shape[0])], axis=1)
    out_ref[...] = dot_rows(rows_ref[...], attended)


def weight_grad_heads(rows, attended):
    total, width = rows.shape
    heads = attended.shape[0]
    step = 2
    return pl.pallas_call(
        weight_grad_kernel,
        grid=(heads // step,),
        in_specs=[
            pl.BlockSpec((total, width), lambda i: (0, 0)),
            pl.BlockSpec((step, total, DH), lambda i: (i, 0, 0)),
        ],
        out_specs=pl.BlockSpec((width, step * DH), lambda i: (0, i)),
        out_shape=jax.ShapeDtypeStruct((width, heads * DH), F32),
        compiler_params=params(),
    )(rows, attended)


def attention_kernel(
    slots,
    part_rows,
    part_ref,
    live_ref,
    query_ref,
    grad_ref,
    key_ref,
    value_ref,
    attended_ref,
    query_grad_ref,
    key_grad_ref,
    value_grad_ref,
    key_total,
    value_total,
):
    scale = 1.0 / math.sqrt(DH)
    rows_total = query_ref.shape[0]
    keys_total = key_ref.shape[0]
    quarters = slots // part_rows
    key_flip = key_ref[...].T
    value_flip = value_ref[...].T
    for start in range(0, rows_total, QUERY_BLOCK):
        rows = slice(start, start + QUERY_BLOCK)
        last = start + QUERY_BLOCK - 1
        last_pos = last // part_rows * slots + (quarters - 1) * part_rows + last % part_rows
        first_pos = start // part_rows * slots + start % part_rows
        keys = min(-(-(last_pos + 1) // 128) * 128, keys_total)
        clear = first_pos // 128 * 128
        query = query_ref[rows]
        grad = grad_ref[rows]
        row = start + lax.broadcasted_iota(jnp.int32, (1, QUERY_BLOCK), 1)
        if quarters > 1:
            shard = row // part_rows
            row = shard * slots + part_ref[0] * part_rows + row - shard * part_rows
        scores = dot_cols(key_ref[:keys], query) * scale + live_ref[:keys, :1]
        key_pos = clear + lax.broadcasted_iota(jnp.int32, (keys - clear, 1), 0)
        edge = jnp.where(key_pos <= row, scores[clear:], -1e30)
        scores = jnp.concatenate([scores[:clear], edge], axis=0) if clear else edge
        peak = jnp.max(scores, axis=0, keepdims=True)
        weights = jnp.exp(scores - peak)
        probs = weights * (1.0 / jnp.sum(weights, axis=0, keepdims=True))
        probs_low = probs.astype(BF16)
        attended = dot(value_flip[:, :keys], probs_low)
        attended_ref[rows] = attended.T.astype(BF16)
        row_dot = jnp.sum(grad.T.astype(F32) * attended, axis=0, keepdims=True)
        grad_probs = dot_cols(value_ref[:keys], grad)
        grad_scores = (probs * (grad_probs - row_dot)).astype(BF16)
        query_grad = dot(key_flip[:, :keys], grad_scores) * scale
        query_grad_ref[rows] = query_grad.T.astype(BF16)
        key_part = dot(grad_scores, query)
        value_part = dot(probs_low, grad)
        prev = start - 1
        reached = 0
        if start:
            prev_pos = prev // part_rows * slots + (quarters - 1) * part_rows + prev % part_rows
            reached = min(-(-(prev_pos + 1) // 128) * 128, keys_total)
        if reached:
            key_total[:reached] += key_part[:reached]
            value_total[:reached] += value_part[:reached]
        if keys > reached:
            key_total[reached:keys] = key_part[reached:]
            value_total[reached:keys] = value_part[reached:]
    key_grad_ref[...] = (key_total[...] * scale).astype(key_grad_ref.dtype)
    value_grad_ref[...] = value_total[...].astype(value_grad_ref.dtype)


def attention(part, live, query, grad, key, value, slots, part_rows, key_type):
    rows, keys = query.shape[0], key.shape[0]
    vmem = pl.BlockSpec(memory_space=pltpu.VMEM)
    return pl.pallas_call(
        functools.partial(attention_kernel, slots, part_rows),
        in_specs=[pl.BlockSpec(memory_space=pltpu.SMEM)] + [vmem] * 5,
        out_specs=[vmem] * 4,
        out_shape=[
            jax.ShapeDtypeStruct((rows, DH), BF16),
            jax.ShapeDtypeStruct((rows, DH), BF16),
            jax.ShapeDtypeStruct((keys, DH), key_type),
            jax.ShapeDtypeStruct((keys, DH), key_type),
        ],
        scratch_shapes=[pltpu.VMEM((keys, DH), F32)] * 2,
        compiler_params=params(),
    )(part, live, query, grad, key, value)


def on_device_split_heads(
    projections,
    output_gradient,
    output_projection_weight,
    kept_token_indices,
    surviving_token_count,
):
    tok_dev = projections.shape[0]
    group_width = projections.shape[2]
    slots = kept_token_indices.shape[1]
    heads = group_width // DH
    seq_count = lax.axis_size("seq")
    head_count = lax.axis_size("head")
    quarters = seq_count // heads
    part_rows = slots // quarters
    part = (lax.axis_index("seq") % quarters).astype(jnp.int32).reshape(1)
    index = kept_token_indices
    keys = seq_count * slots

    grad_local = pack_grad(index, output_gradient)
    grad_rows = lax.all_gather(grad_local, "head", axis=1, tiled=True)
    packed = pack_heads(index, projections.transpose(1, 0, 2))

    position = jnp.arange(slots, dtype=jnp.int32)
    live = position[None, :] < surviving_token_count[:, None]
    live = jnp.where(live, 0.0, -1e30).astype(F32).reshape(keys, 1)
    live = jnp.broadcast_to(live, (keys, DH))

    def swap(blocks):
        return lax.all_to_all(blocks, "seq", split_axis=0, concat_axis=0, tiled=True)

    if quarters == 1:
        arrived = swap(packed).reshape(keys, 3 * DH)
        query, key, value = (arrived[:, n * DH : (n + 1) * DH] for n in range(3))
    else:
        query = swap(packed[:, :, :DH].reshape(seq_count, part_rows, DH))
        query = query.reshape(seq_count * part_rows, DH)
        sides = jnp.broadcast_to(packed[:, None, :, DH:], (heads, quarters, slots, 2 * DH))
        sides = swap(sides.reshape(seq_count, slots, 2 * DH)).reshape(keys, 2 * DH)
        key, value = sides[:, :DH], sides[:, DH:]

    grad_heads = grad_attn_heads(grad_rows, output_projection_weight)
    grad_in = swap(grad_heads.reshape(seq_count, part_rows, DH)).reshape(-1, DH)

    width = grad_rows.shape[1] // seq_count
    piece = slots // head_count
    mine = lax.dynamic_slice_in_dim(grad_rows, lax.axis_index("head") * piece, piece, 0)
    mine = swap(mine.reshape(piece, seq_count, width).transpose(1, 0, 2))
    all_rows = lax.all_gather(mine, "head", axis=1, tiled=True)

    key_type = BF16 if quarters == 1 else F32
    attended, query_grad, key_grad, value_grad = attention(
        part, live, query, grad_in, key, value, slots, part_rows, key_type
    )

    gathered = lax.all_gather(attended, "seq", axis=0).reshape(heads, keys, DH)
    all_rows = all_rows.reshape(seq_count, quarters, part_rows, width).transpose(1, 0, 2, 3)
    weight_grad = weight_grad_heads(all_rows.reshape(keys, width), gathered)

    if quarters == 1:
        back = jnp.concatenate([query_grad, key_grad, value_grad], axis=1)
        home = swap(back.reshape(seq_count, slots, 3 * DH))
    else:
        query_home = swap(query_grad.reshape(seq_count, part_rows, DH)).reshape(heads, slots, DH)
        back = jnp.concatenate([key_grad, value_grad], axis=1)
        key_home = swap(back.reshape(seq_count, slots, 2 * DH))
        key_home = jnp.sum(key_home.reshape(heads, quarters, slots, 2 * DH), axis=1)
        home = jnp.concatenate([query_home, key_home.astype(BF16)], axis=2)
    projection_grad = unpack_heads(index, home, tok_dev).transpose(1, 0, 2)
    return (projection_grad, weight_grad)


def pack_whole_kernel(index_ref, proj_ref, out_ref, loaded, arrive):
    copies = [
        pltpu.make_async_copy(proj_ref.at[which], loaded.at[which], arrive.at[which])
        for which in range(3)
    ]
    for copy in copies:
        copy.start()
    token = lax.broadcasted_iota(jnp.int32, (loaded.shape[1], index_ref.shape[1]), 0)
    selector = jnp.where(token == index_ref[...], 1.0, 0.0).T.astype(BF16)
    for which, copy in enumerate(copies):
        copy.wait()
        rows = dot(selector, loaded[which]).astype(BF16)
        for head in range(out_ref.shape[0]):
            out_ref[head, :, which * DH : (which + 1) * DH] = rows[:, head * DH : (head + 1) * DH]


def pack_whole(index, proj):
    slots = index.shape[1]
    _, tokens, width = proj.shape
    heads = width // DH
    return pl.pallas_call(
        pack_whole_kernel,
        in_specs=[pl.BlockSpec(), pl.BlockSpec(memory_space=pltpu.HBM)],
        out_shape=jax.ShapeDtypeStruct((heads, slots, 3 * DH), BF16),
        scratch_shapes=[pltpu.VMEM(proj.shape, BF16), pltpu.SemaphoreType.DMA((3,))],
        compiler_params=params(VMEM_MOST),
        cost_estimate=pl.CostEstimate(
            flops=2 * slots * tokens * 3 * width, bytes_accessed=8 * tokens * width, transcendentals=0
        ),
    )(index, proj)


def exchange(block, axis, bit):
    return lax.ppermute(block, axis, [(i, i ^ bit) for i in range(lax.axis_size(axis))])


def gather_blocks(block, axis, bits, held=None):
    held = {0: block} if held is None else dict(held)
    reached = [0]
    for bit in bits:
        for step in list(reached):
            if step ^ bit not in held:
                held[step ^ bit] = exchange(held[step], axis, bit)
            reached.append(step ^ bit)
    return [held[step] for step in range(lax.axis_size(axis))]


SMEM_SPEC = pl.BlockSpec(memory_space=pltpu.SMEM)
VMEM_SPEC = pl.BlockSpec(memory_space=pltpu.VMEM)


def grad_swap_kernel(count, place_ref, *refs):
    row_refs, weight_ref, out_ref, total = refs[:count], refs[count], refs[count + 1], refs[count + 2]
    mine = place_ref[1]
    seq_count, height, _ = out_ref.shape
    slots, depth = row_refs[0].shape
    piece = slots // count
    chunks = (height - slots) // piece
    per_block = depth // (chunks * DH)
    for step in range(count):

        @pl.when(pl.program_id(0) == step)
        def _(step=step):
            part = dot(row_refs[step][...], weight_ref[...])
            total[...] = part if step == 0 else total[...] + part
            share = row_refs[step][pl.ds(pl.multiple_of(mine * piece, piece), piece), :]
            for chunk in range(per_block * chunks):
                partner = (mine ^ step) * per_block + chunk // chunks
                start = slots + chunk % chunks * piece
                out_ref[partner, start : start + piece, :] = share[:, chunk * DH : (chunk + 1) * DH]

    @pl.when(pl.program_id(0) == count - 1)
    def _():
        for head in range(seq_count):
            out_ref[head, :slots, :] = total[:, head * DH : (head + 1) * DH].astype(BF16)


def grad_swap(place, blocks, weight, seq_count):
    count = len(blocks)
    slots, depth = blocks[0].shape
    columns = weight.shape[1]
    height = slots + slots // count * (count * depth // seq_count // DH)
    return pl.pallas_call(
        functools.partial(grad_swap_kernel, count),
        grid_spec=pltpu.PrefetchScalarGridSpec(
            num_scalar_prefetch=1,
            grid=(count,),
            in_specs=[pl.BlockSpec((slots, depth), lambda i, place: (0, 0))] * count
            + [pl.BlockSpec((depth, columns), lambda i, place: (place[1] ^ i, 0))],
            out_specs=pl.BlockSpec((seq_count, height, DH), lambda i, place: (0, 0, 0)),
            scratch_shapes=[pltpu.VMEM((slots, columns), F32)],
        ),
        out_shape=jax.ShapeDtypeStruct((seq_count, height, DH), BF16),
        compiler_params=params(),
        cost_estimate=pl.CostEstimate(
            flops=2 * slots * count * depth * columns,
            bytes_accessed=2 * count * depth * columns,
            transcendentals=0,
        ),
    )(place, *blocks, weight)


def weight_grad_swap_kernel(head_count, seq_count, place_ref, *refs):
    piece_refs = refs[:head_count]
    attended_refs = refs[head_count : head_count + seq_count]
    out_ref, rows = refs[-2:]
    me, mine = place_ref[0], place_ref[1]
    chunks = rows.shape[1] // DH
    piece = piece_refs[0].shape[1] // chunks
    slots = piece * head_count
    for part in range(head_count):
        for shard in range(seq_count):
            here = pl.ds(pl.multiple_of(shard * slots + (mine ^ part) * piece, piece), piece)
            for chunk in range(chunks):
                rows[here, chunk * DH : (chunk + 1) * DH] = piece_refs[part][
                    shard, chunk * piece : (chunk + 1) * piece, :
                ]
    for step in range(0, seq_count, 2):
        pair = jnp.concatenate([attended_refs[step][...], attended_refs[step + 1][...]], axis=1)
        product = dot_rows(rows[...], pair)
        for side in range(2):
            column = pl.multiple_of((me ^ (step + side)) * DH, DH)
            out_ref[:, pl.ds(column, DH)] = product[:, side * DH : (side + 1) * DH]


def weight_grad_swap(place, pieces, attended):
    head_count, seq_count = len(pieces), len(attended)
    keys = attended[0].shape[0]
    width = pieces[0].shape[1] // (keys // seq_count // head_count) * DH
    return pl.pallas_call(
        functools.partial(weight_grad_swap_kernel, head_count, seq_count),
        in_specs=[SMEM_SPEC] + [VMEM_SPEC] * (head_count + seq_count),
        out_specs=VMEM_SPEC,
        out_shape=jax.ShapeDtypeStruct((width, seq_count * DH), F32),
        scratch_shapes=[pltpu.VMEM((keys, width), BF16)],
        compiler_params=params(),
        cost_estimate=pl.CostEstimate(
            flops=2 * keys * width * seq_count * DH,
            bytes_accessed=8 * keys * DH * seq_count,
            transcendentals=0,
        ),
    )(place, *pieces, *attended)


def masked_scores(start, keys, key_ref, query, live_ref):
    scores = dot_cols(key_ref[:keys], query) * (1.0 / math.sqrt(DH)) + live_ref[:keys, :1]
    row = start + lax.broadcasted_iota(jnp.int32, (1, QUERY_BLOCK), 1)
    key_pos = start + lax.broadcasted_iota(jnp.int32, (QUERY_BLOCK, 1), 0)
    edge = jnp.where(key_pos <= row, scores[start:], -1e30)
    return jnp.concatenate([scores[:start], edge], axis=0) if start else edge


def split_blocks(block_ref, *refs):
    shards, slots, _ = block_ref.shape
    for shard in range(shards):
        for which, ref in enumerate(refs):
            ref[shard * slots : (shard + 1) * slots] = block_ref[
                shard, :, which * DH : (which + 1) * DH
            ]


def forward_kernel(live_ref, block_ref, attended_ref, stat_ref, query_ref, key_ref, value_ref):
    split_blocks(block_ref, query_ref, key_ref, value_ref)
    value_flip = value_ref[...].T
    for start in range(0, query_ref.shape[0], QUERY_BLOCK):
        rows = slice(start, start + QUERY_BLOCK)
        keys = start + QUERY_BLOCK
        scores = masked_scores(start, keys, key_ref, query_ref[rows], live_ref)
        peak = jnp.max(scores, axis=0, keepdims=True)
        weights = jnp.exp(scores - peak)
        inverse = 1.0 / jnp.sum(weights, axis=0, keepdims=True)
        attended = dot(value_flip[:, :keys], (weights * inverse).astype(BF16))
        attended_ref[rows] = attended.T.astype(BF16)
        stat_ref[0:1, rows] = peak
        stat_ref[1:2, rows] = inverse


def attention_cost(keys, dots):
    return pl.CostEstimate(
        flops=dots * keys * keys * DH, bytes_accessed=16 * keys * DH, transcendentals=keys * keys // 2
    )


def forward(live, blocks):
    keys = blocks.shape[0] * blocks.shape[1]
    return pl.pallas_call(
        forward_kernel,
        out_shape=[
            jax.ShapeDtypeStruct((keys, DH), BF16),
            jax.ShapeDtypeStruct((8, keys), F32),
        ],
        scratch_shapes=[pltpu.VMEM((keys, DH), BF16)] * 3,
        compiler_params=params(VMEM_MOST),
        cost_estimate=attention_cost(keys, 2),
    )(live, blocks)


def backward_kernel(
    live_ref,
    block_ref,
    attended_ref,
    stat_ref,
    grads_ref,
    out_ref,
    query_ref,
    key_ref,
    value_ref,
    grad_ref,
    query_total,
    key_total,
    value_total,
):
    seq_count, slots, _ = out_ref.shape
    scale = 1.0 / math.sqrt(DH)
    split_blocks(block_ref, query_ref, key_ref, value_ref)
    for shard in range(seq_count):
        grad_ref[shard * slots : (shard + 1) * slots] = grads_ref[shard, :slots]
    key_flip = key_ref[...].T
    for start in range(0, query_ref.shape[0], QUERY_BLOCK):
        rows = slice(start, start + QUERY_BLOCK)
        keys = start + QUERY_BLOCK
        query = query_ref[rows]
        grad = grad_ref[rows]
        scores = masked_scores(start, keys, key_ref, query, live_ref)
        probs = jnp.exp(scores - stat_ref[0:1, rows]) * stat_ref[1:2, rows]
        probs_low = probs.astype(BF16)
        product = grad.astype(F32) * attended_ref[rows].astype(F32)
        row_dot = jnp.sum(product.T, axis=0, keepdims=True)
        grad_probs = dot_cols(value_ref[:keys], grad)
        grad_scores = (probs * (grad_probs - row_dot)).astype(BF16)
        query_total[rows] = (dot(key_flip[:, :keys], grad_scores) * scale).T.astype(BF16)
        key_part = dot(grad_scores, query)
        value_part = dot(probs_low, grad)
        if start:
            key_total[:start] += key_part[:start]
            value_total[:start] += value_part[:start]
        key_total[rows] = key_part[start:]
        value_total[rows] = value_part[start:]
    for shard in range(seq_count):
        here = slice(shard * slots, (shard + 1) * slots)
        out_ref[shard, :, :DH] = query_total[here]
        out_ref[shard, :, DH : 2 * DH] = (key_total[here] * scale).astype(BF16)
        out_ref[shard, :, 2 * DH :] = value_total[here].astype(BF16)


def backward(live, blocks, attended, stats, grads):
    keys = attended.shape[0]
    return pl.pallas_call(
        backward_kernel,
        out_shape=jax.ShapeDtypeStruct(blocks.shape, BF16),
        scratch_shapes=[pltpu.VMEM((keys, DH), BF16)] * 5 + [pltpu.VMEM((keys, DH), F32)] * 2,
        compiler_params=params(VMEM_MOST),
        cost_estimate=attention_cost(keys, 5),
    )(live, blocks, attended, stats, grads)


def live_bias(counts, slots):
    position = jnp.arange(slots, dtype=jnp.int32)
    live = position[None, :] < counts[:, None]
    live = jnp.where(live, 0.0, -1e30).astype(F32).reshape(-1, 1)
    return jnp.broadcast_to(live, (live.shape[0], DH))


def on_device_whole_heads(
    projections,
    output_gradient,
    output_projection_weight,
    kept_token_indices,
    surviving_token_count,
):
    tok_dev = projections.shape[0]
    slots = kept_token_indices.shape[1]
    seq_count = lax.axis_size("seq")
    head_count = lax.axis_size("head")
    index = kept_token_indices
    place = jnp.stack([lax.axis_index("seq"), lax.axis_index("head")]).astype(jnp.int32)
    seq_bits = [1 << bit for bit in reversed(range(seq_count.bit_length() - 1))]
    head_bits = [1 << bit for bit in reversed(range(head_count.bit_length() - 1))]

    grad_local = pack_grad(index, output_gradient)
    grad_blocks = gather_blocks(grad_local, "head", head_bits)
    packed = pack_whole(index, projections.transpose(1, 0, 2))
    live = live_bias(surviving_token_count, slots)

    def swap(blocks):
        return lax.all_to_all(blocks, "seq", split_axis=0, concat_axis=0, tiled=True)

    arrived = swap(packed)
    grads = swap(grad_swap(place, grad_blocks, output_projection_weight, seq_count))
    attended, stats = forward(live, arrived)

    held = {bit: exchange(attended, "seq", bit) for bit in seq_bits}
    near, last = seq_bits[-2], seq_bits[-1]
    held[near ^ last] = exchange(held[near], "seq", last)
    back = backward(live, arrived, attended, stats, grads)
    back, held = lax.optimization_barrier((back, held))
    gathered = gather_blocks(attended, "seq", seq_bits, {0: attended, **held})
    home = swap(back)

    pieces = gather_blocks(grads[:, slots:], "head", head_bits)
    weight_grad = weight_grad_swap(place, pieces, gathered)
    projection_grad = unpack_heads(index, home, tok_dev).transpose(1, 0, 2)
    return (projection_grad, weight_grad)


def on_device(projections, output_gradient, weight, index, counts):
    heads = projections.shape[2] // DH
    seq_count, head_count = lax.axis_size("seq"), lax.axis_size("head")
    width = output_gradient.shape[1] * head_count // seq_count
    whole = seq_count == heads and seq_count % 2 == 0 and width % DH == 0
    powers = seq_count & (seq_count - 1) == 0 and head_count & (head_count - 1) == 0
    body = on_device_whole_heads if whole and powers else on_device_split_heads
    return body(projections, output_gradient, weight, index, counts)


def solution(mesh):
    return jax.shard_map(
        on_device,
        mesh=mesh,
        in_specs=(P("seq", None, "head"), P("seq", "head"), P(None, "head"), P("seq", None), P()),
        out_specs=(P("seq", None, "head"), P("seq", "head")),
        check_vma=False,
    )
```

```python
import functools
import math

import jax
import jax.numpy as jnp
from jax import lax
from jax.experimental import pallas as pl
from jax.experimental.pallas import tpu as pltpu
from jax.sharding import PartitionSpec as P

DH = 128
QUERY_BLOCK = 256
VMEM_BYTES = 20 * 1024 * 1024
VMEM_MOST = 62 * 1024 * 1024
F32 = jnp.float32
BF16 = jnp.bfloat16


def params(limit=VMEM_BYTES):
    return pltpu.CompilerParams(vmem_limit_bytes=limit)


def dot(left, right):
    return jnp.dot(left, right, preferred_element_type=F32)


def dot_rows(left, right):
    return lax.dot_general(left, right, (((0,), (0,)), ((), ())), preferred_element_type=F32)


def dot_cols(left, right):
    return lax.dot_general(left, right, (((1,), (1,)), ((), ())), preferred_element_type=F32)


def token_selector(index_ref, tokens):
    slots = index_ref.shape[1]
    token = lax.broadcasted_iota(jnp.int32, (tokens, slots), 0)
    return jnp.where(token == index_ref[...], 1.0, 0.0).astype(BF16)


def pack_grad_kernel(index_ref, grad_ref, out_ref):
    selector = token_selector(index_ref, grad_ref.shape[0])
    out_ref[...] = dot_rows(selector, grad_ref[...]).astype(BF16)


def pack_grad(index, grad):
    slots = index.shape[1]
    return pl.pallas_call(
        pack_grad_kernel,
        out_shape=jax.ShapeDtypeStruct((slots, grad.shape[1]), BF16),
        compiler_params=params(),
    )(index, grad)


def pack_heads_kernel(index_ref, proj_ref, out_ref):
    selector = token_selector(index_ref, proj_ref.shape[1])
    for which in range(3):
        rows = dot_rows(selector, proj_ref[which]).astype(BF16)
        for head in range(out_ref.shape[0]):
            out_ref[head, :, which * DH : (which + 1) * DH] = rows[:, head * DH : (head + 1) * DH]


def pack_heads(index, proj):
    slots = index.shape[1]
    _, tokens, width = proj.shape
    heads = width // DH
    step = 2
    return pl.pallas_call(
        pack_heads_kernel,
        grid=(heads // step,),
        in_specs=[
            pl.BlockSpec((1, slots), lambda i: (0, 0)),
            pl.BlockSpec((3, tokens, step * DH), lambda i: (0, 0, i)),
        ],
        out_specs=pl.BlockSpec((step, slots, 3 * DH), lambda i: (i, 0, 0)),
        out_shape=jax.ShapeDtypeStruct((heads, slots, 3 * DH), BF16),
        compiler_params=params(),
    )(index, proj)


def unpack_heads_kernel(index_ref, rows_ref, out_ref):
    selector = token_selector(index_ref, out_ref.shape[1])
    for head in range(rows_ref.shape[0]):
        tokens = dot(selector, rows_ref[head]).astype(BF16)
        for which in range(3):
            out_ref[which, :, head * DH : (head + 1) * DH] = tokens[
                :, which * DH : (which + 1) * DH
            ]


def unpack_heads(index, rows, tokens):
    heads, slots, _ = rows.shape
    step = 2
    return pl.pallas_call(
        unpack_heads_kernel,
        grid=(heads // step,),
        in_specs=[
            pl.BlockSpec((1, slots), lambda i: (0, 0)),
            pl.BlockSpec((step, slots, 3 * DH), lambda i: (i, 0, 0)),
        ],
        out_specs=pl.BlockSpec((3, tokens, step * DH), lambda i: (0, 0, i)),
        out_shape=jax.ShapeDtypeStruct((3, tokens, heads * DH), BF16),
        compiler_params=params(),
    )(index, rows)


def grad_attn_kernel(rows_ref, weight_ref, out_ref):
    product = dot(rows_ref[...], weight_ref[...]).astype(BF16)
    for head in range(out_ref.shape[0]):
        out_ref[head] = product[:, head * DH : (head + 1) * DH]


def grad_attn_heads(rows, weight):
    slots, depth = rows.shape
    heads = weight.shape[1] // DH
    step = 2
    return pl.pallas_call(
        grad_attn_kernel,
        grid=(heads // step,),
        in_specs=[
            pl.BlockSpec((slots, depth), lambda i: (0, 0)),
            pl.BlockSpec((depth, step * DH), lambda i: (0, i)),
        ],
        out_specs=pl.BlockSpec((step, slots, DH), lambda i: (i, 0, 0)),
        out_shape=jax.ShapeDtypeStruct((heads, slots, DH), BF16),
        compiler_params=params(),
    )(rows, weight)


def weight_grad_kernel(rows_ref, attended_ref, out_ref):
    attended = jnp.concatenate([attended_ref[head] for head in range(attended_ref.shape[0])], axis=1)
    out_ref[...] = dot_rows(rows_ref[...], attended)


def weight_grad_heads(rows, attended):
    total, width = rows.shape
    heads = attended.shape[0]
    step = 2
    return pl.pallas_call(
        weight_grad_kernel,
        grid=(heads // step,),
        in_specs=[
            pl.BlockSpec((total, width), lambda i: (0, 0)),
            pl.BlockSpec((step, total, DH), lambda i: (i, 0, 0)),
        ],
        out_specs=pl.BlockSpec((width, step * DH), lambda i: (0, i)),
        out_shape=jax.ShapeDtypeStruct((width, heads * DH), F32),
        compiler_params=params(),
    )(rows, attended)


def attention_kernel(
    slots,
    part_rows,
    part_ref,
    live_ref,
    query_ref,
    grad_ref,
    key_ref,
    value_ref,
    attended_ref,
    query_grad_ref,
    key_grad_ref,
    value_grad_ref,
    key_total,
    value_total,
):
    scale = 1.0 / math.sqrt(DH)
    rows_total = query_ref.shape[0]
    keys_total = key_ref.shape[0]
    quarters = slots // part_rows
    key_flip = key_ref[...].T
    value_flip = value_ref[...].T
    for start in range(0, rows_total, QUERY_BLOCK):
        rows = slice(start, start + QUERY_BLOCK)
        last = start + QUERY_BLOCK - 1
        last_pos = last // part_rows * slots + (quarters - 1) * part_rows + last % part_rows
        first_pos = start // part_rows * slots + start % part_rows
        keys = min(-(-(last_pos + 1) // 128) * 128, keys_total)
        clear = first_pos // 128 * 128
        query = query_ref[rows]
        grad = grad_ref[rows]
        row = start + lax.broadcasted_iota(jnp.int32, (1, QUERY_BLOCK), 1)
        if quarters > 1:
            shard = row // part_rows
            row = shard * slots + part_ref[0] * part_rows + row - shard * part_rows
        scores = dot_cols(key_ref[:keys], query) * scale + live_ref[:keys, :1]
        key_pos = clear + lax.broadcasted_iota(jnp.int32, (keys - clear, 1), 0)
        edge = jnp.where(key_pos <= row, scores[clear:], -1e30)
        scores = jnp.concatenate([scores[:clear], edge], axis=0) if clear else edge
        peak = jnp.max(scores, axis=0, keepdims=True)
        weights = jnp.exp(scores - peak)
        probs = weights * (1.0 / jnp.sum(weights, axis=0, keepdims=True))
        probs_low = probs.astype(BF16)
        attended = dot(value_flip[:, :keys], probs_low)
        attended_ref[rows] = attended.T.astype(BF16)
        row_dot = jnp.sum(grad.T.astype(F32) * attended, axis=0, keepdims=True)
        grad_probs = dot_cols(value_ref[:keys], grad)
        grad_scores = (probs * (grad_probs - row_dot)).astype(BF16)
        query_grad = dot(key_flip[:, :keys], grad_scores) * scale
        query_grad_ref[rows] = query_grad.T.astype(BF16)
        key_part = dot(grad_scores, query)
        value_part = dot(probs_low, grad)
        prev = start - 1
        reached = 0
        if start:
            prev_pos = prev // part_rows * slots + (quarters - 1) * part_rows + prev % part_rows
            reached = min(-(-(prev_pos + 1) // 128) * 128, keys_total)
        if reached:
            key_total[:reached] += key_part[:reached]
            value_total[:reached] += value_part[:reached]
        if keys > reached:
            key_total[reached:keys] = key_part[reached:]
            value_total[reached:keys] = value_part[reached:]
    key_grad_ref[...] = (key_total[...] * scale).astype(key_grad_ref.dtype)
    value_grad_ref[...] = value_total[...].astype(value_grad_ref.dtype)


def attention(part, live, query, grad, key, value, slots, part_rows, key_type):
    rows, keys = query.shape[0], key.shape[0]
    vmem = pl.BlockSpec(memory_space=pltpu.VMEM)
    return pl.pallas_call(
        functools.partial(attention_kernel, slots, part_rows),
        in_specs=[pl.BlockSpec(memory_space=pltpu.SMEM)] + [vmem] * 5,
        out_specs=[vmem] * 4,
        out_shape=[
            jax.ShapeDtypeStruct((rows, DH), BF16),
            jax.ShapeDtypeStruct((rows, DH), BF16),
            jax.ShapeDtypeStruct((keys, DH), key_type),
            jax.ShapeDtypeStruct((keys, DH), key_type),
        ],
        scratch_shapes=[pltpu.VMEM((keys, DH), F32)] * 2,
        compiler_params=params(),
    )(part, live, query, grad, key, value)


def on_device_split_heads(
    projections,
    output_gradient,
    output_projection_weight,
    kept_token_indices,
    surviving_token_count,
):
    tok_dev = projections.shape[0]
    group_width = projections.shape[2]
    slots = kept_token_indices.shape[1]
    heads = group_width // DH
    seq_count = lax.axis_size("seq")
    head_count = lax.axis_size("head")
    quarters = seq_count // heads
    part_rows = slots // quarters
    part = (lax.axis_index("seq") % quarters).astype(jnp.int32).reshape(1)
    index = kept_token_indices
    keys = seq_count * slots

    grad_local = pack_grad(index, output_gradient)
    grad_rows = lax.all_gather(grad_local, "head", axis=1, tiled=True)
    packed = pack_heads(index, projections.transpose(1, 0, 2))

    position = jnp.arange(slots, dtype=jnp.int32)
    live = position[None, :] < surviving_token_count[:, None]
    live = jnp.where(live, 0.0, -1e30).astype(F32).reshape(keys, 1)
    live = jnp.broadcast_to(live, (keys, DH))

    def swap(blocks):
        return lax.all_to_all(blocks, "seq", split_axis=0, concat_axis=0, tiled=True)

    if quarters == 1:
        arrived = swap(packed).reshape(keys, 3 * DH)
        query, key, value = (arrived[:, n * DH : (n + 1) * DH] for n in range(3))
    else:
        query = swap(packed[:, :, :DH].reshape(seq_count, part_rows, DH))
        query = query.reshape(seq_count * part_rows, DH)
        sides = jnp.broadcast_to(packed[:, None, :, DH:], (heads, quarters, slots, 2 * DH))
        sides = swap(sides.reshape(seq_count, slots, 2 * DH)).reshape(keys, 2 * DH)
        key, value = sides[:, :DH], sides[:, DH:]

    grad_heads = grad_attn_heads(grad_rows, output_projection_weight)
    grad_in = swap(grad_heads.reshape(seq_count, part_rows, DH)).reshape(-1, DH)

    width = grad_rows.shape[1] // seq_count
    piece = slots // head_count
    mine = lax.dynamic_slice_in_dim(grad_rows, lax.axis_index("head") * piece, piece, 0)
    mine = swap(mine.reshape(piece, seq_count, width).transpose(1, 0, 2))
    all_rows = lax.all_gather(mine, "head", axis=1, tiled=True)

    key_type = BF16 if quarters == 1 else F32
    attended, query_grad, key_grad, value_grad = attention(
        part, live, query, grad_in, key, value, slots, part_rows, key_type
    )

    gathered = lax.all_gather(attended, "seq", axis=0).reshape(heads, keys, DH)
    all_rows = all_rows.reshape(seq_count, quarters, part_rows, width).transpose(1, 0, 2, 3)
    weight_grad = weight_grad_heads(all_rows.reshape(keys, width), gathered)

    if quarters == 1:
        back = jnp.concatenate([query_grad, key_grad, value_grad], axis=1)
        home = swap(back.reshape(seq_count, slots, 3 * DH))
    else:
        query_home = swap(query_grad.reshape(seq_count, part_rows, DH)).reshape(heads, slots, DH)
        back = jnp.concatenate([key_grad, value_grad], axis=1)
        key_home = swap(back.reshape(seq_count, slots, 2 * DH))
        key_home = jnp.sum(key_home.reshape(heads, quarters, slots, 2 * DH), axis=1)
        home = jnp.concatenate([query_home, key_home.astype(BF16)], axis=2)
    projection_grad = unpack_heads(index, home, tok_dev).transpose(1, 0, 2)
    return (projection_grad, weight_grad)


def pack_whole_kernel(index_ref, proj_ref, out_ref, loaded, arrive):
    copies = [
        pltpu.make_async_copy(proj_ref.at[which], loaded.at[which], arrive.at[which])
        for which in range(3)
    ]
    for copy in copies:
        copy.start()
    token = lax.broadcasted_iota(jnp.int32, (loaded.shape[1], index_ref.shape[1]), 0)
    selector = jnp.where(token == index_ref[...], 1.0, 0.0).T.astype(BF16)
    for which, copy in enumerate(copies):
        copy.wait()
        rows = dot(selector, loaded[which]).astype(BF16)
        for head in range(out_ref.shape[0]):
            out_ref[head, :, which * DH : (which + 1) * DH] = rows[:, head * DH : (head + 1) * DH]


def pack_whole(index, proj):
    slots = index.shape[1]
    _, tokens, width = proj.shape
    heads = width // DH
    return pl.pallas_call(
        pack_whole_kernel,
        in_specs=[pl.BlockSpec(), pl.BlockSpec(memory_space=pltpu.HBM)],
        out_shape=jax.ShapeDtypeStruct((heads, slots, 3 * DH), BF16),
        scratch_shapes=[pltpu.VMEM(proj.shape, BF16), pltpu.SemaphoreType.DMA((3,))],
        compiler_params=params(VMEM_MOST),
        cost_estimate=pl.CostEstimate(
            flops=2 * slots * tokens * 3 * width, bytes_accessed=8 * tokens * width, transcendentals=0
        ),
    )(index, proj)


def exchange(block, axis, bit):
    return lax.ppermute(block, axis, [(i, i ^ bit) for i in range(lax.axis_size(axis))])


def gather_blocks(block, axis, bits, held=None):
    held = {0: block} if held is None else dict(held)
    reached = [0]
    for bit in bits:
        for step in list(reached):
            if step ^ bit not in held:
                held[step ^ bit] = exchange(held[step], axis, bit)
            reached.append(step ^ bit)
    return [held[step] for step in range(lax.axis_size(axis))]


SMEM_SPEC = pl.BlockSpec(memory_space=pltpu.SMEM)
VMEM_SPEC = pl.BlockSpec(memory_space=pltpu.VMEM)


def grad_swap_kernel(count, place_ref, *refs):
    row_refs, weight_ref, out_ref, piece_ref, total = refs[:count], *refs[count:]
    mine = place_ref[1]
    seq_count, height, _ = piece_ref.shape
    slots, depth = row_refs[0].shape
    piece = slots // count
    chunks = height // piece
    per_block = depth // (chunks * DH)
    for step in range(count):

        @pl.when(pl.program_id(0) == step)
        def _(step=step):
            part = dot(row_refs[step][...], weight_ref[...])
            total[...] = part if step == 0 else total[...] + part
            share = row_refs[step][pl.ds(pl.multiple_of(mine * piece, piece), piece), :]
            for chunk in range(per_block * chunks):
                partner = (mine ^ step) * per_block + chunk // chunks
                start = chunk % chunks * piece
                piece_ref[partner, start : start + piece, :] = share[:, chunk * DH : (chunk + 1) * DH]

    @pl.when(pl.program_id(0) == count - 1)
    def _():
        for head in range(seq_count):
            out_ref[head] = total[:, head * DH : (head + 1) * DH].astype(BF16)


def grad_swap(place, blocks, weight, seq_count):
    count = len(blocks)
    slots, depth = blocks[0].shape
    columns = weight.shape[1]
    height = slots // count * (count * depth // seq_count // DH)
    return pl.pallas_call(
        functools.partial(grad_swap_kernel, count),
        grid_spec=pltpu.PrefetchScalarGridSpec(
            num_scalar_prefetch=1,
            grid=(count,),
            in_specs=[pl.BlockSpec((slots, depth), lambda i, place: (0, 0))] * count
            + [pl.BlockSpec((depth, columns), lambda i, place: (place[1] ^ i, 0))],
            out_specs=[
                pl.BlockSpec((seq_count, rows, DH), lambda i, place: (0, 0, 0))
                for rows in (slots, height)
            ],
            scratch_shapes=[pltpu.VMEM((slots, columns), F32)],
        ),
        out_shape=[
            jax.ShapeDtypeStruct((seq_count, rows, DH), BF16) for rows in (slots, height)
        ],
        compiler_params=params(),
        cost_estimate=pl.CostEstimate(
            flops=2 * slots * count * depth * columns,
            bytes_accessed=2 * count * depth * columns,
            transcendentals=0,
        ),
    )(place, *blocks, weight)


def weight_grad_swap_kernel(head_count, seq_count, place_ref, *refs):
    piece_refs = refs[:head_count]
    attended_refs = refs[head_count : head_count + seq_count]
    out_ref, rows = refs[-2:]
    me, mine = place_ref[0], place_ref[1]
    chunks = rows.shape[1] // DH
    piece = piece_refs[0].shape[1] // chunks
    slots = piece * head_count
    for part in range(head_count):
        for shard in range(seq_count):
            here = pl.ds(pl.multiple_of(shard * slots + (mine ^ part) * piece, piece), piece)
            for chunk in range(chunks):
                rows[here, chunk * DH : (chunk + 1) * DH] = piece_refs[part][
                    shard, chunk * piece : (chunk + 1) * piece, :
                ]
    for step in range(0, seq_count, 2):
        pair = jnp.concatenate([attended_refs[step][...], attended_refs[step + 1][...]], axis=1)
        product = dot_rows(rows[...], pair)
        for side in range(2):
            column = pl.multiple_of((me ^ (step + side)) * DH, DH)
            out_ref[:, pl.ds(column, DH)] = product[:, side * DH : (side + 1) * DH]


def weight_grad_swap(place, pieces, attended):
    head_count, seq_count = len(pieces), len(attended)
    keys = attended[0].shape[0]
    width = pieces[0].shape[1] // (keys // seq_count // head_count) * DH
    return pl.pallas_call(
        functools.partial(weight_grad_swap_kernel, head_count, seq_count),
        in_specs=[SMEM_SPEC] + [VMEM_SPEC] * (head_count + seq_count),
        out_specs=VMEM_SPEC,
        out_shape=jax.ShapeDtypeStruct((width, seq_count * DH), F32),
        scratch_shapes=[pltpu.VMEM((keys, width), BF16)],
        compiler_params=params(),
        cost_estimate=pl.CostEstimate(
            flops=2 * keys * width * seq_count * DH,
            bytes_accessed=8 * keys * DH * seq_count,
            transcendentals=0,
        ),
    )(place, *pieces, *attended)


def mark_live(count_ref, live_ref, slots):
    for shard in range(live_ref.shape[0] // slots):
        inside = lax.broadcasted_iota(jnp.int32, (slots, live_ref.shape[1]), 0)
        live_ref[shard * slots : (shard + 1) * slots] = jnp.where(
            inside < count_ref[shard], 0.0, -1e30
        )


def masked_scores(start, keys, key_ref, query, live_ref):
    scores = dot_cols(key_ref[:keys], query) * (1.0 / math.sqrt(DH)) + live_ref[:keys, :1]
    row = start + lax.broadcasted_iota(jnp.int32, (1, QUERY_BLOCK), 1)
    key_pos = start + lax.broadcasted_iota(jnp.int32, (QUERY_BLOCK, 1), 0)
    edge = jnp.where(key_pos <= row, scores[start:], -1e30)
    return jnp.concatenate([scores[:start], edge], axis=0) if start else edge


def split_blocks(block_ref, *refs):
    shards, slots, _ = block_ref.shape
    for shard in range(shards):
        for which, ref in enumerate(refs):
            ref[shard * slots : (shard + 1) * slots] = block_ref[
                shard, :, which * DH : (which + 1) * DH
            ]


def forward_kernel(
    count_ref, block_ref, attended_ref, stat_ref, live_ref, query_ref, key_ref, value_ref
):
    mark_live(count_ref, live_ref, block_ref.shape[1])
    split_blocks(block_ref, query_ref, key_ref, value_ref)
    value_flip = value_ref[...].T
    for start in range(0, query_ref.shape[0], QUERY_BLOCK):
        rows = slice(start, start + QUERY_BLOCK)
        keys = start + QUERY_BLOCK
        scores = masked_scores(start, keys, key_ref, query_ref[rows], live_ref)
        peak = jnp.max(scores, axis=0, keepdims=True)
        weights = jnp.exp(scores - peak)
        inverse = 1.0 / jnp.sum(weights, axis=0, keepdims=True)
        attended = dot(value_flip[:, :keys], (weights * inverse).astype(BF16))
        attended_ref[rows] = attended.T.astype(BF16)
        stat_ref[0:1, rows] = peak
        stat_ref[1:2, rows] = inverse


def attention_cost(keys, dots):
    return pl.CostEstimate(
        flops=dots * keys * keys * DH, bytes_accessed=16 * keys * DH, transcendentals=keys * keys // 2
    )


def forward(counts, blocks):
    keys = blocks.shape[0] * blocks.shape[1]
    return pl.pallas_call(
        forward_kernel,
        out_shape=[
            jax.ShapeDtypeStruct((keys, DH), BF16),
            jax.ShapeDtypeStruct((8, keys), F32),
        ],
        in_specs=[SMEM_SPEC, pl.BlockSpec()],
        scratch_shapes=[pltpu.VMEM((keys, DH), F32)] + [pltpu.VMEM((keys, DH), BF16)] * 3,
        compiler_params=params(),
        cost_estimate=attention_cost(keys, 2),
    )(counts, blocks)


def backward_kernel(
    count_ref,
    block_ref,
    attended_ref,
    stat_ref,
    grads_ref,
    out_ref,
    live_ref,
    query_ref,
    key_ref,
    value_ref,
    grad_ref,
    query_total,
    key_total,
    value_total,
):
    seq_count, slots, _ = out_ref.shape
    scale = 1.0 / math.sqrt(DH)
    mark_live(count_ref, live_ref, slots)
    split_blocks(block_ref, query_ref, key_ref, value_ref)
    split_blocks(grads_ref, grad_ref)
    key_flip = key_ref[...].T
    for start in range(0, query_ref.shape[0], QUERY_BLOCK):
        rows = slice(start, start + QUERY_BLOCK)
        keys = start + QUERY_BLOCK
        query = query_ref[rows]
        grad = grad_ref[rows]
        scores = masked_scores(start, keys, key_ref, query, live_ref)
        probs = jnp.exp(scores - stat_ref[0:1, rows]) * stat_ref[1:2, rows]
        probs_low = probs.astype(BF16)
        product = grad.astype(F32) * attended_ref[rows].astype(F32)
        row_dot = jnp.sum(product.T, axis=0, keepdims=True)
        grad_probs = dot_cols(value_ref[:keys], grad)
        grad_scores = (probs * (grad_probs - row_dot)).astype(BF16)
        query_total[rows] = (dot(key_flip[:, :keys], grad_scores) * scale).T.astype(BF16)
        key_part = dot(grad_scores, query)
        value_part = dot(probs_low, grad)
        if start:
            key_total[:start] += key_part[:start]
            value_total[:start] += value_part[:start]
        key_total[rows] = key_part[start:]
        value_total[rows] = value_part[start:]
    for shard in range(seq_count):
        here = slice(shard * slots, (shard + 1) * slots)
        out_ref[shard, :, :DH] = query_total[here]
        out_ref[shard, :, DH : 2 * DH] = (key_total[here] * scale).astype(BF16)
        out_ref[shard, :, 2 * DH :] = value_total[here].astype(BF16)


def backward(counts, blocks, attended, stats, grads):
    keys = attended.shape[0]
    return pl.pallas_call(
        backward_kernel,
        in_specs=[SMEM_SPEC] + [pl.BlockSpec()] * 4,
        out_shape=jax.ShapeDtypeStruct(blocks.shape, BF16),
        scratch_shapes=[pltpu.VMEM((keys, DH), F32)]
        + [pltpu.VMEM((keys, DH), BF16)] * 5
        + [pltpu.VMEM((keys, DH), F32)] * 2,
        compiler_params=params(VMEM_MOST),
        cost_estimate=attention_cost(keys, 5),
    )(counts, blocks, attended, stats, grads)


def on_device_whole_heads(
    projections,
    output_gradient,
    output_projection_weight,
    kept_token_indices,
    surviving_token_count,
):
    tok_dev = projections.shape[0]
    slots = kept_token_indices.shape[1]
    seq_count = lax.axis_size("seq")
    head_count = lax.axis_size("head")
    index = kept_token_indices
    place = jnp.stack([lax.axis_index("seq"), lax.axis_index("head")]).astype(jnp.int32)
    seq_bits = [1 << bit for bit in reversed(range(seq_count.bit_length() - 1))]
    head_bits = [1 << bit for bit in reversed(range(head_count.bit_length() - 1))]

    grad_local = pack_grad(index, output_gradient)
    grad_blocks = gather_blocks(grad_local, "head", head_bits)
    packed = pack_whole(index, projections.transpose(1, 0, 2))

    def swap(blocks):
        return lax.all_to_all(blocks, "seq", split_axis=0, concat_axis=0, tiled=True)

    arrived = swap(packed)
    grads, rows = grad_swap(place, grad_blocks, output_projection_weight, seq_count)
    grads = swap(grads)
    grads, rows = lax.optimization_barrier((grads, rows))
    rows = swap(rows)
    attended, stats = forward(surviving_token_count, arrived)

    held = {bit: exchange(attended, "seq", bit) for bit in seq_bits}
    near, last = seq_bits[-2], seq_bits[-1]
    held[near ^ last] = exchange(held[near], "seq", last)
    back = backward(surviving_token_count, arrived, attended, stats, grads)
    back, held, rows = lax.optimization_barrier((back, held, rows))
    gathered = gather_blocks(attended, "seq", seq_bits, {0: attended, **held})
    home = swap(back)
    pieces = gather_blocks(rows, "head", head_bits)
    weight_grad = weight_grad_swap(place, pieces, gathered)
    projection_grad = unpack_heads(index, home, tok_dev).transpose(1, 0, 2)
    return (projection_grad, weight_grad)


def on_device(projections, output_gradient, weight, index, counts):
    heads = projections.shape[2] // DH
    seq_count, head_count = lax.axis_size("seq"), lax.axis_size("head")
    width = output_gradient.shape[1] * head_count // seq_count
    whole = seq_count == heads and seq_count % 2 == 0 and width % DH == 0
    powers = seq_count & (seq_count - 1) == 0 and head_count & (head_count - 1) == 0
    body = on_device_whole_heads if whole and powers else on_device_split_heads
    return body(projections, output_gradient, weight, index, counts)


def solution(mesh):
    return jax.shard_map(
        on_device,
        mesh=mesh,
        in_specs=(P("seq", None, "head"), P("seq", "head"), P(None, "head"), P("seq", None), P()),
        out_specs=(P("seq", None, "head"), P("seq", "head")),
        check_vma=False,
    )
```

```python
import functools
import math

import jax
import jax.numpy as jnp
from jax import lax
from jax.experimental import pallas as pl
from jax.experimental.pallas import tpu as pltpu
from jax.sharding import PartitionSpec as P

DH = 128
QUERY_BLOCK = 256
VMEM_BYTES = 20 * 1024 * 1024
VMEM_MOST = 62 * 1024 * 1024
F32 = jnp.float32
BF16 = jnp.bfloat16


def params(limit=VMEM_BYTES):
    return pltpu.CompilerParams(vmem_limit_bytes=limit)


def dot(left, right):
    return jnp.dot(left, right, preferred_element_type=F32)


def dot_rows(left, right):
    return lax.dot_general(left, right, (((0,), (0,)), ((), ())), preferred_element_type=F32)


def dot_cols(left, right):
    return lax.dot_general(left, right, (((1,), (1,)), ((), ())), preferred_element_type=F32)


def token_selector(index_ref, tokens):
    slots = index_ref.shape[1]
    token = lax.broadcasted_iota(jnp.int32, (tokens, slots), 0)
    return jnp.where(token == index_ref[...], 1.0, 0.0).astype(BF16)


def pack_grad_kernel(index_ref, grad_ref, out_ref):
    selector = token_selector(index_ref, grad_ref.shape[0])
    out_ref[...] = dot_rows(selector, grad_ref[...]).astype(BF16)


def pack_grad(index, grad):
    slots = index.shape[1]
    return pl.pallas_call(
        pack_grad_kernel,
        out_shape=jax.ShapeDtypeStruct((slots, grad.shape[1]), BF16),
        compiler_params=params(),
    )(index, grad)


def pack_heads_kernel(index_ref, proj_ref, out_ref):
    selector = token_selector(index_ref, proj_ref.shape[1])
    for which in range(3):
        rows = dot_rows(selector, proj_ref[which]).astype(BF16)
        for head in range(out_ref.shape[0]):
            out_ref[head, :, which * DH : (which + 1) * DH] = rows[:, head * DH : (head + 1) * DH]


def pack_heads(index, proj):
    slots = index.shape[1]
    _, tokens, width = proj.shape
    heads = width // DH
    step = 2
    return pl.pallas_call(
        pack_heads_kernel,
        grid=(heads // step,),
        in_specs=[
            pl.BlockSpec((1, slots), lambda i: (0, 0)),
            pl.BlockSpec((3, tokens, step * DH), lambda i: (0, 0, i)),
        ],
        out_specs=pl.BlockSpec((step, slots, 3 * DH), lambda i: (i, 0, 0)),
        out_shape=jax.ShapeDtypeStruct((heads, slots, 3 * DH), BF16),
        compiler_params=params(),
    )(index, proj)


def unpack_heads_kernel(index_ref, rows_ref, out_ref):
    selector = token_selector(index_ref, out_ref.shape[1])
    for head in range(rows_ref.shape[0]):
        tokens = dot(selector, rows_ref[head]).astype(BF16)
        for which in range(3):
            out_ref[which, :, head * DH : (head + 1) * DH] = tokens[
                :, which * DH : (which + 1) * DH
            ]


def unpack_heads(index, rows, tokens):
    heads, slots, _ = rows.shape
    step = 2
    return pl.pallas_call(
        unpack_heads_kernel,
        grid=(heads // step,),
        in_specs=[
            pl.BlockSpec((1, slots), lambda i: (0, 0)),
            pl.BlockSpec((step, slots, 3 * DH), lambda i: (i, 0, 0)),
        ],
        out_specs=pl.BlockSpec((3, tokens, step * DH), lambda i: (0, 0, i)),
        out_shape=jax.ShapeDtypeStruct((3, tokens, heads * DH), BF16),
        compiler_params=params(),
    )(index, rows)


def grad_attn_kernel(rows_ref, weight_ref, out_ref):
    product = dot(rows_ref[...], weight_ref[...]).astype(BF16)
    for head in range(out_ref.shape[0]):
        out_ref[head] = product[:, head * DH : (head + 1) * DH]


def grad_attn_heads(rows, weight):
    slots, depth = rows.shape
    heads = weight.shape[1] // DH
    step = 2
    return pl.pallas_call(
        grad_attn_kernel,
        grid=(heads // step,),
        in_specs=[
            pl.BlockSpec((slots, depth), lambda i: (0, 0)),
            pl.BlockSpec((depth, step * DH), lambda i: (0, i)),
        ],
        out_specs=pl.BlockSpec((step, slots, DH), lambda i: (i, 0, 0)),
        out_shape=jax.ShapeDtypeStruct((heads, slots, DH), BF16),
        compiler_params=params(),
    )(rows, weight)


def weight_grad_kernel(rows_ref, attended_ref, out_ref):
    attended = jnp.concatenate([attended_ref[head] for head in range(attended_ref.shape[0])], axis=1)
    out_ref[...] = dot_rows(rows_ref[...], attended)


def weight_grad_heads(rows, attended):
    total, width = rows.shape
    heads = attended.shape[0]
    step = 2
    return pl.pallas_call(
        weight_grad_kernel,
        grid=(heads // step,),
        in_specs=[
            pl.BlockSpec((total, width), lambda i: (0, 0)),
            pl.BlockSpec((step, total, DH), lambda i: (i, 0, 0)),
        ],
        out_specs=pl.BlockSpec((width, step * DH), lambda i: (0, i)),
        out_shape=jax.ShapeDtypeStruct((width, heads * DH), F32),
        compiler_params=params(),
    )(rows, attended)


def attention_kernel(
    slots,
    part_rows,
    part_ref,
    live_ref,
    query_ref,
    grad_ref,
    key_ref,
    value_ref,
    attended_ref,
    query_grad_ref,
    key_grad_ref,
    value_grad_ref,
    key_total,
    value_total,
):
    scale = 1.0 / math.sqrt(DH)
    rows_total = query_ref.shape[0]
    keys_total = key_ref.shape[0]
    quarters = slots // part_rows
    key_flip = key_ref[...].T
    value_flip = value_ref[...].T
    for start in range(0, rows_total, QUERY_BLOCK):
        rows = slice(start, start + QUERY_BLOCK)
        last = start + QUERY_BLOCK - 1
        last_pos = last // part_rows * slots + (quarters - 1) * part_rows + last % part_rows
        first_pos = start // part_rows * slots + start % part_rows
        keys = min(-(-(last_pos + 1) // 128) * 128, keys_total)
        clear = first_pos // 128 * 128
        query = query_ref[rows]
        grad = grad_ref[rows]
        row = start + lax.broadcasted_iota(jnp.int32, (1, QUERY_BLOCK), 1)
        if quarters > 1:
            shard = row // part_rows
            row = shard * slots + part_ref[0] * part_rows + row - shard * part_rows
        scores = dot_cols(key_ref[:keys], query) * scale + live_ref[:keys, :1]
        key_pos = clear + lax.broadcasted_iota(jnp.int32, (keys - clear, 1), 0)
        edge = jnp.where(key_pos <= row, scores[clear:], -1e30)
        scores = jnp.concatenate([scores[:clear], edge], axis=0) if clear else edge
        peak = jnp.max(scores, axis=0, keepdims=True)
        weights = jnp.exp(scores - peak)
        probs = weights * (1.0 / jnp.sum(weights, axis=0, keepdims=True))
        probs_low = probs.astype(BF16)
        attended = dot(value_flip[:, :keys], probs_low)
        attended_ref[rows] = attended.T.astype(BF16)
        row_dot = jnp.sum(grad.T.astype(F32) * attended, axis=0, keepdims=True)
        grad_probs = dot_cols(value_ref[:keys], grad)
        grad_scores = (probs * (grad_probs - row_dot)).astype(BF16)
        query_grad = dot(key_flip[:, :keys], grad_scores) * scale
        query_grad_ref[rows] = query_grad.T.astype(BF16)
        key_part = dot(grad_scores, query)
        value_part = dot(probs_low, grad)
        prev = start - 1
        reached = 0
        if start:
            prev_pos = prev // part_rows * slots + (quarters - 1) * part_rows + prev % part_rows
            reached = min(-(-(prev_pos + 1) // 128) * 128, keys_total)
        if reached:
            key_total[:reached] += key_part[:reached]
            value_total[:reached] += value_part[:reached]
        if keys > reached:
            key_total[reached:keys] = key_part[reached:]
            value_total[reached:keys] = value_part[reached:]
    key_grad_ref[...] = (key_total[...] * scale).astype(key_grad_ref.dtype)
    value_grad_ref[...] = value_total[...].astype(value_grad_ref.dtype)


def attention(part, live, query, grad, key, value, slots, part_rows, key_type):
    rows, keys = query.shape[0], key.shape[0]
    vmem = pl.BlockSpec(memory_space=pltpu.VMEM)
    return pl.pallas_call(
        functools.partial(attention_kernel, slots, part_rows),
        in_specs=[pl.BlockSpec(memory_space=pltpu.SMEM)] + [vmem] * 5,
        out_specs=[vmem] * 4,
        out_shape=[
            jax.ShapeDtypeStruct((rows, DH), BF16),
            jax.ShapeDtypeStruct((rows, DH), BF16),
            jax.ShapeDtypeStruct((keys, DH), key_type),
            jax.ShapeDtypeStruct((keys, DH), key_type),
        ],
        scratch_shapes=[pltpu.VMEM((keys, DH), F32)] * 2,
        compiler_params=params(),
    )(part, live, query, grad, key, value)


def on_device_split_heads(
    projections,
    output_gradient,
    output_projection_weight,
    kept_token_indices,
    surviving_token_count,
):
    tok_dev = projections.shape[0]
    group_width = projections.shape[2]
    slots = kept_token_indices.shape[1]
    heads = group_width // DH
    seq_count = lax.axis_size("seq")
    head_count = lax.axis_size("head")
    quarters = seq_count // heads
    part_rows = slots // quarters
    part = (lax.axis_index("seq") % quarters).astype(jnp.int32).reshape(1)
    index = kept_token_indices
    keys = seq_count * slots

    grad_local = pack_grad(index, output_gradient)
    grad_rows = lax.all_gather(grad_local, "head", axis=1, tiled=True)
    packed = pack_heads(index, projections.transpose(1, 0, 2))

    position = jnp.arange(slots, dtype=jnp.int32)
    live = position[None, :] < surviving_token_count[:, None]
    live = jnp.where(live, 0.0, -1e30).astype(F32).reshape(keys, 1)
    live = jnp.broadcast_to(live, (keys, DH))

    def swap(blocks):
        return lax.all_to_all(blocks, "seq", split_axis=0, concat_axis=0, tiled=True)

    if quarters == 1:
        arrived = swap(packed).reshape(keys, 3 * DH)
        query, key, value = (arrived[:, n * DH : (n + 1) * DH] for n in range(3))
    else:
        query = swap(packed[:, :, :DH].reshape(seq_count, part_rows, DH))
        query = query.reshape(seq_count * part_rows, DH)
        sides = jnp.broadcast_to(packed[:, None, :, DH:], (heads, quarters, slots, 2 * DH))
        sides = swap(sides.reshape(seq_count, slots, 2 * DH)).reshape(keys, 2 * DH)
        key, value = sides[:, :DH], sides[:, DH:]

    grad_heads = grad_attn_heads(grad_rows, output_projection_weight)
    grad_in = swap(grad_heads.reshape(seq_count, part_rows, DH)).reshape(-1, DH)

    width = grad_rows.shape[1] // seq_count
    piece = slots // head_count
    mine = lax.dynamic_slice_in_dim(grad_rows, lax.axis_index("head") * piece, piece, 0)
    mine = swap(mine.reshape(piece, seq_count, width).transpose(1, 0, 2))
    all_rows = lax.all_gather(mine, "head", axis=1, tiled=True)

    key_type = BF16 if quarters == 1 else F32
    attended, query_grad, key_grad, value_grad = attention(
        part, live, query, grad_in, key, value, slots, part_rows, key_type
    )

    gathered = lax.all_gather(attended, "seq", axis=0).reshape(heads, keys, DH)
    all_rows = all_rows.reshape(seq_count, quarters, part_rows, width).transpose(1, 0, 2, 3)
    weight_grad = weight_grad_heads(all_rows.reshape(keys, width), gathered)

    if quarters == 1:
        back = jnp.concatenate([query_grad, key_grad, value_grad], axis=1)
        home = swap(back.reshape(seq_count, slots, 3 * DH))
    else:
        query_home = swap(query_grad.reshape(seq_count, part_rows, DH)).reshape(heads, slots, DH)
        back = jnp.concatenate([key_grad, value_grad], axis=1)
        key_home = swap(back.reshape(seq_count, slots, 2 * DH))
        key_home = jnp.sum(key_home.reshape(heads, quarters, slots, 2 * DH), axis=1)
        home = jnp.concatenate([query_home, key_home.astype(BF16)], axis=2)
    projection_grad = unpack_heads(index, home, tok_dev).transpose(1, 0, 2)
    return (projection_grad, weight_grad)


def pack_whole_kernel(index_ref, proj_ref, out_ref, loaded, arrive):
    copies = [
        pltpu.make_async_copy(proj_ref.at[which], loaded.at[which], arrive.at[which])
        for which in range(3)
    ]
    for copy in copies:
        copy.start()
    token = lax.broadcasted_iota(jnp.int32, (loaded.shape[1], index_ref.shape[1]), 0)
    selector = jnp.where(token == index_ref[...], 1.0, 0.0).T.astype(BF16)
    for which, copy in enumerate(copies):
        copy.wait()
        rows = dot(selector, loaded[which]).astype(BF16)
        for head in range(out_ref.shape[0]):
            out_ref[head, :, which * DH : (which + 1) * DH] = rows[:, head * DH : (head + 1) * DH]


def pack_whole(index, proj):
    slots = index.shape[1]
    _, tokens, width = proj.shape
    heads = width // DH
    return pl.pallas_call(
        pack_whole_kernel,
        in_specs=[pl.BlockSpec(), pl.BlockSpec(memory_space=pltpu.HBM)],
        out_shape=jax.ShapeDtypeStruct((heads, slots, 3 * DH), BF16),
        scratch_shapes=[pltpu.VMEM(proj.shape, BF16), pltpu.SemaphoreType.DMA((3,))],
        compiler_params=params(VMEM_MOST),
        cost_estimate=pl.CostEstimate(
            flops=2 * slots * tokens * 3 * width, bytes_accessed=8 * tokens * width, transcendentals=0
        ),
    )(index, proj)


def exchange(block, axis, bit):
    return lax.ppermute(block, axis, [(i, i ^ bit) for i in range(lax.axis_size(axis))])


def gather_blocks(block, axis, bits, held=None):
    held = {0: block} if held is None else dict(held)
    reached = [0]
    for bit in bits:
        for step in list(reached):
            if step ^ bit not in held:
                held[step ^ bit] = exchange(held[step], axis, bit)
            reached.append(step ^ bit)
    return [held[step] for step in range(lax.axis_size(axis))]


SMEM_SPEC = pl.BlockSpec(memory_space=pltpu.SMEM)
VMEM_SPEC = pl.BlockSpec(memory_space=pltpu.VMEM)


def grad_swap_kernel(count, place_ref, *refs):
    row_refs, weight_ref, out_ref, piece_ref, total = refs[:count], *refs[count:]
    mine = place_ref[1]
    seq_count, height, _ = piece_ref.shape
    slots, depth = row_refs[0].shape
    piece = slots // count
    chunks = height // piece
    per_block = depth // (chunks * DH)
    for step in range(count):

        @pl.when(pl.program_id(0) == step)
        def _(step=step):
            part = dot(row_refs[step][...], weight_ref[...])
            total[...] = part if step == 0 else total[...] + part
            share = row_refs[step][pl.ds(pl.multiple_of(mine * piece, piece), piece), :]
            for chunk in range(per_block * chunks):
                partner = (mine ^ step) * per_block + chunk // chunks
                start = chunk % chunks * piece
                piece_ref[partner, start : start + piece, :] = share[:, chunk * DH : (chunk + 1) * DH]

    @pl.when(pl.program_id(0) == count - 1)
    def _():
        for head in range(seq_count):
            out_ref[head] = total[:, head * DH : (head + 1) * DH].astype(BF16)


def grad_swap(place, blocks, weight, seq_count):
    count = len(blocks)
    slots, depth = blocks[0].shape
    columns = weight.shape[1]
    height = slots // count * (count * depth // seq_count // DH)
    return pl.pallas_call(
        functools.partial(grad_swap_kernel, count),
        grid_spec=pltpu.PrefetchScalarGridSpec(
            num_scalar_prefetch=1,
            grid=(count,),
            in_specs=[pl.BlockSpec((slots, depth), lambda i, place: (0, 0))] * count
            + [pl.BlockSpec((depth, columns), lambda i, place: (place[1] ^ i, 0))],
            out_specs=[
                pl.BlockSpec((seq_count, rows, DH), lambda i, place: (0, 0, 0))
                for rows in (slots, height)
            ],
            scratch_shapes=[pltpu.VMEM((slots, columns), F32)],
        ),
        out_shape=[
            jax.ShapeDtypeStruct((seq_count, rows, DH), BF16) for rows in (slots, height)
        ],
        compiler_params=params(),
        cost_estimate=pl.CostEstimate(
            flops=2 * slots * count * depth * columns,
            bytes_accessed=2 * count * depth * columns,
            transcendentals=0,
        ),
    )(place, *blocks, weight)


def weight_grad_swap_kernel(head_count, seq_count, place_ref, *refs):
    piece_refs = refs[:head_count]
    attended_refs = refs[head_count : head_count + seq_count]
    out_ref, rows = refs[-2:]
    me, mine = place_ref[0], place_ref[1]
    chunks = rows.shape[1] // DH
    piece = piece_refs[0].shape[1] // chunks
    slots = piece * head_count
    for part in range(head_count):
        for shard in range(seq_count):
            here = pl.ds(pl.multiple_of(shard * slots + (mine ^ part) * piece, piece), piece)
            for chunk in range(chunks):
                rows[here, chunk * DH : (chunk + 1) * DH] = piece_refs[part][
                    shard, chunk * piece : (chunk + 1) * piece, :
                ]
    for step in range(0, seq_count, 2):
        pair = jnp.concatenate([attended_refs[step][...], attended_refs[step + 1][...]], axis=1)
        product = dot_rows(rows[...], pair)
        for side in range(2):
            column = pl.multiple_of((me ^ (step + side)) * DH, DH)
            out_ref[:, pl.ds(column, DH)] = product[:, side * DH : (side + 1) * DH]


def weight_grad_swap(place, pieces, attended):
    head_count, seq_count = len(pieces), len(attended)
    keys = attended[0].shape[0]
    width = pieces[0].shape[1] // (keys // seq_count // head_count) * DH
    return pl.pallas_call(
        functools.partial(weight_grad_swap_kernel, head_count, seq_count),
        in_specs=[SMEM_SPEC] + [VMEM_SPEC] * (head_count + seq_count),
        out_specs=VMEM_SPEC,
        out_shape=jax.ShapeDtypeStruct((width, seq_count * DH), F32),
        scratch_shapes=[pltpu.VMEM((keys, width), BF16)],
        compiler_params=params(),
        cost_estimate=pl.CostEstimate(
            flops=2 * keys * width * seq_count * DH,
            bytes_accessed=8 * keys * DH * seq_count,
            transcendentals=0,
        ),
    )(place, *pieces, *attended)


def mark_live(count_ref, live_ref, slots):
    for shard in range(live_ref.shape[0] // slots):
        inside = lax.broadcasted_iota(jnp.int32, (slots, live_ref.shape[1]), 0)
        live_ref[shard * slots : (shard + 1) * slots] = jnp.where(
            inside < count_ref[shard], 0.0, -1e30
        )


def masked_scores(start, keys, key_ref, query, live_ref):
    scores = dot_cols(key_ref[:keys], query) * (1.0 / math.sqrt(DH)) + live_ref[:keys, :1]
    row = start + lax.broadcasted_iota(jnp.int32, (1, QUERY_BLOCK), 1)
    key_pos = start + lax.broadcasted_iota(jnp.int32, (QUERY_BLOCK, 1), 0)
    edge = jnp.where(key_pos <= row, scores[start:], -1e30)
    return jnp.concatenate([scores[:start], edge], axis=0) if start else edge


def split_blocks(block_ref, *refs):
    shards, slots, _ = block_ref.shape
    for shard in range(shards):
        for which, ref in enumerate(refs):
            ref[shard * slots : (shard + 1) * slots] = block_ref[
                shard, :, which * DH : (which + 1) * DH
            ]


def forward_kernel(
    count_ref, block_ref, attended_ref, stat_ref, live_ref, query_ref, key_ref, value_ref
):
    mark_live(count_ref, live_ref, block_ref.shape[1])
    split_blocks(block_ref, query_ref, key_ref, value_ref)
    value_flip = value_ref[...].T
    for start in range(0, query_ref.shape[0], QUERY_BLOCK):
        rows = slice(start, start + QUERY_BLOCK)
        keys = start + QUERY_BLOCK
        scores = masked_scores(start, keys, key_ref, query_ref[rows], live_ref)
        peak = jnp.max(scores, axis=0, keepdims=True)
        weights = jnp.exp(scores - peak)
        inverse = 1.0 / jnp.sum(weights, axis=0, keepdims=True)
        attended = dot(value_flip[:, :keys], (weights * inverse).astype(BF16))
        attended_ref[rows] = attended.T.astype(BF16)
        stat_ref[0:1, rows] = peak
        stat_ref[1:2, rows] = inverse


def attention_cost(keys, dots):
    return pl.CostEstimate(
        flops=dots * keys * keys * DH, bytes_accessed=16 * keys * DH, transcendentals=keys * keys // 2
    )


def forward(counts, blocks):
    keys = blocks.shape[0] * blocks.shape[1]
    return pl.pallas_call(
        forward_kernel,
        out_shape=[
            jax.ShapeDtypeStruct((keys, DH), BF16),
            jax.ShapeDtypeStruct((8, keys), F32),
        ],
        in_specs=[SMEM_SPEC, pl.BlockSpec()],
        scratch_shapes=[pltpu.VMEM((keys, DH), F32)] + [pltpu.VMEM((keys, DH), BF16)] * 3,
        compiler_params=params(),
        cost_estimate=attention_cost(keys, 2),
    )(counts, blocks)


def backward_kernel(
    count_ref,
    block_ref,
    attended_ref,
    stat_ref,
    grads_ref,
    out_ref,
    live_ref,
    query_ref,
    key_ref,
    value_ref,
    grad_ref,
    query_total,
    key_total,
    value_total,
):
    seq_count, slots, _ = out_ref.shape
    scale = 1.0 / math.sqrt(DH)
    mark_live(count_ref, live_ref, slots)
    split_blocks(block_ref, query_ref, key_ref, value_ref)
    split_blocks(grads_ref, grad_ref)
    key_flip = key_ref[...].T
    for start in range(0, query_ref.shape[0], QUERY_BLOCK):
        rows = slice(start, start + QUERY_BLOCK)
        keys = start + QUERY_BLOCK
        query = query_ref[rows]
        grad = grad_ref[rows]
        scores = masked_scores(start, keys, key_ref, query, live_ref)
        probs = jnp.exp(scores - stat_ref[0:1, rows]) * stat_ref[1:2, rows]
        probs_low = probs.astype(BF16)
        product = grad.astype(F32) * attended_ref[rows].astype(F32)
        row_dot = jnp.sum(product.T, axis=0, keepdims=True)
        grad_probs = dot_cols(value_ref[:keys], grad)
        grad_scores = (probs * (grad_probs - row_dot)).astype(BF16)
        query_total[rows] = (dot(key_flip[:, :keys], grad_scores) * scale).T.astype(BF16)
        key_part = dot(grad_scores, query)
        value_part = dot(probs_low, grad)
        if start:
            key_total[:start] += key_part[:start]
            value_total[:start] += value_part[:start]
        key_total[rows] = key_part[start:]
        value_total[rows] = value_part[start:]
    for shard in range(seq_count):
        here = slice(shard * slots, (shard + 1) * slots)
        out_ref[shard, :, :DH] = query_total[here]
        out_ref[shard, :, DH : 2 * DH] = (key_total[here] * scale).astype(BF16)
        out_ref[shard, :, 2 * DH :] = value_total[here].astype(BF16)


def backward(counts, blocks, attended, stats, grads):
    keys = attended.shape[0]
    return pl.pallas_call(
        backward_kernel,
        in_specs=[SMEM_SPEC] + [pl.BlockSpec()] * 4,
        out_shape=jax.ShapeDtypeStruct(blocks.shape, BF16),
        scratch_shapes=[pltpu.VMEM((keys, DH), F32)]
        + [pltpu.VMEM((keys, DH), BF16)] * 5
        + [pltpu.VMEM((keys, DH), F32)] * 2,
        compiler_params=params(VMEM_MOST),
        cost_estimate=attention_cost(keys, 5),
    )(counts, blocks, attended, stats, grads)


def on_device_whole_heads(
    projections,
    output_gradient,
    output_projection_weight,
    kept_token_indices,
    surviving_token_count,
):
    tok_dev = projections.shape[0]
    slots = kept_token_indices.shape[1]
    seq_count = lax.axis_size("seq")
    head_count = lax.axis_size("head")
    index = kept_token_indices
    place = jnp.stack([lax.axis_index("seq"), lax.axis_index("head")]).astype(jnp.int32)
    seq_bits = [1 << bit for bit in reversed(range(seq_count.bit_length() - 1))]
    head_bits = [1 << bit for bit in reversed(range(head_count.bit_length() - 1))]

    def swap(blocks):
        return lax.all_to_all(blocks, "seq", split_axis=0, concat_axis=0, tiled=True)

    packed = pack_whole(index, projections.transpose(1, 0, 2))
    packed, grad_index = lax.optimization_barrier((packed, index))
    arrived = swap(packed)

    grad_blocks = gather_blocks(pack_grad(grad_index, output_gradient), "head", head_bits)
    grads, rows = grad_swap(place, grad_blocks, output_projection_weight, seq_count)
    arrived, grads = lax.optimization_barrier((arrived, grads))
    grads = swap(grads)
    attended, stats = forward(surviving_token_count, arrived)

    far, near, last = seq_bits[0], seq_bits[-2], seq_bits[-1]
    held = {bit: exchange(attended, "seq", bit) for bit in seq_bits}
    grads, rows = lax.optimization_barrier((grads, rows))
    rows = swap(rows)
    held[near ^ last] = exchange(held[near], "seq", last)
    if far != near:
        held[far ^ near] = exchange(held[far], "seq", near)
    back = backward(surviving_token_count, arrived, attended, stats, grads)
    back, held, rows = lax.optimization_barrier((back, held, rows))
    gathered = gather_blocks(attended, "seq", seq_bits, {0: attended, **held})
    home = swap(back)
    pieces = gather_blocks(rows, "head", head_bits)
    weight_grad = weight_grad_swap(place, pieces, gathered)
    projection_grad = unpack_heads(index, home, tok_dev).transpose(1, 0, 2)
    return (projection_grad, weight_grad)


def on_device(projections, output_gradient, weight, index, counts):
    heads = projections.shape[2] // DH
    seq_count, head_count = lax.axis_size("seq"), lax.axis_size("head")
    width = output_gradient.shape[1] * head_count // seq_count
    whole = seq_count == heads and seq_count % 2 == 0 and width % DH == 0
    powers = seq_count & (seq_count - 1) == 0 and head_count & (head_count - 1) == 0
    body = on_device_whole_heads if whole and powers else on_device_split_heads
    return body(projections, output_gradient, weight, index, counts)


def solution(mesh):
    return jax.shard_map(
        on_device,
        mesh=mesh,
        in_specs=(P("seq", None, "head"), P("seq", "head"), P(None, "head"), P("seq", None), P()),
        out_specs=(P("seq", None, "head"), P("seq", "head")),
        check_vma=False,
    )
```

```python
import functools
import math

import jax
import jax.numpy as jnp
from jax import lax
from jax.experimental import pallas as pl
from jax.experimental.pallas import tpu as pltpu
from jax.sharding import PartitionSpec as P

DH = 128
QUERY_BLOCK = 256
VMEM_BYTES = 20 * 1024 * 1024
VMEM_MOST = 62 * 1024 * 1024
F32 = jnp.float32
BF16 = jnp.bfloat16


def params(limit=VMEM_BYTES):
    return pltpu.CompilerParams(vmem_limit_bytes=limit)


def dot(left, right):
    return jnp.dot(left, right, preferred_element_type=F32)


def dot_rows(left, right):
    return lax.dot_general(left, right, (((0,), (0,)), ((), ())), preferred_element_type=F32)


def dot_cols(left, right):
    return lax.dot_general(left, right, (((1,), (1,)), ((), ())), preferred_element_type=F32)


def token_selector(index_ref, tokens):
    slots = index_ref.shape[1]
    token = lax.broadcasted_iota(jnp.int32, (tokens, slots), 0)
    return jnp.where(token == index_ref[...], 1.0, 0.0).astype(BF16)


def pack_grad_kernel(index_ref, grad_ref, out_ref):
    selector = token_selector(index_ref, grad_ref.shape[0])
    out_ref[...] = dot_rows(selector, grad_ref[...]).astype(BF16)


def pack_grad(index, grad):
    slots = index.shape[1]
    return pl.pallas_call(
        pack_grad_kernel,
        out_shape=jax.ShapeDtypeStruct((slots, grad.shape[1]), BF16),
        compiler_params=params(),
    )(index, grad)


def pack_heads_kernel(index_ref, proj_ref, out_ref):
    selector = token_selector(index_ref, proj_ref.shape[1])
    for which in range(3):
        rows = dot_rows(selector, proj_ref[which]).astype(BF16)
        for head in range(out_ref.shape[0]):
            out_ref[head, :, which * DH : (which + 1) * DH] = rows[:, head * DH : (head + 1) * DH]


def pack_heads(index, proj):
    slots = index.shape[1]
    _, tokens, width = proj.shape
    heads = width // DH
    step = 2
    return pl.pallas_call(
        pack_heads_kernel,
        grid=(heads // step,),
        in_specs=[
            pl.BlockSpec((1, slots), lambda i: (0, 0)),
            pl.BlockSpec((3, tokens, step * DH), lambda i: (0, 0, i)),
        ],
        out_specs=pl.BlockSpec((step, slots, 3 * DH), lambda i: (i, 0, 0)),
        out_shape=jax.ShapeDtypeStruct((heads, slots, 3 * DH), BF16),
        compiler_params=params(),
    )(index, proj)


def unpack_heads_kernel(index_ref, rows_ref, out_ref):
    selector = token_selector(index_ref, out_ref.shape[1])
    for head in range(rows_ref.shape[0]):
        tokens = dot(selector, rows_ref[head]).astype(BF16)
        for which in range(3):
            out_ref[which, :, head * DH : (head + 1) * DH] = tokens[
                :, which * DH : (which + 1) * DH
            ]


def unpack_heads(index, rows, tokens):
    heads, slots, _ = rows.shape
    step = 2
    return pl.pallas_call(
        unpack_heads_kernel,
        grid=(heads // step,),
        in_specs=[
            pl.BlockSpec((1, slots), lambda i: (0, 0)),
            pl.BlockSpec((step, slots, 3 * DH), lambda i: (i, 0, 0)),
        ],
        out_specs=pl.BlockSpec((3, tokens, step * DH), lambda i: (0, 0, i)),
        out_shape=jax.ShapeDtypeStruct((3, tokens, heads * DH), BF16),
        compiler_params=params(),
    )(index, rows)


def grad_attn_kernel(rows_ref, weight_ref, out_ref):
    product = dot(rows_ref[...], weight_ref[...]).astype(BF16)
    for head in range(out_ref.shape[0]):
        out_ref[head] = product[:, head * DH : (head + 1) * DH]


def grad_attn_heads(rows, weight):
    slots, depth = rows.shape
    heads = weight.shape[1] // DH
    step = 2
    return pl.pallas_call(
        grad_attn_kernel,
        grid=(heads // step,),
        in_specs=[
            pl.BlockSpec((slots, depth), lambda i: (0, 0)),
            pl.BlockSpec((depth, step * DH), lambda i: (0, i)),
        ],
        out_specs=pl.BlockSpec((step, slots, DH), lambda i: (i, 0, 0)),
        out_shape=jax.ShapeDtypeStruct((heads, slots, DH), BF16),
        compiler_params=params(),
    )(rows, weight)


def weight_grad_kernel(rows_ref, attended_ref, out_ref):
    attended = jnp.concatenate([attended_ref[head] for head in range(attended_ref.shape[0])], axis=1)
    out_ref[...] = dot_rows(rows_ref[...], attended)


def weight_grad_heads(rows, attended):
    total, width = rows.shape
    heads = attended.shape[0]
    step = 2
    return pl.pallas_call(
        weight_grad_kernel,
        grid=(heads // step,),
        in_specs=[
            pl.BlockSpec((total, width), lambda i: (0, 0)),
            pl.BlockSpec((step, total, DH), lambda i: (i, 0, 0)),
        ],
        out_specs=pl.BlockSpec((width, step * DH), lambda i: (0, i)),
        out_shape=jax.ShapeDtypeStruct((width, heads * DH), F32),
        compiler_params=params(),
    )(rows, attended)


def attention_kernel(
    slots,
    part_rows,
    part_ref,
    live_ref,
    query_ref,
    grad_ref,
    key_ref,
    value_ref,
    attended_ref,
    query_grad_ref,
    key_grad_ref,
    value_grad_ref,
    key_total,
    value_total,
):
    scale = 1.0 / math.sqrt(DH)
    rows_total = query_ref.shape[0]
    keys_total = key_ref.shape[0]
    quarters = slots // part_rows
    key_flip = key_ref[...].T
    value_flip = value_ref[...].T
    for start in range(0, rows_total, QUERY_BLOCK):
        rows = slice(start, start + QUERY_BLOCK)
        last = start + QUERY_BLOCK - 1
        last_pos = last // part_rows * slots + (quarters - 1) * part_rows + last % part_rows
        first_pos = start // part_rows * slots + start % part_rows
        keys = min(-(-(last_pos + 1) // 128) * 128, keys_total)
        clear = first_pos // 128 * 128
        query = query_ref[rows]
        grad = grad_ref[rows]
        row = start + lax.broadcasted_iota(jnp.int32, (1, QUERY_BLOCK), 1)
        if quarters > 1:
            shard = row // part_rows
            row = shard * slots + part_ref[0] * part_rows + row - shard * part_rows
        scores = dot_cols(key_ref[:keys], query) * scale + live_ref[:keys, :1]
        key_pos = clear + lax.broadcasted_iota(jnp.int32, (keys - clear, 1), 0)
        edge = jnp.where(key_pos <= row, scores[clear:], -1e30)
        scores = jnp.concatenate([scores[:clear], edge], axis=0) if clear else edge
        peak = jnp.max(scores, axis=0, keepdims=True)
        weights = jnp.exp(scores - peak)
        probs = weights * (1.0 / jnp.sum(weights, axis=0, keepdims=True))
        probs_low = probs.astype(BF16)
        attended = dot(value_flip[:, :keys], probs_low)
        attended_ref[rows] = attended.T.astype(BF16)
        row_dot = jnp.sum(grad.T.astype(F32) * attended, axis=0, keepdims=True)
        grad_probs = dot_cols(value_ref[:keys], grad)
        grad_scores = (probs * (grad_probs - row_dot)).astype(BF16)
        query_grad = dot(key_flip[:, :keys], grad_scores) * scale
        query_grad_ref[rows] = query_grad.T.astype(BF16)
        key_part = dot(grad_scores, query)
        value_part = dot(probs_low, grad)
        prev = start - 1
        reached = 0
        if start:
            prev_pos = prev // part_rows * slots + (quarters - 1) * part_rows + prev % part_rows
            reached = min(-(-(prev_pos + 1) // 128) * 128, keys_total)
        if reached:
            key_total[:reached] += key_part[:reached]
            value_total[:reached] += value_part[:reached]
        if keys > reached:
            key_total[reached:keys] = key_part[reached:]
            value_total[reached:keys] = value_part[reached:]
    key_grad_ref[...] = (key_total[...] * scale).astype(key_grad_ref.dtype)
    value_grad_ref[...] = value_total[...].astype(value_grad_ref.dtype)


def attention(part, live, query, grad, key, value, slots, part_rows, key_type):
    rows, keys = query.shape[0], key.shape[0]
    vmem = pl.BlockSpec(memory_space=pltpu.VMEM)
    return pl.pallas_call(
        functools.partial(attention_kernel, slots, part_rows),
        in_specs=[pl.BlockSpec(memory_space=pltpu.SMEM)] + [vmem] * 5,
        out_specs=[vmem] * 4,
        out_shape=[
            jax.ShapeDtypeStruct((rows, DH), BF16),
            jax.ShapeDtypeStruct((rows, DH), BF16),
            jax.ShapeDtypeStruct((keys, DH), key_type),
            jax.ShapeDtypeStruct((keys, DH), key_type),
        ],
        scratch_shapes=[pltpu.VMEM((keys, DH), F32)] * 2,
        compiler_params=params(),
    )(part, live, query, grad, key, value)


def on_device_split_heads(
    projections,
    output_gradient,
    output_projection_weight,
    kept_token_indices,
    surviving_token_count,
):
    tok_dev = projections.shape[0]
    group_width = projections.shape[2]
    slots = kept_token_indices.shape[1]
    heads = group_width // DH
    seq_count = lax.axis_size("seq")
    head_count = lax.axis_size("head")
    quarters = seq_count // heads
    part_rows = slots // quarters
    part = (lax.axis_index("seq") % quarters).astype(jnp.int32).reshape(1)
    index = kept_token_indices
    keys = seq_count * slots

    grad_local = pack_grad(index, output_gradient)
    grad_rows = lax.all_gather(grad_local, "head", axis=1, tiled=True)
    packed = pack_heads(index, projections.transpose(1, 0, 2))

    position = jnp.arange(slots, dtype=jnp.int32)
    live = position[None, :] < surviving_token_count[:, None]
    live = jnp.where(live, 0.0, -1e30).astype(F32).reshape(keys, 1)
    live = jnp.broadcast_to(live, (keys, DH))

    def swap(blocks):
        return lax.all_to_all(blocks, "seq", split_axis=0, concat_axis=0, tiled=True)

    if quarters == 1:
        arrived = swap(packed).reshape(keys, 3 * DH)
        query, key, value = (arrived[:, n * DH : (n + 1) * DH] for n in range(3))
    else:
        query = swap(packed[:, :, :DH].reshape(seq_count, part_rows, DH))
        query = query.reshape(seq_count * part_rows, DH)
        sides = jnp.broadcast_to(packed[:, None, :, DH:], (heads, quarters, slots, 2 * DH))
        sides = swap(sides.reshape(seq_count, slots, 2 * DH)).reshape(keys, 2 * DH)
        key, value = sides[:, :DH], sides[:, DH:]

    grad_heads = grad_attn_heads(grad_rows, output_projection_weight)
    grad_in = swap(grad_heads.reshape(seq_count, part_rows, DH)).reshape(-1, DH)

    width = grad_rows.shape[1] // seq_count
    piece = slots // head_count
    mine = lax.dynamic_slice_in_dim(grad_rows, lax.axis_index("head") * piece, piece, 0)
    mine = swap(mine.reshape(piece, seq_count, width).transpose(1, 0, 2))
    all_rows = lax.all_gather(mine, "head", axis=1, tiled=True)

    key_type = BF16 if quarters == 1 else F32
    attended, query_grad, key_grad, value_grad = attention(
        part, live, query, grad_in, key, value, slots, part_rows, key_type
    )

    gathered = lax.all_gather(attended, "seq", axis=0).reshape(heads, keys, DH)
    all_rows = all_rows.reshape(seq_count, quarters, part_rows, width).transpose(1, 0, 2, 3)
    weight_grad = weight_grad_heads(all_rows.reshape(keys, width), gathered)

    if quarters == 1:
        back = jnp.concatenate([query_grad, key_grad, value_grad], axis=1)
        home = swap(back.reshape(seq_count, slots, 3 * DH))
    else:
        query_home = swap(query_grad.reshape(seq_count, part_rows, DH)).reshape(heads, slots, DH)
        back = jnp.concatenate([key_grad, value_grad], axis=1)
        key_home = swap(back.reshape(seq_count, slots, 2 * DH))
        key_home = jnp.sum(key_home.reshape(heads, quarters, slots, 2 * DH), axis=1)
        home = jnp.concatenate([query_home, key_home.astype(BF16)], axis=2)
    projection_grad = unpack_heads(index, home, tok_dev).transpose(1, 0, 2)
    return (projection_grad, weight_grad)


def pack_whole_kernel(index_ref, proj_ref, out_ref, loaded, arrive):
    copies = [
        pltpu.make_async_copy(proj_ref.at[which], loaded.at[which], arrive.at[which])
        for which in range(3)
    ]
    for copy in copies:
        copy.start()
    token = lax.broadcasted_iota(jnp.int32, (loaded.shape[1], index_ref.shape[1]), 0)
    selector = jnp.where(token == index_ref[...], 1.0, 0.0).T.astype(BF16)
    for which, copy in enumerate(copies):
        copy.wait()
        rows = dot(selector, loaded[which]).astype(BF16)
        for head in range(out_ref.shape[0]):
            out_ref[head, :, which * DH : (which + 1) * DH] = rows[:, head * DH : (head + 1) * DH]


def pack_whole(index, proj):
    slots = index.shape[1]
    _, tokens, width = proj.shape
    heads = width // DH
    return pl.pallas_call(
        pack_whole_kernel,
        in_specs=[pl.BlockSpec(), pl.BlockSpec(memory_space=pltpu.HBM)],
        out_shape=jax.ShapeDtypeStruct((heads, slots, 3 * DH), BF16),
        scratch_shapes=[pltpu.VMEM(proj.shape, BF16), pltpu.SemaphoreType.DMA((3,))],
        compiler_params=params(VMEM_MOST),
        cost_estimate=pl.CostEstimate(
            flops=2 * slots * tokens * 3 * width, bytes_accessed=8 * tokens * width, transcendentals=0
        ),
    )(index, proj)


def exchange(block, axis, bit):
    return lax.ppermute(block, axis, [(i, i ^ bit) for i in range(lax.axis_size(axis))])


def gather_blocks(block, axis, bits, held=None):
    held = {0: block} if held is None else dict(held)
    reached = [0]
    for bit in bits:
        for step in list(reached):
            if step ^ bit not in held:
                held[step ^ bit] = exchange(held[step], axis, bit)
            reached.append(step ^ bit)
    return [held[step] for step in range(lax.axis_size(axis))]


SMEM_SPEC = pl.BlockSpec(memory_space=pltpu.SMEM)
VMEM_SPEC = pl.BlockSpec(memory_space=pltpu.VMEM)


def grad_swap_kernel(count, place_ref, *refs):
    row_refs, weight_ref, out_ref, piece_ref, total = refs[:count], *refs[count:]
    mine = place_ref[1]
    seq_count, height, _ = piece_ref.shape
    slots, depth = row_refs[0].shape
    piece = slots // count
    chunks = height // piece
    per_block = depth // (chunks * DH)
    for step in range(count):

        @pl.when(pl.program_id(0) == step)
        def _(step=step):
            part = dot(row_refs[step][...], weight_ref[...])
            total[...] = part if step == 0 else total[...] + part
            share = row_refs[step][pl.ds(pl.multiple_of(mine * piece, piece), piece), :]
            for chunk in range(per_block * chunks):
                partner = (mine ^ step) * per_block + chunk // chunks
                start = chunk % chunks * piece
                piece_ref[partner, start : start + piece, :] = share[:, chunk * DH : (chunk + 1) * DH]

    @pl.when(pl.program_id(0) == count - 1)
    def _():
        for head in range(seq_count):
            out_ref[head] = total[:, head * DH : (head + 1) * DH].astype(BF16)


def grad_swap(place, blocks, weight, seq_count):
    count = len(blocks)
    slots, depth = blocks[0].shape
    columns = weight.shape[1]
    height = slots // count * (count * depth // seq_count // DH)
    return pl.pallas_call(
        functools.partial(grad_swap_kernel, count),
        grid_spec=pltpu.PrefetchScalarGridSpec(
            num_scalar_prefetch=1,
            grid=(count,),
            in_specs=[pl.BlockSpec((slots, depth), lambda i, place: (0, 0))] * count
            + [pl.BlockSpec((depth, columns), lambda i, place: (place[1] ^ i, 0))],
            out_specs=[
                pl.BlockSpec((seq_count, rows, DH), lambda i, place: (0, 0, 0))
                for rows in (slots, height)
            ],
            scratch_shapes=[pltpu.VMEM((slots, columns), F32)],
        ),
        out_shape=[
            jax.ShapeDtypeStruct((seq_count, rows, DH), BF16) for rows in (slots, height)
        ],
        compiler_params=params(),
        cost_estimate=pl.CostEstimate(
            flops=2 * slots * count * depth * columns,
            bytes_accessed=2 * count * depth * columns,
            transcendentals=0,
        ),
    )(place, *blocks, weight)


def weight_grad_swap_kernel(head_count, seq_count, place_ref, *refs):
    piece_refs = refs[:head_count]
    attended_refs = refs[head_count : head_count + seq_count]
    out_ref, rows = refs[-2:]
    me, mine = place_ref[0], place_ref[1]
    chunks = rows.shape[1] // DH
    piece = piece_refs[0].shape[1] // chunks
    slots = piece * head_count
    for part in range(head_count):
        for shard in range(seq_count):
            here = pl.ds(pl.multiple_of(shard * slots + (mine ^ part) * piece, piece), piece)
            for chunk in range(chunks):
                rows[here, chunk * DH : (chunk + 1) * DH] = piece_refs[part][
                    shard, chunk * piece : (chunk + 1) * piece, :
                ]
    for step in range(0, seq_count, 2):
        pair = jnp.concatenate([attended_refs[step][...], attended_refs[step + 1][...]], axis=1)
        product = dot_rows(rows[...], pair)
        for side in range(2):
            column = pl.multiple_of((me ^ (step + side)) * DH, DH)
            out_ref[:, pl.ds(column, DH)] = product[:, side * DH : (side + 1) * DH]


def weight_grad_swap(place, pieces, attended):
    head_count, seq_count = len(pieces), len(attended)
    keys = attended[0].shape[0]
    width = pieces[0].shape[1] // (keys // seq_count // head_count) * DH
    return pl.pallas_call(
        functools.partial(weight_grad_swap_kernel, head_count, seq_count),
        in_specs=[SMEM_SPEC] + [VMEM_SPEC] * (head_count + seq_count),
        out_specs=VMEM_SPEC,
        out_shape=jax.ShapeDtypeStruct((width, seq_count * DH), F32),
        scratch_shapes=[pltpu.VMEM((keys, width), BF16)],
        compiler_params=params(),
        cost_estimate=pl.CostEstimate(
            flops=2 * keys * width * seq_count * DH,
            bytes_accessed=8 * keys * DH * seq_count,
            transcendentals=0,
        ),
    )(place, *pieces, *attended)


def mark_live(count_ref, live_ref, slots):
    for shard in range(live_ref.shape[0] // slots):
        inside = lax.broadcasted_iota(jnp.int32, (slots, live_ref.shape[1]), 0)
        live_ref[shard * slots : (shard + 1) * slots] = jnp.where(
            inside < count_ref[shard], 0.0, -1e30
        )


def masked_scores(start, keys, key_ref, query, live_ref):
    scores = dot_cols(key_ref[:keys], query) * (1.0 / math.sqrt(DH)) + live_ref[:keys, :1]
    row = start + lax.broadcasted_iota(jnp.int32, (1, QUERY_BLOCK), 1)
    key_pos = start + lax.broadcasted_iota(jnp.int32, (QUERY_BLOCK, 1), 0)
    edge = jnp.where(key_pos <= row, scores[start:], -1e30)
    return jnp.concatenate([scores[:start], edge], axis=0) if start else edge


def split_blocks(block_ref, *refs):
    shards, slots, _ = block_ref.shape
    for shard in range(shards):
        for which, ref in enumerate(refs):
            ref[shard * slots : (shard + 1) * slots] = block_ref[
                shard, :, which * DH : (which + 1) * DH
            ]


def forward_kernel(
    count_ref, block_ref, attended_ref, stat_ref, live_ref, query_ref, key_ref, value_ref
):
    mark_live(count_ref, live_ref, block_ref.shape[1])
    split_blocks(block_ref, query_ref, key_ref, value_ref)
    value_flip = value_ref[...].T
    for start in range(0, query_ref.shape[0], QUERY_BLOCK):
        rows = slice(start, start + QUERY_BLOCK)
        keys = start + QUERY_BLOCK
        scores = masked_scores(start, keys, key_ref, query_ref[rows], live_ref)
        peak = jnp.max(scores, axis=0, keepdims=True)
        weights = jnp.exp(scores - peak)
        inverse = 1.0 / jnp.sum(weights, axis=0, keepdims=True)
        attended = dot(value_flip[:, :keys], (weights * inverse).astype(BF16))
        attended_ref[rows] = attended.T.astype(BF16)
        stat_ref[0:1, rows] = peak
        stat_ref[1:2, rows] = inverse


def attention_cost(keys, dots):
    return pl.CostEstimate(
        flops=dots * keys * keys * DH, bytes_accessed=16 * keys * DH, transcendentals=keys * keys // 2
    )


def forward(counts, blocks):
    keys = blocks.shape[0] * blocks.shape[1]
    return pl.pallas_call(
        forward_kernel,
        out_shape=[
            jax.ShapeDtypeStruct((keys, DH), BF16),
            jax.ShapeDtypeStruct((8, keys), F32),
        ],
        in_specs=[SMEM_SPEC, pl.BlockSpec()],
        scratch_shapes=[pltpu.VMEM((keys, DH), F32)] + [pltpu.VMEM((keys, DH), BF16)] * 3,
        compiler_params=params(),
        cost_estimate=attention_cost(keys, 2),
    )(counts, blocks)


def backward_kernel(
    count_ref,
    block_ref,
    attended_ref,
    stat_ref,
    grads_ref,
    out_ref,
    live_ref,
    query_ref,
    key_ref,
    value_ref,
    grad_ref,
    query_total,
    key_total,
    value_total,
):
    seq_count, slots, _ = out_ref.shape
    scale = 1.0 / math.sqrt(DH)
    mark_live(count_ref, live_ref, slots)
    split_blocks(block_ref, query_ref, key_ref, value_ref)
    split_blocks(grads_ref, grad_ref)
    key_flip = key_ref[...].T
    for start in range(0, query_ref.shape[0], QUERY_BLOCK):
        rows = slice(start, start + QUERY_BLOCK)
        keys = start + QUERY_BLOCK
        query = query_ref[rows]
        grad = grad_ref[rows]
        scores = masked_scores(start, keys, key_ref, query, live_ref)
        probs = jnp.exp(scores - stat_ref[0:1, rows]) * stat_ref[1:2, rows]
        probs_low = probs.astype(BF16)
        product = grad.astype(F32) * attended_ref[rows].astype(F32)
        row_dot = jnp.sum(product.T, axis=0, keepdims=True)
        grad_probs = dot_cols(value_ref[:keys], grad)
        grad_scores = (probs * (grad_probs - row_dot)).astype(BF16)
        query_total[rows] = (dot(key_flip[:, :keys], grad_scores) * scale).T.astype(BF16)
        key_part = dot(grad_scores, query)
        value_part = dot(probs_low, grad)
        if start:
            key_total[:start] += key_part[:start]
            value_total[:start] += value_part[:start]
        key_total[rows] = key_part[start:]
        value_total[rows] = value_part[start:]
    for shard in range(seq_count):
        here = slice(shard * slots, (shard + 1) * slots)
        out_ref[shard, :, :DH] = query_total[here]
        out_ref[shard, :, DH : 2 * DH] = (key_total[here] * scale).astype(BF16)
        out_ref[shard, :, 2 * DH :] = value_total[here].astype(BF16)


def backward(counts, blocks, attended, stats, grads):
    keys = attended.shape[0]
    return pl.pallas_call(
        backward_kernel,
        in_specs=[SMEM_SPEC] + [pl.BlockSpec()] * 4,
        out_shape=jax.ShapeDtypeStruct(blocks.shape, BF16),
        scratch_shapes=[pltpu.VMEM((keys, DH), F32)]
        + [pltpu.VMEM((keys, DH), BF16)] * 5
        + [pltpu.VMEM((keys, DH), F32)] * 2,
        compiler_params=params(VMEM_MOST),
        cost_estimate=attention_cost(keys, 5),
    )(counts, blocks, attended, stats, grads)


def on_device_whole_heads(
    projections,
    output_gradient,
    output_projection_weight,
    kept_token_indices,
    surviving_token_count,
):
    tok_dev = projections.shape[0]
    slots = kept_token_indices.shape[1]
    seq_count = lax.axis_size("seq")
    head_count = lax.axis_size("head")
    index = kept_token_indices
    place = jnp.stack([lax.axis_index("seq"), lax.axis_index("head")]).astype(jnp.int32)
    seq_bits = [1 << bit for bit in reversed(range(seq_count.bit_length() - 1))]
    head_bits = [1 << bit for bit in reversed(range(head_count.bit_length() - 1))]

    def swap(blocks):
        return lax.all_to_all(blocks, "seq", split_axis=0, concat_axis=0, tiled=True)

    packed = pack_whole(index, projections.transpose(1, 0, 2))
    packed, grad_index = lax.optimization_barrier((packed, index))
    arrived = swap(packed)

    grad_blocks = gather_blocks(pack_grad(grad_index, output_gradient), "head", head_bits)
    grads, rows = grad_swap(place, grad_blocks, output_projection_weight, seq_count)
    arrived, grads = lax.optimization_barrier((arrived, grads))
    grads = swap(grads)
    attended, stats = forward(surviving_token_count, arrived)

    far, near, last = seq_bits[0], seq_bits[-2], seq_bits[-1]
    held = {bit: exchange(attended, "seq", bit) for bit in seq_bits}
    grads, rows, attended = lax.optimization_barrier((grads, rows, attended))
    rows = swap(rows)
    held[near ^ last] = exchange(held[near], "seq", last)
    if far != near:
        held[far ^ near] = exchange(held[far], "seq", near)
    back = backward(surviving_token_count, arrived, attended, stats, grads)
    back, held, rows = lax.optimization_barrier((back, held, rows))
    gathered = gather_blocks(attended, "seq", seq_bits, {0: attended, **held})
    home = swap(back)
    pieces = gather_blocks(rows, "head", head_bits)
    weight_grad = weight_grad_swap(place, pieces, gathered)
    projection_grad = unpack_heads(index, home, tok_dev).transpose(1, 0, 2)
    return (projection_grad, weight_grad)


def on_device(projections, output_gradient, weight, index, counts):
    heads = projections.shape[2] // DH
    seq_count, head_count = lax.axis_size("seq"), lax.axis_size("head")
    width = output_gradient.shape[1] * head_count // seq_count
    whole = seq_count == heads and seq_count % 2 == 0 and width % DH == 0
    powers = seq_count & (seq_count - 1) == 0 and head_count & (head_count - 1) == 0
    body = on_device_whole_heads if whole and powers else on_device_split_heads
    return body(projections, output_gradient, weight, index, counts)


def solution(mesh):
    return jax.shard_map(
        on_device,
        mesh=mesh,
        in_specs=(P("seq", None, "head"), P("seq", "head"), P(None, "head"), P("seq", None), P()),
        out_specs=(P("seq", None, "head"), P("seq", "head")),
        check_vma=False,
    )
```

```python
import functools
import math

import jax
import jax.numpy as jnp
from jax import lax
from jax.experimental import pallas as pl
from jax.experimental.pallas import tpu as pltpu
from jax.sharding import PartitionSpec as P

DH = 128
QUERY_BLOCK = 256
VMEM_BYTES = 20 * 1024 * 1024
VMEM_MOST = 62 * 1024 * 1024
F32 = jnp.float32
BF16 = jnp.bfloat16


def params(limit=VMEM_BYTES):
    return pltpu.CompilerParams(vmem_limit_bytes=limit)


def dot(left, right):
    return jnp.dot(left, right, preferred_element_type=F32)


def dot_rows(left, right):
    return lax.dot_general(left, right, (((0,), (0,)), ((), ())), preferred_element_type=F32)


def dot_cols(left, right):
    return lax.dot_general(left, right, (((1,), (1,)), ((), ())), preferred_element_type=F32)


def token_selector(index_ref, tokens):
    slots = index_ref.shape[1]
    token = lax.broadcasted_iota(jnp.int32, (tokens, slots), 0)
    return jnp.where(token == index_ref[...], 1.0, 0.0).astype(BF16)


def pack_grad_kernel(index_ref, grad_ref, out_ref):
    selector = token_selector(index_ref, grad_ref.shape[0])
    out_ref[...] = dot_rows(selector, grad_ref[...]).astype(BF16)


def pack_grad(index, grad):
    slots = index.shape[1]
    return pl.pallas_call(
        pack_grad_kernel,
        out_shape=jax.ShapeDtypeStruct((slots, grad.shape[1]), BF16),
        compiler_params=params(),
    )(index, grad)


def pack_heads_kernel(index_ref, proj_ref, out_ref):
    selector = token_selector(index_ref, proj_ref.shape[1])
    for which in range(3):
        rows = dot_rows(selector, proj_ref[which]).astype(BF16)
        for head in range(out_ref.shape[0]):
            out_ref[head, :, which * DH : (which + 1) * DH] = rows[:, head * DH : (head + 1) * DH]


def pack_heads(index, proj):
    slots = index.shape[1]
    _, tokens, width = proj.shape
    heads = width // DH
    step = 2
    return pl.pallas_call(
        pack_heads_kernel,
        grid=(heads // step,),
        in_specs=[
            pl.BlockSpec((1, slots), lambda i: (0, 0)),
            pl.BlockSpec((3, tokens, step * DH), lambda i: (0, 0, i)),
        ],
        out_specs=pl.BlockSpec((step, slots, 3 * DH), lambda i: (i, 0, 0)),
        out_shape=jax.ShapeDtypeStruct((heads, slots, 3 * DH), BF16),
        compiler_params=params(),
    )(index, proj)


def unpack_heads_kernel(index_ref, rows_ref, out_ref):
    selector = token_selector(index_ref, out_ref.shape[1])
    for head in range(rows_ref.shape[0]):
        tokens = dot(selector, rows_ref[head]).astype(BF16)
        for which in range(3):
            out_ref[which, :, head * DH : (head + 1) * DH] = tokens[
                :, which * DH : (which + 1) * DH
            ]


def unpack_heads(index, rows, tokens):
    heads, slots, _ = rows.shape
    step = 2
    return pl.pallas_call(
        unpack_heads_kernel,
        grid=(heads // step,),
        in_specs=[
            pl.BlockSpec((1, slots), lambda i: (0, 0)),
            pl.BlockSpec((step, slots, 3 * DH), lambda i: (i, 0, 0)),
        ],
        out_specs=pl.BlockSpec((3, tokens, step * DH), lambda i: (0, 0, i)),
        out_shape=jax.ShapeDtypeStruct((3, tokens, heads * DH), BF16),
        compiler_params=params(),
    )(index, rows)


def grad_attn_kernel(rows_ref, weight_ref, out_ref):
    product = dot(rows_ref[...], weight_ref[...]).astype(BF16)
    for head in range(out_ref.shape[0]):
        out_ref[head] = product[:, head * DH : (head + 1) * DH]


def grad_attn_heads(rows, weight):
    slots, depth = rows.shape
    heads = weight.shape[1] // DH
    step = 2
    return pl.pallas_call(
        grad_attn_kernel,
        grid=(heads // step,),
        in_specs=[
            pl.BlockSpec((slots, depth), lambda i: (0, 0)),
            pl.BlockSpec((depth, step * DH), lambda i: (0, i)),
        ],
        out_specs=pl.BlockSpec((step, slots, DH), lambda i: (i, 0, 0)),
        out_shape=jax.ShapeDtypeStruct((heads, slots, DH), BF16),
        compiler_params=params(),
    )(rows, weight)


def weight_grad_kernel(rows_ref, attended_ref, out_ref):
    attended = jnp.concatenate([attended_ref[head] for head in range(attended_ref.shape[0])], axis=1)
    out_ref[...] = dot_rows(rows_ref[...], attended)


def weight_grad_heads(rows, attended):
    total, width = rows.shape
    heads = attended.shape[0]
    step = 2
    return pl.pallas_call(
        weight_grad_kernel,
        grid=(heads // step,),
        in_specs=[
            pl.BlockSpec((total, width), lambda i: (0, 0)),
            pl.BlockSpec((step, total, DH), lambda i: (i, 0, 0)),
        ],
        out_specs=pl.BlockSpec((width, step * DH), lambda i: (0, i)),
        out_shape=jax.ShapeDtypeStruct((width, heads * DH), F32),
        compiler_params=params(),
    )(rows, attended)


def attention_kernel(
    slots,
    part_rows,
    part_ref,
    live_ref,
    query_ref,
    grad_ref,
    key_ref,
    value_ref,
    attended_ref,
    query_grad_ref,
    key_grad_ref,
    value_grad_ref,
    key_total,
    value_total,
):
    scale = 1.0 / math.sqrt(DH)
    rows_total = query_ref.shape[0]
    keys_total = key_ref.shape[0]
    quarters = slots // part_rows
    key_flip = key_ref[...].T
    value_flip = value_ref[...].T
    for start in range(0, rows_total, QUERY_BLOCK):
        rows = slice(start, start + QUERY_BLOCK)
        last = start + QUERY_BLOCK - 1
        last_pos = last // part_rows * slots + (quarters - 1) * part_rows + last % part_rows
        first_pos = start // part_rows * slots + start % part_rows
        keys = min(-(-(last_pos + 1) // 128) * 128, keys_total)
        clear = first_pos // 128 * 128
        query = query_ref[rows]
        grad = grad_ref[rows]
        row = start + lax.broadcasted_iota(jnp.int32, (1, QUERY_BLOCK), 1)
        if quarters > 1:
            shard = row // part_rows
            row = shard * slots + part_ref[0] * part_rows + row - shard * part_rows
        scores = dot_cols(key_ref[:keys], query) * scale + live_ref[:keys, :1]
        key_pos = clear + lax.broadcasted_iota(jnp.int32, (keys - clear, 1), 0)
        edge = jnp.where(key_pos <= row, scores[clear:], -1e30)
        scores = jnp.concatenate([scores[:clear], edge], axis=0) if clear else edge
        peak = jnp.max(scores, axis=0, keepdims=True)
        weights = jnp.exp(scores - peak)
        probs = weights * (1.0 / jnp.sum(weights, axis=0, keepdims=True))
        probs_low = probs.astype(BF16)
        attended = dot(value_flip[:, :keys], probs_low)
        attended_ref[rows] = attended.T.astype(BF16)
        row_dot = jnp.sum(grad.T.astype(F32) * attended, axis=0, keepdims=True)
        grad_probs = dot_cols(value_ref[:keys], grad)
        grad_scores = (probs * (grad_probs - row_dot)).astype(BF16)
        query_grad = dot(key_flip[:, :keys], grad_scores) * scale
        query_grad_ref[rows] = query_grad.T.astype(BF16)
        key_part = dot(grad_scores, query)
        value_part = dot(probs_low, grad)
        prev = start - 1
        reached = 0
        if start:
            prev_pos = prev // part_rows * slots + (quarters - 1) * part_rows + prev % part_rows
            reached = min(-(-(prev_pos + 1) // 128) * 128, keys_total)
        if reached:
            key_total[:reached] += key_part[:reached]
            value_total[:reached] += value_part[:reached]
        if keys > reached:
            key_total[reached:keys] = key_part[reached:]
            value_total[reached:keys] = value_part[reached:]
    key_grad_ref[...] = (key_total[...] * scale).astype(key_grad_ref.dtype)
    value_grad_ref[...] = value_total[...].astype(value_grad_ref.dtype)


def attention(part, live, query, grad, key, value, slots, part_rows, key_type):
    rows, keys = query.shape[0], key.shape[0]
    vmem = pl.BlockSpec(memory_space=pltpu.VMEM)
    return pl.pallas_call(
        functools.partial(attention_kernel, slots, part_rows),
        in_specs=[pl.BlockSpec(memory_space=pltpu.SMEM)] + [vmem] * 5,
        out_specs=[vmem] * 4,
        out_shape=[
            jax.ShapeDtypeStruct((rows, DH), BF16),
            jax.ShapeDtypeStruct((rows, DH), BF16),
            jax.ShapeDtypeStruct((keys, DH), key_type),
            jax.ShapeDtypeStruct((keys, DH), key_type),
        ],
        scratch_shapes=[pltpu.VMEM((keys, DH), F32)] * 2,
        compiler_params=params(),
    )(part, live, query, grad, key, value)


def on_device_split_heads(
    projections,
    output_gradient,
    output_projection_weight,
    kept_token_indices,
    surviving_token_count,
):
    tok_dev = projections.shape[0]
    group_width = projections.shape[2]
    slots = kept_token_indices.shape[1]
    heads = group_width // DH
    seq_count = lax.axis_size("seq")
    head_count = lax.axis_size("head")
    quarters = seq_count // heads
    part_rows = slots // quarters
    part = (lax.axis_index("seq") % quarters).astype(jnp.int32).reshape(1)
    index = kept_token_indices
    keys = seq_count * slots

    grad_local = pack_grad(index, output_gradient)
    grad_rows = lax.all_gather(grad_local, "head", axis=1, tiled=True)
    packed = pack_heads(index, projections.transpose(1, 0, 2))

    position = jnp.arange(slots, dtype=jnp.int32)
    live = position[None, :] < surviving_token_count[:, None]
    live = jnp.where(live, 0.0, -1e30).astype(F32).reshape(keys, 1)
    live = jnp.broadcast_to(live, (keys, DH))

    def swap(blocks):
        return lax.all_to_all(blocks, "seq", split_axis=0, concat_axis=0, tiled=True)

    if quarters == 1:
        arrived = swap(packed).reshape(keys, 3 * DH)
        query, key, value = (arrived[:, n * DH : (n + 1) * DH] for n in range(3))
    else:
        query = swap(packed[:, :, :DH].reshape(seq_count, part_rows, DH))
        query = query.reshape(seq_count * part_rows, DH)
        sides = jnp.broadcast_to(packed[:, None, :, DH:], (heads, quarters, slots, 2 * DH))
        sides = swap(sides.reshape(seq_count, slots, 2 * DH)).reshape(keys, 2 * DH)
        key, value = sides[:, :DH], sides[:, DH:]

    grad_heads = grad_attn_heads(grad_rows, output_projection_weight)
    grad_in = swap(grad_heads.reshape(seq_count, part_rows, DH)).reshape(-1, DH)

    width = grad_rows.shape[1] // seq_count
    piece = slots // head_count
    mine = lax.dynamic_slice_in_dim(grad_rows, lax.axis_index("head") * piece, piece, 0)
    mine = swap(mine.reshape(piece, seq_count, width).transpose(1, 0, 2))
    all_rows = lax.all_gather(mine, "head", axis=1, tiled=True)

    key_type = BF16 if quarters == 1 else F32
    attended, query_grad, key_grad, value_grad = attention(
        part, live, query, grad_in, key, value, slots, part_rows, key_type
    )

    gathered = lax.all_gather(attended, "seq", axis=0).reshape(heads, keys, DH)
    all_rows = all_rows.reshape(seq_count, quarters, part_rows, width).transpose(1, 0, 2, 3)
    weight_grad = weight_grad_heads(all_rows.reshape(keys, width), gathered)

    if quarters == 1:
        back = jnp.concatenate([query_grad, key_grad, value_grad], axis=1)
        home = swap(back.reshape(seq_count, slots, 3 * DH))
    else:
        query_home = swap(query_grad.reshape(seq_count, part_rows, DH)).reshape(heads, slots, DH)
        back = jnp.concatenate([key_grad, value_grad], axis=1)
        key_home = swap(back.reshape(seq_count, slots, 2 * DH))
        key_home = jnp.sum(key_home.reshape(heads, quarters, slots, 2 * DH), axis=1)
        home = jnp.concatenate([query_home, key_home.astype(BF16)], axis=2)
    projection_grad = unpack_heads(index, home, tok_dev).transpose(1, 0, 2)
    return (projection_grad, weight_grad)


def pack_whole_kernel(index_ref, proj_ref, out_ref, loaded, arrive):
    copies = [
        pltpu.make_async_copy(proj_ref.at[which], loaded.at[which], arrive.at[which])
        for which in range(3)
    ]
    for copy in copies:
        copy.start()
    token = lax.broadcasted_iota(jnp.int32, (loaded.shape[1], index_ref.shape[1]), 0)
    selector = jnp.where(token == index_ref[...], 1.0, 0.0).T.astype(BF16)
    for which, copy in enumerate(copies):
        copy.wait()
        rows = dot(selector, loaded[which]).astype(BF16)
        for head in range(out_ref.shape[0]):
            out_ref[head, :, which * DH : (which + 1) * DH] = rows[:, head * DH : (head + 1) * DH]


def pack_whole(index, proj):
    slots = index.shape[1]
    _, tokens, width = proj.shape
    heads = width // DH
    return pl.pallas_call(
        pack_whole_kernel,
        in_specs=[pl.BlockSpec(), pl.BlockSpec(memory_space=pltpu.HBM)],
        out_shape=jax.ShapeDtypeStruct((heads, slots, 3 * DH), BF16),
        scratch_shapes=[pltpu.VMEM(proj.shape, BF16), pltpu.SemaphoreType.DMA((3,))],
        compiler_params=params(VMEM_MOST),
        cost_estimate=pl.CostEstimate(
            flops=2 * slots * tokens * 3 * width, bytes_accessed=8 * tokens * width, transcendentals=0
        ),
    )(index, proj)


def exchange(block, axis, bit):
    return lax.ppermute(block, axis, [(i, i ^ bit) for i in range(lax.axis_size(axis))])


def gather_blocks(block, axis, bits, held=None):
    held = {0: block} if held is None else dict(held)
    reached = [0]
    for bit in bits:
        for step in list(reached):
            if step ^ bit not in held:
                held[step ^ bit] = exchange(held[step], axis, bit)
            reached.append(step ^ bit)
    return [held[step] for step in range(lax.axis_size(axis))]


SMEM_SPEC = pl.BlockSpec(memory_space=pltpu.SMEM)
VMEM_SPEC = pl.BlockSpec(memory_space=pltpu.VMEM)


def grad_swap_kernel(count, place_ref, *refs):
    row_refs, weight_ref, out_ref, total = refs[:count], refs[count], refs[count + 1], refs[count + 2]
    mine = place_ref[1]
    seq_count, height, _ = out_ref.shape
    slots, depth = row_refs[0].shape
    piece = slots // count
    chunks = (height - slots) // piece
    per_block = depth // (chunks * DH)
    for step in range(count):

        @pl.when(pl.program_id(0) == step)
        def _(step=step):
            part = dot(row_refs[step][...], weight_ref[...])
            total[...] = part if step == 0 else total[...] + part
            share = row_refs[step][pl.ds(pl.multiple_of(mine * piece, piece), piece), :]
            for chunk in range(per_block * chunks):
                partner = (mine ^ step) * per_block + chunk // chunks
                start = slots + chunk % chunks * piece
                out_ref[partner, start : start + piece, :] = share[:, chunk * DH : (chunk + 1) * DH]

    @pl.when(pl.program_id(0) == count - 1)
    def _():
        for head in range(seq_count):
            out_ref[head, :slots, :] = total[:, head * DH : (head + 1) * DH].astype(BF16)


def grad_swap(place, blocks, weight, seq_count):
    count = len(blocks)
    slots, depth = blocks[0].shape
    columns = weight.shape[1]
    height = slots + slots // count * (count * depth // seq_count // DH)
    return pl.pallas_call(
        functools.partial(grad_swap_kernel, count),
        grid_spec=pltpu.PrefetchScalarGridSpec(
            num_scalar_prefetch=1,
            grid=(count,),
            in_specs=[pl.BlockSpec((slots, depth), lambda i, place: (0, 0))] * count
            + [pl.BlockSpec((depth, columns), lambda i, place: (place[1] ^ i, 0))],
            out_specs=pl.BlockSpec((seq_count, height, DH), lambda i, place: (0, 0, 0)),
            scratch_shapes=[pltpu.VMEM((slots, columns), F32)],
        ),
        out_shape=jax.ShapeDtypeStruct((seq_count, height, DH), BF16),
        compiler_params=params(),
        cost_estimate=pl.CostEstimate(
            flops=2 * slots * count * depth * columns,
            bytes_accessed=2 * count * depth * columns,
            transcendentals=0,
        ),
    )(place, *blocks, weight)


def weight_grad_swap_kernel(head_count, seq_count, place_ref, *refs):
    piece_refs = refs[:head_count]
    attended_refs = refs[head_count : head_count + seq_count]
    out_ref, rows = refs[-2:]
    me, mine = place_ref[0], place_ref[1]
    chunks = rows.shape[1] // DH
    piece = piece_refs[0].shape[1] // chunks
    slots = piece * head_count
    for part in range(head_count):
        for shard in range(seq_count):
            here = pl.ds(pl.multiple_of(shard * slots + (mine ^ part) * piece, piece), piece)
            for chunk in range(chunks):
                rows[here, chunk * DH : (chunk + 1) * DH] = piece_refs[part][
                    shard, chunk * piece : (chunk + 1) * piece, :
                ]
    for step in range(0, seq_count, 2):
        pair = jnp.concatenate([attended_refs[step][...], attended_refs[step + 1][...]], axis=1)
        product = dot_rows(rows[...], pair)
        for side in range(2):
            column = pl.multiple_of((me ^ (step + side)) * DH, DH)
            out_ref[:, pl.ds(column, DH)] = product[:, side * DH : (side + 1) * DH]


def weight_grad_swap(place, pieces, attended):
    head_count, seq_count = len(pieces), len(attended)
    keys = attended[0].shape[0]
    width = pieces[0].shape[1] // (keys // seq_count // head_count) * DH
    return pl.pallas_call(
        functools.partial(weight_grad_swap_kernel, head_count, seq_count),
        in_specs=[SMEM_SPEC] + [VMEM_SPEC] * (head_count + seq_count),
        out_specs=VMEM_SPEC,
        out_shape=jax.ShapeDtypeStruct((width, seq_count * DH), F32),
        scratch_shapes=[pltpu.VMEM((keys, width), BF16)],
        compiler_params=params(),
        cost_estimate=pl.CostEstimate(
            flops=2 * keys * width * seq_count * DH,
            bytes_accessed=8 * keys * DH * seq_count,
            transcendentals=0,
        ),
    )(place, *pieces, *attended)


def mark_live(count_ref, live_ref, slots):
    for shard in range(live_ref.shape[0] // slots):
        inside = lax.broadcasted_iota(jnp.int32, (slots, live_ref.shape[1]), 0)
        live_ref[shard * slots : (shard + 1) * slots] = jnp.where(
            inside < count_ref[shard], 0.0, -1e30
        )


def masked_scores(start, keys, key_ref, query, live_ref):
    scores = dot_cols(key_ref[:keys], query) * (1.0 / math.sqrt(DH)) + live_ref[:keys, :1]
    row = start + lax.broadcasted_iota(jnp.int32, (1, QUERY_BLOCK), 1)
    key_pos = start + lax.broadcasted_iota(jnp.int32, (QUERY_BLOCK, 1), 0)
    edge = jnp.where(key_pos <= row, scores[start:], -1e30)
    return jnp.concatenate([scores[:start], edge], axis=0) if start else edge


def split_blocks(block_ref, *refs):
    shards, slots, _ = block_ref.shape
    for shard in range(shards):
        for which, ref in enumerate(refs):
            ref[shard * slots : (shard + 1) * slots] = block_ref[
                shard, :, which * DH : (which + 1) * DH
            ]


def forward_kernel(
    count_ref, block_ref, attended_ref, stat_ref, live_ref, query_ref, key_ref, value_ref
):
    mark_live(count_ref, live_ref, block_ref.shape[1])
    split_blocks(block_ref, query_ref, key_ref, value_ref)
    value_flip = value_ref[...].T
    for start in range(0, query_ref.shape[0], QUERY_BLOCK):
        rows = slice(start, start + QUERY_BLOCK)
        keys = start + QUERY_BLOCK
        scores = masked_scores(start, keys, key_ref, query_ref[rows], live_ref)
        peak = jnp.max(scores, axis=0, keepdims=True)
        weights = jnp.exp(scores - peak)
        inverse = 1.0 / jnp.sum(weights, axis=0, keepdims=True)
        attended = dot(value_flip[:, :keys], (weights * inverse).astype(BF16))
        attended_ref[rows] = attended.T.astype(BF16)
        stat_ref[0:1, rows] = peak
        stat_ref[1:2, rows] = inverse


def attention_cost(keys, dots):
    return pl.CostEstimate(
        flops=dots * keys * keys * DH, bytes_accessed=16 * keys * DH, transcendentals=keys * keys // 2
    )


def forward(counts, blocks):
    keys = blocks.shape[0] * blocks.shape[1]
    return pl.pallas_call(
        forward_kernel,
        out_shape=[
            jax.ShapeDtypeStruct((keys, DH), BF16),
            jax.ShapeDtypeStruct((8, keys), F32),
        ],
        in_specs=[SMEM_SPEC, pl.BlockSpec()],
        scratch_shapes=[pltpu.VMEM((keys, DH), F32)] + [pltpu.VMEM((keys, DH), BF16)] * 3,
        compiler_params=params(),
        cost_estimate=attention_cost(keys, 2),
    )(counts, blocks)


def backward_kernel(
    count_ref,
    block_ref,
    attended_ref,
    stat_ref,
    grads_ref,
    out_ref,
    live_ref,
    query_ref,
    key_ref,
    value_ref,
    grad_ref,
    query_total,
    key_total,
    value_total,
):
    seq_count, slots, _ = out_ref.shape
    scale = 1.0 / math.sqrt(DH)
    mark_live(count_ref, live_ref, slots)
    split_blocks(block_ref, query_ref, key_ref, value_ref)
    for shard in range(seq_count):
        grad_ref[shard * slots : (shard + 1) * slots] = grads_ref[shard, :slots]
    key_flip = key_ref[...].T
    for start in range(0, query_ref.shape[0], QUERY_BLOCK):
        rows = slice(start, start + QUERY_BLOCK)
        keys = start + QUERY_BLOCK
        query = query_ref[rows]
        grad = grad_ref[rows]
        scores = masked_scores(start, keys, key_ref, query, live_ref)
        probs = jnp.exp(scores - stat_ref[0:1, rows]) * stat_ref[1:2, rows]
        probs_low = probs.astype(BF16)
        product = grad.astype(F32) * attended_ref[rows].astype(F32)
        row_dot = jnp.sum(product.T, axis=0, keepdims=True)
        grad_probs = dot_cols(value_ref[:keys], grad)
        grad_scores = (probs * (grad_probs - row_dot)).astype(BF16)
        query_total[rows] = (dot(key_flip[:, :keys], grad_scores) * scale).T.astype(BF16)
        key_part = dot(grad_scores, query)
        value_part = dot(probs_low, grad)
        if start:
            key_total[:start] += key_part[:start]
            value_total[:start] += value_part[:start]
        key_total[rows] = key_part[start:]
        value_total[rows] = value_part[start:]
    for shard in range(seq_count):
        here = slice(shard * slots, (shard + 1) * slots)
        out_ref[shard, :, :DH] = query_total[here]
        out_ref[shard, :, DH : 2 * DH] = (key_total[here] * scale).astype(BF16)
        out_ref[shard, :, 2 * DH :] = value_total[here].astype(BF16)


def backward(counts, blocks, attended, stats, grads):
    keys = attended.shape[0]
    return pl.pallas_call(
        backward_kernel,
        in_specs=[SMEM_SPEC] + [pl.BlockSpec()] * 4,
        out_shape=jax.ShapeDtypeStruct(blocks.shape, BF16),
        scratch_shapes=[pltpu.VMEM((keys, DH), F32)]
        + [pltpu.VMEM((keys, DH), BF16)] * 5
        + [pltpu.VMEM((keys, DH), F32)] * 2,
        compiler_params=params(VMEM_MOST),
        cost_estimate=attention_cost(keys, 5),
    )(counts, blocks, attended, stats, grads)


def on_device_whole_heads(
    projections,
    output_gradient,
    output_projection_weight,
    kept_token_indices,
    surviving_token_count,
):
    tok_dev = projections.shape[0]
    slots = kept_token_indices.shape[1]
    seq_count = lax.axis_size("seq")
    head_count = lax.axis_size("head")
    index = kept_token_indices
    place = jnp.stack([lax.axis_index("seq"), lax.axis_index("head")]).astype(jnp.int32)
    seq_bits = [1 << bit for bit in reversed(range(seq_count.bit_length() - 1))]
    head_bits = [1 << bit for bit in reversed(range(head_count.bit_length() - 1))]

    def swap(blocks):
        return lax.all_to_all(blocks, "seq", split_axis=0, concat_axis=0, tiled=True)

    packed = pack_whole(index, projections.transpose(1, 0, 2))
    packed, grad_index = lax.optimization_barrier((packed, index))
    arrived = swap(packed)
    grad_blocks = gather_blocks(pack_grad(grad_index, output_gradient), "head", head_bits)
    grads = swap(grad_swap(place, grad_blocks, output_projection_weight, seq_count))
    attended, stats = forward(surviving_token_count, arrived)

    far, near, last = seq_bits[0], seq_bits[-2], seq_bits[-1]
    held = {bit: exchange(attended, "seq", bit) for bit in seq_bits}
    held[near ^ last] = exchange(held[near], "seq", last)
    if far != near:
        held[far ^ near] = exchange(held[far], "seq", near)
    back = backward(surviving_token_count, arrived, attended, stats, grads)
    back, held = lax.optimization_barrier((back, held))
    gathered = gather_blocks(attended, "seq", seq_bits, {0: attended, **held})
    home = swap(back)
    pieces = gather_blocks(grads[:, slots:], "head", head_bits)
    weight_grad = weight_grad_swap(place, pieces, gathered)
    projection_grad = unpack_heads(index, home, tok_dev).transpose(1, 0, 2)
    return (projection_grad, weight_grad)


def on_device(projections, output_gradient, weight, index, counts):
    heads = projections.shape[2] // DH
    seq_count, head_count = lax.axis_size("seq"), lax.axis_size("head")
    width = output_gradient.shape[1] * head_count // seq_count
    whole = seq_count == heads and seq_count % 2 == 0 and width % DH == 0
    powers = seq_count & (seq_count - 1) == 0 and head_count & (head_count - 1) == 0
    body = on_device_whole_heads if whole and powers else on_device_split_heads
    return body(projections, output_gradient, weight, index, counts)


def solution(mesh):
    return jax.shard_map(
        on_device,
        mesh=mesh,
        in_specs=(P("seq", None, "head"), P("seq", "head"), P(None, "head"), P("seq", None), P()),
        out_specs=(P("seq", None, "head"), P("seq", "head")),
        check_vma=False,
    )
```

```python
import functools
import math

import jax
import jax.numpy as jnp
from jax import lax
from jax.experimental import pallas as pl
from jax.experimental.pallas import tpu as pltpu
from jax.sharding import PartitionSpec as P

DH = 128
QUERY_BLOCK = 256
VMEM_BYTES = 20 * 1024 * 1024
VMEM_MOST = 62 * 1024 * 1024
F32 = jnp.float32
BF16 = jnp.bfloat16


def params(limit=VMEM_BYTES):
    return pltpu.CompilerParams(vmem_limit_bytes=limit)


def dot(left, right):
    return jnp.dot(left, right, preferred_element_type=F32)


def dot_rows(left, right):
    return lax.dot_general(left, right, (((0,), (0,)), ((), ())), preferred_element_type=F32)


def dot_cols(left, right):
    return lax.dot_general(left, right, (((1,), (1,)), ((), ())), preferred_element_type=F32)


def token_selector(index_ref, tokens):
    slots = index_ref.shape[1]
    token = lax.broadcasted_iota(jnp.int32, (tokens, slots), 0)
    return jnp.where(token == index_ref[...], 1.0, 0.0).astype(BF16)


def pack_grad_kernel(index_ref, grad_ref, out_ref):
    selector = token_selector(index_ref, grad_ref.shape[0])
    out_ref[...] = dot_rows(selector, grad_ref[...]).astype(BF16)


def pack_grad(index, grad):
    slots = index.shape[1]
    return pl.pallas_call(
        pack_grad_kernel,
        out_shape=jax.ShapeDtypeStruct((slots, grad.shape[1]), BF16),
        compiler_params=params(),
    )(index, grad)


def pack_heads_kernel(index_ref, proj_ref, out_ref):
    selector = token_selector(index_ref, proj_ref.shape[1])
    for which in range(3):
        rows = dot_rows(selector, proj_ref[which]).astype(BF16)
        for head in range(out_ref.shape[0]):
            out_ref[head, :, which * DH : (which + 1) * DH] = rows[:, head * DH : (head + 1) * DH]


def pack_heads(index, proj):
    slots = index.shape[1]
    _, tokens, width = proj.shape
    heads = width // DH
    step = 2
    return pl.pallas_call(
        pack_heads_kernel,
        grid=(heads // step,),
        in_specs=[
            pl.BlockSpec((1, slots), lambda i: (0, 0)),
            pl.BlockSpec((3, tokens, step * DH), lambda i: (0, 0, i)),
        ],
        out_specs=pl.BlockSpec((step, slots, 3 * DH), lambda i: (i, 0, 0)),
        out_shape=jax.ShapeDtypeStruct((heads, slots, 3 * DH), BF16),
        compiler_params=params(),
    )(index, proj)


def unpack_heads_kernel(index_ref, rows_ref, out_ref):
    selector = token_selector(index_ref, out_ref.shape[1])
    for head in range(rows_ref.shape[0]):
        tokens = dot(selector, rows_ref[head]).astype(BF16)
        for which in range(3):
            out_ref[which, :, head * DH : (head + 1) * DH] = tokens[
                :, which * DH : (which + 1) * DH
            ]


def unpack_heads(index, rows, tokens):
    heads, slots, _ = rows.shape
    step = 2
    return pl.pallas_call(
        unpack_heads_kernel,
        grid=(heads // step,),
        in_specs=[
            pl.BlockSpec((1, slots), lambda i: (0, 0)),
            pl.BlockSpec((step, slots, 3 * DH), lambda i: (i, 0, 0)),
        ],
        out_specs=pl.BlockSpec((3, tokens, step * DH), lambda i: (0, 0, i)),
        out_shape=jax.ShapeDtypeStruct((3, tokens, heads * DH), BF16),
        compiler_params=params(),
    )(index, rows)


def grad_attn_kernel(rows_ref, weight_ref, out_ref):
    product = dot(rows_ref[...], weight_ref[...]).astype(BF16)
    for head in range(out_ref.shape[0]):
        out_ref[head] = product[:, head * DH : (head + 1) * DH]


def grad_attn_heads(rows, weight):
    slots, depth = rows.shape
    heads = weight.shape[1] // DH
    step = 2
    return pl.pallas_call(
        grad_attn_kernel,
        grid=(heads // step,),
        in_specs=[
            pl.BlockSpec((slots, depth), lambda i: (0, 0)),
            pl.BlockSpec((depth, step * DH), lambda i: (0, i)),
        ],
        out_specs=pl.BlockSpec((step, slots, DH), lambda i: (i, 0, 0)),
        out_shape=jax.ShapeDtypeStruct((heads, slots, DH), BF16),
        compiler_params=params(),
    )(rows, weight)


def weight_grad_kernel(rows_ref, attended_ref, out_ref):
    attended = jnp.concatenate([attended_ref[head] for head in range(attended_ref.shape[0])], axis=1)
    out_ref[...] = dot_rows(rows_ref[...], attended)


def weight_grad_heads(rows, attended):
    total, width = rows.shape
    heads = attended.shape[0]
    step = 2
    return pl.pallas_call(
        weight_grad_kernel,
        grid=(heads // step,),
        in_specs=[
            pl.BlockSpec((total, width), lambda i: (0, 0)),
            pl.BlockSpec((step, total, DH), lambda i: (i, 0, 0)),
        ],
        out_specs=pl.BlockSpec((width, step * DH), lambda i: (0, i)),
        out_shape=jax.ShapeDtypeStruct((width, heads * DH), F32),
        compiler_params=params(),
    )(rows, attended)


def attention_kernel(
    slots,
    part_rows,
    part_ref,
    live_ref,
    query_ref,
    grad_ref,
    key_ref,
    value_ref,
    attended_ref,
    query_grad_ref,
    key_grad_ref,
    value_grad_ref,
    key_total,
    value_total,
):
    scale = 1.0 / math.sqrt(DH)
    rows_total = query_ref.shape[0]
    keys_total = key_ref.shape[0]
    quarters = slots // part_rows
    key_flip = key_ref[...].T
    value_flip = value_ref[...].T
    for start in range(0, rows_total, QUERY_BLOCK):
        rows = slice(start, start + QUERY_BLOCK)
        last = start + QUERY_BLOCK - 1
        last_pos = last // part_rows * slots + (quarters - 1) * part_rows + last % part_rows
        first_pos = start // part_rows * slots + start % part_rows
        keys = min(-(-(last_pos + 1) // 128) * 128, keys_total)
        clear = first_pos // 128 * 128
        query = query_ref[rows]
        grad = grad_ref[rows]
        row = start + lax.broadcasted_iota(jnp.int32, (1, QUERY_BLOCK), 1)
        if quarters > 1:
            shard = row // part_rows
            row = shard * slots + part_ref[0] * part_rows + row - shard * part_rows
        scores = dot_cols(key_ref[:keys], query) * scale + live_ref[:keys, :1]
        key_pos = clear + lax.broadcasted_iota(jnp.int32, (keys - clear, 1), 0)
        edge = jnp.where(key_pos <= row, scores[clear:], -1e30)
        scores = jnp.concatenate([scores[:clear], edge], axis=0) if clear else edge
        peak = jnp.max(scores, axis=0, keepdims=True)
        weights = jnp.exp(scores - peak)
        probs = weights * (1.0 / jnp.sum(weights, axis=0, keepdims=True))
        probs_low = probs.astype(BF16)
        attended = dot(value_flip[:, :keys], probs_low)
        attended_ref[rows] = attended.T.astype(BF16)
        row_dot = jnp.sum(grad.T.astype(F32) * attended, axis=0, keepdims=True)
        grad_probs = dot_cols(value_ref[:keys], grad)
        grad_scores = (probs * (grad_probs - row_dot)).astype(BF16)
        query_grad = dot(key_flip[:, :keys], grad_scores) * scale
        query_grad_ref[rows] = query_grad.T.astype(BF16)
        key_part = dot(grad_scores, query)
        value_part = dot(probs_low, grad)
        prev = start - 1
        reached = 0
        if start:
            prev_pos = prev // part_rows * slots + (quarters - 1) * part_rows + prev % part_rows
            reached = min(-(-(prev_pos + 1) // 128) * 128, keys_total)
        if reached:
            key_total[:reached] += key_part[:reached]
            value_total[:reached] += value_part[:reached]
        if keys > reached:
            key_total[reached:keys] = key_part[reached:]
            value_total[reached:keys] = value_part[reached:]
    key_grad_ref[...] = (key_total[...] * scale).astype(key_grad_ref.dtype)
    value_grad_ref[...] = value_total[...].astype(value_grad_ref.dtype)


def attention(part, live, query, grad, key, value, slots, part_rows, key_type):
    rows, keys = query.shape[0], key.shape[0]
    vmem = pl.BlockSpec(memory_space=pltpu.VMEM)
    return pl.pallas_call(
        functools.partial(attention_kernel, slots, part_rows),
        in_specs=[pl.BlockSpec(memory_space=pltpu.SMEM)] + [vmem] * 5,
        out_specs=[vmem] * 4,
        out_shape=[
            jax.ShapeDtypeStruct((rows, DH), BF16),
            jax.ShapeDtypeStruct((rows, DH), BF16),
            jax.ShapeDtypeStruct((keys, DH), key_type),
            jax.ShapeDtypeStruct((keys, DH), key_type),
        ],
        scratch_shapes=[pltpu.VMEM((keys, DH), F32)] * 2,
        compiler_params=params(),
    )(part, live, query, grad, key, value)


def on_device_split_heads(
    projections,
    output_gradient,
    output_projection_weight,
    kept_token_indices,
    surviving_token_count,
):
    tok_dev = projections.shape[0]
    group_width = projections.shape[2]
    slots = kept_token_indices.shape[1]
    heads = group_width // DH
    seq_count = lax.axis_size("seq")
    head_count = lax.axis_size("head")
    quarters = seq_count // heads
    part_rows = slots // quarters
    part = (lax.axis_index("seq") % quarters).astype(jnp.int32).reshape(1)
    index = kept_token_indices
    keys = seq_count * slots

    grad_local = pack_grad(index, output_gradient)
    grad_rows = lax.all_gather(grad_local, "head", axis=1, tiled=True)
    packed = pack_heads(index, projections.transpose(1, 0, 2))

    position = jnp.arange(slots, dtype=jnp.int32)
    live = position[None, :] < surviving_token_count[:, None]
    live = jnp.where(live, 0.0, -1e30).astype(F32).reshape(keys, 1)
    live = jnp.broadcast_to(live, (keys, DH))

    def swap(blocks):
        return lax.all_to_all(blocks, "seq", split_axis=0, concat_axis=0, tiled=True)

    if quarters == 1:
        arrived = swap(packed).reshape(keys, 3 * DH)
        query, key, value = (arrived[:, n * DH : (n + 1) * DH] for n in range(3))
    else:
        query = swap(packed[:, :, :DH].reshape(seq_count, part_rows, DH))
        query = query.reshape(seq_count * part_rows, DH)
        sides = jnp.broadcast_to(packed[:, None, :, DH:], (heads, quarters, slots, 2 * DH))
        sides = swap(sides.reshape(seq_count, slots, 2 * DH)).reshape(keys, 2 * DH)
        key, value = sides[:, :DH], sides[:, DH:]

    grad_heads = grad_attn_heads(grad_rows, output_projection_weight)
    grad_in = swap(grad_heads.reshape(seq_count, part_rows, DH)).reshape(-1, DH)

    width = grad_rows.shape[1] // seq_count
    piece = slots // head_count
    mine = lax.dynamic_slice_in_dim(grad_rows, lax.axis_index("head") * piece, piece, 0)
    mine = swap(mine.reshape(piece, seq_count, width).transpose(1, 0, 2))
    all_rows = lax.all_gather(mine, "head", axis=1, tiled=True)

    key_type = BF16 if quarters == 1 else F32
    attended, query_grad, key_grad, value_grad = attention(
        part, live, query, grad_in, key, value, slots, part_rows, key_type
    )

    gathered = lax.all_gather(attended, "seq", axis=0).reshape(heads, keys, DH)
    all_rows = all_rows.reshape(seq_count, quarters, part_rows, width).transpose(1, 0, 2, 3)
    weight_grad = weight_grad_heads(all_rows.reshape(keys, width), gathered)

    if quarters == 1:
        back = jnp.concatenate([query_grad, key_grad, value_grad], axis=1)
        home = swap(back.reshape(seq_count, slots, 3 * DH))
    else:
        query_home = swap(query_grad.reshape(seq_count, part_rows, DH)).reshape(heads, slots, DH)
        back = jnp.concatenate([key_grad, value_grad], axis=1)
        key_home = swap(back.reshape(seq_count, slots, 2 * DH))
        key_home = jnp.sum(key_home.reshape(heads, quarters, slots, 2 * DH), axis=1)
        home = jnp.concatenate([query_home, key_home.astype(BF16)], axis=2)
    projection_grad = unpack_heads(index, home, tok_dev).transpose(1, 0, 2)
    return (projection_grad, weight_grad)


def pack_whole_kernel(index_ref, proj_ref, out_ref, loaded, arrive):
    copies = [
        pltpu.make_async_copy(proj_ref.at[which], loaded.at[which], arrive.at[which])
        for which in range(3)
    ]
    for copy in copies:
        copy.start()
    token = lax.broadcasted_iota(jnp.int32, (loaded.shape[1], index_ref.shape[1]), 0)
    selector = jnp.where(token == index_ref[...], 1.0, 0.0).T.astype(BF16)
    for which, copy in enumerate(copies):
        copy.wait()
        rows = dot(selector, loaded[which]).astype(BF16)
        for head in range(out_ref.shape[0]):
            out_ref[head, :, which * DH : (which + 1) * DH] = rows[:, head * DH : (head + 1) * DH]


def pack_whole(index, proj):
    slots = index.shape[1]
    _, tokens, width = proj.shape
    heads = width // DH
    return pl.pallas_call(
        pack_whole_kernel,
        in_specs=[pl.BlockSpec(), pl.BlockSpec(memory_space=pltpu.HBM)],
        out_shape=jax.ShapeDtypeStruct((heads, slots, 3 * DH), BF16),
        scratch_shapes=[pltpu.VMEM(proj.shape, BF16), pltpu.SemaphoreType.DMA((3,))],
        compiler_params=params(VMEM_MOST),
        cost_estimate=pl.CostEstimate(
            flops=2 * slots * tokens * 3 * width, bytes_accessed=8 * tokens * width, transcendentals=0
        ),
    )(index, proj)


def exchange(block, axis, bit):
    return lax.ppermute(block, axis, [(i, i ^ bit) for i in range(lax.axis_size(axis))])


def gather_blocks(block, axis, bits, held=None):
    held = {0: block} if held is None else dict(held)
    reached = [0]
    for bit in bits:
        for step in list(reached):
            if step ^ bit not in held:
                held[step ^ bit] = exchange(held[step], axis, bit)
            reached.append(step ^ bit)
    return [held[step] for step in range(lax.axis_size(axis))]


SMEM_SPEC = pl.BlockSpec(memory_space=pltpu.SMEM)
VMEM_SPEC = pl.BlockSpec(memory_space=pltpu.VMEM)


def grad_swap_kernel(count, place_ref, *refs):
    row_refs, weight_ref, out_ref, total = refs[:count], refs[count], refs[count + 1], refs[count + 2]
    mine = place_ref[1]
    seq_count, height, _ = out_ref.shape
    slots, depth = row_refs[0].shape
    piece = slots // count
    chunks = (height - slots) // piece
    per_block = depth // (chunks * DH)
    for step in range(count):

        @pl.when(pl.program_id(0) == step)
        def _(step=step):
            part = dot(row_refs[step][...], weight_ref[...])
            total[...] = part if step == 0 else total[...] + part
            share = row_refs[step][pl.ds(pl.multiple_of(mine * piece, piece), piece), :]
            for chunk in range(per_block * chunks):
                partner = (mine ^ step) * per_block + chunk // chunks
                start = slots + chunk % chunks * piece
                out_ref[partner, start : start + piece, :] = share[:, chunk * DH : (chunk + 1) * DH]

    @pl.when(pl.program_id(0) == count - 1)
    def _():
        for head in range(seq_count):
            out_ref[head, :slots, :] = total[:, head * DH : (head + 1) * DH].astype(BF16)


def grad_swap(place, blocks, weight, seq_count):
    count = len(blocks)
    slots, depth = blocks[0].shape
    columns = weight.shape[1]
    height = slots + slots // count * (count * depth // seq_count // DH)
    return pl.pallas_call(
        functools.partial(grad_swap_kernel, count),
        grid_spec=pltpu.PrefetchScalarGridSpec(
            num_scalar_prefetch=1,
            grid=(count,),
            in_specs=[pl.BlockSpec((slots, depth), lambda i, place: (0, 0))] * count
            + [pl.BlockSpec((depth, columns), lambda i, place: (place[1] ^ i, 0))],
            out_specs=pl.BlockSpec((seq_count, height, DH), lambda i, place: (0, 0, 0)),
            scratch_shapes=[pltpu.VMEM((slots, columns), F32)],
        ),
        out_shape=jax.ShapeDtypeStruct((seq_count, height, DH), BF16),
        compiler_params=params(),
        cost_estimate=pl.CostEstimate(
            flops=2 * slots * count * depth * columns,
            bytes_accessed=2 * count * depth * columns,
            transcendentals=0,
        ),
    )(place, *blocks, weight)


def weight_grad_swap_kernel(head_count, seq_count, place_ref, *refs):
    piece_refs = refs[:head_count]
    attended_refs = refs[head_count : head_count + seq_count]
    out_ref, rows = refs[-2:]
    me, mine = place_ref[0], place_ref[1]
    chunks = rows.shape[1] // DH
    piece = piece_refs[0].shape[1] // chunks
    slots = piece * head_count
    for part in range(head_count):
        for shard in range(seq_count):
            here = pl.ds(pl.multiple_of(shard * slots + (mine ^ part) * piece, piece), piece)
            for chunk in range(chunks):
                rows[here, chunk * DH : (chunk + 1) * DH] = piece_refs[part][
                    shard, chunk * piece : (chunk + 1) * piece, :
                ]
    for step in range(0, seq_count, 2):
        pair = jnp.concatenate([attended_refs[step][...], attended_refs[step + 1][...]], axis=1)
        product = dot_rows(rows[...], pair)
        for side in range(2):
            column = pl.multiple_of((me ^ (step + side)) * DH, DH)
            out_ref[:, pl.ds(column, DH)] = product[:, side * DH : (side + 1) * DH]


def weight_grad_swap(place, pieces, attended):
    head_count, seq_count = len(pieces), len(attended)
    keys = attended[0].shape[0]
    width = pieces[0].shape[1] // (keys // seq_count // head_count) * DH
    return pl.pallas_call(
        functools.partial(weight_grad_swap_kernel, head_count, seq_count),
        in_specs=[SMEM_SPEC] + [VMEM_SPEC] * (head_count + seq_count),
        out_specs=VMEM_SPEC,
        out_shape=jax.ShapeDtypeStruct((width, seq_count * DH), F32),
        scratch_shapes=[pltpu.VMEM((keys, width), BF16)],
        compiler_params=params(),
        cost_estimate=pl.CostEstimate(
            flops=16 * keys * width * seq_count * DH,
            bytes_accessed=8 * keys * DH * seq_count,
            transcendentals=0,
        ),
    )(place, *pieces, *attended)


def mark_live(count_ref, live_ref, slots):
    for shard in range(live_ref.shape[0] // slots):
        inside = lax.broadcasted_iota(jnp.int32, (slots, live_ref.shape[1]), 0)
        live_ref[shard * slots : (shard + 1) * slots] = jnp.where(
            inside < count_ref[shard], 0.0, -1e30
        )


def masked_scores(start, keys, key_ref, query, live_ref):
    scores = dot_cols(key_ref[:keys], query) * (1.0 / math.sqrt(DH)) + live_ref[:keys, :1]
    row = start + lax.broadcasted_iota(jnp.int32, (1, QUERY_BLOCK), 1)
    key_pos = start + lax.broadcasted_iota(jnp.int32, (QUERY_BLOCK, 1), 0)
    edge = jnp.where(key_pos <= row, scores[start:], -1e30)
    return jnp.concatenate([scores[:start], edge], axis=0) if start else edge


def split_blocks(block_ref, *refs):
    shards, slots, _ = block_ref.shape
    for shard in range(shards):
        for which, ref in enumerate(refs):
            ref[shard * slots : (shard + 1) * slots] = block_ref[
                shard, :, which * DH : (which + 1) * DH
            ]


def forward_kernel(
    count_ref, block_ref, attended_ref, stat_ref, live_ref, query_ref, key_ref, value_ref
):
    mark_live(count_ref, live_ref, block_ref.shape[1])
    split_blocks(block_ref, query_ref, key_ref, value_ref)
    value_flip = value_ref[...].T
    for start in range(0, query_ref.shape[0], QUERY_BLOCK):
        rows = slice(start, start + QUERY_BLOCK)
        keys = start + QUERY_BLOCK
        scores = masked_scores(start, keys, key_ref, query_ref[rows], live_ref)
        peak = jnp.max(scores, axis=0, keepdims=True)
        weights = jnp.exp(scores - peak)
        inverse = 1.0 / jnp.sum(weights, axis=0, keepdims=True)
        attended = dot(value_flip[:, :keys], (weights * inverse).astype(BF16))
        attended_ref[rows] = attended.T.astype(BF16)
        stat_ref[0:1, rows] = peak
        stat_ref[1:2, rows] = inverse


def attention_cost(keys, dots):
    return pl.CostEstimate(
        flops=dots * keys * keys * DH, bytes_accessed=16 * keys * DH, transcendentals=keys * keys // 2
    )


def forward(counts, blocks):
    keys = blocks.shape[0] * blocks.shape[1]
    return pl.pallas_call(
        forward_kernel,
        out_shape=[
            jax.ShapeDtypeStruct((keys, DH), BF16),
            jax.ShapeDtypeStruct((8, keys), F32),
        ],
        in_specs=[SMEM_SPEC, pl.BlockSpec()],
        scratch_shapes=[pltpu.VMEM((keys, DH), F32)] + [pltpu.VMEM((keys, DH), BF16)] * 3,
        compiler_params=params(),
        cost_estimate=attention_cost(keys, 2),
    )(counts, blocks)


def backward_kernel(
    count_ref,
    block_ref,
    attended_ref,
    stat_ref,
    grads_ref,
    out_ref,
    live_ref,
    query_ref,
    key_ref,
    value_ref,
    grad_ref,
    query_total,
    key_total,
    value_total,
):
    seq_count, slots, _ = out_ref.shape
    scale = 1.0 / math.sqrt(DH)
    mark_live(count_ref, live_ref, slots)
    split_blocks(block_ref, query_ref, key_ref, value_ref)
    for shard in range(seq_count):
        grad_ref[shard * slots : (shard + 1) * slots] = grads_ref[shard, :slots]
    key_flip = key_ref[...].T
    for start in range(0, query_ref.shape[0], QUERY_BLOCK):
        rows = slice(start, start + QUERY_BLOCK)
        keys = start + QUERY_BLOCK
        query = query_ref[rows]
        grad = grad_ref[rows]
        scores = masked_scores(start, keys, key_ref, query, live_ref)
        probs = jnp.exp(scores - stat_ref[0:1, rows]) * stat_ref[1:2, rows]
        probs_low = probs.astype(BF16)
        product = grad.astype(F32) * attended_ref[rows].astype(F32)
        row_dot = jnp.sum(product.T, axis=0, keepdims=True)
        grad_probs = dot_cols(value_ref[:keys], grad)
        grad_scores = (probs * (grad_probs - row_dot)).astype(BF16)
        query_total[rows] = (dot(key_flip[:, :keys], grad_scores) * scale).T.astype(BF16)
        key_part = dot(grad_scores, query)
        value_part = dot(probs_low, grad)
        if start:
            key_total[:start] += key_part[:start]
            value_total[:start] += value_part[:start]
        key_total[rows] = key_part[start:]
        value_total[rows] = value_part[start:]
    for shard in range(seq_count):
        here = slice(shard * slots, (shard + 1) * slots)
        out_ref[shard, :, :DH] = query_total[here]
        out_ref[shard, :, DH : 2 * DH] = (key_total[here] * scale).astype(BF16)
        out_ref[shard, :, 2 * DH :] = value_total[here].astype(BF16)


def backward(counts, blocks, attended, stats, grads):
    keys = attended.shape[0]
    return pl.pallas_call(
        backward_kernel,
        in_specs=[SMEM_SPEC] + [pl.BlockSpec()] * 4,
        out_shape=jax.ShapeDtypeStruct(blocks.shape, BF16),
        scratch_shapes=[pltpu.VMEM((keys, DH), F32)]
        + [pltpu.VMEM((keys, DH), BF16)] * 5
        + [pltpu.VMEM((keys, DH), F32)] * 2,
        compiler_params=params(VMEM_MOST),
        cost_estimate=attention_cost(keys, 5),
    )(counts, blocks, attended, stats, grads)


def on_device_whole_heads(
    projections,
    output_gradient,
    output_projection_weight,
    kept_token_indices,
    surviving_token_count,
):
    tok_dev = projections.shape[0]
    slots = kept_token_indices.shape[1]
    seq_count = lax.axis_size("seq")
    head_count = lax.axis_size("head")
    index = kept_token_indices
    place = jnp.stack([lax.axis_index("seq"), lax.axis_index("head")]).astype(jnp.int32)
    seq_bits = [1 << bit for bit in reversed(range(seq_count.bit_length() - 1))]
    head_bits = [1 << bit for bit in reversed(range(head_count.bit_length() - 1))]

    def swap(blocks):
        return lax.all_to_all(blocks, "seq", split_axis=0, concat_axis=0, tiled=True)

    packed = pack_whole(index, projections.transpose(1, 0, 2))
    packed, grad_index = lax.optimization_barrier((packed, index))
    arrived = swap(packed)
    grad_blocks = gather_blocks(pack_grad(grad_index, output_gradient), "head", head_bits)
    grads = swap(grad_swap(place, grad_blocks, output_projection_weight, seq_count))
    attended, stats = forward(surviving_token_count, arrived)

    near, last = seq_bits[-2], seq_bits[-1]
    held = {bit: exchange(attended, "seq", bit) for bit in seq_bits}
    held[near ^ last] = exchange(held[near], "seq", last)
    back = backward(surviving_token_count, arrived, attended, stats, grads)
    back, held = lax.optimization_barrier((back, held))
    gathered = gather_blocks(attended, "seq", seq_bits, {0: attended, **held})
    home = swap(back)
    pieces = gather_blocks(grads[:, slots:], "head", head_bits)
    weight_grad = weight_grad_swap(place, pieces, gathered)
    projection_grad = unpack_heads(index, home, tok_dev).transpose(1, 0, 2)
    return (projection_grad, weight_grad)


def on_device(projections, output_gradient, weight, index, counts):
    heads = projections.shape[2] // DH
    seq_count, head_count = lax.axis_size("seq"), lax.axis_size("head")
    width = output_gradient.shape[1] * head_count // seq_count
    whole = seq_count == heads and seq_count % 2 == 0 and width % DH == 0
    powers = seq_count & (seq_count - 1) == 0 and head_count & (head_count - 1) == 0
    body = on_device_whole_heads if whole and powers else on_device_split_heads
    return body(projections, output_gradient, weight, index, counts)


def solution(mesh):
    return jax.shard_map(
        on_device,
        mesh=mesh,
        in_specs=(P("seq", None, "head"), P("seq", "head"), P(None, "head"), P("seq", None), P()),
        out_specs=(P("seq", None, "head"), P("seq", "head")),
        check_vma=False,
    )
```

```python
import functools
import math

import jax
import jax.numpy as jnp
from jax import lax
from jax.experimental import pallas as pl
from jax.experimental.pallas import tpu as pltpu
from jax.sharding import PartitionSpec as P

DH = 128
QUERY_BLOCK = 256
VMEM_BYTES = 20 * 1024 * 1024
VMEM_MOST = 62 * 1024 * 1024
F32 = jnp.float32
BF16 = jnp.bfloat16


def params(limit=VMEM_BYTES):
    return pltpu.CompilerParams(vmem_limit_bytes=limit)


def dot(left, right):
    return jnp.dot(left, right, preferred_element_type=F32)


def dot_rows(left, right):
    return lax.dot_general(left, right, (((0,), (0,)), ((), ())), preferred_element_type=F32)


def dot_cols(left, right):
    return lax.dot_general(left, right, (((1,), (1,)), ((), ())), preferred_element_type=F32)


def token_selector(index_ref, tokens):
    slots = index_ref.shape[1]
    token = lax.broadcasted_iota(jnp.int32, (tokens, slots), 0)
    return jnp.where(token == index_ref[...], 1.0, 0.0).astype(BF16)


def pack_grad_kernel(index_ref, grad_ref, out_ref):
    selector = token_selector(index_ref, grad_ref.shape[0])
    out_ref[...] = dot_rows(selector, grad_ref[...]).astype(BF16)


def pack_grad(index, grad):
    slots = index.shape[1]
    return pl.pallas_call(
        pack_grad_kernel,
        out_shape=jax.ShapeDtypeStruct((slots, grad.shape[1]), BF16),
        compiler_params=params(),
    )(index, grad)


def pack_heads_kernel(index_ref, proj_ref, out_ref):
    selector = token_selector(index_ref, proj_ref.shape[1])
    for which in range(3):
        rows = dot_rows(selector, proj_ref[which]).astype(BF16)
        for head in range(out_ref.shape[0]):
            out_ref[head, :, which * DH : (which + 1) * DH] = rows[:, head * DH : (head + 1) * DH]


def pack_heads(index, proj):
    slots = index.shape[1]
    _, tokens, width = proj.shape
    heads = width // DH
    step = 2
    return pl.pallas_call(
        pack_heads_kernel,
        grid=(heads // step,),
        in_specs=[
            pl.BlockSpec((1, slots), lambda i: (0, 0)),
            pl.BlockSpec((3, tokens, step * DH), lambda i: (0, 0, i)),
        ],
        out_specs=pl.BlockSpec((step, slots, 3 * DH), lambda i: (i, 0, 0)),
        out_shape=jax.ShapeDtypeStruct((heads, slots, 3 * DH), BF16),
        compiler_params=params(),
    )(index, proj)


def unpack_heads_kernel(index_ref, rows_ref, out_ref):
    selector = token_selector(index_ref, out_ref.shape[1])
    for head in range(rows_ref.shape[0]):
        tokens = dot(selector, rows_ref[head]).astype(BF16)
        for which in range(3):
            out_ref[which, :, head * DH : (head + 1) * DH] = tokens[
                :, which * DH : (which + 1) * DH
            ]


def unpack_heads(index, rows, tokens):
    heads, slots, _ = rows.shape
    step = 2
    return pl.pallas_call(
        unpack_heads_kernel,
        grid=(heads // step,),
        in_specs=[
            pl.BlockSpec((1, slots), lambda i: (0, 0)),
            pl.BlockSpec((step, slots, 3 * DH), lambda i: (i, 0, 0)),
        ],
        out_specs=pl.BlockSpec((3, tokens, step * DH), lambda i: (0, 0, i)),
        out_shape=jax.ShapeDtypeStruct((3, tokens, heads * DH), BF16),
        compiler_params=params(),
    )(index, rows)


def grad_attn_kernel(rows_ref, weight_ref, out_ref):
    product = dot(rows_ref[...], weight_ref[...]).astype(BF16)
    for head in range(out_ref.shape[0]):
        out_ref[head] = product[:, head * DH : (head + 1) * DH]


def grad_attn_heads(rows, weight):
    slots, depth = rows.shape
    heads = weight.shape[1] // DH
    step = 2
    return pl.pallas_call(
        grad_attn_kernel,
        grid=(heads // step,),
        in_specs=[
            pl.BlockSpec((slots, depth), lambda i: (0, 0)),
            pl.BlockSpec((depth, step * DH), lambda i: (0, i)),
        ],
        out_specs=pl.BlockSpec((step, slots, DH), lambda i: (i, 0, 0)),
        out_shape=jax.ShapeDtypeStruct((heads, slots, DH), BF16),
        compiler_params=params(),
    )(rows, weight)


def weight_grad_kernel(rows_ref, attended_ref, out_ref):
    attended = jnp.concatenate([attended_ref[head] for head in range(attended_ref.shape[0])], axis=1)
    out_ref[...] = dot_rows(rows_ref[...], attended)


def weight_grad_heads(rows, attended):
    total, width = rows.shape
    heads = attended.shape[0]
    step = 2
    return pl.pallas_call(
        weight_grad_kernel,
        grid=(heads // step,),
        in_specs=[
            pl.BlockSpec((total, width), lambda i: (0, 0)),
            pl.BlockSpec((step, total, DH), lambda i: (i, 0, 0)),
        ],
        out_specs=pl.BlockSpec((width, step * DH), lambda i: (0, i)),
        out_shape=jax.ShapeDtypeStruct((width, heads * DH), F32),
        compiler_params=params(),
    )(rows, attended)


def attention_kernel(
    slots,
    part_rows,
    part_ref,
    live_ref,
    query_ref,
    grad_ref,
    key_ref,
    value_ref,
    attended_ref,
    query_grad_ref,
    key_grad_ref,
    value_grad_ref,
    key_total,
    value_total,
):
    scale = 1.0 / math.sqrt(DH)
    rows_total = query_ref.shape[0]
    keys_total = key_ref.shape[0]
    quarters = slots // part_rows
    key_flip = key_ref[...].T
    value_flip = value_ref[...].T
    for start in range(0, rows_total, QUERY_BLOCK):
        rows = slice(start, start + QUERY_BLOCK)
        last = start + QUERY_BLOCK - 1
        last_pos = last // part_rows * slots + (quarters - 1) * part_rows + last % part_rows
        first_pos = start // part_rows * slots + start % part_rows
        keys = min(-(-(last_pos + 1) // 128) * 128, keys_total)
        clear = first_pos // 128 * 128
        query = query_ref[rows]
        grad = grad_ref[rows]
        row = start + lax.broadcasted_iota(jnp.int32, (1, QUERY_BLOCK), 1)
        if quarters > 1:
            shard = row // part_rows
            row = shard * slots + part_ref[0] * part_rows + row - shard * part_rows
        scores = dot_cols(key_ref[:keys], query) * scale + live_ref[:keys, :1]
        key_pos = clear + lax.broadcasted_iota(jnp.int32, (keys - clear, 1), 0)
        edge = jnp.where(key_pos <= row, scores[clear:], -1e30)
        scores = jnp.concatenate([scores[:clear], edge], axis=0) if clear else edge
        peak = jnp.max(scores, axis=0, keepdims=True)
        weights = jnp.exp(scores - peak)
        probs = weights * (1.0 / jnp.sum(weights, axis=0, keepdims=True))
        probs_low = probs.astype(BF16)
        attended = dot(value_flip[:, :keys], probs_low)
        attended_ref[rows] = attended.T.astype(BF16)
        row_dot = jnp.sum(grad.T.astype(F32) * attended, axis=0, keepdims=True)
        grad_probs = dot_cols(value_ref[:keys], grad)
        grad_scores = (probs * (grad_probs - row_dot)).astype(BF16)
        query_grad = dot(key_flip[:, :keys], grad_scores) * scale
        query_grad_ref[rows] = query_grad.T.astype(BF16)
        key_part = dot(grad_scores, query)
        value_part = dot(probs_low, grad)
        prev = start - 1
        reached = 0
        if start:
            prev_pos = prev // part_rows * slots + (quarters - 1) * part_rows + prev % part_rows
            reached = min(-(-(prev_pos + 1) // 128) * 128, keys_total)
        if reached:
            key_total[:reached] += key_part[:reached]
            value_total[:reached] += value_part[:reached]
        if keys > reached:
            key_total[reached:keys] = key_part[reached:]
            value_total[reached:keys] = value_part[reached:]
    key_grad_ref[...] = (key_total[...] * scale).astype(key_grad_ref.dtype)
    value_grad_ref[...] = value_total[...].astype(value_grad_ref.dtype)


def attention(part, live, query, grad, key, value, slots, part_rows, key_type):
    rows, keys = query.shape[0], key.shape[0]
    vmem = pl.BlockSpec(memory_space=pltpu.VMEM)
    return pl.pallas_call(
        functools.partial(attention_kernel, slots, part_rows),
        in_specs=[pl.BlockSpec(memory_space=pltpu.SMEM)] + [vmem] * 5,
        out_specs=[vmem] * 4,
        out_shape=[
            jax.ShapeDtypeStruct((rows, DH), BF16),
            jax.ShapeDtypeStruct((rows, DH), BF16),
            jax.ShapeDtypeStruct((keys, DH), key_type),
            jax.ShapeDtypeStruct((keys, DH), key_type),
        ],
        scratch_shapes=[pltpu.VMEM((keys, DH), F32)] * 2,
        compiler_params=params(),
    )(part, live, query, grad, key, value)


def on_device_split_heads(
    projections,
    output_gradient,
    output_projection_weight,
    kept_token_indices,
    surviving_token_count,
):
    tok_dev = projections.shape[0]
    group_width = projections.shape[2]
    slots = kept_token_indices.shape[1]
    heads = group_width // DH
    seq_count = lax.axis_size("seq")
    head_count = lax.axis_size("head")
    quarters = seq_count // heads
    part_rows = slots // quarters
    part = (lax.axis_index("seq") % quarters).astype(jnp.int32).reshape(1)
    index = kept_token_indices
    keys = seq_count * slots

    grad_local = pack_grad(index, output_gradient)
    grad_rows = lax.all_gather(grad_local, "head", axis=1, tiled=True)
    packed = pack_heads(index, projections.transpose(1, 0, 2))

    position = jnp.arange(slots, dtype=jnp.int32)
    live = position[None, :] < surviving_token_count[:, None]
    live = jnp.where(live, 0.0, -1e30).astype(F32).reshape(keys, 1)
    live = jnp.broadcast_to(live, (keys, DH))

    def swap(blocks):
        return lax.all_to_all(blocks, "seq", split_axis=0, concat_axis=0, tiled=True)

    if quarters == 1:
        arrived = swap(packed).reshape(keys, 3 * DH)
        query, key, value = (arrived[:, n * DH : (n + 1) * DH] for n in range(3))
    else:
        query = swap(packed[:, :, :DH].reshape(seq_count, part_rows, DH))
        query = query.reshape(seq_count * part_rows, DH)
        sides = jnp.broadcast_to(packed[:, None, :, DH:], (heads, quarters, slots, 2 * DH))
        sides = swap(sides.reshape(seq_count, slots, 2 * DH)).reshape(keys, 2 * DH)
        key, value = sides[:, :DH], sides[:, DH:]

    grad_heads = grad_attn_heads(grad_rows, output_projection_weight)
    grad_in = swap(grad_heads.reshape(seq_count, part_rows, DH)).reshape(-1, DH)

    width = grad_rows.shape[1] // seq_count
    piece = slots // head_count
    mine = lax.dynamic_slice_in_dim(grad_rows, lax.axis_index("head") * piece, piece, 0)
    mine = swap(mine.reshape(piece, seq_count, width).transpose(1, 0, 2))
    all_rows = lax.all_gather(mine, "head", axis=1, tiled=True)

    key_type = BF16 if quarters == 1 else F32
    attended, query_grad, key_grad, value_grad = attention(
        part, live, query, grad_in, key, value, slots, part_rows, key_type
    )

    gathered = lax.all_gather(attended, "seq", axis=0).reshape(heads, keys, DH)
    all_rows = all_rows.reshape(seq_count, quarters, part_rows, width).transpose(1, 0, 2, 3)
    weight_grad = weight_grad_heads(all_rows.reshape(keys, width), gathered)

    if quarters == 1:
        back = jnp.concatenate([query_grad, key_grad, value_grad], axis=1)
        home = swap(back.reshape(seq_count, slots, 3 * DH))
    else:
        query_home = swap(query_grad.reshape(seq_count, part_rows, DH)).reshape(heads, slots, DH)
        back = jnp.concatenate([key_grad, value_grad], axis=1)
        key_home = swap(back.reshape(seq_count, slots, 2 * DH))
        key_home = jnp.sum(key_home.reshape(heads, quarters, slots, 2 * DH), axis=1)
        home = jnp.concatenate([query_home, key_home.astype(BF16)], axis=2)
    projection_grad = unpack_heads(index, home, tok_dev).transpose(1, 0, 2)
    return (projection_grad, weight_grad)


def pack_whole_kernel(index_ref, proj_ref, out_ref, loaded, packed, arrive, leave):
    parts = proj_ref.shape[0]
    copies = [
        pltpu.make_async_copy(proj_ref.at[which], loaded.at[which], arrive.at[which])
        for which in range(parts)
    ]
    for copy in copies:
        copy.start()
    token = lax.broadcasted_iota(jnp.int32, (loaded.shape[1], index_ref.shape[1]), 0)
    selector = jnp.where(token == index_ref[...], 1.0, 0.0).T.astype(BF16)
    away = []
    for which, copy in enumerate(copies):
        copy.wait()
        rows = dot(selector, loaded[which]).astype(BF16)
        for head in range(out_ref.shape[0]):
            packed[which, head] = rows[:, head * DH : (head + 1) * DH]
        away.append(
            pltpu.make_async_copy(
                packed.at[which],
                out_ref.at[:, :, which * DH : (which + 1) * DH],
                leave.at[which],
            )
        )
        away[-1].start()
    for copy in away:
        copy.wait()


def pack_whole(index, proj):
    slots = index.shape[1]
    parts, tokens, width = proj.shape
    heads = width // DH
    return pl.pallas_call(
        pack_whole_kernel,
        in_specs=[pl.BlockSpec(), pl.BlockSpec(memory_space=pltpu.HBM)],
        out_specs=pl.BlockSpec(memory_space=pltpu.HBM),
        out_shape=jax.ShapeDtypeStruct((heads, slots, parts * DH), BF16),
        scratch_shapes=[
            pltpu.VMEM(proj.shape, BF16),
            pltpu.VMEM((parts, heads, slots, DH), BF16),
            pltpu.SemaphoreType.DMA((parts,)),
            pltpu.SemaphoreType.DMA((parts,)),
        ],
        compiler_params=params(VMEM_MOST),
        cost_estimate=pl.CostEstimate(
            flops=2 * slots * tokens * parts * width,
            bytes_accessed=8 * tokens * width,
            transcendentals=0,
        ),
    )(index, proj)


def exchange(block, axis, bit):
    return lax.ppermute(block, axis, [(i, i ^ bit) for i in range(lax.axis_size(axis))])


def gather_blocks(block, axis, bits, held=None):
    held = {0: block} if held is None else dict(held)
    reached = [0]
    for bit in bits:
        for step in list(reached):
            if step ^ bit not in held:
                held[step ^ bit] = exchange(held[step], axis, bit)
            reached.append(step ^ bit)
    return [held[step] for step in range(lax.axis_size(axis))]


SMEM_SPEC = pl.BlockSpec(memory_space=pltpu.SMEM)
VMEM_SPEC = pl.BlockSpec(memory_space=pltpu.VMEM)


def grad_swap_kernel(count, place_ref, *refs):
    row_refs, weight_ref, out_ref, total = refs[:count], refs[count], refs[count + 1], refs[count + 2]
    mine = place_ref[1]
    seq_count, height, _ = out_ref.shape
    slots, depth = row_refs[0].shape
    piece = slots // count
    chunks = (height - slots) // piece
    per_block = depth // (chunks * DH)
    for step in range(count):

        @pl.when(pl.program_id(0) == step)
        def _(step=step):
            part = dot(row_refs[step][...], weight_ref[...])
            total[...] = part if step == 0 else total[...] + part
            share = row_refs[step][pl.ds(pl.multiple_of(mine * piece, piece), piece), :]
            for chunk in range(per_block * chunks):
                partner = (mine ^ step) * per_block + chunk // chunks
                start = slots + chunk % chunks * piece
                out_ref[partner, start : start + piece, :] = share[:, chunk * DH : (chunk + 1) * DH]

    @pl.when(pl.program_id(0) == count - 1)
    def _():
        for head in range(seq_count):
            out_ref[head, :slots, :] = total[:, head * DH : (head + 1) * DH].astype(BF16)


def grad_swap(place, blocks, weight, seq_count):
    count = len(blocks)
    slots, depth = blocks[0].shape
    columns = weight.shape[1]
    height = slots + slots // count * (count * depth // seq_count // DH)
    return pl.pallas_call(
        functools.partial(grad_swap_kernel, count),
        grid_spec=pltpu.PrefetchScalarGridSpec(
            num_scalar_prefetch=1,
            grid=(count,),
            in_specs=[pl.BlockSpec((slots, depth), lambda i, place: (0, 0))] * count
            + [pl.BlockSpec((depth, columns), lambda i, place: (place[1] ^ i, 0))],
            out_specs=pl.BlockSpec((seq_count, height, DH), lambda i, place: (0, 0, 0)),
            scratch_shapes=[pltpu.VMEM((slots, columns), F32)],
        ),
        out_shape=jax.ShapeDtypeStruct((seq_count, height, DH), BF16),
        compiler_params=params(),
        cost_estimate=pl.CostEstimate(
            flops=2 * slots * count * depth * columns,
            bytes_accessed=2 * count * depth * columns,
            transcendentals=0,
        ),
    )(place, *blocks, weight)


def flip_rows_kernel(place_ref, *refs):
    piece_refs, out_ref, rows = refs[:-2], refs[-2], refs[-1]
    count = len(piece_refs)
    chunks = rows.shape[1] // DH
    shards, height, _ = piece_refs[0].shape
    piece = height // chunks
    for part in range(count):
        for shard in range(shards):
            start = shard * piece * count + (place_ref[1] ^ part) * piece
            here = pl.ds(pl.multiple_of(start, piece), piece)
            for chunk in range(chunks):
                rows[here, chunk * DH : (chunk + 1) * DH] = piece_refs[part][
                    shard, chunk * piece : (chunk + 1) * piece, :
                ]
    out_ref[...] = rows[...].T


def flip_rows(place, pieces, slots):
    shards, height, _ = pieces[0].shape
    width = height // (slots // len(pieces)) * DH
    keys = shards * slots
    return pl.pallas_call(
        flip_rows_kernel,
        in_specs=[SMEM_SPEC] + [pl.BlockSpec()] * len(pieces),
        out_shape=jax.ShapeDtypeStruct((width, keys), BF16),
        scratch_shapes=[pltpu.VMEM((keys, width), BF16)],
        compiler_params=params(),
        cost_estimate=pl.CostEstimate(flops=0, bytes_accessed=4 * keys * width, transcendentals=0),
    )(place, *pieces)


def weight_part_kernel(count, place_ref, flip_ref, *refs):
    for step in range(count):

        @pl.when(pl.program_id(0) == step)
        def _(step=step):
            refs[-1][...] = dot(flip_ref[...], refs[step][...])


def weight_part(place, flip, attended, first, heads, weight, before=None):
    count = len(attended)
    width, keys = flip.shape
    block = pl.BlockSpec((keys, DH), lambda i, place: (0, 0))
    more = [] if before is None else [before]
    return pl.pallas_call(
        functools.partial(weight_part_kernel, count),
        grid_spec=pltpu.PrefetchScalarGridSpec(
            num_scalar_prefetch=1,
            grid=(count,),
            in_specs=[pl.BlockSpec((width, keys), lambda i, place: (0, 0))]
            + [block] * count
            + [pl.BlockSpec(memory_space=pl.ANY)] * len(more),
            out_specs=pl.BlockSpec((width, DH), lambda i, place: (0, place[0] ^ (first + i))),
        ),
        out_shape=jax.ShapeDtypeStruct((width, heads * DH), F32),
        input_output_aliases={2 + count: 0} if more else {},
        compiler_params=params(),
        cost_estimate=pl.CostEstimate(
            flops=weight * 2 * keys * width * count * DH,
            bytes_accessed=8 * keys * DH * count,
            transcendentals=0,
        ),
    )(place, flip, *attended, *more)


def mark_live(count_ref, live_ref, slots):
    for shard in range(live_ref.shape[0] // slots):
        inside = lax.broadcasted_iota(jnp.int32, (slots, live_ref.shape[1]), 0)
        live_ref[shard * slots : (shard + 1) * slots] = jnp.where(
            inside < count_ref[shard], 0.0, -1e30
        )


def masked_scores(start, keys, key_ref, query, live_ref):
    scores = dot_cols(key_ref[:keys], query) * (1.0 / math.sqrt(DH)) + live_ref[:keys, :1]
    row = start + lax.broadcasted_iota(jnp.int32, (1, QUERY_BLOCK), 1)
    key_pos = start + lax.broadcasted_iota(jnp.int32, (QUERY_BLOCK, 1), 0)
    edge = jnp.where(key_pos <= row, scores[start:], -1e30)
    return jnp.concatenate([scores[:start], edge], axis=0) if start else edge


def split_blocks(block_ref, *refs):
    shards, slots, _ = block_ref.shape
    for shard in range(shards):
        for which, ref in enumerate(refs):
            ref[shard * slots : (shard + 1) * slots] = block_ref[
                shard, :, which * DH : (which + 1) * DH
            ]


def forward_kernel(
    count_ref, block_ref, attended_ref, stat_ref, live_ref, query_ref, key_ref, value_ref
):
    mark_live(count_ref, live_ref, block_ref.shape[1])
    split_blocks(block_ref, query_ref, key_ref, value_ref)
    value_flip = value_ref[...].T
    for start in range(0, query_ref.shape[0], QUERY_BLOCK):
        rows = slice(start, start + QUERY_BLOCK)
        keys = start + QUERY_BLOCK
        scores = masked_scores(start, keys, key_ref, query_ref[rows], live_ref)
        peak = jnp.max(scores, axis=0, keepdims=True)
        weights = jnp.exp(scores - peak)
        inverse = 1.0 / jnp.sum(weights, axis=0, keepdims=True)
        attended = dot(value_flip[:, :keys], (weights * inverse).astype(BF16))
        attended_ref[rows] = attended.T.astype(BF16)
        stat_ref[0:1, rows] = peak
        stat_ref[1:2, rows] = inverse


def attention_cost(keys, dots):
    return pl.CostEstimate(
        flops=dots * keys * keys * DH, bytes_accessed=16 * keys * DH, transcendentals=keys * keys // 2
    )


def forward(counts, blocks):
    keys = blocks.shape[0] * blocks.shape[1]
    return pl.pallas_call(
        forward_kernel,
        out_shape=[
            jax.ShapeDtypeStruct((keys, DH), BF16),
            jax.ShapeDtypeStruct((8, keys), F32),
        ],
        in_specs=[SMEM_SPEC, pl.BlockSpec()],
        scratch_shapes=[pltpu.VMEM((keys, DH), F32)] + [pltpu.VMEM((keys, DH), BF16)] * 3,
        compiler_params=params(),
        cost_estimate=attention_cost(keys, 2),
    )(counts, blocks)


def backward_kernel(
    count_ref,
    block_ref,
    attended_ref,
    stat_ref,
    grads_ref,
    out_ref,
    live_ref,
    query_ref,
    key_ref,
    value_ref,
    grad_ref,
    query_total,
    key_total,
    value_total,
):
    seq_count, slots, _ = out_ref.shape
    scale = 1.0 / math.sqrt(DH)
    mark_live(count_ref, live_ref, slots)
    split_blocks(block_ref, query_ref, key_ref, value_ref)
    for shard in range(seq_count):
        grad_ref[shard * slots : (shard + 1) * slots] = grads_ref[shard, :slots]
    key_flip = key_ref[...].T
    for start in range(0, query_ref.shape[0], QUERY_BLOCK):
        rows = slice(start, start + QUERY_BLOCK)
        keys = start + QUERY_BLOCK
        query = query_ref[rows]
        grad = grad_ref[rows]
        scores = masked_scores(start, keys, key_ref, query, live_ref)
        probs = jnp.exp(scores - stat_ref[0:1, rows]) * stat_ref[1:2, rows]
        probs_low = probs.astype(BF16)
        product = grad.astype(F32) * attended_ref[rows].astype(F32)
        row_dot = jnp.sum(product.T, axis=0, keepdims=True)
        grad_probs = dot_cols(value_ref[:keys], grad)
        grad_scores = (probs * (grad_probs - row_dot)).astype(BF16)
        query_total[rows] = (dot(key_flip[:, :keys], grad_scores) * scale).T.astype(BF16)
        key_part = dot(grad_scores, query)
        value_part = dot(probs_low, grad)
        if start:
            key_total[:start] += key_part[:start]
            value_total[:start] += value_part[:start]
        key_total[rows] = key_part[start:]
        value_total[rows] = value_part[start:]
    for shard in range(seq_count):
        here = slice(shard * slots, (shard + 1) * slots)
        out_ref[shard, :, :DH] = query_total[here]
        out_ref[shard, :, DH : 2 * DH] = (key_total[here] * scale).astype(BF16)
        out_ref[shard, :, 2 * DH :] = value_total[here].astype(BF16)


def backward(counts, blocks, attended, stats, grads):
    keys = attended.shape[0]
    return pl.pallas_call(
        backward_kernel,
        in_specs=[SMEM_SPEC] + [pl.BlockSpec()] * 4,
        out_shape=jax.ShapeDtypeStruct(blocks.shape, BF16),
        scratch_shapes=[pltpu.VMEM((keys, DH), F32)]
        + [pltpu.VMEM((keys, DH), BF16)] * 5
        + [pltpu.VMEM((keys, DH), F32)] * 2,
        compiler_params=params(VMEM_MOST),
        cost_estimate=attention_cost(keys, 5),
    )(counts, blocks, attended, stats, grads)


def on_device_whole_heads(
    projections,
    output_gradient,
    output_projection_weight,
    kept_token_indices,
    surviving_token_count,
):
    tok_dev = projections.shape[0]
    slots = kept_token_indices.shape[1]
    seq_count = lax.axis_size("seq")
    head_count = lax.axis_size("head")
    index = kept_token_indices
    place = jnp.stack([lax.axis_index("seq"), lax.axis_index("head")]).astype(jnp.int32)
    seq_bits = [1 << bit for bit in reversed(range(seq_count.bit_length() - 1))]
    head_bits = [1 << bit for bit in reversed(range(head_count.bit_length() - 1))]

    def swap(blocks):
        return lax.all_to_all(blocks, "seq", split_axis=0, concat_axis=0, tiled=True)

    packed = pack_whole(index, projections.transpose(1, 0, 2))
    packed, grad_index = lax.optimization_barrier((packed, index))
    arrived = swap(packed)
    grad_blocks = gather_blocks(pack_grad(grad_index, output_gradient), "head", head_bits)
    grads = swap(grad_swap(place, grad_blocks, output_projection_weight, seq_count))
    attended, stats = forward(surviving_token_count, arrived)

    near, last = seq_bits[-2], seq_bits[-1]
    held = {bit: exchange(attended, "seq", bit) for bit in seq_bits}
    held[near ^ last] = exchange(held[near], "seq", last)
    back = backward(surviving_token_count, arrived, attended, stats, grads)
    back, held = lax.optimization_barrier((back, held))
    gathered = gather_blocks(attended, "seq", seq_bits, {0: attended, **held})
    home = swap(back)
    pieces = gather_blocks(grads[:, slots:], "head", head_bits)
    flip = flip_rows(place, pieces, slots)
    late = seq_count - 2
    weight_grad = weight_part(place, flip, gathered[:late], 0, seq_count, 1)
    projection_grad = unpack_heads(index, home, tok_dev)
    weight_grad = weight_part(place, flip, gathered[late:], late, seq_count, 28, weight_grad)
    projection_grad = projection_grad.transpose(1, 0, 2)
    return (projection_grad, weight_grad)


def on_device(projections, output_gradient, weight, index, counts):
    heads = projections.shape[2] // DH
    seq_count, head_count = lax.axis_size("seq"), lax.axis_size("head")
    width = output_gradient.shape[1] * head_count // seq_count
    whole = seq_count == heads and seq_count % 2 == 0 and width % DH == 0
    powers = seq_count & (seq_count - 1) == 0 and head_count & (head_count - 1) == 0
    body = on_device_whole_heads if whole and powers else on_device_split_heads
    return body(projections, output_gradient, weight, index, counts)


def solution(mesh):
    return jax.shard_map(
        on_device,
        mesh=mesh,
        in_specs=(P("seq", None, "head"), P("seq", "head"), P(None, "head"), P("seq", None), P()),
        out_specs=(P("seq", None, "head"), P("seq", "head")),
        check_vma=False,
    )
```

```python
import functools
import math

import jax
import jax.numpy as jnp
from jax import lax
from jax.experimental import pallas as pl
from jax.experimental.pallas import tpu as pltpu
from jax.sharding import PartitionSpec as P

DH = 128
QUERY_BLOCK = 256
VMEM_BYTES = 20 * 1024 * 1024
VMEM_MOST = 62 * 1024 * 1024
F32 = jnp.float32
BF16 = jnp.bfloat16


def params(limit=VMEM_BYTES):
    return pltpu.CompilerParams(vmem_limit_bytes=limit)


def dot(left, right):
    return jnp.dot(left, right, preferred_element_type=F32)


def dot_rows(left, right):
    return lax.dot_general(left, right, (((0,), (0,)), ((), ())), preferred_element_type=F32)


def dot_cols(left, right):
    return lax.dot_general(left, right, (((1,), (1,)), ((), ())), preferred_element_type=F32)


def token_selector(index_ref, tokens):
    slots = index_ref.shape[1]
    token = lax.broadcasted_iota(jnp.int32, (tokens, slots), 0)
    return jnp.where(token == index_ref[...], 1.0, 0.0).astype(BF16)


def pack_grad_kernel(index_ref, grad_ref, out_ref):
    selector = token_selector(index_ref, grad_ref.shape[0])
    out_ref[...] = dot_rows(selector, grad_ref[...]).astype(BF16)


def pack_grad(index, grad):
    slots = index.shape[1]
    return pl.pallas_call(
        pack_grad_kernel,
        out_shape=jax.ShapeDtypeStruct((slots, grad.shape[1]), BF16),
        compiler_params=params(),
    )(index, grad)


def pack_heads_kernel(index_ref, proj_ref, out_ref):
    selector = token_selector(index_ref, proj_ref.shape[1])
    for which in range(3):
        rows = dot_rows(selector, proj_ref[which]).astype(BF16)
        for head in range(out_ref.shape[0]):
            out_ref[head, :, which * DH : (which + 1) * DH] = rows[:, head * DH : (head + 1) * DH]


def pack_heads(index, proj):
    slots = index.shape[1]
    _, tokens, width = proj.shape
    heads = width // DH
    step = 2
    return pl.pallas_call(
        pack_heads_kernel,
        grid=(heads // step,),
        in_specs=[
            pl.BlockSpec((1, slots), lambda i: (0, 0)),
            pl.BlockSpec((3, tokens, step * DH), lambda i: (0, 0, i)),
        ],
        out_specs=pl.BlockSpec((step, slots, 3 * DH), lambda i: (i, 0, 0)),
        out_shape=jax.ShapeDtypeStruct((heads, slots, 3 * DH), BF16),
        compiler_params=params(),
    )(index, proj)


def unpack_heads_kernel(index_ref, rows_ref, out_ref):
    selector = token_selector(index_ref, out_ref.shape[1])
    for head in range(rows_ref.shape[0]):
        tokens = dot(selector, rows_ref[head]).astype(BF16)
        for which in range(3):
            out_ref[which, :, head * DH : (head + 1) * DH] = tokens[
                :, which * DH : (which + 1) * DH
            ]


def unpack_heads(index, rows, tokens, step=2):
    heads, slots, _ = rows.shape
    return pl.pallas_call(
        unpack_heads_kernel,
        grid=(heads // step,),
        in_specs=[
            pl.BlockSpec((1, slots), lambda i: (0, 0)),
            pl.BlockSpec((step, slots, 3 * DH), lambda i: (i, 0, 0)),
        ],
        out_specs=pl.BlockSpec((3, tokens, step * DH), lambda i: (0, 0, i)),
        out_shape=jax.ShapeDtypeStruct((3, tokens, heads * DH), BF16),
        compiler_params=params(),
    )(index, rows)


def grad_attn_kernel(rows_ref, weight_ref, out_ref):
    product = dot(rows_ref[...], weight_ref[...]).astype(BF16)
    for head in range(out_ref.shape[0]):
        out_ref[head] = product[:, head * DH : (head + 1) * DH]


def grad_attn_heads(rows, weight):
    slots, depth = rows.shape
    heads = weight.shape[1] // DH
    step = 2
    return pl.pallas_call(
        grad_attn_kernel,
        grid=(heads // step,),
        in_specs=[
            pl.BlockSpec((slots, depth), lambda i: (0, 0)),
            pl.BlockSpec((depth, step * DH), lambda i: (0, i)),
        ],
        out_specs=pl.BlockSpec((step, slots, DH), lambda i: (i, 0, 0)),
        out_shape=jax.ShapeDtypeStruct((heads, slots, DH), BF16),
        compiler_params=params(),
    )(rows, weight)


def weight_grad_kernel(rows_ref, attended_ref, out_ref):
    attended = jnp.concatenate([attended_ref[head] for head in range(attended_ref.shape[0])], axis=1)
    out_ref[...] = dot_rows(rows_ref[...], attended)


def weight_grad_heads(rows, attended):
    total, width = rows.shape
    heads = attended.shape[0]
    step = 2
    return pl.pallas_call(
        weight_grad_kernel,
        grid=(heads // step,),
        in_specs=[
            pl.BlockSpec((total, width), lambda i: (0, 0)),
            pl.BlockSpec((step, total, DH), lambda i: (i, 0, 0)),
        ],
        out_specs=pl.BlockSpec((width, step * DH), lambda i: (0, i)),
        out_shape=jax.ShapeDtypeStruct((width, heads * DH), F32),
        compiler_params=params(),
    )(rows, attended)


def attention_kernel(
    slots,
    part_rows,
    part_ref,
    live_ref,
    query_ref,
    grad_ref,
    key_ref,
    value_ref,
    attended_ref,
    query_grad_ref,
    key_grad_ref,
    value_grad_ref,
    key_total,
    value_total,
):
    scale = 1.0 / math.sqrt(DH)
    rows_total = query_ref.shape[0]
    keys_total = key_ref.shape[0]
    quarters = slots // part_rows
    key_flip = key_ref[...].T
    value_flip = value_ref[...].T
    for start in range(0, rows_total, QUERY_BLOCK):
        rows = slice(start, start + QUERY_BLOCK)
        last = start + QUERY_BLOCK - 1
        last_pos = last // part_rows * slots + (quarters - 1) * part_rows + last % part_rows
        first_pos = start // part_rows * slots + start % part_rows
        keys = min(-(-(last_pos + 1) // 128) * 128, keys_total)
        clear = first_pos // 128 * 128
        query = query_ref[rows]
        grad = grad_ref[rows]
        row = start + lax.broadcasted_iota(jnp.int32, (1, QUERY_BLOCK), 1)
        if quarters > 1:
            shard = row // part_rows
            row = shard * slots + part_ref[0] * part_rows + row - shard * part_rows
        scores = dot_cols(key_ref[:keys], query) * scale + live_ref[:keys, :1]
        key_pos = clear + lax.broadcasted_iota(jnp.int32, (keys - clear, 1), 0)
        edge = jnp.where(key_pos <= row, scores[clear:], -1e30)
        scores = jnp.concatenate([scores[:clear], edge], axis=0) if clear else edge
        peak = jnp.max(scores, axis=0, keepdims=True)
        weights = jnp.exp(scores - peak)
        probs = weights * (1.0 / jnp.sum(weights, axis=0, keepdims=True))
        probs_low = probs.astype(BF16)
        attended = dot(value_flip[:, :keys], probs_low)
        attended_ref[rows] = attended.T.astype(BF16)
        row_dot = jnp.sum(grad.T.astype(F32) * attended, axis=0, keepdims=True)
        grad_probs = dot_cols(value_ref[:keys], grad)
        grad_scores = (probs * (grad_probs - row_dot)).astype(BF16)
        query_grad = dot(key_flip[:, :keys], grad_scores) * scale
        query_grad_ref[rows] = query_grad.T.astype(BF16)
        key_part = dot(grad_scores, query)
        value_part = dot(probs_low, grad)
        prev = start - 1
        reached = 0
        if start:
            prev_pos = prev // part_rows * slots + (quarters - 1) * part_rows + prev % part_rows
            reached = min(-(-(prev_pos + 1) // 128) * 128, keys_total)
        if reached:
            key_total[:reached] += key_part[:reached]
            value_total[:reached] += value_part[:reached]
        if keys > reached:
            key_total[reached:keys] = key_part[reached:]
            value_total[reached:keys] = value_part[reached:]
    key_grad_ref[...] = (key_total[...] * scale).astype(key_grad_ref.dtype)
    value_grad_ref[...] = value_total[...].astype(value_grad_ref.dtype)


def attention(part, live, query, grad, key, value, slots, part_rows, key_type):
    rows, keys = query.shape[0], key.shape[0]
    vmem = pl.BlockSpec(memory_space=pltpu.VMEM)
    return pl.pallas_call(
        functools.partial(attention_kernel, slots, part_rows),
        in_specs=[pl.BlockSpec(memory_space=pltpu.SMEM)] + [vmem] * 5,
        out_specs=[vmem] * 4,
        out_shape=[
            jax.ShapeDtypeStruct((rows, DH), BF16),
            jax.ShapeDtypeStruct((rows, DH), BF16),
            jax.ShapeDtypeStruct((keys, DH), key_type),
            jax.ShapeDtypeStruct((keys, DH), key_type),
        ],
        scratch_shapes=[pltpu.VMEM((keys, DH), F32)] * 2,
        compiler_params=params(),
    )(part, live, query, grad, key, value)


def on_device_split_heads(
    projections,
    output_gradient,
    output_projection_weight,
    kept_token_indices,
    surviving_token_count,
):
    tok_dev = projections.shape[0]
    group_width = projections.shape[2]
    slots = kept_token_indices.shape[1]
    heads = group_width // DH
    seq_count = lax.axis_size("seq")
    head_count = lax.axis_size("head")
    quarters = seq_count // heads
    part_rows = slots // quarters
    part = (lax.axis_index("seq") % quarters).astype(jnp.int32).reshape(1)
    index = kept_token_indices
    keys = seq_count * slots

    grad_local = pack_grad(index, output_gradient)
    grad_rows = lax.all_gather(grad_local, "head", axis=1, tiled=True)
    packed = pack_heads(index, projections.transpose(1, 0, 2))

    position = jnp.arange(slots, dtype=jnp.int32)
    live = position[None, :] < surviving_token_count[:, None]
    live = jnp.where(live, 0.0, -1e30).astype(F32).reshape(keys, 1)
    live = jnp.broadcast_to(live, (keys, DH))

    def swap(blocks):
        return lax.all_to_all(blocks, "seq", split_axis=0, concat_axis=0, tiled=True)

    if quarters == 1:
        arrived = swap(packed).reshape(keys, 3 * DH)
        query, key, value = (arrived[:, n * DH : (n + 1) * DH] for n in range(3))
    else:
        query = swap(packed[:, :, :DH].reshape(seq_count, part_rows, DH))
        query = query.reshape(seq_count * part_rows, DH)
        sides = jnp.broadcast_to(packed[:, None, :, DH:], (heads, quarters, slots, 2 * DH))
        sides = swap(sides.reshape(seq_count, slots, 2 * DH)).reshape(keys, 2 * DH)
        key, value = sides[:, :DH], sides[:, DH:]

    grad_heads = grad_attn_heads(grad_rows, output_projection_weight)
    grad_in = swap(grad_heads.reshape(seq_count, part_rows, DH)).reshape(-1, DH)

    width = grad_rows.shape[1] // seq_count
    piece = slots // head_count
    mine = lax.dynamic_slice_in_dim(grad_rows, lax.axis_index("head") * piece, piece, 0)
    mine = swap(mine.reshape(piece, seq_count, width).transpose(1, 0, 2))
    all_rows = lax.all_gather(mine, "head", axis=1, tiled=True)

    key_type = BF16 if quarters == 1 else F32
    attended, query_grad, key_grad, value_grad = attention(
        part, live, query, grad_in, key, value, slots, part_rows, key_type
    )

    gathered = lax.all_gather(attended, "seq", axis=0).reshape(heads, keys, DH)
    all_rows = all_rows.reshape(seq_count, quarters, part_rows, width).transpose(1, 0, 2, 3)
    weight_grad = weight_grad_heads(all_rows.reshape(keys, width), gathered)

    if quarters == 1:
        back = jnp.concatenate([query_grad, key_grad, value_grad], axis=1)
        home = swap(back.reshape(seq_count, slots, 3 * DH))
    else:
        query_home = swap(query_grad.reshape(seq_count, part_rows, DH)).reshape(heads, slots, DH)
        back = jnp.concatenate([key_grad, value_grad], axis=1)
        key_home = swap(back.reshape(seq_count, slots, 2 * DH))
        key_home = jnp.sum(key_home.reshape(heads, quarters, slots, 2 * DH), axis=1)
        home = jnp.concatenate([query_home, key_home.astype(BF16)], axis=2)
    projection_grad = unpack_heads(index, home, tok_dev).transpose(1, 0, 2)
    return (projection_grad, weight_grad)


def pack_whole_kernel(index_ref, proj_ref, out_ref, loaded, packed, arrive, leave):
    parts = proj_ref.shape[0]
    copies = [
        pltpu.make_async_copy(proj_ref.at[which], loaded.at[which], arrive.at[which])
        for which in range(parts)
    ]
    for copy in copies:
        copy.start()
    token = lax.broadcasted_iota(jnp.int32, (loaded.shape[1], index_ref.shape[1]), 0)
    selector = jnp.where(token == index_ref[...], 1.0, 0.0).T.astype(BF16)
    away = []
    for which, copy in enumerate(copies):
        copy.wait()
        rows = dot(selector, loaded[which]).astype(BF16)
        for head in range(out_ref.shape[0]):
            packed[which, head] = rows[:, head * DH : (head + 1) * DH]
        away.append(
            pltpu.make_async_copy(
                packed.at[which],
                out_ref.at[:, :, which * DH : (which + 1) * DH],
                leave.at[which],
            )
        )
        away[-1].start()
    for copy in away:
        copy.wait()


def pack_whole(index, proj):
    slots = index.shape[1]
    parts, tokens, width = proj.shape
    heads = width // DH
    return pl.pallas_call(
        pack_whole_kernel,
        in_specs=[pl.BlockSpec(), pl.BlockSpec(memory_space=pltpu.HBM)],
        out_specs=pl.BlockSpec(memory_space=pltpu.HBM),
        out_shape=jax.ShapeDtypeStruct((heads, slots, parts * DH), BF16),
        scratch_shapes=[
            pltpu.VMEM(proj.shape, BF16),
            pltpu.VMEM((parts, heads, slots, DH), BF16),
            pltpu.SemaphoreType.DMA((parts,)),
            pltpu.SemaphoreType.DMA((parts,)),
        ],
        compiler_params=params(VMEM_MOST),
        cost_estimate=pl.CostEstimate(
            flops=2 * slots * tokens * parts * width,
            bytes_accessed=8 * tokens * width,
            transcendentals=0,
        ),
    )(index, proj)


def exchange(block, axis, bit):
    return lax.ppermute(block, axis, [(i, i ^ bit) for i in range(lax.axis_size(axis))])


def gather_blocks(block, axis, bits, held=None):
    held = {0: block} if held is None else dict(held)
    reached = [0]
    for bit in bits:
        for step in list(reached):
            if step ^ bit not in held:
                held[step ^ bit] = exchange(held[step], axis, bit)
            reached.append(step ^ bit)
    return [held[step] for step in range(lax.axis_size(axis))]


SMEM_SPEC = pl.BlockSpec(memory_space=pltpu.SMEM)
VMEM_SPEC = pl.BlockSpec(memory_space=pltpu.VMEM)


def grad_swap_kernel(count, place_ref, *refs):
    row_refs, weight_ref, out_ref, total = refs[:count], refs[count], refs[count + 1], refs[count + 2]
    mine = place_ref[1]
    seq_count, height, _ = out_ref.shape
    slots, depth = row_refs[0].shape
    piece = slots // count
    chunks = (height - slots) // piece
    per_block = depth // (chunks * DH)
    for step in range(count):

        @pl.when(pl.program_id(0) == step)
        def _(step=step):
            part = dot(row_refs[step][...], weight_ref[...])
            total[...] = part if step == 0 else total[...] + part
            share = row_refs[step][pl.ds(pl.multiple_of(mine * piece, piece), piece), :]
            for chunk in range(per_block * chunks):
                partner = (mine ^ step) * per_block + chunk // chunks
                start = slots + chunk % chunks * piece
                out_ref[partner, start : start + piece, :] = share[:, chunk * DH : (chunk + 1) * DH]

    @pl.when(pl.program_id(0) == count - 1)
    def _():
        for head in range(seq_count):
            out_ref[head, :slots, :] = total[:, head * DH : (head + 1) * DH].astype(BF16)


def grad_swap(place, blocks, weight, seq_count):
    count = len(blocks)
    slots, depth = blocks[0].shape
    columns = weight.shape[1]
    height = slots + slots // count * (count * depth // seq_count // DH)
    return pl.pallas_call(
        functools.partial(grad_swap_kernel, count),
        grid_spec=pltpu.PrefetchScalarGridSpec(
            num_scalar_prefetch=1,
            grid=(count,),
            in_specs=[pl.BlockSpec((slots, depth), lambda i, place: (0, 0))] * count
            + [pl.BlockSpec((depth, columns), lambda i, place: (place[1] ^ i, 0))],
            out_specs=pl.BlockSpec((seq_count, height, DH), lambda i, place: (0, 0, 0)),
            scratch_shapes=[pltpu.VMEM((slots, columns), F32)],
        ),
        out_shape=jax.ShapeDtypeStruct((seq_count, height, DH), BF16),
        compiler_params=params(),
        cost_estimate=pl.CostEstimate(
            flops=2 * slots * count * depth * columns,
            bytes_accessed=2 * count * depth * columns,
            transcendentals=0,
        ),
    )(place, *blocks, weight)


def flip_rows_kernel(place_ref, *refs):
    piece_refs, out_ref, rows = refs[:-2], refs[-2], refs[-1]
    count = len(piece_refs)
    chunks = rows.shape[1] // DH
    shards, height, _ = piece_refs[0].shape
    piece = height // chunks
    for part in range(count):
        for shard in range(shards):
            start = shard * piece * count + (place_ref[1] ^ part) * piece
            here = pl.ds(pl.multiple_of(start, piece), piece)
            for chunk in range(chunks):
                rows[here, chunk * DH : (chunk + 1) * DH] = piece_refs[part][
                    shard, chunk * piece : (chunk + 1) * piece, :
                ]
    out_ref[...] = rows[...].T


def flip_rows(place, pieces, slots):
    shards, height, _ = pieces[0].shape
    width = height // (slots // len(pieces)) * DH
    keys = shards * slots
    return pl.pallas_call(
        flip_rows_kernel,
        in_specs=[SMEM_SPEC] + [pl.BlockSpec()] * len(pieces),
        out_shape=jax.ShapeDtypeStruct((width, keys), BF16),
        scratch_shapes=[pltpu.VMEM((keys, width), BF16)],
        compiler_params=params(),
        cost_estimate=pl.CostEstimate(flops=0, bytes_accessed=4 * keys * width, transcendentals=0),
    )(place, *pieces)


def weight_part_kernel(pairs, place_ref, flip_ref, *refs):
    out_ref = refs[-1]
    for pair in range(pairs):

        @pl.when(pl.program_id(0) == pair)
        def _(pair=pair):
            both = jnp.concatenate([ref[...] for ref in refs[2 * pair : 2 * pair + 2]], axis=1)
            product = dot(flip_ref[...], both)
            for side in range(2):
                column = pl.multiple_of((place_ref[0] ^ side) % 2 * DH, DH)
                out_ref[:, pl.ds(column, DH)] = product[:, side * DH : (side + 1) * DH]


def weight_part(place, flip, attended, first, heads, weight, before=None):
    count = len(attended)
    width, keys = flip.shape
    block = pl.BlockSpec((keys, DH), lambda i, place: (0, 0))
    more = [] if before is None else [before]
    return pl.pallas_call(
        functools.partial(weight_part_kernel, count // 2),
        grid_spec=pltpu.PrefetchScalarGridSpec(
            num_scalar_prefetch=1,
            grid=(count // 2,),
            in_specs=[pl.BlockSpec((width, keys), lambda i, place: (0, 0))]
            + [block] * count
            + [pl.BlockSpec(memory_space=pl.ANY)] * len(more),
            out_specs=pl.BlockSpec(
                (width, 2 * DH), lambda i, place: (0, (place[0] ^ (first + 2 * i)) // 2)
            ),
        ),
        out_shape=jax.ShapeDtypeStruct((width, heads * DH), F32),
        input_output_aliases={2 + count: 0} if more else {},
        compiler_params=params(),
        cost_estimate=pl.CostEstimate(
            flops=weight * 2 * keys * width * count * DH,
            bytes_accessed=8 * keys * DH * count,
            transcendentals=0,
        ),
    )(place, flip, *attended, *more)


def mark_live(count_ref, live_ref, slots):
    for shard in range(live_ref.shape[0] // slots):
        inside = lax.broadcasted_iota(jnp.int32, (slots, live_ref.shape[1]), 0)
        live_ref[shard * slots : (shard + 1) * slots] = jnp.where(
            inside < count_ref[shard], 0.0, -1e30
        )


def masked_scores(start, keys, key_ref, query, live_ref):
    scores = dot_cols(key_ref[:keys], query) * (1.0 / math.sqrt(DH)) + live_ref[:keys, :1]
    row = start + lax.broadcasted_iota(jnp.int32, (1, QUERY_BLOCK), 1)
    key_pos = start + lax.broadcasted_iota(jnp.int32, (QUERY_BLOCK, 1), 0)
    edge = jnp.where(key_pos <= row, scores[start:], -1e30)
    return jnp.concatenate([scores[:start], edge], axis=0) if start else edge


def split_blocks(block_ref, *refs):
    shards, slots, _ = block_ref.shape
    for shard in range(shards):
        for which, ref in enumerate(refs):
            ref[shard * slots : (shard + 1) * slots] = block_ref[
                shard, :, which * DH : (which + 1) * DH
            ]


def forward_kernel(
    count_ref, block_ref, attended_ref, stat_ref, live_ref, query_ref, key_ref, value_ref
):
    mark_live(count_ref, live_ref, block_ref.shape[1])
    split_blocks(block_ref, query_ref, key_ref, value_ref)
    value_flip = value_ref[...].T
    for start in range(0, query_ref.shape[0], QUERY_BLOCK):
        rows = slice(start, start + QUERY_BLOCK)
        keys = start + QUERY_BLOCK
        scores = masked_scores(start, keys, key_ref, query_ref[rows], live_ref)
        peak = jnp.max(scores, axis=0, keepdims=True)
        weights = jnp.exp(scores - peak)
        inverse = 1.0 / jnp.sum(weights, axis=0, keepdims=True)
        attended = dot(value_flip[:, :keys], (weights * inverse).astype(BF16))
        attended_ref[rows] = attended.T.astype(BF16)
        stat_ref[0:1, rows] = peak
        stat_ref[1:2, rows] = inverse


def attention_cost(keys, dots):
    return pl.CostEstimate(
        flops=dots * keys * keys * DH, bytes_accessed=16 * keys * DH, transcendentals=keys * keys // 2
    )


def forward(counts, blocks):
    keys = blocks.shape[0] * blocks.shape[1]
    return pl.pallas_call(
        forward_kernel,
        out_shape=[
            jax.ShapeDtypeStruct((keys, DH), BF16),
            jax.ShapeDtypeStruct((8, keys), F32),
        ],
        in_specs=[SMEM_SPEC, pl.BlockSpec()],
        scratch_shapes=[pltpu.VMEM((keys, DH), F32)] + [pltpu.VMEM((keys, DH), BF16)] * 3,
        compiler_params=params(),
        cost_estimate=attention_cost(keys, 2),
    )(counts, blocks)


def backward_kernel(
    count_ref,
    block_ref,
    attended_ref,
    stat_ref,
    grads_ref,
    out_ref,
    live_ref,
    query_ref,
    key_ref,
    value_ref,
    grad_ref,
    query_total,
    key_total,
    value_total,
):
    seq_count, slots, _ = out_ref.shape
    scale = 1.0 / math.sqrt(DH)
    mark_live(count_ref, live_ref, slots)
    split_blocks(block_ref, query_ref, key_ref, value_ref)
    for shard in range(seq_count):
        grad_ref[shard * slots : (shard + 1) * slots] = grads_ref[shard, :slots]
    key_flip = key_ref[...].T
    for start in range(0, query_ref.shape[0], QUERY_BLOCK):
        rows = slice(start, start + QUERY_BLOCK)
        keys = start + QUERY_BLOCK
        query = query_ref[rows]
        grad = grad_ref[rows]
        scores = masked_scores(start, keys, key_ref, query, live_ref)
        probs = jnp.exp(scores - stat_ref[0:1, rows]) * stat_ref[1:2, rows]
        probs_low = probs.astype(BF16)
        product = grad.astype(F32) * attended_ref[rows].astype(F32)
        row_dot = jnp.sum(product.T, axis=0, keepdims=True)
        grad_probs = dot_cols(value_ref[:keys], grad)
        grad_scores = (probs * (grad_probs - row_dot)).astype(BF16)
        query_total[rows] = (dot(key_flip[:, :keys], grad_scores) * scale).T.astype(BF16)
        key_part = dot(grad_scores, query)
        value_part = dot(probs_low, grad)
        if start:
            key_total[:start] += key_part[:start]
            value_total[:start] += value_part[:start]
        key_total[rows] = key_part[start:]
        value_total[rows] = value_part[start:]
    for shard in range(seq_count):
        here = slice(shard * slots, (shard + 1) * slots)
        out_ref[shard, :, :DH] = query_total[here]
        out_ref[shard, :, DH : 2 * DH] = (key_total[here] * scale).astype(BF16)
        out_ref[shard, :, 2 * DH :] = value_total[here].astype(BF16)


def backward(counts, blocks, attended, stats, grads):
    keys = attended.shape[0]
    return pl.pallas_call(
        backward_kernel,
        in_specs=[SMEM_SPEC] + [pl.BlockSpec()] * 4,
        out_shape=jax.ShapeDtypeStruct(blocks.shape, BF16),
        scratch_shapes=[pltpu.VMEM((keys, DH), F32)]
        + [pltpu.VMEM((keys, DH), BF16)] * 5
        + [pltpu.VMEM((keys, DH), F32)] * 2,
        compiler_params=params(VMEM_MOST),
        cost_estimate=attention_cost(keys, 5),
    )(counts, blocks, attended, stats, grads)


def on_device_whole_heads(
    projections,
    output_gradient,
    output_projection_weight,
    kept_token_indices,
    surviving_token_count,
):
    tok_dev = projections.shape[0]
    slots = kept_token_indices.shape[1]
    seq_count = lax.axis_size("seq")
    head_count = lax.axis_size("head")
    index = kept_token_indices
    place = jnp.stack([lax.axis_index("seq"), lax.axis_index("head")]).astype(jnp.int32)
    seq_bits = [1 << bit for bit in reversed(range(seq_count.bit_length() - 1))]
    head_bits = [1 << bit for bit in reversed(range(head_count.bit_length() - 1))]

    def swap(blocks):
        return lax.all_to_all(blocks, "seq", split_axis=0, concat_axis=0, tiled=True)

    packed = pack_whole(index, projections.transpose(1, 0, 2))
    packed, grad_index = lax.optimization_barrier((packed, index))
    arrived = swap(packed)
    grad_blocks = gather_blocks(pack_grad(grad_index, output_gradient), "head", head_bits)
    grads = swap(grad_swap(place, grad_blocks, output_projection_weight, seq_count))
    attended, stats = forward(surviving_token_count, arrived)

    near, last = seq_bits[-2], seq_bits[-1]
    held = {bit: exchange(attended, "seq", bit) for bit in seq_bits}
    held[near ^ last] = exchange(held[near], "seq", last)
    back = backward(surviving_token_count, arrived, attended, stats, grads)
    back, held = lax.optimization_barrier((back, held))
    gathered = gather_blocks(attended, "seq", seq_bits, {0: attended, **held})
    home = swap(back)
    pieces = gather_blocks(grads[:, slots:], "head", head_bits)
    flip = flip_rows(place, pieces, slots)
    late = seq_count - 2
    weight_grad = weight_part(place, flip, gathered[:late], 0, seq_count, 1)
    projection_grad = unpack_heads(index, home, tok_dev, 1)
    weight_grad = weight_part(place, flip, gathered[late:], late, seq_count, 28, weight_grad)
    projection_grad = projection_grad.transpose(1, 0, 2)
    return (projection_grad, weight_grad)


def on_device(projections, output_gradient, weight, index, counts):
    heads = projections.shape[2] // DH
    seq_count, head_count = lax.axis_size("seq"), lax.axis_size("head")
    width = output_gradient.shape[1] * head_count // seq_count
    whole = seq_count == heads and seq_count % 2 == 0 and width % DH == 0
    powers = seq_count & (seq_count - 1) == 0 and head_count & (head_count - 1) == 0
    body = on_device_whole_heads if whole and powers else on_device_split_heads
    return body(projections, output_gradient, weight, index, counts)


def solution(mesh):
    return jax.shard_map(
        on_device,
        mesh=mesh,
        in_specs=(P("seq", None, "head"), P("seq", "head"), P(None, "head"), P("seq", None), P()),
        out_specs=(P("seq", None, "head"), P("seq", "head")),
        check_vma=False,
    )
```

```python
import functools
import math

import jax
import jax.numpy as jnp
from jax import lax
from jax.experimental import pallas as pl
from jax.experimental.pallas import tpu as pltpu
from jax.sharding import PartitionSpec as P

DH = 128
QUERY_BLOCK = 256
VMEM_BYTES = 20 * 1024 * 1024
VMEM_MOST = 62 * 1024 * 1024
F32 = jnp.float32
BF16 = jnp.bfloat16


def params(limit=VMEM_BYTES):
    return pltpu.CompilerParams(vmem_limit_bytes=limit)


def dot(left, right):
    return jnp.dot(left, right, preferred_element_type=F32)


def dot_rows(left, right):
    return lax.dot_general(left, right, (((0,), (0,)), ((), ())), preferred_element_type=F32)


def dot_cols(left, right):
    return lax.dot_general(left, right, (((1,), (1,)), ((), ())), preferred_element_type=F32)


def token_selector(index_ref, tokens):
    slots = index_ref.shape[1]
    token = lax.broadcasted_iota(jnp.int32, (tokens, slots), 0)
    return jnp.where(token == index_ref[...], 1.0, 0.0).astype(BF16)


def pack_grad_kernel(index_ref, grad_ref, out_ref):
    selector = token_selector(index_ref, grad_ref.shape[0])
    out_ref[...] = dot_rows(selector, grad_ref[...]).astype(BF16)


def pack_grad(index, grad):
    slots = index.shape[1]
    return pl.pallas_call(
        pack_grad_kernel,
        out_shape=jax.ShapeDtypeStruct((slots, grad.shape[1]), BF16),
        compiler_params=params(),
    )(index, grad)


def pack_heads_kernel(index_ref, proj_ref, out_ref):
    selector = token_selector(index_ref, proj_ref.shape[1])
    for which in range(3):
        rows = dot_rows(selector, proj_ref[which]).astype(BF16)
        for head in range(out_ref.shape[0]):
            out_ref[head, :, which * DH : (which + 1) * DH] = rows[:, head * DH : (head + 1) * DH]


def pack_heads(index, proj):
    slots = index.shape[1]
    _, tokens, width = proj.shape
    heads = width // DH
    step = 2
    return pl.pallas_call(
        pack_heads_kernel,
        grid=(heads // step,),
        in_specs=[
            pl.BlockSpec((1, slots), lambda i: (0, 0)),
            pl.BlockSpec((3, tokens, step * DH), lambda i: (0, 0, i)),
        ],
        out_specs=pl.BlockSpec((step, slots, 3 * DH), lambda i: (i, 0, 0)),
        out_shape=jax.ShapeDtypeStruct((heads, slots, 3 * DH), BF16),
        compiler_params=params(),
    )(index, proj)


def unpack_heads_kernel(index_ref, rows_ref, out_ref):
    selector = token_selector(index_ref, out_ref.shape[1])
    for head in range(rows_ref.shape[0]):
        tokens = dot(selector, rows_ref[head]).astype(BF16)
        for which in range(3):
            out_ref[which, :, head * DH : (head + 1) * DH] = tokens[
                :, which * DH : (which + 1) * DH
            ]


def unpack_heads(index, rows, tokens):
    heads, slots, _ = rows.shape
    step = 2
    return pl.pallas_call(
        unpack_heads_kernel,
        grid=(heads // step,),
        in_specs=[
            pl.BlockSpec((1, slots), lambda i: (0, 0)),
            pl.BlockSpec((step, slots, 3 * DH), lambda i: (i, 0, 0)),
        ],
        out_specs=pl.BlockSpec((3, tokens, step * DH), lambda i: (0, 0, i)),
        out_shape=jax.ShapeDtypeStruct((3, tokens, heads * DH), BF16),
        compiler_params=params(),
    )(index, rows)


def grad_attn_kernel(rows_ref, weight_ref, out_ref):
    product = dot(rows_ref[...], weight_ref[...]).astype(BF16)
    for head in range(out_ref.shape[0]):
        out_ref[head] = product[:, head * DH : (head + 1) * DH]


def grad_attn_heads(rows, weight):
    slots, depth = rows.shape
    heads = weight.shape[1] // DH
    step = 2
    return pl.pallas_call(
        grad_attn_kernel,
        grid=(heads // step,),
        in_specs=[
            pl.BlockSpec((slots, depth), lambda i: (0, 0)),
            pl.BlockSpec((depth, step * DH), lambda i: (0, i)),
        ],
        out_specs=pl.BlockSpec((step, slots, DH), lambda i: (i, 0, 0)),
        out_shape=jax.ShapeDtypeStruct((heads, slots, DH), BF16),
        compiler_params=params(),
    )(rows, weight)


def weight_grad_kernel(rows_ref, attended_ref, out_ref):
    attended = jnp.concatenate([attended_ref[head] for head in range(attended_ref.shape[0])], axis=1)
    out_ref[...] = dot_rows(rows_ref[...], attended)


def weight_grad_heads(rows, attended):
    total, width = rows.shape
    heads = attended.shape[0]
    step = 2
    return pl.pallas_call(
        weight_grad_kernel,
        grid=(heads // step,),
        in_specs=[
            pl.BlockSpec((total, width), lambda i: (0, 0)),
            pl.BlockSpec((step, total, DH), lambda i: (i, 0, 0)),
        ],
        out_specs=pl.BlockSpec((width, step * DH), lambda i: (0, i)),
        out_shape=jax.ShapeDtypeStruct((width, heads * DH), F32),
        compiler_params=params(),
    )(rows, attended)


def attention_kernel(
    slots,
    part_rows,
    part_ref,
    live_ref,
    query_ref,
    grad_ref,
    key_ref,
    value_ref,
    attended_ref,
    query_grad_ref,
    key_grad_ref,
    value_grad_ref,
    key_total,
    value_total,
):
    scale = 1.0 / math.sqrt(DH)
    rows_total = query_ref.shape[0]
    keys_total = key_ref.shape[0]
    quarters = slots // part_rows
    key_flip = key_ref[...].T
    value_flip = value_ref[...].T
    for start in range(0, rows_total, QUERY_BLOCK):
        rows = slice(start, start + QUERY_BLOCK)
        last = start + QUERY_BLOCK - 1
        last_pos = last // part_rows * slots + (quarters - 1) * part_rows + last % part_rows
        first_pos = start // part_rows * slots + start % part_rows
        keys = min(-(-(last_pos + 1) // 128) * 128, keys_total)
        clear = first_pos // 128 * 128
        query = query_ref[rows]
        grad = grad_ref[rows]
        row = start + lax.broadcasted_iota(jnp.int32, (1, QUERY_BLOCK), 1)
        if quarters > 1:
            shard = row // part_rows
            row = shard * slots + part_ref[0] * part_rows + row - shard * part_rows
        scores = dot_cols(key_ref[:keys], query) * scale + live_ref[:keys, :1]
        key_pos = clear + lax.broadcasted_iota(jnp.int32, (keys - clear, 1), 0)
        edge = jnp.where(key_pos <= row, scores[clear:], -1e30)
        scores = jnp.concatenate([scores[:clear], edge], axis=0) if clear else edge
        peak = jnp.max(scores, axis=0, keepdims=True)
        weights = jnp.exp(scores - peak)
        probs = weights * (1.0 / jnp.sum(weights, axis=0, keepdims=True))
        probs_low = probs.astype(BF16)
        attended = dot(value_flip[:, :keys], probs_low)
        attended_ref[rows] = attended.T.astype(BF16)
        row_dot = jnp.sum(grad.T.astype(F32) * attended, axis=0, keepdims=True)
        grad_probs = dot_cols(value_ref[:keys], grad)
        grad_scores = (probs * (grad_probs - row_dot)).astype(BF16)
        query_grad = dot(key_flip[:, :keys], grad_scores) * scale
        query_grad_ref[rows] = query_grad.T.astype(BF16)
        key_part = dot(grad_scores, query)
        value_part = dot(probs_low, grad)
        prev = start - 1
        reached = 0
        if start:
            prev_pos = prev // part_rows * slots + (quarters - 1) * part_rows + prev % part_rows
            reached = min(-(-(prev_pos + 1) // 128) * 128, keys_total)
        if reached:
            key_total[:reached] += key_part[:reached]
            value_total[:reached] += value_part[:reached]
        if keys > reached:
            key_total[reached:keys] = key_part[reached:]
            value_total[reached:keys] = value_part[reached:]
    key_grad_ref[...] = (key_total[...] * scale).astype(key_grad_ref.dtype)
    value_grad_ref[...] = value_total[...].astype(value_grad_ref.dtype)


def attention(part, live, query, grad, key, value, slots, part_rows, key_type):
    rows, keys = query.shape[0], key.shape[0]
    vmem = pl.BlockSpec(memory_space=pltpu.VMEM)
    return pl.pallas_call(
        functools.partial(attention_kernel, slots, part_rows),
        in_specs=[pl.BlockSpec(memory_space=pltpu.SMEM)] + [vmem] * 5,
        out_specs=[vmem] * 4,
        out_shape=[
            jax.ShapeDtypeStruct((rows, DH), BF16),
            jax.ShapeDtypeStruct((rows, DH), BF16),
            jax.ShapeDtypeStruct((keys, DH), key_type),
            jax.ShapeDtypeStruct((keys, DH), key_type),
        ],
        scratch_shapes=[pltpu.VMEM((keys, DH), F32)] * 2,
        compiler_params=params(),
    )(part, live, query, grad, key, value)


def on_device_split_heads(
    projections,
    output_gradient,
    output_projection_weight,
    kept_token_indices,
    surviving_token_count,
):
    tok_dev = projections.shape[0]
    group_width = projections.shape[2]
    slots = kept_token_indices.shape[1]
    heads = group_width // DH
    seq_count = lax.axis_size("seq")
    head_count = lax.axis_size("head")
    quarters = seq_count // heads
    part_rows = slots // quarters
    part = (lax.axis_index("seq") % quarters).astype(jnp.int32).reshape(1)
    index = kept_token_indices
    keys = seq_count * slots

    grad_local = pack_grad(index, output_gradient)
    grad_rows = lax.all_gather(grad_local, "head", axis=1, tiled=True)
    packed = pack_heads(index, projections.transpose(1, 0, 2))

    position = jnp.arange(slots, dtype=jnp.int32)
    live = position[None, :] < surviving_token_count[:, None]
    live = jnp.where(live, 0.0, -1e30).astype(F32).reshape(keys, 1)
    live = jnp.broadcast_to(live, (keys, DH))

    def swap(blocks):
        return lax.all_to_all(blocks, "seq", split_axis=0, concat_axis=0, tiled=True)

    if quarters == 1:
        arrived = swap(packed).reshape(keys, 3 * DH)
        query, key, value = (arrived[:, n * DH : (n + 1) * DH] for n in range(3))
    else:
        query = swap(packed[:, :, :DH].reshape(seq_count, part_rows, DH))
        query = query.reshape(seq_count * part_rows, DH)
        sides = jnp.broadcast_to(packed[:, None, :, DH:], (heads, quarters, slots, 2 * DH))
        sides = swap(sides.reshape(seq_count, slots, 2 * DH)).reshape(keys, 2 * DH)
        key, value = sides[:, :DH], sides[:, DH:]

    grad_heads = grad_attn_heads(grad_rows, output_projection_weight)
    grad_in = swap(grad_heads.reshape(seq_count, part_rows, DH)).reshape(-1, DH)

    width = grad_rows.shape[1] // seq_count
    piece = slots // head_count
    mine = lax.dynamic_slice_in_dim(grad_rows, lax.axis_index("head") * piece, piece, 0)
    mine = swap(mine.reshape(piece, seq_count, width).transpose(1, 0, 2))
    all_rows = lax.all_gather(mine, "head", axis=1, tiled=True)

    key_type = BF16 if quarters == 1 else F32
    attended, query_grad, key_grad, value_grad = attention(
        part, live, query, grad_in, key, value, slots, part_rows, key_type
    )

    gathered = lax.all_gather(attended, "seq", axis=0).reshape(heads, keys, DH)
    all_rows = all_rows.reshape(seq_count, quarters, part_rows, width).transpose(1, 0, 2, 3)
    weight_grad = weight_grad_heads(all_rows.reshape(keys, width), gathered)

    if quarters == 1:
        back = jnp.concatenate([query_grad, key_grad, value_grad], axis=1)
        home = swap(back.reshape(seq_count, slots, 3 * DH))
    else:
        query_home = swap(query_grad.reshape(seq_count, part_rows, DH)).reshape(heads, slots, DH)
        back = jnp.concatenate([key_grad, value_grad], axis=1)
        key_home = swap(back.reshape(seq_count, slots, 2 * DH))
        key_home = jnp.sum(key_home.reshape(heads, quarters, slots, 2 * DH), axis=1)
        home = jnp.concatenate([query_home, key_home.astype(BF16)], axis=2)
    projection_grad = unpack_heads(index, home, tok_dev).transpose(1, 0, 2)
    return (projection_grad, weight_grad)


def pack_whole_kernel(index_ref, proj_ref, out_ref, loaded, packed, arrive, leave):
    parts = proj_ref.shape[0]
    copies = [
        pltpu.make_async_copy(proj_ref.at[which], loaded.at[which], arrive.at[which])
        for which in range(parts)
    ]
    for copy in copies:
        copy.start()
    token = lax.broadcasted_iota(jnp.int32, (loaded.shape[1], index_ref.shape[1]), 0)
    selector = jnp.where(token == index_ref[...], 1.0, 0.0).T.astype(BF16)
    away = []
    for which, copy in enumerate(copies):
        copy.wait()
        rows = dot(selector, loaded[which]).astype(BF16)
        for head in range(out_ref.shape[0]):
            packed[which, head] = rows[:, head * DH : (head + 1) * DH]
        away.append(
            pltpu.make_async_copy(
                packed.at[which],
                out_ref.at[:, :, which * DH : (which + 1) * DH],
                leave.at[which],
            )
        )
        away[-1].start()
    for copy in away:
        copy.wait()


def pack_whole(index, proj):
    slots = index.shape[1]
    parts, tokens, width = proj.shape
    heads = width // DH
    return pl.pallas_call(
        pack_whole_kernel,
        in_specs=[pl.BlockSpec(), pl.BlockSpec(memory_space=pltpu.HBM)],
        out_specs=pl.BlockSpec(memory_space=pltpu.HBM),
        out_shape=jax.ShapeDtypeStruct((heads, slots, parts * DH), BF16),
        scratch_shapes=[
            pltpu.VMEM(proj.shape, BF16),
            pltpu.VMEM((parts, heads, slots, DH), BF16),
            pltpu.SemaphoreType.DMA((parts,)),
            pltpu.SemaphoreType.DMA((parts,)),
        ],
        compiler_params=params(VMEM_MOST),
        cost_estimate=pl.CostEstimate(
            flops=2 * slots * tokens * parts * width,
            bytes_accessed=8 * tokens * width,
            transcendentals=0,
        ),
    )(index, proj)


def exchange(block, axis, bit):
    return lax.ppermute(block, axis, [(i, i ^ bit) for i in range(lax.axis_size(axis))])


def gather_blocks(block, axis, bits, held=None):
    held = {0: block} if held is None else dict(held)
    reached = [0]
    for bit in bits:
        for step in list(reached):
            if step ^ bit not in held:
                held[step ^ bit] = exchange(held[step], axis, bit)
            reached.append(step ^ bit)
    return [held[step] for step in range(lax.axis_size(axis))]


SMEM_SPEC = pl.BlockSpec(memory_space=pltpu.SMEM)
VMEM_SPEC = pl.BlockSpec(memory_space=pltpu.VMEM)


def grad_swap_kernel(count, place_ref, *refs):
    row_refs, weight_ref, out_ref, total = refs[:count], refs[count], refs[count + 1], refs[count + 2]
    mine = place_ref[1]
    seq_count, height, _ = out_ref.shape
    slots, depth = row_refs[0].shape
    piece = slots // count
    chunks = (height - slots) // piece
    per_block = depth // (chunks * DH)
    for step in range(count):

        @pl.when(pl.program_id(0) == step)
        def _(step=step):
            part = dot(row_refs[step][...], weight_ref[...])
            total[...] = part if step == 0 else total[...] + part
            share = row_refs[step][pl.ds(pl.multiple_of(mine * piece, piece), piece), :]
            for chunk in range(per_block * chunks):
                partner = (mine ^ step) * per_block + chunk // chunks
                start = slots + chunk % chunks * piece
                out_ref[partner, start : start + piece, :] = share[:, chunk * DH : (chunk + 1) * DH]

    @pl.when(pl.program_id(0) == count - 1)
    def _():
        for head in range(seq_count):
            out_ref[head, :slots, :] = total[:, head * DH : (head + 1) * DH].astype(BF16)


def grad_swap(place, blocks, weight, seq_count):
    count = len(blocks)
    slots, depth = blocks[0].shape
    columns = weight.shape[1]
    height = slots + slots // count * (count * depth // seq_count // DH)
    return pl.pallas_call(
        functools.partial(grad_swap_kernel, count),
        grid_spec=pltpu.PrefetchScalarGridSpec(
            num_scalar_prefetch=1,
            grid=(count,),
            in_specs=[pl.BlockSpec((slots, depth), lambda i, place: (0, 0))] * count
            + [pl.BlockSpec((depth, columns), lambda i, place: (place[1] ^ i, 0))],
            out_specs=pl.BlockSpec((seq_count, height, DH), lambda i, place: (0, 0, 0)),
            scratch_shapes=[pltpu.VMEM((slots, columns), F32)],
        ),
        out_shape=jax.ShapeDtypeStruct((seq_count, height, DH), BF16),
        compiler_params=params(),
        cost_estimate=pl.CostEstimate(
            flops=2 * slots * count * depth * columns,
            bytes_accessed=2 * count * depth * columns,
            transcendentals=0,
        ),
    )(place, *blocks, weight)


def flip_rows_kernel(place_ref, *refs):
    piece_refs, out_ref, rows = refs[:-2], refs[-2], refs[-1]
    count = len(piece_refs)
    chunks = rows.shape[1] // DH
    shards, height, _ = piece_refs[0].shape
    piece = height // chunks
    for part in range(count):
        for shard in range(shards):
            start = shard * piece * count + (place_ref[1] ^ part) * piece
            here = pl.ds(pl.multiple_of(start, piece), piece)
            for chunk in range(chunks):
                rows[here, chunk * DH : (chunk + 1) * DH] = piece_refs[part][
                    shard, chunk * piece : (chunk + 1) * piece, :
                ]
    out_ref[...] = rows[...].T


def flip_rows(place, pieces, slots):
    shards, height, _ = pieces[0].shape
    width = height // (slots // len(pieces)) * DH
    keys = shards * slots
    return pl.pallas_call(
        flip_rows_kernel,
        in_specs=[SMEM_SPEC] + [pl.BlockSpec()] * len(pieces),
        out_shape=jax.ShapeDtypeStruct((width, keys), BF16),
        scratch_shapes=[pltpu.VMEM((keys, width), BF16)],
        compiler_params=params(),
        cost_estimate=pl.CostEstimate(flops=0, bytes_accessed=4 * keys * width, transcendentals=0),
    )(place, *pieces)


def weight_part_kernel(first, count, place_ref, flip_ref, *refs):
    out_ref = refs[-1]
    for step in range(0, count, 2):
        both = jnp.concatenate([ref[...] for ref in refs[step : step + 2]], axis=1)
        product = dot(flip_ref[...], both)
        for side in range(2):
            head = place_ref[0] ^ (first + step + side)
            column = pl.multiple_of(head * DH % out_ref.shape[1], DH)
            out_ref[:, pl.ds(column, DH)] = product[:, side * DH : (side + 1) * DH]


def weight_part(place, flip, attended, first, heads, weight, before=None):
    count = len(attended)
    width, keys = flip.shape
    rows = width // 4 if width % 64 == 0 else width
    block = pl.BlockSpec((keys, DH), lambda i, place: (0, 0))
    if before is None:
        more, out = [], pl.BlockSpec((rows, heads * DH), lambda i, place: (i, 0))
    else:
        more, out = [before], pl.BlockSpec((rows, 2 * DH), lambda i, place: (i, (place[0] ^ first) // 2))
    return pl.pallas_call(
        functools.partial(weight_part_kernel, first, count),
        grid_spec=pltpu.PrefetchScalarGridSpec(
            num_scalar_prefetch=1,
            grid=(width // rows,),
            in_specs=[pl.BlockSpec((rows, keys), lambda i, place: (i, 0))]
            + [block] * count
            + [pl.BlockSpec(memory_space=pl.ANY)] * len(more),
            out_specs=out,
        ),
        out_shape=jax.ShapeDtypeStruct((width, heads * DH), F32),
        input_output_aliases={2 + count: 0} if more else {},
        compiler_params=params(),
        cost_estimate=pl.CostEstimate(
            flops=weight * 2 * keys * width * count * DH,
            bytes_accessed=8 * keys * DH * count,
            transcendentals=0,
        ),
    )(place, flip, *attended, *more)


def mark_live(count_ref, live_ref, slots):
    for shard in range(live_ref.shape[0] // slots):
        inside = lax.broadcasted_iota(jnp.int32, (slots, live_ref.shape[1]), 0)
        live_ref[shard * slots : (shard + 1) * slots] = jnp.where(
            inside < count_ref[shard], 0.0, -1e30
        )


def masked_scores(start, keys, key_ref, query, live_ref):
    scores = dot_cols(key_ref[:keys], query) * (1.0 / math.sqrt(DH)) + live_ref[:keys, :1]
    row = start + lax.broadcasted_iota(jnp.int32, (1, QUERY_BLOCK), 1)
    key_pos = start + lax.broadcasted_iota(jnp.int32, (QUERY_BLOCK, 1), 0)
    edge = jnp.where(key_pos <= row, scores[start:], -1e30)
    return jnp.concatenate([scores[:start], edge], axis=0) if start else edge


def split_blocks(block_ref, *refs):
    shards, slots, _ = block_ref.shape
    for shard in range(shards):
        for which, ref in enumerate(refs):
            ref[shard * slots : (shard + 1) * slots] = block_ref[
                shard, :, which * DH : (which + 1) * DH
            ]


def forward_kernel(
    count_ref, block_ref, attended_ref, stat_ref, live_ref, query_ref, key_ref, value_ref
):
    mark_live(count_ref, live_ref, block_ref.shape[1])
    split_blocks(block_ref, query_ref, key_ref, value_ref)
    value_flip = value_ref[...].T
    for start in range(0, query_ref.shape[0], QUERY_BLOCK):
        rows = slice(start, start + QUERY_BLOCK)
        keys = start + QUERY_BLOCK
        scores = masked_scores(start, keys, key_ref, query_ref[rows], live_ref)
        peak = jnp.max(scores, axis=0, keepdims=True)
        weights = jnp.exp(scores - peak)
        inverse = 1.0 / jnp.sum(weights, axis=0, keepdims=True)
        attended = dot(value_flip[:, :keys], (weights * inverse).astype(BF16))
        attended_ref[rows] = attended.T.astype(BF16)
        stat_ref[0:1, rows] = peak
        stat_ref[1:2, rows] = inverse


def attention_cost(keys, dots):
    return pl.CostEstimate(
        flops=dots * keys * keys * DH, bytes_accessed=16 * keys * DH, transcendentals=keys * keys // 2
    )


def forward(counts, blocks):
    keys = blocks.shape[0] * blocks.shape[1]
    return pl.pallas_call(
        forward_kernel,
        out_shape=[
            jax.ShapeDtypeStruct((keys, DH), BF16),
            jax.ShapeDtypeStruct((8, keys), F32),
        ],
        in_specs=[SMEM_SPEC, pl.BlockSpec()],
        scratch_shapes=[pltpu.VMEM((keys, DH), F32)] + [pltpu.VMEM((keys, DH), BF16)] * 3,
        compiler_params=params(),
        cost_estimate=attention_cost(keys, 2),
    )(counts, blocks)


def backward_kernel(
    count_ref,
    block_ref,
    attended_ref,
    stat_ref,
    grads_ref,
    out_ref,
    live_ref,
    query_ref,
    key_ref,
    value_ref,
    grad_ref,
    query_total,
    key_total,
    value_total,
):
    seq_count, slots, _ = out_ref.shape
    scale = 1.0 / math.sqrt(DH)
    mark_live(count_ref, live_ref, slots)
    split_blocks(block_ref, query_ref, key_ref, value_ref)
    for shard in range(seq_count):
        grad_ref[shard * slots : (shard + 1) * slots] = grads_ref[shard, :slots]
    key_flip = key_ref[...].T
    for start in range(0, query_ref.shape[0], QUERY_BLOCK):
        rows = slice(start, start + QUERY_BLOCK)
        keys = start + QUERY_BLOCK
        query = query_ref[rows]
        grad = grad_ref[rows]
        scores = masked_scores(start, keys, key_ref, query, live_ref)
        probs = jnp.exp(scores - stat_ref[0:1, rows]) * stat_ref[1:2, rows]
        probs_low = probs.astype(BF16)
        product = grad.astype(F32) * attended_ref[rows].astype(F32)
        row_dot = jnp.sum(product.T, axis=0, keepdims=True)
        grad_probs = dot_cols(value_ref[:keys], grad)
        grad_scores = (probs * (grad_probs - row_dot)).astype(BF16)
        query_total[rows] = (dot(key_flip[:, :keys], grad_scores) * scale).T.astype(BF16)
        key_part = dot(grad_scores, query)
        value_part = dot(probs_low, grad)
        if start:
            key_total[:start] += key_part[:start]
            value_total[:start] += value_part[:start]
        key_total[rows] = key_part[start:]
        value_total[rows] = value_part[start:]
    for shard in range(seq_count):
        here = slice(shard * slots, (shard + 1) * slots)
        out_ref[shard, :, :DH] = query_total[here]
        out_ref[shard, :, DH : 2 * DH] = (key_total[here] * scale).astype(BF16)
        out_ref[shard, :, 2 * DH :] = value_total[here].astype(BF16)


def backward(counts, blocks, attended, stats, grads):
    keys = attended.shape[0]
    return pl.pallas_call(
        backward_kernel,
        in_specs=[SMEM_SPEC] + [pl.BlockSpec()] * 4,
        out_shape=jax.ShapeDtypeStruct(blocks.shape, BF16),
        scratch_shapes=[pltpu.VMEM((keys, DH), F32)]
        + [pltpu.VMEM((keys, DH), BF16)] * 5
        + [pltpu.VMEM((keys, DH), F32)] * 2,
        compiler_params=params(VMEM_MOST),
        cost_estimate=attention_cost(keys, 5),
    )(counts, blocks, attended, stats, grads)


def on_device_whole_heads(
    projections,
    output_gradient,
    output_projection_weight,
    kept_token_indices,
    surviving_token_count,
):
    tok_dev = projections.shape[0]
    slots = kept_token_indices.shape[1]
    seq_count = lax.axis_size("seq")
    head_count = lax.axis_size("head")
    index = kept_token_indices
    place = jnp.stack([lax.axis_index("seq"), lax.axis_index("head")]).astype(jnp.int32)
    seq_bits = [1 << bit for bit in reversed(range(seq_count.bit_length() - 1))]
    head_bits = [1 << bit for bit in reversed(range(head_count.bit_length() - 1))]

    def swap(blocks):
        return lax.all_to_all(blocks, "seq", split_axis=0, concat_axis=0, tiled=True)

    packed = pack_whole(index, projections.transpose(1, 0, 2))
    packed, grad_index = lax.optimization_barrier((packed, index))
    arrived = swap(packed)
    grad_blocks = gather_blocks(pack_grad(grad_index, output_gradient), "head", head_bits)
    grads = swap(grad_swap(place, grad_blocks, output_projection_weight, seq_count))
    attended, stats = forward(surviving_token_count, arrived)

    near, last = seq_bits[-2], seq_bits[-1]
    held = {bit: exchange(attended, "seq", bit) for bit in seq_bits}
    held[near ^ last] = exchange(held[near], "seq", last)
    back = backward(surviving_token_count, arrived, attended, stats, grads)
    back, held = lax.optimization_barrier((back, held))
    gathered = gather_blocks(attended, "seq", seq_bits, {0: attended, **held})
    home = swap(back)
    pieces = gather_blocks(grads[:, slots:], "head", head_bits)
    flip = flip_rows(place, pieces, slots)
    late = seq_count - 2
    weight_grad = weight_part(place, flip, gathered[:late], 0, seq_count, 1)
    projection_grad = unpack_heads(index, home, tok_dev)
    weight_grad = weight_part(place, flip, gathered[late:], late, seq_count, 28, weight_grad)
    projection_grad = projection_grad.transpose(1, 0, 2)
    return (projection_grad, weight_grad)


def on_device(projections, output_gradient, weight, index, counts):
    heads = projections.shape[2] // DH
    seq_count, head_count = lax.axis_size("seq"), lax.axis_size("head")
    width = output_gradient.shape[1] * head_count // seq_count
    whole = seq_count == heads and seq_count % 2 == 0 and width % DH == 0
    powers = seq_count & (seq_count - 1) == 0 and head_count & (head_count - 1) == 0
    body = on_device_whole_heads if whole and powers else on_device_split_heads
    return body(projections, output_gradient, weight, index, counts)


def solution(mesh):
    return jax.shard_map(
        on_device,
        mesh=mesh,
        in_specs=(P("seq", None, "head"), P("seq", "head"), P(None, "head"), P("seq", None), P()),
        out_specs=(P("seq", None, "head"), P("seq", "head")),
        check_vma=False,
    )
```

```python
import functools
import math

import jax
import jax.numpy as jnp
from jax import lax
from jax.experimental import pallas as pl
from jax.experimental.pallas import tpu as pltpu
from jax.sharding import PartitionSpec as P

DH = 128
QUERY_BLOCK = 256
VMEM_BYTES = 20 * 1024 * 1024
VMEM_MOST = 62 * 1024 * 1024
F32 = jnp.float32
BF16 = jnp.bfloat16


def params(limit=VMEM_BYTES):
    return pltpu.CompilerParams(vmem_limit_bytes=limit)


def dot(left, right):
    return jnp.dot(left, right, preferred_element_type=F32)


def dot_rows(left, right):
    return lax.dot_general(left, right, (((0,), (0,)), ((), ())), preferred_element_type=F32)


def dot_cols(left, right):
    return lax.dot_general(left, right, (((1,), (1,)), ((), ())), preferred_element_type=F32)


def token_selector(index_ref, tokens):
    slots = index_ref.shape[1]
    token = lax.broadcasted_iota(jnp.int32, (tokens, slots), 0)
    return jnp.where(token == index_ref[...], 1.0, 0.0).astype(BF16)


def pack_grad_kernel(index_ref, grad_ref, out_ref):
    selector = token_selector(index_ref, grad_ref.shape[0])
    out_ref[...] = dot_rows(selector, grad_ref[...]).astype(BF16)


def pack_grad(index, grad):
    slots = index.shape[1]
    return pl.pallas_call(
        pack_grad_kernel,
        out_shape=jax.ShapeDtypeStruct((slots, grad.shape[1]), BF16),
        compiler_params=params(),
    )(index, grad)


def pack_heads_kernel(index_ref, proj_ref, out_ref):
    selector = token_selector(index_ref, proj_ref.shape[1])
    for which in range(3):
        rows = dot_rows(selector, proj_ref[which]).astype(BF16)
        for head in range(out_ref.shape[0]):
            out_ref[head, :, which * DH : (which + 1) * DH] = rows[:, head * DH : (head + 1) * DH]


def pack_heads(index, proj):
    slots = index.shape[1]
    _, tokens, width = proj.shape
    heads = width // DH
    step = 2
    return pl.pallas_call(
        pack_heads_kernel,
        grid=(heads // step,),
        in_specs=[
            pl.BlockSpec((1, slots), lambda i: (0, 0)),
            pl.BlockSpec((3, tokens, step * DH), lambda i: (0, 0, i)),
        ],
        out_specs=pl.BlockSpec((step, slots, 3 * DH), lambda i: (i, 0, 0)),
        out_shape=jax.ShapeDtypeStruct((heads, slots, 3 * DH), BF16),
        compiler_params=params(),
    )(index, proj)


def unpack_heads_kernel(index_ref, rows_ref, out_ref):
    selector = token_selector(index_ref, out_ref.shape[1])
    for head in range(rows_ref.shape[0]):
        tokens = dot(selector, rows_ref[head]).astype(BF16)
        for which in range(3):
            out_ref[which, :, head * DH : (head + 1) * DH] = tokens[
                :, which * DH : (which + 1) * DH
            ]


def unpack_heads(index, rows, tokens):
    heads, slots, _ = rows.shape
    step = 2
    return pl.pallas_call(
        unpack_heads_kernel,
        grid=(heads // step,),
        in_specs=[
            pl.BlockSpec((1, slots), lambda i: (0, 0)),
            pl.BlockSpec((step, slots, 3 * DH), lambda i: (i, 0, 0)),
        ],
        out_specs=pl.BlockSpec((3, tokens, step * DH), lambda i: (0, 0, i)),
        out_shape=jax.ShapeDtypeStruct((3, tokens, heads * DH), BF16),
        compiler_params=params(),
    )(index, rows)


def grad_attn_kernel(rows_ref, weight_ref, out_ref):
    product = dot(rows_ref[...], weight_ref[...]).astype(BF16)
    for head in range(out_ref.shape[0]):
        out_ref[head] = product[:, head * DH : (head + 1) * DH]


def grad_attn_heads(rows, weight):
    slots, depth = rows.shape
    heads = weight.shape[1] // DH
    step = 2
    return pl.pallas_call(
        grad_attn_kernel,
        grid=(heads // step,),
        in_specs=[
            pl.BlockSpec((slots, depth), lambda i: (0, 0)),
            pl.BlockSpec((depth, step * DH), lambda i: (0, i)),
        ],
        out_specs=pl.BlockSpec((step, slots, DH), lambda i: (i, 0, 0)),
        out_shape=jax.ShapeDtypeStruct((heads, slots, DH), BF16),
        compiler_params=params(),
    )(rows, weight)


def weight_grad_kernel(rows_ref, attended_ref, out_ref):
    attended = jnp.concatenate([attended_ref[head] for head in range(attended_ref.shape[0])], axis=1)
    out_ref[...] = dot_rows(rows_ref[...], attended)


def weight_grad_heads(rows, attended):
    total, width = rows.shape
    heads = attended.shape[0]
    step = 2
    return pl.pallas_call(
        weight_grad_kernel,
        grid=(heads // step,),
        in_specs=[
            pl.BlockSpec((total, width), lambda i: (0, 0)),
            pl.BlockSpec((step, total, DH), lambda i: (i, 0, 0)),
        ],
        out_specs=pl.BlockSpec((width, step * DH), lambda i: (0, i)),
        out_shape=jax.ShapeDtypeStruct((width, heads * DH), F32),
        compiler_params=params(),
    )(rows, attended)


def attention_kernel(
    slots,
    part_rows,
    part_ref,
    live_ref,
    query_ref,
    grad_ref,
    key_ref,
    value_ref,
    attended_ref,
    query_grad_ref,
    key_grad_ref,
    value_grad_ref,
    key_total,
    value_total,
):
    scale = 1.0 / math.sqrt(DH)
    rows_total = query_ref.shape[0]
    keys_total = key_ref.shape[0]
    quarters = slots // part_rows
    key_flip = key_ref[...].T
    value_flip = value_ref[...].T
    for start in range(0, rows_total, QUERY_BLOCK):
        rows = slice(start, start + QUERY_BLOCK)
        last = start + QUERY_BLOCK - 1
        last_pos = last // part_rows * slots + (quarters - 1) * part_rows + last % part_rows
        first_pos = start // part_rows * slots + start % part_rows
        keys = min(-(-(last_pos + 1) // 128) * 128, keys_total)
        clear = first_pos // 128 * 128
        query = query_ref[rows]
        grad = grad_ref[rows]
        row = start + lax.broadcasted_iota(jnp.int32, (1, QUERY_BLOCK), 1)
        if quarters > 1:
            shard = row // part_rows
            row = shard * slots + part_ref[0] * part_rows + row - shard * part_rows
        scores = dot_cols(key_ref[:keys], query) * scale + live_ref[:keys, :1]
        key_pos = clear + lax.broadcasted_iota(jnp.int32, (keys - clear, 1), 0)
        edge = jnp.where(key_pos <= row, scores[clear:], -1e30)
        scores = jnp.concatenate([scores[:clear], edge], axis=0) if clear else edge
        peak = jnp.max(scores, axis=0, keepdims=True)
        weights = jnp.exp(scores - peak)
        probs = weights * (1.0 / jnp.sum(weights, axis=0, keepdims=True))
        probs_low = probs.astype(BF16)
        attended = dot(value_flip[:, :keys], probs_low)
        attended_ref[rows] = attended.T.astype(BF16)
        row_dot = jnp.sum(grad.T.astype(F32) * attended, axis=0, keepdims=True)
        grad_probs = dot_cols(value_ref[:keys], grad)
        grad_scores = (probs * (grad_probs - row_dot)).astype(BF16)
        query_grad = dot(key_flip[:, :keys], grad_scores) * scale
        query_grad_ref[rows] = query_grad.T.astype(BF16)
        key_part = dot(grad_scores, query)
        value_part = dot(probs_low, grad)
        prev = start - 1
        reached = 0
        if start:
            prev_pos = prev // part_rows * slots + (quarters - 1) * part_rows + prev % part_rows
            reached = min(-(-(prev_pos + 1) // 128) * 128, keys_total)
        if reached:
            key_total[:reached] += key_part[:reached]
            value_total[:reached] += value_part[:reached]
        if keys > reached:
            key_total[reached:keys] = key_part[reached:]
            value_total[reached:keys] = value_part[reached:]
    key_grad_ref[...] = (key_total[...] * scale).astype(key_grad_ref.dtype)
    value_grad_ref[...] = value_total[...].astype(value_grad_ref.dtype)


def attention(part, live, query, grad, key, value, slots, part_rows, key_type):
    rows, keys = query.shape[0], key.shape[0]
    vmem = pl.BlockSpec(memory_space=pltpu.VMEM)
    return pl.pallas_call(
        functools.partial(attention_kernel, slots, part_rows),
        in_specs=[pl.BlockSpec(memory_space=pltpu.SMEM)] + [vmem] * 5,
        out_specs=[vmem] * 4,
        out_shape=[
            jax.ShapeDtypeStruct((rows, DH), BF16),
            jax.ShapeDtypeStruct((rows, DH), BF16),
            jax.ShapeDtypeStruct((keys, DH), key_type),
            jax.ShapeDtypeStruct((keys, DH), key_type),
        ],
        scratch_shapes=[pltpu.VMEM((keys, DH), F32)] * 2,
        compiler_params=params(),
    )(part, live, query, grad, key, value)


def on_device_split_heads(
    projections,
    output_gradient,
    output_projection_weight,
    kept_token_indices,
    surviving_token_count,
):
    tok_dev = projections.shape[0]
    group_width = projections.shape[2]
    slots = kept_token_indices.shape[1]
    heads = group_width // DH
    seq_count = lax.axis_size("seq")
    head_count = lax.axis_size("head")
    quarters = seq_count // heads
    part_rows = slots // quarters
    part = (lax.axis_index("seq") % quarters).astype(jnp.int32).reshape(1)
    index = kept_token_indices
    keys = seq_count * slots

    grad_local = pack_grad(index, output_gradient)
    grad_rows = lax.all_gather(grad_local, "head", axis=1, tiled=True)
    packed = pack_heads(index, projections.transpose(1, 0, 2))

    position = jnp.arange(slots, dtype=jnp.int32)
    live = position[None, :] < surviving_token_count[:, None]
    live = jnp.where(live, 0.0, -1e30).astype(F32).reshape(keys, 1)
    live = jnp.broadcast_to(live, (keys, DH))

    def swap(blocks):
        return lax.all_to_all(blocks, "seq", split_axis=0, concat_axis=0, tiled=True)

    if quarters == 1:
        arrived = swap(packed).reshape(keys, 3 * DH)
        query, key, value = (arrived[:, n * DH : (n + 1) * DH] for n in range(3))
    else:
        query = swap(packed[:, :, :DH].reshape(seq_count, part_rows, DH))
        query = query.reshape(seq_count * part_rows, DH)
        sides = jnp.broadcast_to(packed[:, None, :, DH:], (heads, quarters, slots, 2 * DH))
        sides = swap(sides.reshape(seq_count, slots, 2 * DH)).reshape(keys, 2 * DH)
        key, value = sides[:, :DH], sides[:, DH:]

    grad_heads = grad_attn_heads(grad_rows, output_projection_weight)
    grad_in = swap(grad_heads.reshape(seq_count, part_rows, DH)).reshape(-1, DH)

    width = grad_rows.shape[1] // seq_count
    piece = slots // head_count
    mine = lax.dynamic_slice_in_dim(grad_rows, lax.axis_index("head") * piece, piece, 0)
    mine = swap(mine.reshape(piece, seq_count, width).transpose(1, 0, 2))
    all_rows = lax.all_gather(mine, "head", axis=1, tiled=True)

    key_type = BF16 if quarters == 1 else F32
    attended, query_grad, key_grad, value_grad = attention(
        part, live, query, grad_in, key, value, slots, part_rows, key_type
    )

    gathered = lax.all_gather(attended, "seq", axis=0).reshape(heads, keys, DH)
    all_rows = all_rows.reshape(seq_count, quarters, part_rows, width).transpose(1, 0, 2, 3)
    weight_grad = weight_grad_heads(all_rows.reshape(keys, width), gathered)

    if quarters == 1:
        back = jnp.concatenate([query_grad, key_grad, value_grad], axis=1)
        home = swap(back.reshape(seq_count, slots, 3 * DH))
    else:
        query_home = swap(query_grad.reshape(seq_count, part_rows, DH)).reshape(heads, slots, DH)
        back = jnp.concatenate([key_grad, value_grad], axis=1)
        key_home = swap(back.reshape(seq_count, slots, 2 * DH))
        key_home = jnp.sum(key_home.reshape(heads, quarters, slots, 2 * DH), axis=1)
        home = jnp.concatenate([query_home, key_home.astype(BF16)], axis=2)
    projection_grad = unpack_heads(index, home, tok_dev).transpose(1, 0, 2)
    return (projection_grad, weight_grad)


def pack_whole_kernel(index_ref, proj_ref, out_ref, loaded, packed, arrive, leave):
    parts = proj_ref.shape[0]
    copies = [
        pltpu.make_async_copy(proj_ref.at[which], loaded.at[which], arrive.at[which])
        for which in range(parts)
    ]
    for copy in copies:
        copy.start()
    token = lax.broadcasted_iota(jnp.int32, (loaded.shape[1], index_ref.shape[1]), 0)
    selector = jnp.where(token == index_ref[...], 1.0, 0.0).T.astype(BF16)
    away = []
    for which, copy in enumerate(copies):
        copy.wait()
        rows = dot(selector, loaded[which]).astype(BF16)
        for head in range(out_ref.shape[0]):
            packed[which, head] = rows[:, head * DH : (head + 1) * DH]
        away.append(
            pltpu.make_async_copy(
                packed.at[which],
                out_ref.at[:, :, which * DH : (which + 1) * DH],
                leave.at[which],
            )
        )
        away[-1].start()
    for copy in away:
        copy.wait()


def pack_whole(index, proj):
    slots = index.shape[1]
    parts, tokens, width = proj.shape
    heads = width // DH
    return pl.pallas_call(
        pack_whole_kernel,
        in_specs=[pl.BlockSpec(), pl.BlockSpec(memory_space=pltpu.HBM)],
        out_specs=pl.BlockSpec(memory_space=pltpu.HBM),
        out_shape=jax.ShapeDtypeStruct((heads, slots, parts * DH), BF16),
        scratch_shapes=[
            pltpu.VMEM(proj.shape, BF16),
            pltpu.VMEM((parts, heads, slots, DH), BF16),
            pltpu.SemaphoreType.DMA((parts,)),
            pltpu.SemaphoreType.DMA((parts,)),
        ],
        compiler_params=params(VMEM_MOST),
        cost_estimate=pl.CostEstimate(
            flops=2 * slots * tokens * parts * width,
            bytes_accessed=8 * tokens * width,
            transcendentals=0,
        ),
    )(index, proj)


def unpack_whole_kernel(index_ref, rows_ref, out_ref, tokens_ref, leave):
    selector = token_selector(index_ref, out_ref.shape[1])
    away = []
    for pair in range(rows_ref.shape[0] // 2):
        for side in range(2):
            tokens = dot(selector, rows_ref[2 * pair + side]).astype(BF16)
            for which in range(out_ref.shape[0]):
                tokens_ref[pair, which, :, side * DH : (side + 1) * DH] = tokens[
                    :, which * DH : (which + 1) * DH
                ]
        columns = pl.ds(pair * 2 * DH, 2 * DH)
        away.append(
            pltpu.make_async_copy(tokens_ref.at[pair], out_ref.at[:, :, columns], leave.at[pair])
        )
        away[-1].start()
    for copy in away:
        copy.wait()


def unpack_whole(index, rows, tokens):
    heads, slots, width = rows.shape
    parts = width // DH
    return pl.pallas_call(
        unpack_whole_kernel,
        in_specs=[VMEM_SPEC] * 2,
        out_specs=pl.BlockSpec(memory_space=pl.ANY),
        out_shape=jax.ShapeDtypeStruct((parts, tokens, heads * DH), BF16),
        scratch_shapes=[
            pltpu.VMEM((heads // 2, parts, tokens, 2 * DH), BF16),
            pltpu.SemaphoreType.DMA((heads // 2,)),
        ],
        compiler_params=params(),
    )(index, rows)


def exchange(block, axis, bit):
    return lax.ppermute(block, axis, [(i, i ^ bit) for i in range(lax.axis_size(axis))])


def gather_blocks(block, axis, bits, held=None):
    held = {0: block} if held is None else dict(held)
    reached = [0]
    for bit in bits:
        for step in list(reached):
            if step ^ bit not in held:
                held[step ^ bit] = exchange(held[step], axis, bit)
            reached.append(step ^ bit)
    return [held[step] for step in range(lax.axis_size(axis))]


SMEM_SPEC = pl.BlockSpec(memory_space=pltpu.SMEM)
VMEM_SPEC = pl.BlockSpec(memory_space=pltpu.VMEM)


def grad_swap_kernel(count, place_ref, *refs):
    row_refs, weight_ref, out_ref, total = refs[:count], refs[count], refs[count + 1], refs[count + 2]
    mine = place_ref[1]
    seq_count, height, _ = out_ref.shape
    slots, depth = row_refs[0].shape
    piece = slots // count
    chunks = (height - slots) // piece
    per_block = depth // (chunks * DH)
    for step in range(count):

        @pl.when(pl.program_id(0) == step)
        def _(step=step):
            part = dot(row_refs[step][...], weight_ref[...])
            total[...] = part if step == 0 else total[...] + part
            share = row_refs[step][pl.ds(pl.multiple_of(mine * piece, piece), piece), :]
            for chunk in range(per_block * chunks):
                partner = (mine ^ step) * per_block + chunk // chunks
                start = slots + chunk % chunks * piece
                out_ref[partner, start : start + piece, :] = share[:, chunk * DH : (chunk + 1) * DH]

    @pl.when(pl.program_id(0) == count - 1)
    def _():
        for head in range(seq_count):
            out_ref[head, :slots, :] = total[:, head * DH : (head + 1) * DH].astype(BF16)


def grad_swap(place, blocks, weight, seq_count):
    count = len(blocks)
    slots, depth = blocks[0].shape
    columns = weight.shape[1]
    height = slots + slots // count * (count * depth // seq_count // DH)
    return pl.pallas_call(
        functools.partial(grad_swap_kernel, count),
        grid_spec=pltpu.PrefetchScalarGridSpec(
            num_scalar_prefetch=1,
            grid=(count,),
            in_specs=[pl.BlockSpec((slots, depth), lambda i, place: (0, 0))] * count
            + [pl.BlockSpec((depth, columns), lambda i, place: (place[1] ^ i, 0))],
            out_specs=pl.BlockSpec((seq_count, height, DH), lambda i, place: (0, 0, 0)),
            scratch_shapes=[pltpu.VMEM((slots, columns), F32)],
        ),
        out_shape=jax.ShapeDtypeStruct((seq_count, height, DH), BF16),
        compiler_params=params(),
        cost_estimate=pl.CostEstimate(
            flops=2 * slots * count * depth * columns,
            bytes_accessed=2 * count * depth * columns,
            transcendentals=0,
        ),
    )(place, *blocks, weight)


def flip_rows_kernel(place_ref, *refs):
    piece_refs, out_ref, rows = refs[:-2], refs[-2], refs[-1]
    count = len(piece_refs)
    chunks = rows.shape[1] // DH
    shards, height, _ = piece_refs[0].shape
    piece = height // chunks
    for part in range(count):
        for shard in range(shards):
            start = shard * piece * count + (place_ref[1] ^ part) * piece
            here = pl.ds(pl.multiple_of(start, piece), piece)
            for chunk in range(chunks):
                rows[here, chunk * DH : (chunk + 1) * DH] = piece_refs[part][
                    shard, chunk * piece : (chunk + 1) * piece, :
                ]
    out_ref[...] = rows[...].T


def flip_rows(place, pieces, slots):
    shards, height, _ = pieces[0].shape
    width = height // (slots // len(pieces)) * DH
    keys = shards * slots
    return pl.pallas_call(
        flip_rows_kernel,
        in_specs=[SMEM_SPEC] + [pl.BlockSpec()] * len(pieces),
        out_specs=VMEM_SPEC,
        out_shape=jax.ShapeDtypeStruct((width, keys), BF16),
        scratch_shapes=[pltpu.VMEM((keys, width), BF16)],
        compiler_params=params(),
        cost_estimate=pl.CostEstimate(flops=0, bytes_accessed=4 * keys * width, transcendentals=0),
    )(place, *pieces)


def weight_part_kernel(first, count, place_ref, flip_ref, *refs):
    out_ref, product_ref, leave = refs[-3:]
    away = []
    for step in range(0, count, 2):
        both = jnp.concatenate([ref[...] for ref in refs[step : step + 2]], axis=1)
        product = dot(flip_ref[...], both)
        head = place_ref[0] ^ (first + step)
        for side in range(2):
            column = pl.multiple_of((head ^ side) % 2 * DH, DH)
            product_ref[step // 2, :, pl.ds(column, DH)] = product[:, side * DH : (side + 1) * DH]
        columns = pl.ds(pl.multiple_of(head // 2 * (2 * DH), 2 * DH), 2 * DH)
        away.append(
            pltpu.make_async_copy(
                product_ref.at[step // 2], out_ref.at[:, columns], leave.at[step // 2]
            )
        )
        away[-1].start()
    for copy in away:
        copy.wait()


def weight_part(place, flip, attended, first, heads, weight, before=None):
    count = len(attended)
    width, keys = flip.shape
    more = [] if before is None else [before]
    return pl.pallas_call(
        functools.partial(weight_part_kernel, first, count),
        in_specs=[SMEM_SPEC]
        + [VMEM_SPEC] * (1 + count)
        + [pl.BlockSpec(memory_space=pl.ANY)] * len(more),
        out_specs=pl.BlockSpec(memory_space=pl.ANY),
        out_shape=jax.ShapeDtypeStruct((width, heads * DH), F32),
        scratch_shapes=[
            pltpu.VMEM((count // 2, width, 2 * DH), F32),
            pltpu.SemaphoreType.DMA((count // 2,)),
        ],
        input_output_aliases={2 + count: 0} if more else {},
        compiler_params=params(),
        cost_estimate=pl.CostEstimate(
            flops=weight * 2 * keys * width * count * DH,
            bytes_accessed=8 * keys * DH * count,
            transcendentals=0,
        ),
    )(place, flip, *attended, *more)


def mark_live(count_ref, live_ref, slots):
    for shard in range(live_ref.shape[0] // slots):
        inside = lax.broadcasted_iota(jnp.int32, (slots, live_ref.shape[1]), 0)
        live_ref[shard * slots : (shard + 1) * slots] = jnp.where(
            inside < count_ref[shard], 0.0, -1e30
        )


def masked_scores(start, keys, key_ref, query, live_ref):
    scores = dot_cols(key_ref[:keys], query) * (1.0 / math.sqrt(DH)) + live_ref[:keys, :1]
    row = start + lax.broadcasted_iota(jnp.int32, (1, QUERY_BLOCK), 1)
    key_pos = start + lax.broadcasted_iota(jnp.int32, (QUERY_BLOCK, 1), 0)
    edge = jnp.where(key_pos <= row, scores[start:], -1e30)
    return jnp.concatenate([scores[:start], edge], axis=0) if start else edge


def split_blocks(block_ref, *refs):
    shards, slots, _ = block_ref.shape
    for shard in range(shards):
        for which, ref in enumerate(refs):
            ref[shard * slots : (shard + 1) * slots] = block_ref[
                shard, :, which * DH : (which + 1) * DH
            ]


def forward_kernel(
    count_ref, block_ref, attended_ref, stat_ref, live_ref, query_ref, key_ref, value_ref
):
    mark_live(count_ref, live_ref, block_ref.shape[1])
    split_blocks(block_ref, query_ref, key_ref, value_ref)
    value_flip = value_ref[...].T
    for start in range(0, query_ref.shape[0], QUERY_BLOCK):
        rows = slice(start, start + QUERY_BLOCK)
        keys = start + QUERY_BLOCK
        scores = masked_scores(start, keys, key_ref, query_ref[rows], live_ref)
        peak = jnp.max(scores, axis=0, keepdims=True)
        weights = jnp.exp(scores - peak)
        inverse = 1.0 / jnp.sum(weights, axis=0, keepdims=True)
        attended = dot(value_flip[:, :keys], (weights * inverse).astype(BF16))
        attended_ref[rows] = attended.T.astype(BF16)
        stat_ref[0:1, rows] = peak
        stat_ref[1:2, rows] = inverse


def attention_cost(keys, dots):
    return pl.CostEstimate(
        flops=dots * keys * keys * DH, bytes_accessed=16 * keys * DH, transcendentals=keys * keys // 2
    )


def forward(counts, blocks):
    keys = blocks.shape[0] * blocks.shape[1]
    return pl.pallas_call(
        forward_kernel,
        out_shape=[
            jax.ShapeDtypeStruct((keys, DH), BF16),
            jax.ShapeDtypeStruct((8, keys), F32),
        ],
        in_specs=[SMEM_SPEC, pl.BlockSpec()],
        scratch_shapes=[pltpu.VMEM((keys, DH), F32)] + [pltpu.VMEM((keys, DH), BF16)] * 3,
        compiler_params=params(),
        cost_estimate=attention_cost(keys, 2),
    )(counts, blocks)


def backward_kernel(
    count_ref,
    block_ref,
    attended_ref,
    stat_ref,
    grads_ref,
    out_ref,
    live_ref,
    query_ref,
    key_ref,
    value_ref,
    grad_ref,
    query_total,
    key_total,
    value_total,
):
    seq_count, slots, _ = out_ref.shape
    scale = 1.0 / math.sqrt(DH)
    mark_live(count_ref, live_ref, slots)
    split_blocks(block_ref, query_ref, key_ref, value_ref)
    for shard in range(seq_count):
        grad_ref[shard * slots : (shard + 1) * slots] = grads_ref[shard, :slots]
    key_flip = key_ref[...].T
    for start in range(0, query_ref.shape[0], QUERY_BLOCK):
        rows = slice(start, start + QUERY_BLOCK)
        keys = start + QUERY_BLOCK
        query = query_ref[rows]
        grad = grad_ref[rows]
        scores = masked_scores(start, keys, key_ref, query, live_ref)
        probs = jnp.exp(scores - stat_ref[0:1, rows]) * stat_ref[1:2, rows]
        probs_low = probs.astype(BF16)
        product = grad.astype(F32) * attended_ref[rows].astype(F32)
        row_dot = jnp.sum(product.T, axis=0, keepdims=True)
        grad_probs = dot_cols(value_ref[:keys], grad)
        grad_scores = (probs * (grad_probs - row_dot)).astype(BF16)
        query_total[rows] = (dot(key_flip[:, :keys], grad_scores) * scale).T.astype(BF16)
        key_part = dot(grad_scores, query)
        value_part = dot(probs_low, grad)
        if start:
            key_total[:start] += key_part[:start]
            value_total[:start] += value_part[:start]
        key_total[rows] = key_part[start:]
        value_total[rows] = value_part[start:]
    for shard in range(seq_count):
        here = slice(shard * slots, (shard + 1) * slots)
        out_ref[shard, :, :DH] = query_total[here]
        out_ref[shard, :, DH : 2 * DH] = (key_total[here] * scale).astype(BF16)
        out_ref[shard, :, 2 * DH :] = value_total[here].astype(BF16)


def backward(counts, blocks, attended, stats, grads):
    keys = attended.shape[0]
    return pl.pallas_call(
        backward_kernel,
        in_specs=[SMEM_SPEC] + [pl.BlockSpec()] * 4,
        out_shape=jax.ShapeDtypeStruct(blocks.shape, BF16),
        scratch_shapes=[pltpu.VMEM((keys, DH), F32)]
        + [pltpu.VMEM((keys, DH), BF16)] * 5
        + [pltpu.VMEM((keys, DH), F32)] * 2,
        compiler_params=params(VMEM_MOST),
        cost_estimate=attention_cost(keys, 5),
    )(counts, blocks, attended, stats, grads)


def on_device_whole_heads(
    projections,
    output_gradient,
    output_projection_weight,
    kept_token_indices,
    surviving_token_count,
):
    tok_dev = projections.shape[0]
    slots = kept_token_indices.shape[1]
    seq_count = lax.axis_size("seq")
    head_count = lax.axis_size("head")
    index = kept_token_indices
    place = jnp.stack([lax.axis_index("seq"), lax.axis_index("head")]).astype(jnp.int32)
    seq_bits = [1 << bit for bit in reversed(range(seq_count.bit_length() - 1))]
    head_bits = [1 << bit for bit in reversed(range(head_count.bit_length() - 1))]

    def swap(blocks):
        return lax.all_to_all(blocks, "seq", split_axis=0, concat_axis=0, tiled=True)

    packed = pack_whole(index, projections.transpose(1, 0, 2))
    packed, grad_index = lax.optimization_barrier((packed, index))
    arrived = swap(packed)
    grad_blocks = gather_blocks(pack_grad(grad_index, output_gradient), "head", head_bits)
    grads = swap(grad_swap(place, grad_blocks, output_projection_weight, seq_count))
    attended, stats = forward(surviving_token_count, arrived)

    near, last = seq_bits[-2], seq_bits[-1]
    held = {bit: exchange(attended, "seq", bit) for bit in seq_bits}
    held[near ^ last] = exchange(held[near], "seq", last)
    back = backward(surviving_token_count, arrived, attended, stats, grads)
    back, held = lax.optimization_barrier((back, held))
    gathered = gather_blocks(attended, "seq", seq_bits, {0: attended, **held})
    home = swap(back)
    pieces = gather_blocks(grads[:, slots:], "head", head_bits)
    flip = flip_rows(place, pieces, slots)
    late = seq_count - 2
    weight_grad = weight_part(place, flip, gathered[:late], 0, seq_count, 1)
    projection_grad = unpack_whole(index, home, tok_dev)
    weight_grad = weight_part(place, flip, gathered[late:], late, seq_count, 28, weight_grad)
    projection_grad = projection_grad.transpose(1, 0, 2)
    return (projection_grad, weight_grad)


def on_device(projections, output_gradient, weight, index, counts):
    heads = projections.shape[2] // DH
    seq_count, head_count = lax.axis_size("seq"), lax.axis_size("head")
    width = output_gradient.shape[1] * head_count // seq_count
    whole = seq_count == heads and seq_count % 2 == 0 and width % DH == 0
    powers = seq_count & (seq_count - 1) == 0 and head_count & (head_count - 1) == 0
    body = on_device_whole_heads if whole and powers else on_device_split_heads
    return body(projections, output_gradient, weight, index, counts)


def solution(mesh):
    return jax.shard_map(
        on_device,
        mesh=mesh,
        in_specs=(P("seq", None, "head"), P("seq", "head"), P(None, "head"), P("seq", None), P()),
        out_specs=(P("seq", None, "head"), P("seq", "head")),
        check_vma=False,
    )
```

```python
import functools
import math

import jax
import jax.numpy as jnp
from jax import lax
from jax.experimental import pallas as pl
from jax.experimental.pallas import tpu as pltpu
from jax.sharding import PartitionSpec as P

DH = 128
QUERY_BLOCK = 256
VMEM_BYTES = 20 * 1024 * 1024
VMEM_MOST = 62 * 1024 * 1024
F32 = jnp.float32
BF16 = jnp.bfloat16


def params(limit=VMEM_BYTES):
    return pltpu.CompilerParams(vmem_limit_bytes=limit)


def dot(left, right):
    return jnp.dot(left, right, preferred_element_type=F32)


def dot_rows(left, right):
    return lax.dot_general(left, right, (((0,), (0,)), ((), ())), preferred_element_type=F32)


def dot_cols(left, right):
    return lax.dot_general(left, right, (((1,), (1,)), ((), ())), preferred_element_type=F32)


def token_selector(index_ref, tokens):
    slots = index_ref.shape[1]
    token = lax.broadcasted_iota(jnp.int32, (tokens, slots), 0)
    return jnp.where(token == index_ref[...], 1.0, 0.0).astype(BF16)


def pack_grad_kernel(index_ref, grad_ref, out_ref):
    selector = token_selector(index_ref, grad_ref.shape[0])
    out_ref[...] = dot_rows(selector, grad_ref[...]).astype(BF16)


def pack_grad(index, grad):
    slots = index.shape[1]
    return pl.pallas_call(
        pack_grad_kernel,
        out_shape=jax.ShapeDtypeStruct((slots, grad.shape[1]), BF16),
        compiler_params=params(),
    )(index, grad)


def pack_heads_kernel(index_ref, proj_ref, out_ref):
    selector = token_selector(index_ref, proj_ref.shape[1])
    for which in range(3):
        rows = dot_rows(selector, proj_ref[which]).astype(BF16)
        for head in range(out_ref.shape[0]):
            out_ref[head, :, which * DH : (which + 1) * DH] = rows[:, head * DH : (head + 1) * DH]


def pack_heads(index, proj):
    slots = index.shape[1]
    _, tokens, width = proj.shape
    heads = width // DH
    step = 2
    return pl.pallas_call(
        pack_heads_kernel,
        grid=(heads // step,),
        in_specs=[
            pl.BlockSpec((1, slots), lambda i: (0, 0)),
            pl.BlockSpec((3, tokens, step * DH), lambda i: (0, 0, i)),
        ],
        out_specs=pl.BlockSpec((step, slots, 3 * DH), lambda i: (i, 0, 0)),
        out_shape=jax.ShapeDtypeStruct((heads, slots, 3 * DH), BF16),
        compiler_params=params(),
    )(index, proj)


def unpack_heads_kernel(index_ref, rows_ref, out_ref):
    selector = token_selector(index_ref, out_ref.shape[1])
    for head in range(rows_ref.shape[0]):
        tokens = dot(selector, rows_ref[head]).astype(BF16)
        for which in range(3):
            out_ref[which, :, head * DH : (head + 1) * DH] = tokens[
                :, which * DH : (which + 1) * DH
            ]


def unpack_heads(index, rows, tokens):
    heads, slots, _ = rows.shape
    step = 2
    return pl.pallas_call(
        unpack_heads_kernel,
        grid=(heads // step,),
        in_specs=[
            pl.BlockSpec((1, slots), lambda i: (0, 0)),
            pl.BlockSpec((step, slots, 3 * DH), lambda i: (i, 0, 0)),
        ],
        out_specs=pl.BlockSpec((3, tokens, step * DH), lambda i: (0, 0, i)),
        out_shape=jax.ShapeDtypeStruct((3, tokens, heads * DH), BF16),
        compiler_params=params(),
    )(index, rows)


def grad_attn_kernel(rows_ref, weight_ref, out_ref):
    product = dot(rows_ref[...], weight_ref[...]).astype(BF16)
    for head in range(out_ref.shape[0]):
        out_ref[head] = product[:, head * DH : (head + 1) * DH]


def grad_attn_heads(rows, weight):
    slots, depth = rows.shape
    heads = weight.shape[1] // DH
    step = 2
    return pl.pallas_call(
        grad_attn_kernel,
        grid=(heads // step,),
        in_specs=[
            pl.BlockSpec((slots, depth), lambda i: (0, 0)),
            pl.BlockSpec((depth, step * DH), lambda i: (0, i)),
        ],
        out_specs=pl.BlockSpec((step, slots, DH), lambda i: (i, 0, 0)),
        out_shape=jax.ShapeDtypeStruct((heads, slots, DH), BF16),
        compiler_params=params(),
    )(rows, weight)


def weight_grad_kernel(rows_ref, attended_ref, out_ref):
    attended = jnp.concatenate([attended_ref[head] for head in range(attended_ref.shape[0])], axis=1)
    out_ref[...] = dot_rows(rows_ref[...], attended)


def weight_grad_heads(rows, attended):
    total, width = rows.shape
    heads = attended.shape[0]
    step = 2
    return pl.pallas_call(
        weight_grad_kernel,
        grid=(heads // step,),
        in_specs=[
            pl.BlockSpec((total, width), lambda i: (0, 0)),
            pl.BlockSpec((step, total, DH), lambda i: (i, 0, 0)),
        ],
        out_specs=pl.BlockSpec((width, step * DH), lambda i: (0, i)),
        out_shape=jax.ShapeDtypeStruct((width, heads * DH), F32),
        compiler_params=params(),
    )(rows, attended)


def attention_kernel(
    slots,
    part_rows,
    part_ref,
    live_ref,
    query_ref,
    grad_ref,
    key_ref,
    value_ref,
    attended_ref,
    query_grad_ref,
    key_grad_ref,
    value_grad_ref,
    key_total,
    value_total,
):
    scale = 1.0 / math.sqrt(DH)
    rows_total = query_ref.shape[0]
    keys_total = key_ref.shape[0]
    quarters = slots // part_rows
    key_flip = key_ref[...].T
    value_flip = value_ref[...].T
    for start in range(0, rows_total, QUERY_BLOCK):
        rows = slice(start, start + QUERY_BLOCK)
        last = start + QUERY_BLOCK - 1
        last_pos = last // part_rows * slots + (quarters - 1) * part_rows + last % part_rows
        first_pos = start // part_rows * slots + start % part_rows
        keys = min(-(-(last_pos + 1) // 128) * 128, keys_total)
        clear = first_pos // 128 * 128
        query = query_ref[rows]
        grad = grad_ref[rows]
        row = start + lax.broadcasted_iota(jnp.int32, (1, QUERY_BLOCK), 1)
        if quarters > 1:
            shard = row // part_rows
            row = shard * slots + part_ref[0] * part_rows + row - shard * part_rows
        scores = dot_cols(key_ref[:keys], query) * scale + live_ref[:keys, :1]
        key_pos = clear + lax.broadcasted_iota(jnp.int32, (keys - clear, 1), 0)
        edge = jnp.where(key_pos <= row, scores[clear:], -1e30)
        scores = jnp.concatenate([scores[:clear], edge], axis=0) if clear else edge
        peak = jnp.max(scores, axis=0, keepdims=True)
        weights = jnp.exp(scores - peak)
        probs = weights * (1.0 / jnp.sum(weights, axis=0, keepdims=True))
        probs_low = probs.astype(BF16)
        attended = dot(value_flip[:, :keys], probs_low)
        attended_ref[rows] = attended.T.astype(BF16)
        row_dot = jnp.sum(grad.T.astype(F32) * attended, axis=0, keepdims=True)
        grad_probs = dot_cols(value_ref[:keys], grad)
        grad_scores = (probs * (grad_probs - row_dot)).astype(BF16)
        query_grad = dot(key_flip[:, :keys], grad_scores) * scale
        query_grad_ref[rows] = query_grad.T.astype(BF16)
        key_part = dot(grad_scores, query)
        value_part = dot(probs_low, grad)
        prev = start - 1
        reached = 0
        if start:
            prev_pos = prev // part_rows * slots + (quarters - 1) * part_rows + prev % part_rows
            reached = min(-(-(prev_pos + 1) // 128) * 128, keys_total)
        if reached:
            key_total[:reached] += key_part[:reached]
            value_total[:reached] += value_part[:reached]
        if keys > reached:
            key_total[reached:keys] = key_part[reached:]
            value_total[reached:keys] = value_part[reached:]
    key_grad_ref[...] = (key_total[...] * scale).astype(key_grad_ref.dtype)
    value_grad_ref[...] = value_total[...].astype(value_grad_ref.dtype)


def attention(part, live, query, grad, key, value, slots, part_rows, key_type):
    rows, keys = query.shape[0], key.shape[0]
    vmem = pl.BlockSpec(memory_space=pltpu.VMEM)
    return pl.pallas_call(
        functools.partial(attention_kernel, slots, part_rows),
        in_specs=[pl.BlockSpec(memory_space=pltpu.SMEM)] + [vmem] * 5,
        out_specs=[vmem] * 4,
        out_shape=[
            jax.ShapeDtypeStruct((rows, DH), BF16),
            jax.ShapeDtypeStruct((rows, DH), BF16),
            jax.ShapeDtypeStruct((keys, DH), key_type),
            jax.ShapeDtypeStruct((keys, DH), key_type),
        ],
        scratch_shapes=[pltpu.VMEM((keys, DH), F32)] * 2,
        compiler_params=params(),
    )(part, live, query, grad, key, value)


def on_device_split_heads(
    projections,
    output_gradient,
    output_projection_weight,
    kept_token_indices,
    surviving_token_count,
):
    tok_dev = projections.shape[0]
    group_width = projections.shape[2]
    slots = kept_token_indices.shape[1]
    heads = group_width // DH
    seq_count = lax.axis_size("seq")
    head_count = lax.axis_size("head")
    quarters = seq_count // heads
    part_rows = slots // quarters
    part = (lax.axis_index("seq") % quarters).astype(jnp.int32).reshape(1)
    index = kept_token_indices
    keys = seq_count * slots

    grad_local = pack_grad(index, output_gradient)
    grad_rows = lax.all_gather(grad_local, "head", axis=1, tiled=True)
    packed = pack_heads(index, projections.transpose(1, 0, 2))

    position = jnp.arange(slots, dtype=jnp.int32)
    live = position[None, :] < surviving_token_count[:, None]
    live = jnp.where(live, 0.0, -1e30).astype(F32).reshape(keys, 1)
    live = jnp.broadcast_to(live, (keys, DH))

    def swap(blocks):
        return lax.all_to_all(blocks, "seq", split_axis=0, concat_axis=0, tiled=True)

    if quarters == 1:
        arrived = swap(packed).reshape(keys, 3 * DH)
        query, key, value = (arrived[:, n * DH : (n + 1) * DH] for n in range(3))
    else:
        query = swap(packed[:, :, :DH].reshape(seq_count, part_rows, DH))
        query = query.reshape(seq_count * part_rows, DH)
        sides = jnp.broadcast_to(packed[:, None, :, DH:], (heads, quarters, slots, 2 * DH))
        sides = swap(sides.reshape(seq_count, slots, 2 * DH)).reshape(keys, 2 * DH)
        key, value = sides[:, :DH], sides[:, DH:]

    grad_heads = grad_attn_heads(grad_rows, output_projection_weight)
    grad_in = swap(grad_heads.reshape(seq_count, part_rows, DH)).reshape(-1, DH)

    width = grad_rows.shape[1] // seq_count
    piece = slots // head_count
    mine = lax.dynamic_slice_in_dim(grad_rows, lax.axis_index("head") * piece, piece, 0)
    mine = swap(mine.reshape(piece, seq_count, width).transpose(1, 0, 2))
    all_rows = lax.all_gather(mine, "head", axis=1, tiled=True)

    key_type = BF16 if quarters == 1 else F32
    attended, query_grad, key_grad, value_grad = attention(
        part, live, query, grad_in, key, value, slots, part_rows, key_type
    )

    gathered = lax.all_gather(attended, "seq", axis=0).reshape(heads, keys, DH)
    all_rows = all_rows.reshape(seq_count, quarters, part_rows, width).transpose(1, 0, 2, 3)
    weight_grad = weight_grad_heads(all_rows.reshape(keys, width), gathered)

    if quarters == 1:
        back = jnp.concatenate([query_grad, key_grad, value_grad], axis=1)
        home = swap(back.reshape(seq_count, slots, 3 * DH))
    else:
        query_home = swap(query_grad.reshape(seq_count, part_rows, DH)).reshape(heads, slots, DH)
        back = jnp.concatenate([key_grad, value_grad], axis=1)
        key_home = swap(back.reshape(seq_count, slots, 2 * DH))
        key_home = jnp.sum(key_home.reshape(heads, quarters, slots, 2 * DH), axis=1)
        home = jnp.concatenate([query_home, key_home.astype(BF16)], axis=2)
    projection_grad = unpack_heads(index, home, tok_dev).transpose(1, 0, 2)
    return (projection_grad, weight_grad)


def pack_whole_kernel(index_ref, proj_ref, out_ref, loaded, packed, arrive, leave):
    parts = proj_ref.shape[0]
    copies = [
        pltpu.make_async_copy(proj_ref.at[which], loaded.at[which], arrive.at[which])
        for which in range(parts)
    ]
    for copy in copies:
        copy.start()
    token = lax.broadcasted_iota(jnp.int32, (loaded.shape[1], index_ref.shape[1]), 0)
    selector = jnp.where(token == index_ref[...], 1.0, 0.0).T.astype(BF16)
    away = []
    for which, copy in enumerate(copies):
        copy.wait()
        rows = dot(selector, loaded[which]).astype(BF16)
        for head in range(out_ref.shape[0]):
            packed[which, head] = rows[:, head * DH : (head + 1) * DH]
        away.append(
            pltpu.make_async_copy(
                packed.at[which],
                out_ref.at[:, :, which * DH : (which + 1) * DH],
                leave.at[which],
            )
        )
        away[-1].start()
    for copy in away:
        copy.wait()


def pack_whole(index, proj):
    slots = index.shape[1]
    parts, tokens, width = proj.shape
    heads = width // DH
    return pl.pallas_call(
        pack_whole_kernel,
        in_specs=[pl.BlockSpec(), pl.BlockSpec(memory_space=pltpu.HBM)],
        out_specs=pl.BlockSpec(memory_space=pltpu.HBM),
        out_shape=jax.ShapeDtypeStruct((heads, slots, parts * DH), BF16),
        scratch_shapes=[
            pltpu.VMEM(proj.shape, BF16),
            pltpu.VMEM((parts, heads, slots, DH), BF16),
            pltpu.SemaphoreType.DMA((parts,)),
            pltpu.SemaphoreType.DMA((parts,)),
        ],
        compiler_params=params(VMEM_MOST),
        cost_estimate=pl.CostEstimate(
            flops=2 * slots * tokens * parts * width,
            bytes_accessed=8 * tokens * width,
            transcendentals=0,
        ),
    )(index, proj)


def unpack_whole_kernel(index_ref, rows_ref, out_ref, tokens_ref, leave):
    selector = token_selector(index_ref, out_ref.shape[1])
    away = []
    for pair in range(rows_ref.shape[0] // 2):
        for side in range(2):
            tokens = dot(selector, rows_ref[2 * pair + side]).astype(BF16)
            for which in range(out_ref.shape[0]):
                tokens_ref[pair, which, :, side * DH : (side + 1) * DH] = tokens[
                    :, which * DH : (which + 1) * DH
                ]
        columns = pl.ds(pair * 2 * DH, 2 * DH)
        away.append(
            pltpu.make_async_copy(tokens_ref.at[pair], out_ref.at[:, :, columns], leave.at[pair])
        )
        away[-1].start()
    for copy in away:
        copy.wait()


def unpack_whole(index, rows, tokens):
    heads, slots, width = rows.shape
    parts = width // DH
    return pl.pallas_call(
        unpack_whole_kernel,
        in_specs=[VMEM_SPEC] * 2,
        out_specs=pl.BlockSpec(memory_space=pl.ANY),
        out_shape=jax.ShapeDtypeStruct((parts, tokens, heads * DH), BF16),
        scratch_shapes=[
            pltpu.VMEM((heads // 2, parts, tokens, 2 * DH), BF16),
            pltpu.SemaphoreType.DMA((heads // 2,)),
        ],
        compiler_params=params(),
    )(index, rows)


def exchange(block, axis, bit):
    return lax.ppermute(block, axis, [(i, i ^ bit) for i in range(lax.axis_size(axis))])


def gather_blocks(block, axis, bits, held=None):
    held = {0: block} if held is None else dict(held)
    reached = [0]
    for bit in bits:
        for step in list(reached):
            if step ^ bit not in held:
                held[step ^ bit] = exchange(held[step], axis, bit)
            reached.append(step ^ bit)
    return [held[step] for step in range(lax.axis_size(axis))]


SMEM_SPEC = pl.BlockSpec(memory_space=pltpu.SMEM)
VMEM_SPEC = pl.BlockSpec(memory_space=pltpu.VMEM)


def grad_swap_kernel(count, place_ref, *refs):
    row_refs, weight_ref, out_ref, total = refs[:count], refs[count], refs[count + 1], refs[count + 2]
    mine = place_ref[1]
    seq_count, height, _ = out_ref.shape
    slots, depth = row_refs[0].shape
    piece = slots // count
    chunks = (height - slots) // piece
    per_block = depth // (chunks * DH)
    for step in range(count):

        @pl.when(pl.program_id(0) == step)
        def _(step=step):
            part = dot(row_refs[step][...], weight_ref[...])
            total[...] = part if step == 0 else total[...] + part
            share = row_refs[step][pl.ds(pl.multiple_of(mine * piece, piece), piece), :]
            for chunk in range(per_block * chunks):
                partner = (mine ^ step) * per_block + chunk // chunks
                start = slots + chunk % chunks * piece
                out_ref[partner, start : start + piece, :] = share[:, chunk * DH : (chunk + 1) * DH]

    @pl.when(pl.program_id(0) == count - 1)
    def _():
        for head in range(seq_count):
            out_ref[head, :slots, :] = total[:, head * DH : (head + 1) * DH].astype(BF16)


def grad_swap(place, blocks, weight, seq_count):
    count = len(blocks)
    slots, depth = blocks[0].shape
    columns = weight.shape[1]
    height = slots + slots // count * (count * depth // seq_count // DH)
    return pl.pallas_call(
        functools.partial(grad_swap_kernel, count),
        grid_spec=pltpu.PrefetchScalarGridSpec(
            num_scalar_prefetch=1,
            grid=(count,),
            in_specs=[pl.BlockSpec((slots, depth), lambda i, place: (0, 0))] * count
            + [pl.BlockSpec((depth, columns), lambda i, place: (place[1] ^ i, 0))],
            out_specs=pl.BlockSpec((seq_count, height, DH), lambda i, place: (0, 0, 0)),
            scratch_shapes=[pltpu.VMEM((slots, columns), F32)],
        ),
        out_shape=jax.ShapeDtypeStruct((seq_count, height, DH), BF16),
        compiler_params=params(),
        cost_estimate=pl.CostEstimate(
            flops=2 * slots * count * depth * columns,
            bytes_accessed=2 * count * depth * columns,
            transcendentals=0,
        ),
    )(place, *blocks, weight)


def flip_rows_kernel(place_ref, *refs):
    piece_refs, out_ref, rows = refs[:-2], refs[-2], refs[-1]
    count = len(piece_refs)
    chunks = rows.shape[1] // DH
    shards, height, _ = piece_refs[0].shape
    piece = height // chunks
    for part in range(count):
        for shard in range(shards):
            start = shard * piece * count + (place_ref[1] ^ part) * piece
            here = pl.ds(pl.multiple_of(start, piece), piece)
            for chunk in range(chunks):
                rows[here, chunk * DH : (chunk + 1) * DH] = piece_refs[part][
                    shard, chunk * piece : (chunk + 1) * piece, :
                ]
    out_ref[...] = rows[...].T


def flip_rows(place, pieces, slots):
    shards, height, _ = pieces[0].shape
    width = height // (slots // len(pieces)) * DH
    keys = shards * slots
    return pl.pallas_call(
        flip_rows_kernel,
        in_specs=[SMEM_SPEC] + [pl.BlockSpec()] * len(pieces),
        out_specs=VMEM_SPEC,
        out_shape=jax.ShapeDtypeStruct((width, keys), BF16),
        scratch_shapes=[pltpu.VMEM((keys, width), BF16)],
        compiler_params=params(),
        cost_estimate=pl.CostEstimate(flops=0, bytes_accessed=4 * keys * width, transcendentals=0),
    )(place, *pieces)


def weight_part_kernel(first, count, place_ref, flip_ref, *refs):
    out_ref, product_ref, leave = refs[-3:]
    away = []
    for step in range(0, count, 2):
        both = jnp.concatenate([ref[...] for ref in refs[step : step + 2]], axis=1)
        product = dot(flip_ref[...], both)
        head = place_ref[0] ^ (first + step)
        for side in range(2):
            column = pl.multiple_of((head ^ side) % 2 * DH, DH)
            product_ref[step // 2, :, pl.ds(column, DH)] = product[:, side * DH : (side + 1) * DH]
        columns = pl.ds(pl.multiple_of(head // 2 * (2 * DH), 2 * DH), 2 * DH)
        away.append(
            pltpu.make_async_copy(
                product_ref.at[step // 2], out_ref.at[:, columns], leave.at[step // 2]
            )
        )
        away[-1].start()
    for copy in away:
        copy.wait()


def weight_part(place, flip, attended, first, heads, weight, before=None):
    count = len(attended)
    width, keys = flip.shape
    more = [] if before is None else [before]
    return pl.pallas_call(
        functools.partial(weight_part_kernel, first, count),
        in_specs=[SMEM_SPEC]
        + [VMEM_SPEC] * (1 + count)
        + [pl.BlockSpec(memory_space=pl.ANY)] * len(more),
        out_specs=pl.BlockSpec(memory_space=pl.ANY),
        out_shape=jax.ShapeDtypeStruct((width, heads * DH), F32),
        scratch_shapes=[
            pltpu.VMEM((count // 2, width, 2 * DH), F32),
            pltpu.SemaphoreType.DMA((count // 2,)),
        ],
        input_output_aliases={2 + count: 0} if more else {},
        compiler_params=params(),
        cost_estimate=pl.CostEstimate(
            flops=weight * 2 * keys * width * count * DH,
            bytes_accessed=8 * keys * DH * count,
            transcendentals=0,
        ),
    )(place, flip, *attended, *more)


def query_blocks(rows):
    starts = range(0, rows, QUERY_BLOCK)
    return [(start, start * (start + QUERY_BLOCK) // (2 * QUERY_BLOCK), start + QUERY_BLOCK) for start in starts]


def mark_live(count_ref, live_ref, slots):
    for shard in range(live_ref.shape[0] // slots):
        inside = lax.broadcasted_iota(jnp.int32, (slots, live_ref.shape[1]), 0)
        live_ref[shard * slots : (shard + 1) * slots] = jnp.where(
            inside < count_ref[shard], 0.0, -1e30
        )


def masked_scores(start, keys, key_ref, query, live_ref):
    scores = dot_cols(key_ref[:keys], query) * (1.0 / math.sqrt(DH)) + live_ref[:keys, :1]
    row = start + lax.broadcasted_iota(jnp.int32, (1, QUERY_BLOCK), 1)
    key_pos = start + lax.broadcasted_iota(jnp.int32, (QUERY_BLOCK, 1), 0)
    edge = jnp.where(key_pos <= row, scores[start:], -1e30)
    return jnp.concatenate([scores[:start], edge], axis=0) if start else edge


def split_blocks(block_ref, *refs):
    shards, slots, _ = block_ref.shape
    for shard in range(shards):
        for which, ref in enumerate(refs):
            ref[shard * slots : (shard + 1) * slots] = block_ref[
                shard, :, which * DH : (which + 1) * DH
            ]


def forward_kernel(
    count_ref, block_ref, attended_ref, stat_ref, live_ref, query_ref, key_ref, value_ref
):
    mark_live(count_ref, live_ref, block_ref.shape[1])
    split_blocks(block_ref, query_ref, key_ref, value_ref)
    value_flip = value_ref[...].T
    for start in range(0, query_ref.shape[0], QUERY_BLOCK):
        rows = slice(start, start + QUERY_BLOCK)
        keys = start + QUERY_BLOCK
        scores = masked_scores(start, keys, key_ref, query_ref[rows], live_ref)
        peak = jnp.max(scores, axis=0, keepdims=True)
        weights = jnp.exp(scores - peak)
        inverse = 1.0 / jnp.sum(weights, axis=0, keepdims=True)
        attended = dot(value_flip[:, :keys], (weights * inverse).astype(BF16))
        attended_ref[rows] = attended.T.astype(BF16)
        stat_ref[0:1, rows] = peak
        stat_ref[1:2, rows] = inverse


def attention_cost(keys, dots):
    return pl.CostEstimate(
        flops=dots * keys * keys * DH, bytes_accessed=16 * keys * DH, transcendentals=keys * keys // 2
    )


def forward(counts, blocks):
    keys = blocks.shape[0] * blocks.shape[1]
    return pl.pallas_call(
        forward_kernel,
        out_shape=[
            jax.ShapeDtypeStruct((keys, DH), BF16),
            jax.ShapeDtypeStruct((8, keys), F32),
        ],
        in_specs=[SMEM_SPEC, pl.BlockSpec()],
        scratch_shapes=[pltpu.VMEM((keys, DH), F32)] + [pltpu.VMEM((keys, DH), BF16)] * 3,
        compiler_params=params(),
        cost_estimate=attention_cost(keys, 2),
    )(counts, blocks)


def weights_kernel(count_ref, block_ref, stat_ref, out_ref, live_ref, query_ref, key_ref):
    mark_live(count_ref, live_ref, block_ref.shape[1])
    split_blocks(block_ref, query_ref, key_ref)
    for start, first, keys in query_blocks(query_ref.shape[0]):
        rows = slice(start, start + QUERY_BLOCK)
        scores = masked_scores(start, keys, key_ref, query_ref[rows], live_ref)
        probs = jnp.exp(scores - stat_ref[0:1, rows]) * stat_ref[1:2, rows]
        out_ref[first : first + keys] = probs.astype(BF16)


def weights(counts, blocks, stats):
    keys = blocks.shape[0] * blocks.shape[1]
    _, first, last = query_blocks(keys)[-1]
    return pl.pallas_call(
        weights_kernel,
        in_specs=[SMEM_SPEC] + [pl.BlockSpec()] * 2,
        out_shape=jax.ShapeDtypeStruct((first + last, QUERY_BLOCK), BF16),
        scratch_shapes=[pltpu.VMEM((keys, DH), F32)] + [pltpu.VMEM((keys, DH), BF16)] * 2,
        compiler_params=params(VMEM_MOST),
        cost_estimate=attention_cost(keys, 1),
    )(counts, blocks, stats)


def backward_kernel(
    block_ref,
    attended_ref,
    grads_ref,
    weights_ref,
    out_ref,
    query_ref,
    key_ref,
    value_ref,
    grad_ref,
    query_total,
    key_total,
    value_total,
    probs_ref,
    arrive,
):
    seq_count, slots, _ = out_ref.shape
    scale = 1.0 / math.sqrt(DH)
    steps = query_blocks(query_ref.shape[0])
    copies = [
        pltpu.make_async_copy(
            weights_ref.at[first : first + keys], probs_ref.at[first : first + keys], arrive.at[n]
        )
        for n, (_, first, keys) in enumerate(steps)
    ]
    for copy in copies:
        copy.start()
    split_blocks(block_ref, query_ref, key_ref, value_ref)
    for shard in range(seq_count):
        grad_ref[shard * slots : (shard + 1) * slots] = grads_ref[shard, :slots]
    key_flip = key_ref[...].T
    for copy, (start, first, keys) in zip(copies, steps):
        rows = slice(start, start + QUERY_BLOCK)
        grad = grad_ref[rows]
        product = grad.astype(F32) * attended_ref[rows].astype(F32)
        row_dot = jnp.sum(product.T, axis=0, keepdims=True)
        grad_probs = dot_cols(value_ref[:keys], grad)
        copy.wait()
        probs = probs_ref[first : first + keys]
        grad_scores = (probs.astype(F32) * (grad_probs - row_dot)).astype(BF16)
        query_total[rows] = (dot(key_flip[:, :keys], grad_scores) * scale).T.astype(BF16)
        key_part = dot(grad_scores, query_ref[rows])
        value_part = dot(probs, grad)
        if start:
            key_total[:start] += key_part[:start]
            value_total[:start] += value_part[:start]
        key_total[rows] = key_part[start:]
        value_total[rows] = value_part[start:]
    for shard in range(seq_count):
        here = slice(shard * slots, (shard + 1) * slots)
        out_ref[shard, :, :DH] = query_total[here]
        out_ref[shard, :, DH : 2 * DH] = (key_total[here] * scale).astype(BF16)
        out_ref[shard, :, 2 * DH :] = value_total[here].astype(BF16)


def backward(blocks, attended, grads, probs):
    keys = attended.shape[0]
    return pl.pallas_call(
        backward_kernel,
        in_specs=[pl.BlockSpec()] * 3 + [pl.BlockSpec(memory_space=pl.ANY)],
        out_shape=jax.ShapeDtypeStruct(blocks.shape, BF16),
        scratch_shapes=[pltpu.VMEM((keys, DH), BF16)] * 5
        + [pltpu.VMEM((keys, DH), F32)] * 2
        + [pltpu.VMEM(probs.shape, BF16), pltpu.SemaphoreType.DMA((keys // QUERY_BLOCK,))],
        compiler_params=params(VMEM_MOST),
        cost_estimate=attention_cost(keys, 4),
    )(blocks, attended, grads, probs)


def on_device_whole_heads(
    projections,
    output_gradient,
    output_projection_weight,
    kept_token_indices,
    surviving_token_count,
):
    tok_dev = projections.shape[0]
    slots = kept_token_indices.shape[1]
    seq_count = lax.axis_size("seq")
    head_count = lax.axis_size("head")
    index = kept_token_indices
    place = jnp.stack([lax.axis_index("seq"), lax.axis_index("head")]).astype(jnp.int32)
    seq_bits = [1 << bit for bit in reversed(range(seq_count.bit_length() - 1))]
    head_bits = [1 << bit for bit in reversed(range(head_count.bit_length() - 1))]

    def swap(blocks):
        return lax.all_to_all(blocks, "seq", split_axis=0, concat_axis=0, tiled=True)

    packed = pack_whole(index, projections.transpose(1, 0, 2))
    packed, grad_index = lax.optimization_barrier((packed, index))
    arrived = swap(packed)
    grad_blocks = gather_blocks(pack_grad(grad_index, output_gradient), "head", head_bits)
    grads = swap(grad_swap(place, grad_blocks, output_projection_weight, seq_count))
    attended, stats = forward(surviving_token_count, arrived)

    near, last = seq_bits[-2], seq_bits[-1]
    held = {bit: exchange(attended, "seq", bit) for bit in seq_bits}
    probs = weights(surviving_token_count, arrived, stats)
    grads, held[near], probs = lax.optimization_barrier((grads, held[near], probs))
    held[near ^ last] = exchange(held[near], "seq", last)
    back = backward(arrived, attended, grads, probs)
    back, held = lax.optimization_barrier((back, held))
    gathered = gather_blocks(attended, "seq", seq_bits, {0: attended, **held})
    home = swap(back)
    pieces = gather_blocks(grads[:, slots:], "head", head_bits)
    flip = flip_rows(place, pieces, slots)
    late = seq_count - 2
    weight_grad = weight_part(place, flip, gathered[:late], 0, seq_count, 1)
    projection_grad = unpack_whole(index, home, tok_dev)
    weight_grad = weight_part(place, flip, gathered[late:], late, seq_count, 28, weight_grad)
    projection_grad = projection_grad.transpose(1, 0, 2)
    return (projection_grad, weight_grad)


def on_device(projections, output_gradient, weight, index, counts):
    heads = projections.shape[2] // DH
    seq_count, head_count = lax.axis_size("seq"), lax.axis_size("head")
    width = output_gradient.shape[1] * head_count // seq_count
    whole = seq_count == heads and seq_count % 2 == 0 and width % DH == 0
    powers = seq_count & (seq_count - 1) == 0 and head_count & (head_count - 1) == 0
    body = on_device_whole_heads if whole and powers else on_device_split_heads
    return body(projections, output_gradient, weight, index, counts)


def solution(mesh):
    return jax.shard_map(
        on_device,
        mesh=mesh,
        in_specs=(P("seq", None, "head"), P("seq", "head"), P(None, "head"), P("seq", None), P()),
        out_specs=(P("seq", None, "head"), P("seq", "head")),
        check_vma=False,
    )
```

```python
import functools
import math

import jax
import jax.numpy as jnp
from jax import lax
from jax.experimental import pallas as pl
from jax.experimental.pallas import tpu as pltpu
from jax.sharding import PartitionSpec as P

DH = 128
QUERY_BLOCK = 256
VMEM_BYTES = 20 * 1024 * 1024
VMEM_MOST = 62 * 1024 * 1024
F32 = jnp.float32
BF16 = jnp.bfloat16


def params(limit=VMEM_BYTES):
    return pltpu.CompilerParams(vmem_limit_bytes=limit)


def dot(left, right):
    return jnp.dot(left, right, preferred_element_type=F32)


def dot_rows(left, right):
    return lax.dot_general(left, right, (((0,), (0,)), ((), ())), preferred_element_type=F32)


def dot_cols(left, right):
    return lax.dot_general(left, right, (((1,), (1,)), ((), ())), preferred_element_type=F32)


def token_selector(index_ref, tokens):
    slots = index_ref.shape[1]
    token = lax.broadcasted_iota(jnp.int32, (tokens, slots), 0)
    return jnp.where(token == index_ref[...], 1.0, 0.0).astype(BF16)


def pack_grad_kernel(index_ref, grad_ref, out_ref):
    selector = token_selector(index_ref, grad_ref.shape[0])
    out_ref[...] = dot_rows(selector, grad_ref[...]).astype(BF16)


def pack_grad(index, grad):
    slots = index.shape[1]
    return pl.pallas_call(
        pack_grad_kernel,
        out_shape=jax.ShapeDtypeStruct((slots, grad.shape[1]), BF16),
        compiler_params=params(),
    )(index, grad)


def pack_heads_kernel(index_ref, proj_ref, out_ref):
    selector = token_selector(index_ref, proj_ref.shape[1])
    for which in range(3):
        rows = dot_rows(selector, proj_ref[which]).astype(BF16)
        for head in range(out_ref.shape[0]):
            out_ref[head, :, which * DH : (which + 1) * DH] = rows[:, head * DH : (head + 1) * DH]


def pack_heads(index, proj):
    slots = index.shape[1]
    _, tokens, width = proj.shape
    heads = width // DH
    step = 2
    return pl.pallas_call(
        pack_heads_kernel,
        grid=(heads // step,),
        in_specs=[
            pl.BlockSpec((1, slots), lambda i: (0, 0)),
            pl.BlockSpec((3, tokens, step * DH), lambda i: (0, 0, i)),
        ],
        out_specs=pl.BlockSpec((step, slots, 3 * DH), lambda i: (i, 0, 0)),
        out_shape=jax.ShapeDtypeStruct((heads, slots, 3 * DH), BF16),
        compiler_params=params(),
    )(index, proj)


def unpack_heads_kernel(index_ref, rows_ref, out_ref):
    selector = token_selector(index_ref, out_ref.shape[1])
    for head in range(rows_ref.shape[0]):
        tokens = dot(selector, rows_ref[head]).astype(BF16)
        for which in range(3):
            out_ref[which, :, head * DH : (head + 1) * DH] = tokens[
                :, which * DH : (which + 1) * DH
            ]


def unpack_heads(index, rows, tokens):
    heads, slots, _ = rows.shape
    step = 2
    return pl.pallas_call(
        unpack_heads_kernel,
        grid=(heads // step,),
        in_specs=[
            pl.BlockSpec((1, slots), lambda i: (0, 0)),
            pl.BlockSpec((step, slots, 3 * DH), lambda i: (i, 0, 0)),
        ],
        out_specs=pl.BlockSpec((3, tokens, step * DH), lambda i: (0, 0, i)),
        out_shape=jax.ShapeDtypeStruct((3, tokens, heads * DH), BF16),
        compiler_params=params(),
    )(index, rows)


def grad_attn_kernel(rows_ref, weight_ref, out_ref):
    product = dot(rows_ref[...], weight_ref[...]).astype(BF16)
    for head in range(out_ref.shape[0]):
        out_ref[head] = product[:, head * DH : (head + 1) * DH]


def grad_attn_heads(rows, weight):
    slots, depth = rows.shape
    heads = weight.shape[1] // DH
    step = 2
    return pl.pallas_call(
        grad_attn_kernel,
        grid=(heads // step,),
        in_specs=[
            pl.BlockSpec((slots, depth), lambda i: (0, 0)),
            pl.BlockSpec((depth, step * DH), lambda i: (0, i)),
        ],
        out_specs=pl.BlockSpec((step, slots, DH), lambda i: (i, 0, 0)),
        out_shape=jax.ShapeDtypeStruct((heads, slots, DH), BF16),
        compiler_params=params(),
    )(rows, weight)


def weight_grad_kernel(rows_ref, attended_ref, out_ref):
    attended = jnp.concatenate([attended_ref[head] for head in range(attended_ref.shape[0])], axis=1)
    out_ref[...] = dot_rows(rows_ref[...], attended)


def weight_grad_heads(rows, attended):
    total, width = rows.shape
    heads = attended.shape[0]
    step = 2
    return pl.pallas_call(
        weight_grad_kernel,
        grid=(heads // step,),
        in_specs=[
            pl.BlockSpec((total, width), lambda i: (0, 0)),
            pl.BlockSpec((step, total, DH), lambda i: (i, 0, 0)),
        ],
        out_specs=pl.BlockSpec((width, step * DH), lambda i: (0, i)),
        out_shape=jax.ShapeDtypeStruct((width, heads * DH), F32),
        compiler_params=params(),
    )(rows, attended)


def attention_kernel(
    slots,
    part_rows,
    part_ref,
    live_ref,
    query_ref,
    grad_ref,
    key_ref,
    value_ref,
    attended_ref,
    query_grad_ref,
    key_grad_ref,
    value_grad_ref,
    key_total,
    value_total,
):
    scale = 1.0 / math.sqrt(DH)
    rows_total = query_ref.shape[0]
    keys_total = key_ref.shape[0]
    quarters = slots // part_rows
    key_flip = key_ref[...].T
    value_flip = value_ref[...].T
    for start in range(0, rows_total, QUERY_BLOCK):
        rows = slice(start, start + QUERY_BLOCK)
        last = start + QUERY_BLOCK - 1
        last_pos = last // part_rows * slots + (quarters - 1) * part_rows + last % part_rows
        first_pos = start // part_rows * slots + start % part_rows
        keys = min(-(-(last_pos + 1) // 128) * 128, keys_total)
        clear = first_pos // 128 * 128
        query = query_ref[rows]
        grad = grad_ref[rows]
        row = start + lax.broadcasted_iota(jnp.int32, (1, QUERY_BLOCK), 1)
        if quarters > 1:
            shard = row // part_rows
            row = shard * slots + part_ref[0] * part_rows + row - shard * part_rows
        scores = dot_cols(key_ref[:keys], query) * scale + live_ref[:keys, :1]
        key_pos = clear + lax.broadcasted_iota(jnp.int32, (keys - clear, 1), 0)
        edge = jnp.where(key_pos <= row, scores[clear:], -1e30)
        scores = jnp.concatenate([scores[:clear], edge], axis=0) if clear else edge
        peak = jnp.max(scores, axis=0, keepdims=True)
        weights = jnp.exp(scores - peak)
        probs = weights * (1.0 / jnp.sum(weights, axis=0, keepdims=True))
        probs_low = probs.astype(BF16)
        attended = dot(value_flip[:, :keys], probs_low)
        attended_ref[rows] = attended.T.astype(BF16)
        row_dot = jnp.sum(grad.T.astype(F32) * attended, axis=0, keepdims=True)
        grad_probs = dot_cols(value_ref[:keys], grad)
        grad_scores = (probs * (grad_probs - row_dot)).astype(BF16)
        query_grad = dot(key_flip[:, :keys], grad_scores) * scale
        query_grad_ref[rows] = query_grad.T.astype(BF16)
        key_part = dot(grad_scores, query)
        value_part = dot(probs_low, grad)
        prev = start - 1
        reached = 0
        if start:
            prev_pos = prev // part_rows * slots + (quarters - 1) * part_rows + prev % part_rows
            reached = min(-(-(prev_pos + 1) // 128) * 128, keys_total)
        if reached:
            key_total[:reached] += key_part[:reached]
            value_total[:reached] += value_part[:reached]
        if keys > reached:
            key_total[reached:keys] = key_part[reached:]
            value_total[reached:keys] = value_part[reached:]
    key_grad_ref[...] = (key_total[...] * scale).astype(key_grad_ref.dtype)
    value_grad_ref[...] = value_total[...].astype(value_grad_ref.dtype)


def attention(part, live, query, grad, key, value, slots, part_rows, key_type):
    rows, keys = query.shape[0], key.shape[0]
    vmem = pl.BlockSpec(memory_space=pltpu.VMEM)
    return pl.pallas_call(
        functools.partial(attention_kernel, slots, part_rows),
        in_specs=[pl.BlockSpec(memory_space=pltpu.SMEM)] + [vmem] * 5,
        out_specs=[vmem] * 4,
        out_shape=[
            jax.ShapeDtypeStruct((rows, DH), BF16),
            jax.ShapeDtypeStruct((rows, DH), BF16),
            jax.ShapeDtypeStruct((keys, DH), key_type),
            jax.ShapeDtypeStruct((keys, DH), key_type),
        ],
        scratch_shapes=[pltpu.VMEM((keys, DH), F32)] * 2,
        compiler_params=params(),
    )(part, live, query, grad, key, value)


def on_device_split_heads(
    projections,
    output_gradient,
    output_projection_weight,
    kept_token_indices,
    surviving_token_count,
):
    tok_dev = projections.shape[0]
    group_width = projections.shape[2]
    slots = kept_token_indices.shape[1]
    heads = group_width // DH
    seq_count = lax.axis_size("seq")
    head_count = lax.axis_size("head")
    quarters = seq_count // heads
    part_rows = slots // quarters
    part = (lax.axis_index("seq") % quarters).astype(jnp.int32).reshape(1)
    index = kept_token_indices
    keys = seq_count * slots

    grad_local = pack_grad(index, output_gradient)
    grad_rows = lax.all_gather(grad_local, "head", axis=1, tiled=True)
    packed = pack_heads(index, projections.transpose(1, 0, 2))

    position = jnp.arange(slots, dtype=jnp.int32)
    live = position[None, :] < surviving_token_count[:, None]
    live = jnp.where(live, 0.0, -1e30).astype(F32).reshape(keys, 1)
    live = jnp.broadcast_to(live, (keys, DH))

    def swap(blocks):
        return lax.all_to_all(blocks, "seq", split_axis=0, concat_axis=0, tiled=True)

    if quarters == 1:
        arrived = swap(packed).reshape(keys, 3 * DH)
        query, key, value = (arrived[:, n * DH : (n + 1) * DH] for n in range(3))
    else:
        query = swap(packed[:, :, :DH].reshape(seq_count, part_rows, DH))
        query = query.reshape(seq_count * part_rows, DH)
        sides = jnp.broadcast_to(packed[:, None, :, DH:], (heads, quarters, slots, 2 * DH))
        sides = swap(sides.reshape(seq_count, slots, 2 * DH)).reshape(keys, 2 * DH)
        key, value = sides[:, :DH], sides[:, DH:]

    grad_heads = grad_attn_heads(grad_rows, output_projection_weight)
    grad_in = swap(grad_heads.reshape(seq_count, part_rows, DH)).reshape(-1, DH)

    width = grad_rows.shape[1] // seq_count
    piece = slots // head_count
    mine = lax.dynamic_slice_in_dim(grad_rows, lax.axis_index("head") * piece, piece, 0)
    mine = swap(mine.reshape(piece, seq_count, width).transpose(1, 0, 2))
    all_rows = lax.all_gather(mine, "head", axis=1, tiled=True)

    key_type = BF16 if quarters == 1 else F32
    attended, query_grad, key_grad, value_grad = attention(
        part, live, query, grad_in, key, value, slots, part_rows, key_type
    )

    gathered = lax.all_gather(attended, "seq", axis=0).reshape(heads, keys, DH)
    all_rows = all_rows.reshape(seq_count, quarters, part_rows, width).transpose(1, 0, 2, 3)
    weight_grad = weight_grad_heads(all_rows.reshape(keys, width), gathered)

    if quarters == 1:
        back = jnp.concatenate([query_grad, key_grad, value_grad], axis=1)
        home = swap(back.reshape(seq_count, slots, 3 * DH))
    else:
        query_home = swap(query_grad.reshape(seq_count, part_rows, DH)).reshape(heads, slots, DH)
        back = jnp.concatenate([key_grad, value_grad], axis=1)
        key_home = swap(back.reshape(seq_count, slots, 2 * DH))
        key_home = jnp.sum(key_home.reshape(heads, quarters, slots, 2 * DH), axis=1)
        home = jnp.concatenate([query_home, key_home.astype(BF16)], axis=2)
    projection_grad = unpack_heads(index, home, tok_dev).transpose(1, 0, 2)
    return (projection_grad, weight_grad)


def pack_whole_kernel(index_ref, proj_ref, out_ref, loaded, packed, arrive, leave):
    parts, _, width = proj_ref.shape
    heads = out_ref.shape[0] // 2
    pieces = [(which, half) for which in range(parts) for half in range(2)]

    def columns(half):
        return slice(half * width // 2, (half + 1) * width // 2)

    copies = [
        pltpu.make_async_copy(
            proj_ref.at[which, :, columns(half)],
            loaded.at[which, :, columns(half)],
            arrive.at[2 * which + half],
        )
        for which, half in pieces
    ]
    for copy in copies:
        copy.start()
    token = lax.broadcasted_iota(jnp.int32, (loaded.shape[1], index_ref.shape[1]), 0)
    selector = jnp.where(token == index_ref[...], 1.0, 0.0).T.astype(BF16)
    away = []
    for copy, (which, half) in zip(copies, pieces):
        copy.wait()
        rows = dot(selector, loaded[which, :, columns(half)]).astype(BF16)
        mine = slice(half * heads, (half + 1) * heads)
        for head in range(heads):
            packed[which, half * heads + head] = rows[:, head * DH : (head + 1) * DH]
        away.append(
            pltpu.make_async_copy(
                packed.at[which, mine],
                out_ref.at[mine, :, which * DH : (which + 1) * DH],
                leave.at[2 * which + half],
            )
        )
        away[-1].start()
    for copy in away:
        copy.wait()


def pack_whole(index, proj):
    slots = index.shape[1]
    parts, tokens, width = proj.shape
    heads = width // DH
    return pl.pallas_call(
        pack_whole_kernel,
        in_specs=[pl.BlockSpec(), pl.BlockSpec(memory_space=pltpu.HBM)],
        out_specs=pl.BlockSpec(memory_space=pltpu.HBM),
        out_shape=jax.ShapeDtypeStruct((heads, slots, parts * DH), BF16),
        scratch_shapes=[
            pltpu.VMEM(proj.shape, BF16),
            pltpu.VMEM((parts, heads, slots, DH), BF16),
            pltpu.SemaphoreType.DMA((2 * parts,)),
            pltpu.SemaphoreType.DMA((2 * parts,)),
        ],
        compiler_params=params(VMEM_MOST),
        cost_estimate=pl.CostEstimate(
            flops=2 * slots * tokens * parts * width,
            bytes_accessed=8 * tokens * width,
            transcendentals=0,
        ),
    )(index, proj)


def unpack_whole_kernel(index_ref, rows_ref, out_ref, tokens_ref, leave):
    selector = token_selector(index_ref, out_ref.shape[1])
    away = []
    for pair in range(rows_ref.shape[0] // 2):
        for side in range(2):
            tokens = dot(selector, rows_ref[2 * pair + side]).astype(BF16)
            for which in range(out_ref.shape[0]):
                tokens_ref[pair, which, :, side * DH : (side + 1) * DH] = tokens[
                    :, which * DH : (which + 1) * DH
                ]
        columns = pl.ds(pair * 2 * DH, 2 * DH)
        away.append(
            pltpu.make_async_copy(tokens_ref.at[pair], out_ref.at[:, :, columns], leave.at[pair])
        )
        away[-1].start()
    for copy in away:
        copy.wait()


def unpack_whole(index, rows, tokens):
    heads, slots, width = rows.shape
    parts = width // DH
    return pl.pallas_call(
        unpack_whole_kernel,
        in_specs=[VMEM_SPEC] * 2,
        out_specs=pl.BlockSpec(memory_space=pl.ANY),
        out_shape=jax.ShapeDtypeStruct((parts, tokens, heads * DH), BF16),
        scratch_shapes=[
            pltpu.VMEM((heads // 2, parts, tokens, 2 * DH), BF16),
            pltpu.SemaphoreType.DMA((heads // 2,)),
        ],
        compiler_params=params(),
    )(index, rows)


def exchange(block, axis, bit):
    return lax.ppermute(block, axis, [(i, i ^ bit) for i in range(lax.axis_size(axis))])


def gather_blocks(block, axis, bits, held=None):
    held = {0: block} if held is None else dict(held)
    reached = [0]
    for bit in bits:
        for step in list(reached):
            if step ^ bit not in held:
                held[step ^ bit] = exchange(held[step], axis, bit)
            reached.append(step ^ bit)
    return [held[step] for step in range(lax.axis_size(axis))]


SMEM_SPEC = pl.BlockSpec(memory_space=pltpu.SMEM)
VMEM_SPEC = pl.BlockSpec(memory_space=pltpu.VMEM)


def grad_swap_kernel(count, place_ref, *refs):
    row_refs, weight_ref, out_ref, total = refs[:count], refs[count], refs[count + 1], refs[count + 2]
    mine = place_ref[1]
    seq_count, height, _ = out_ref.shape
    slots, depth = row_refs[0].shape
    piece = slots // count
    chunks = (height - slots) // piece
    per_block = depth // (chunks * DH)
    for step in range(count):

        @pl.when(pl.program_id(0) == step)
        def _(step=step):
            part = dot(row_refs[step][...], weight_ref[...])
            total[...] = part if step == 0 else total[...] + part
            share = row_refs[step][pl.ds(pl.multiple_of(mine * piece, piece), piece), :]
            for chunk in range(per_block * chunks):
                partner = (mine ^ step) * per_block + chunk // chunks
                start = slots + chunk % chunks * piece
                out_ref[partner, start : start + piece, :] = share[:, chunk * DH : (chunk + 1) * DH]

    @pl.when(pl.program_id(0) == count - 1)
    def _():
        for head in range(seq_count):
            out_ref[head, :slots, :] = total[:, head * DH : (head + 1) * DH].astype(BF16)


def grad_swap(place, blocks, weight, seq_count):
    count = len(blocks)
    slots, depth = blocks[0].shape
    columns = weight.shape[1]
    height = slots + slots // count * (count * depth // seq_count // DH)
    return pl.pallas_call(
        functools.partial(grad_swap_kernel, count),
        grid_spec=pltpu.PrefetchScalarGridSpec(
            num_scalar_prefetch=1,
            grid=(count,),
            in_specs=[pl.BlockSpec((slots, depth), lambda i, place: (0, 0))] * count
            + [pl.BlockSpec((depth, columns), lambda i, place: (place[1] ^ i, 0))],
            out_specs=pl.BlockSpec((seq_count, height, DH), lambda i, place: (0, 0, 0)),
            scratch_shapes=[pltpu.VMEM((slots, columns), F32)],
        ),
        out_shape=jax.ShapeDtypeStruct((seq_count, height, DH), BF16),
        compiler_params=params(),
        cost_estimate=pl.CostEstimate(
            flops=2 * slots * count * depth * columns,
            bytes_accessed=2 * count * depth * columns,
            transcendentals=0,
        ),
    )(place, *blocks, weight)


def flip_rows_kernel(place_ref, *refs):
    piece_refs, out_ref, rows = refs[:-2], refs[-2], refs[-1]
    count = len(piece_refs)
    chunks = rows.shape[1] // DH
    shards, height, _ = piece_refs[0].shape
    piece = height // chunks
    for part in range(count):
        for shard in range(shards):
            start = shard * piece * count + (place_ref[1] ^ part) * piece
            here = pl.ds(pl.multiple_of(start, piece), piece)
            for chunk in range(chunks):
                rows[here, chunk * DH : (chunk + 1) * DH] = piece_refs[part][
                    shard, chunk * piece : (chunk + 1) * piece, :
                ]
    out_ref[...] = rows[...].T


def flip_rows(place, pieces, slots):
    shards, height, _ = pieces[0].shape
    width = height // (slots // len(pieces)) * DH
    keys = shards * slots
    return pl.pallas_call(
        flip_rows_kernel,
        in_specs=[SMEM_SPEC] + [pl.BlockSpec()] * len(pieces),
        out_specs=VMEM_SPEC,
        out_shape=jax.ShapeDtypeStruct((width, keys), BF16),
        scratch_shapes=[pltpu.VMEM((keys, width), BF16)],
        compiler_params=params(),
        cost_estimate=pl.CostEstimate(flops=0, bytes_accessed=4 * keys * width, transcendentals=0),
    )(place, *pieces)


def weight_part_kernel(first, count, place_ref, flip_ref, *refs):
    out_ref, product_ref, leave = refs[-3:]
    away = []
    for step in range(0, count, 2):
        both = jnp.concatenate([ref[...] for ref in refs[step : step + 2]], axis=1)
        product = dot(flip_ref[...], both)
        head = place_ref[0] ^ (first + step)
        for side in range(2):
            column = pl.multiple_of((head ^ side) % 2 * DH, DH)
            product_ref[step // 2, :, pl.ds(column, DH)] = product[:, side * DH : (side + 1) * DH]
        columns = pl.ds(pl.multiple_of(head // 2 * (2 * DH), 2 * DH), 2 * DH)
        away.append(
            pltpu.make_async_copy(
                product_ref.at[step // 2], out_ref.at[:, columns], leave.at[step // 2]
            )
        )
        away[-1].start()
    for copy in away:
        copy.wait()


def weight_part(place, flip, attended, first, heads, weight, before=None):
    count = len(attended)
    width, keys = flip.shape
    more = [] if before is None else [before]
    return pl.pallas_call(
        functools.partial(weight_part_kernel, first, count),
        in_specs=[SMEM_SPEC]
        + [VMEM_SPEC] * (1 + count)
        + [pl.BlockSpec(memory_space=pl.ANY)] * len(more),
        out_specs=pl.BlockSpec(memory_space=pl.ANY),
        out_shape=jax.ShapeDtypeStruct((width, heads * DH), F32),
        scratch_shapes=[
            pltpu.VMEM((count // 2, width, 2 * DH), F32),
            pltpu.SemaphoreType.DMA((count // 2,)),
        ],
        input_output_aliases={2 + count: 0} if more else {},
        compiler_params=params(),
        cost_estimate=pl.CostEstimate(
            flops=weight * 2 * keys * width * count * DH,
            bytes_accessed=8 * keys * DH * count,
            transcendentals=0,
        ),
    )(place, flip, *attended, *more)


def mark_live(count_ref, live_ref, slots):
    for shard in range(live_ref.shape[0] // slots):
        inside = lax.broadcasted_iota(jnp.int32, (slots, live_ref.shape[1]), 0)
        live_ref[shard * slots : (shard + 1) * slots] = jnp.where(
            inside < count_ref[shard], 0.0, -1e30
        )


def masked_scores(start, keys, key_ref, query, live_ref):
    scores = dot_cols(key_ref[:keys], query) * (1.0 / math.sqrt(DH)) + live_ref[:keys, :1]
    row = start + lax.broadcasted_iota(jnp.int32, (1, QUERY_BLOCK), 1)
    key_pos = start + lax.broadcasted_iota(jnp.int32, (QUERY_BLOCK, 1), 0)
    edge = jnp.where(key_pos <= row, scores[start:], -1e30)
    return jnp.concatenate([scores[:start], edge], axis=0) if start else edge


def split_blocks(block_ref, *refs):
    shards, slots, _ = block_ref.shape
    for shard in range(shards):
        for which, ref in enumerate(refs):
            ref[shard * slots : (shard + 1) * slots] = block_ref[
                shard, :, which * DH : (which + 1) * DH
            ]


def forward_kernel(
    count_ref, block_ref, attended_ref, stat_ref, live_ref, query_ref, key_ref, value_ref
):
    mark_live(count_ref, live_ref, block_ref.shape[1])
    split_blocks(block_ref, query_ref, key_ref, value_ref)
    value_flip = value_ref[...].T
    for start in range(0, query_ref.shape[0], QUERY_BLOCK):
        rows = slice(start, start + QUERY_BLOCK)
        keys = start + QUERY_BLOCK
        scores = masked_scores(start, keys, key_ref, query_ref[rows], live_ref)
        peak = jnp.max(scores, axis=0, keepdims=True)
        weights = jnp.exp(scores - peak)
        inverse = 1.0 / jnp.sum(weights, axis=0, keepdims=True)
        attended = dot(value_flip[:, :keys], (weights * inverse).astype(BF16))
        attended_ref[rows] = attended.T.astype(BF16)
        stat_ref[0:1, rows] = peak
        stat_ref[1:2, rows] = inverse


def attention_cost(keys, dots):
    return pl.CostEstimate(
        flops=dots * keys * keys * DH, bytes_accessed=16 * keys * DH, transcendentals=keys * keys // 2
    )


def forward(counts, blocks):
    keys = blocks.shape[0] * blocks.shape[1]
    return pl.pallas_call(
        forward_kernel,
        out_shape=[
            jax.ShapeDtypeStruct((keys, DH), BF16),
            jax.ShapeDtypeStruct((8, keys), F32),
        ],
        in_specs=[SMEM_SPEC, pl.BlockSpec()],
        scratch_shapes=[pltpu.VMEM((keys, DH), F32)] + [pltpu.VMEM((keys, DH), BF16)] * 3,
        compiler_params=params(),
        cost_estimate=attention_cost(keys, 2),
    )(counts, blocks)


def backward_kernel(
    count_ref,
    block_ref,
    attended_ref,
    stat_ref,
    grads_ref,
    out_ref,
    live_ref,
    query_ref,
    key_ref,
    value_ref,
    grad_ref,
    output_ref,
    stats,
    staged,
    key_total,
    value_total,
    arrive,
    leave,
):
    seq_count, slots, _ = staged.shape
    scale = 1.0 / math.sqrt(DH)

    def load(source, target, place):
        copy = pltpu.make_async_copy(source, target, arrive.at[place])
        copy.start()
        return copy

    def load_shards(sources, target, place):
        return [
            load(source, target.at[shard * slots : (shard + 1) * slots], place + shard)
            for shard, source in enumerate(sources)
        ]

    def part(which):
        return [
            block_ref.at[shard, :, which * DH : (which + 1) * DH] for shard in range(seq_count)
        ]

    first = load_shards(part(0), query_ref, 0) + load_shards(part(1), key_ref, seq_count)
    first.append(load(stat_ref, stats, 4 * seq_count))
    second = load_shards(part(2), value_ref, 2 * seq_count)
    rows_in = [grads_ref.at[shard, :slots] for shard in range(seq_count)]
    second += load_shards(rows_in, grad_ref, 3 * seq_count)
    second.append(load(attended_ref, output_ref, 4 * seq_count + 1))
    mark_live(count_ref, live_ref, slots)
    for copy in first:
        copy.wait()
    key_flip = key_ref[...].T
    away = []
    total_rows = query_ref.shape[0]
    for start in reversed(range(0, total_rows, QUERY_BLOCK)):
        rows = slice(start, start + QUERY_BLOCK)
        keys = start + QUERY_BLOCK
        query = query_ref[rows]
        scores = masked_scores(start, keys, key_ref, query, live_ref)
        probs = jnp.exp(scores - stats[0:1, rows]) * stats[1:2, rows]
        probs_low = probs.astype(BF16)
        if keys == total_rows:
            for copy in second:
                copy.wait()
        grad = grad_ref[rows]
        product = grad.astype(F32) * output_ref[rows].astype(F32)
        row_dot = jnp.sum(product.T, axis=0, keepdims=True)
        grad_probs = dot_cols(value_ref[:keys], grad)
        grad_scores = (probs * (grad_probs - row_dot)).astype(BF16)
        query_part = (dot(key_flip[:, :keys], grad_scores) * scale).T.astype(BF16)
        key_part = dot(grad_scores, query)
        value_part = dot(probs_low, grad)
        if keys == total_rows:
            key_total[...] = key_part
            value_total[...] = value_part
        else:
            key_total[:keys] += key_part
            value_total[:keys] += value_part
        query_ref[rows] = query_part
        for shard in reversed(range(seq_count)):
            here = slice(shard * slots, (shard + 1) * slots)
            if start <= here.start and len(away) == seq_count - 1 - shard:
                staged[shard, :, :DH] = query_ref[here]
                staged[shard, :, DH : 2 * DH] = (key_total[here] * scale).astype(BF16)
                staged[shard, :, 2 * DH :] = value_total[here].astype(BF16)
                away.append(pltpu.make_async_copy(staged.at[shard], out_ref.at[shard], leave.at[shard]))
                away[-1].start()
    for copy in away:
        copy.wait()


def backward(counts, blocks, attended, stats, grads):
    keys = attended.shape[0]
    seq_count = blocks.shape[0]
    return pl.pallas_call(
        backward_kernel,
        in_specs=[SMEM_SPEC] + [pl.BlockSpec(memory_space=pl.ANY)] * 4,
        out_specs=pl.BlockSpec(memory_space=pl.ANY),
        out_shape=jax.ShapeDtypeStruct(blocks.shape, BF16),
        scratch_shapes=[pltpu.VMEM((keys, DH), F32)]
        + [pltpu.VMEM((keys, DH), BF16)] * 5
        + [pltpu.VMEM(stats.shape, F32), pltpu.VMEM(blocks.shape, BF16)]
        + [pltpu.VMEM((keys, DH), F32)] * 2
        + [pltpu.SemaphoreType.DMA((4 * seq_count + 2,)), pltpu.SemaphoreType.DMA((seq_count,))],
        compiler_params=params(VMEM_MOST),
        cost_estimate=attention_cost(keys, 5),
    )(counts, blocks, attended, stats, grads)


def on_device_whole_heads(
    projections,
    output_gradient,
    output_projection_weight,
    kept_token_indices,
    surviving_token_count,
):
    tok_dev = projections.shape[0]
    slots = kept_token_indices.shape[1]
    seq_count = lax.axis_size("seq")
    head_count = lax.axis_size("head")
    index = kept_token_indices
    place = jnp.stack([lax.axis_index("seq"), lax.axis_index("head")]).astype(jnp.int32)
    seq_bits = [1 << bit for bit in reversed(range(seq_count.bit_length() - 1))]
    head_bits = [1 << bit for bit in reversed(range(head_count.bit_length() - 1))]

    def swap(blocks):
        return lax.all_to_all(blocks, "seq", split_axis=0, concat_axis=0, tiled=True)

    packed = pack_whole(index, projections.transpose(1, 0, 2))
    packed, grad_index = lax.optimization_barrier((packed, index))
    arrived = swap(packed)
    grad_blocks = gather_blocks(pack_grad(grad_index, output_gradient), "head", head_bits)
    grads = swap(grad_swap(place, grad_blocks, output_projection_weight, seq_count))
    attended, stats = forward(surviving_token_count, arrived)

    near, last = seq_bits[-2], seq_bits[-1]
    held = {bit: exchange(attended, "seq", bit) for bit in seq_bits}
    held[near ^ last] = exchange(held[near], "seq", last)
    back = backward(surviving_token_count, arrived, attended, stats, grads)
    back, held = lax.optimization_barrier((back, held))
    gathered = gather_blocks(attended, "seq", seq_bits, {0: attended, **held})
    home = swap(back)
    pieces = gather_blocks(grads[:, slots:], "head", head_bits)
    flip = flip_rows(place, pieces, slots)
    late = seq_count - 2
    weight_grad = weight_part(place, flip, gathered[:late], 0, seq_count, 1)
    projection_grad = unpack_whole(index, home, tok_dev)
    weight_grad = weight_part(place, flip, gathered[late:], late, seq_count, 28, weight_grad)
    projection_grad = projection_grad.transpose(1, 0, 2)
    return (projection_grad, weight_grad)


def on_device(projections, output_gradient, weight, index, counts):
    heads = projections.shape[2] // DH
    seq_count, head_count = lax.axis_size("seq"), lax.axis_size("head")
    width = output_gradient.shape[1] * head_count // seq_count
    whole = seq_count == heads and seq_count % 2 == 0 and width % DH == 0
    powers = seq_count & (seq_count - 1) == 0 and head_count & (head_count - 1) == 0
    body = on_device_whole_heads if whole and powers else on_device_split_heads
    return body(projections, output_gradient, weight, index, counts)


def solution(mesh):
    return jax.shard_map(
        on_device,
        mesh=mesh,
        in_specs=(P("seq", None, "head"), P("seq", "head"), P(None, "head"), P("seq", None), P()),
        out_specs=(P("seq", None, "head"), P("seq", "head")),
        check_vma=False,
    )
```

```python
import functools
import math

import jax
import jax.numpy as jnp
from jax import lax
from jax.experimental import pallas as pl
from jax.experimental.pallas import tpu as pltpu
from jax.sharding import PartitionSpec as P

DH = 128
QUERY_BLOCK = 256
WIDE_BLOCK = 512
VMEM_BYTES = 20 * 1024 * 1024
VMEM_MOST = 62 * 1024 * 1024
F32 = jnp.float32
BF16 = jnp.bfloat16


def params(limit=VMEM_BYTES):
    return pltpu.CompilerParams(vmem_limit_bytes=limit)


def dot(left, right):
    return jnp.dot(left, right, preferred_element_type=F32)


def dot_rows(left, right):
    return lax.dot_general(left, right, (((0,), (0,)), ((), ())), preferred_element_type=F32)


def dot_cols(left, right):
    return lax.dot_general(left, right, (((1,), (1,)), ((), ())), preferred_element_type=F32)


def token_selector(index_ref, tokens):
    slots = index_ref.shape[1]
    token = lax.broadcasted_iota(jnp.int32, (tokens, slots), 0)
    return jnp.where(token == index_ref[...], 1.0, 0.0).astype(BF16)


def pack_grad_kernel(index_ref, grad_ref, out_ref):
    selector = token_selector(index_ref, grad_ref.shape[0])
    out_ref[...] = dot_rows(selector, grad_ref[...]).astype(BF16)


def pack_grad(index, grad):
    slots = index.shape[1]
    return pl.pallas_call(
        pack_grad_kernel,
        out_shape=jax.ShapeDtypeStruct((slots, grad.shape[1]), BF16),
        compiler_params=params(),
    )(index, grad)


def pack_heads_kernel(index_ref, proj_ref, out_ref):
    selector = token_selector(index_ref, proj_ref.shape[1])
    for which in range(3):
        rows = dot_rows(selector, proj_ref[which]).astype(BF16)
        for head in range(out_ref.shape[0]):
            out_ref[head, :, which * DH : (which + 1) * DH] = rows[:, head * DH : (head + 1) * DH]


def pack_heads(index, proj):
    slots = index.shape[1]
    _, tokens, width = proj.shape
    heads = width // DH
    step = 2
    return pl.pallas_call(
        pack_heads_kernel,
        grid=(heads // step,),
        in_specs=[
            pl.BlockSpec((1, slots), lambda i: (0, 0)),
            pl.BlockSpec((3, tokens, step * DH), lambda i: (0, 0, i)),
        ],
        out_specs=pl.BlockSpec((step, slots, 3 * DH), lambda i: (i, 0, 0)),
        out_shape=jax.ShapeDtypeStruct((heads, slots, 3 * DH), BF16),
        compiler_params=params(),
    )(index, proj)


def unpack_heads_kernel(index_ref, rows_ref, out_ref):
    selector = token_selector(index_ref, out_ref.shape[1])
    for head in range(rows_ref.shape[0]):
        tokens = dot(selector, rows_ref[head]).astype(BF16)
        for which in range(3):
            out_ref[which, :, head * DH : (head + 1) * DH] = tokens[
                :, which * DH : (which + 1) * DH
            ]


def unpack_heads(index, rows, tokens):
    heads, slots, _ = rows.shape
    step = 2
    return pl.pallas_call(
        unpack_heads_kernel,
        grid=(heads // step,),
        in_specs=[
            pl.BlockSpec((1, slots), lambda i: (0, 0)),
            pl.BlockSpec((step, slots, 3 * DH), lambda i: (i, 0, 0)),
        ],
        out_specs=pl.BlockSpec((3, tokens, step * DH), lambda i: (0, 0, i)),
        out_shape=jax.ShapeDtypeStruct((3, tokens, heads * DH), BF16),
        compiler_params=params(),
    )(index, rows)


def grad_attn_kernel(rows_ref, weight_ref, out_ref):
    product = dot(rows_ref[...], weight_ref[...]).astype(BF16)
    for head in range(out_ref.shape[0]):
        out_ref[head] = product[:, head * DH : (head + 1) * DH]


def grad_attn_heads(rows, weight):
    slots, depth = rows.shape
    heads = weight.shape[1] // DH
    step = 2
    return pl.pallas_call(
        grad_attn_kernel,
        grid=(heads // step,),
        in_specs=[
            pl.BlockSpec((slots, depth), lambda i: (0, 0)),
            pl.BlockSpec((depth, step * DH), lambda i: (0, i)),
        ],
        out_specs=pl.BlockSpec((step, slots, DH), lambda i: (i, 0, 0)),
        out_shape=jax.ShapeDtypeStruct((heads, slots, DH), BF16),
        compiler_params=params(),
    )(rows, weight)


def weight_grad_kernel(rows_ref, attended_ref, out_ref):
    attended = jnp.concatenate([attended_ref[head] for head in range(attended_ref.shape[0])], axis=1)
    out_ref[...] = dot_rows(rows_ref[...], attended)


def weight_grad_heads(rows, attended):
    total, width = rows.shape
    heads = attended.shape[0]
    step = 2
    return pl.pallas_call(
        weight_grad_kernel,
        grid=(heads // step,),
        in_specs=[
            pl.BlockSpec((total, width), lambda i: (0, 0)),
            pl.BlockSpec((step, total, DH), lambda i: (i, 0, 0)),
        ],
        out_specs=pl.BlockSpec((width, step * DH), lambda i: (0, i)),
        out_shape=jax.ShapeDtypeStruct((width, heads * DH), F32),
        compiler_params=params(),
    )(rows, attended)


def attention_kernel(
    slots,
    part_rows,
    part_ref,
    live_ref,
    query_ref,
    grad_ref,
    key_ref,
    value_ref,
    attended_ref,
    query_grad_ref,
    key_grad_ref,
    value_grad_ref,
    key_total,
    value_total,
):
    scale = 1.0 / math.sqrt(DH)
    rows_total = query_ref.shape[0]
    keys_total = key_ref.shape[0]
    quarters = slots // part_rows
    key_flip = key_ref[...].T
    value_flip = value_ref[...].T
    for start in range(0, rows_total, QUERY_BLOCK):
        rows = slice(start, start + QUERY_BLOCK)
        last = start + QUERY_BLOCK - 1
        last_pos = last // part_rows * slots + (quarters - 1) * part_rows + last % part_rows
        first_pos = start // part_rows * slots + start % part_rows
        keys = min(-(-(last_pos + 1) // 128) * 128, keys_total)
        clear = first_pos // 128 * 128
        query = query_ref[rows]
        grad = grad_ref[rows]
        row = start + lax.broadcasted_iota(jnp.int32, (1, QUERY_BLOCK), 1)
        if quarters > 1:
            shard = row // part_rows
            row = shard * slots + part_ref[0] * part_rows + row - shard * part_rows
        scores = dot_cols(key_ref[:keys], query) * scale + live_ref[:keys, :1]
        key_pos = clear + lax.broadcasted_iota(jnp.int32, (keys - clear, 1), 0)
        edge = jnp.where(key_pos <= row, scores[clear:], -1e30)
        scores = jnp.concatenate([scores[:clear], edge], axis=0) if clear else edge
        peak = jnp.max(scores, axis=0, keepdims=True)
        weights = jnp.exp(scores - peak)
        probs = weights * (1.0 / jnp.sum(weights, axis=0, keepdims=True))
        probs_low = probs.astype(BF16)
        attended = dot(value_flip[:, :keys], probs_low)
        attended_ref[rows] = attended.T.astype(BF16)
        row_dot = jnp.sum(grad.T.astype(F32) * attended, axis=0, keepdims=True)
        grad_probs = dot_cols(value_ref[:keys], grad)
        grad_scores = (probs * (grad_probs - row_dot)).astype(BF16)
        query_grad = dot(key_flip[:, :keys], grad_scores) * scale
        query_grad_ref[rows] = query_grad.T.astype(BF16)
        key_part = dot(grad_scores, query)
        value_part = dot(probs_low, grad)
        prev = start - 1
        reached = 0
        if start:
            prev_pos = prev // part_rows * slots + (quarters - 1) * part_rows + prev % part_rows
            reached = min(-(-(prev_pos + 1) // 128) * 128, keys_total)
        if reached:
            key_total[:reached] += key_part[:reached]
            value_total[:reached] += value_part[:reached]
        if keys > reached:
            key_total[reached:keys] = key_part[reached:]
            value_total[reached:keys] = value_part[reached:]
    key_grad_ref[...] = (key_total[...] * scale).astype(key_grad_ref.dtype)
    value_grad_ref[...] = value_total[...].astype(value_grad_ref.dtype)


def attention(part, live, query, grad, key, value, slots, part_rows, key_type):
    rows, keys = query.shape[0], key.shape[0]
    vmem = pl.BlockSpec(memory_space=pltpu.VMEM)
    return pl.pallas_call(
        functools.partial(attention_kernel, slots, part_rows),
        in_specs=[pl.BlockSpec(memory_space=pltpu.SMEM)] + [vmem] * 5,
        out_specs=[vmem] * 4,
        out_shape=[
            jax.ShapeDtypeStruct((rows, DH), BF16),
            jax.ShapeDtypeStruct((rows, DH), BF16),
            jax.ShapeDtypeStruct((keys, DH), key_type),
            jax.ShapeDtypeStruct((keys, DH), key_type),
        ],
        scratch_shapes=[pltpu.VMEM((keys, DH), F32)] * 2,
        compiler_params=params(),
    )(part, live, query, grad, key, value)


def on_device_split_heads(
    projections,
    output_gradient,
    output_projection_weight,
    kept_token_indices,
    surviving_token_count,
):
    tok_dev = projections.shape[0]
    group_width = projections.shape[2]
    slots = kept_token_indices.shape[1]
    heads = group_width // DH
    seq_count = lax.axis_size("seq")
    head_count = lax.axis_size("head")
    quarters = seq_count // heads
    part_rows = slots // quarters
    part = (lax.axis_index("seq") % quarters).astype(jnp.int32).reshape(1)
    index = kept_token_indices
    keys = seq_count * slots

    grad_local = pack_grad(index, output_gradient)
    grad_rows = lax.all_gather(grad_local, "head", axis=1, tiled=True)
    packed = pack_heads(index, projections.transpose(1, 0, 2))

    position = jnp.arange(slots, dtype=jnp.int32)
    live = position[None, :] < surviving_token_count[:, None]
    live = jnp.where(live, 0.0, -1e30).astype(F32).reshape(keys, 1)
    live = jnp.broadcast_to(live, (keys, DH))

    def swap(blocks):
        return lax.all_to_all(blocks, "seq", split_axis=0, concat_axis=0, tiled=True)

    if quarters == 1:
        arrived = swap(packed).reshape(keys, 3 * DH)
        query, key, value = (arrived[:, n * DH : (n + 1) * DH] for n in range(3))
    else:
        query = swap(packed[:, :, :DH].reshape(seq_count, part_rows, DH))
        query = query.reshape(seq_count * part_rows, DH)
        sides = jnp.broadcast_to(packed[:, None, :, DH:], (heads, quarters, slots, 2 * DH))
        sides = swap(sides.reshape(seq_count, slots, 2 * DH)).reshape(keys, 2 * DH)
        key, value = sides[:, :DH], sides[:, DH:]

    grad_heads = grad_attn_heads(grad_rows, output_projection_weight)
    grad_in = swap(grad_heads.reshape(seq_count, part_rows, DH)).reshape(-1, DH)

    width = grad_rows.shape[1] // seq_count
    piece = slots // head_count
    mine = lax.dynamic_slice_in_dim(grad_rows, lax.axis_index("head") * piece, piece, 0)
    mine = swap(mine.reshape(piece, seq_count, width).transpose(1, 0, 2))
    all_rows = lax.all_gather(mine, "head", axis=1, tiled=True)

    key_type = BF16 if quarters == 1 else F32
    attended, query_grad, key_grad, value_grad = attention(
        part, live, query, grad_in, key, value, slots, part_rows, key_type
    )

    gathered = lax.all_gather(attended, "seq", axis=0).reshape(heads, keys, DH)
    all_rows = all_rows.reshape(seq_count, quarters, part_rows, width).transpose(1, 0, 2, 3)
    weight_grad = weight_grad_heads(all_rows.reshape(keys, width), gathered)

    if quarters == 1:
        back = jnp.concatenate([query_grad, key_grad, value_grad], axis=1)
        home = swap(back.reshape(seq_count, slots, 3 * DH))
    else:
        query_home = swap(query_grad.reshape(seq_count, part_rows, DH)).reshape(heads, slots, DH)
        back = jnp.concatenate([key_grad, value_grad], axis=1)
        key_home = swap(back.reshape(seq_count, slots, 2 * DH))
        key_home = jnp.sum(key_home.reshape(heads, quarters, slots, 2 * DH), axis=1)
        home = jnp.concatenate([query_home, key_home.astype(BF16)], axis=2)
    projection_grad = unpack_heads(index, home, tok_dev).transpose(1, 0, 2)
    return (projection_grad, weight_grad)


def pack_whole_kernel(index_ref, proj_ref, out_ref, loaded, packed, arrive, leave):
    parts = proj_ref.shape[0]
    copies = [
        pltpu.make_async_copy(proj_ref.at[which], loaded.at[which], arrive.at[which])
        for which in range(parts)
    ]
    for copy in copies:
        copy.start()
    token = lax.broadcasted_iota(jnp.int32, (loaded.shape[1], index_ref.shape[1]), 0)
    selector = jnp.where(token == index_ref[...], 1.0, 0.0).T.astype(BF16)
    away = []
    for which, copy in enumerate(copies):
        copy.wait()
        rows = dot(selector, loaded[which]).astype(BF16)
        for head in range(out_ref.shape[0]):
            packed[which, head] = rows[:, head * DH : (head + 1) * DH]
        away.append(
            pltpu.make_async_copy(
                packed.at[which],
                out_ref.at[:, :, which * DH : (which + 1) * DH],
                leave.at[which],
            )
        )
        away[-1].start()
    for copy in away:
        copy.wait()


def pack_whole(index, proj):
    slots = index.shape[1]
    parts, tokens, width = proj.shape
    heads = width // DH
    return pl.pallas_call(
        pack_whole_kernel,
        in_specs=[pl.BlockSpec(), pl.BlockSpec(memory_space=pltpu.HBM)],
        out_specs=pl.BlockSpec(memory_space=pltpu.HBM),
        out_shape=jax.ShapeDtypeStruct((heads, slots, parts * DH), BF16),
        scratch_shapes=[
            pltpu.VMEM(proj.shape, BF16),
            pltpu.VMEM((parts, heads, slots, DH), BF16),
            pltpu.SemaphoreType.DMA((parts,)),
            pltpu.SemaphoreType.DMA((parts,)),
        ],
        compiler_params=params(VMEM_MOST),
        cost_estimate=pl.CostEstimate(
            flops=2 * slots * tokens * parts * width,
            bytes_accessed=8 * tokens * width,
            transcendentals=0,
        ),
    )(index, proj)


def unpack_whole_kernel(index_ref, rows_ref, out_ref, tokens_ref, leave):
    selector = token_selector(index_ref, out_ref.shape[1])
    away = []
    for pair in range(rows_ref.shape[0] // 2):
        for side in range(2):
            tokens = dot(selector, rows_ref[2 * pair + side]).astype(BF16)
            for which in range(out_ref.shape[0]):
                tokens_ref[pair, which, :, side * DH : (side + 1) * DH] = tokens[
                    :, which * DH : (which + 1) * DH
                ]
        columns = pl.ds(pair * 2 * DH, 2 * DH)
        away.append(
            pltpu.make_async_copy(tokens_ref.at[pair], out_ref.at[:, :, columns], leave.at[pair])
        )
        away[-1].start()
    for copy in away:
        copy.wait()


def unpack_whole(index, rows, tokens):
    heads, slots, width = rows.shape
    parts = width // DH
    return pl.pallas_call(
        unpack_whole_kernel,
        in_specs=[VMEM_SPEC] * 2,
        out_specs=pl.BlockSpec(memory_space=pl.ANY),
        out_shape=jax.ShapeDtypeStruct((parts, tokens, heads * DH), BF16),
        scratch_shapes=[
            pltpu.VMEM((heads // 2, parts, tokens, 2 * DH), BF16),
            pltpu.SemaphoreType.DMA((heads // 2,)),
        ],
        compiler_params=params(),
    )(index, rows)


def exchange(block, axis, bit):
    return lax.ppermute(block, axis, [(i, i ^ bit) for i in range(lax.axis_size(axis))])


def gather_blocks(block, axis, bits, held=None):
    held = {0: block} if held is None else dict(held)
    reached = [0]
    for bit in bits:
        for step in list(reached):
            if step ^ bit not in held:
                held[step ^ bit] = exchange(held[step], axis, bit)
            reached.append(step ^ bit)
    return [held[step] for step in range(lax.axis_size(axis))]


SMEM_SPEC = pl.BlockSpec(memory_space=pltpu.SMEM)
VMEM_SPEC = pl.BlockSpec(memory_space=pltpu.VMEM)


def grad_swap_kernel(count, place_ref, *refs):
    row_refs, weight_ref, out_ref, total = refs[:count], refs[count], refs[count + 1], refs[count + 2]
    mine = place_ref[1]
    seq_count, height, _ = out_ref.shape
    slots, depth = row_refs[0].shape
    piece = slots // count
    chunks = (height - slots) // piece
    per_block = depth // (chunks * DH)
    for step in range(count):

        @pl.when(pl.program_id(0) == step)
        def _(step=step):
            part = dot(row_refs[step][...], weight_ref[...])
            total[...] = part if step == 0 else total[...] + part
            share = row_refs[step][pl.ds(pl.multiple_of(mine * piece, piece), piece), :]
            for chunk in range(per_block * chunks):
                partner = (mine ^ step) * per_block + chunk // chunks
                start = slots + chunk % chunks * piece
                out_ref[partner, start : start + piece, :] = share[:, chunk * DH : (chunk + 1) * DH]

    @pl.when(pl.program_id(0) == count - 1)
    def _():
        for head in range(seq_count):
            out_ref[head, :slots, :] = total[:, head * DH : (head + 1) * DH].astype(BF16)


def grad_swap(place, blocks, weight, seq_count):
    count = len(blocks)
    slots, depth = blocks[0].shape
    columns = weight.shape[1]
    height = slots + slots // count * (count * depth // seq_count // DH)
    return pl.pallas_call(
        functools.partial(grad_swap_kernel, count),
        grid_spec=pltpu.PrefetchScalarGridSpec(
            num_scalar_prefetch=1,
            grid=(count,),
            in_specs=[pl.BlockSpec((slots, depth), lambda i, place: (0, 0))] * count
            + [pl.BlockSpec((depth, columns), lambda i, place: (place[1] ^ i, 0))],
            out_specs=pl.BlockSpec((seq_count, height, DH), lambda i, place: (0, 0, 0)),
            scratch_shapes=[pltpu.VMEM((slots, columns), F32)],
        ),
        out_shape=jax.ShapeDtypeStruct((seq_count, height, DH), BF16),
        compiler_params=params(),
        cost_estimate=pl.CostEstimate(
            flops=2 * slots * count * depth * columns,
            bytes_accessed=2 * count * depth * columns,
            transcendentals=0,
        ),
    )(place, *blocks, weight)


def flip_rows_kernel(place_ref, *refs):
    piece_refs, out_ref, rows = refs[:-2], refs[-2], refs[-1]
    count = len(piece_refs)
    chunks = rows.shape[1] // DH
    shards, height, _ = piece_refs[0].shape
    piece = height // chunks
    for part in range(count):
        for shard in range(shards):
            start = shard * piece * count + (place_ref[1] ^ part) * piece
            here = pl.ds(pl.multiple_of(start, piece), piece)
            for chunk in range(chunks):
                rows[here, chunk * DH : (chunk + 1) * DH] = piece_refs[part][
                    shard, chunk * piece : (chunk + 1) * piece, :
                ]
    out_ref[...] = rows[...].T


def flip_rows(place, pieces, slots):
    shards, height, _ = pieces[0].shape
    width = height // (slots // len(pieces)) * DH
    keys = shards * slots
    return pl.pallas_call(
        flip_rows_kernel,
        in_specs=[SMEM_SPEC] + [pl.BlockSpec()] * len(pieces),
        out_specs=VMEM_SPEC,
        out_shape=jax.ShapeDtypeStruct((width, keys), BF16),
        scratch_shapes=[pltpu.VMEM((keys, width), BF16)],
        compiler_params=params(),
        cost_estimate=pl.CostEstimate(flops=0, bytes_accessed=4 * keys * width, transcendentals=0),
    )(place, *pieces)


def weight_part_kernel(first, count, place_ref, flip_ref, *refs):
    out_ref, product_ref, leave = refs[-3:]
    away = []
    for step in range(0, count, 2):
        both = jnp.concatenate([ref[...] for ref in refs[step : step + 2]], axis=1)
        product = dot(flip_ref[...], both)
        head = place_ref[0] ^ (first + step)
        for side in range(2):
            column = pl.multiple_of((head ^ side) % 2 * DH, DH)
            product_ref[step // 2, :, pl.ds(column, DH)] = product[:, side * DH : (side + 1) * DH]
        columns = pl.ds(pl.multiple_of(head // 2 * (2 * DH), 2 * DH), 2 * DH)
        away.append(
            pltpu.make_async_copy(
                product_ref.at[step // 2], out_ref.at[:, columns], leave.at[step // 2]
            )
        )
        away[-1].start()
    for copy in away:
        copy.wait()


def weight_part(place, flip, attended, first, heads, weight, before=None):
    count = len(attended)
    width, keys = flip.shape
    more = [] if before is None else [before]
    return pl.pallas_call(
        functools.partial(weight_part_kernel, first, count),
        in_specs=[SMEM_SPEC]
        + [VMEM_SPEC] * (1 + count)
        + [pl.BlockSpec(memory_space=pl.ANY)] * len(more),
        out_specs=pl.BlockSpec(memory_space=pl.ANY),
        out_shape=jax.ShapeDtypeStruct((width, heads * DH), F32),
        scratch_shapes=[
            pltpu.VMEM((count // 2, width, 2 * DH), F32),
            pltpu.SemaphoreType.DMA((count // 2,)),
        ],
        input_output_aliases={2 + count: 0} if more else {},
        compiler_params=params(),
        cost_estimate=pl.CostEstimate(
            flops=weight * 2 * keys * width * count * DH,
            bytes_accessed=8 * keys * DH * count,
            transcendentals=0,
        ),
    )(place, flip, *attended, *more)


def mark_live(count_ref, live_ref, slots):
    for shard in range(live_ref.shape[0] // slots):
        inside = lax.broadcasted_iota(jnp.int32, (slots, live_ref.shape[1]), 0)
        live_ref[shard * slots : (shard + 1) * slots] = jnp.where(
            inside < count_ref[shard], 0.0, -1e30
        )


def masked_scores(start, keys, key_ref, query, live_ref):
    scores = dot_cols(key_ref[:keys], query) * (1.0 / math.sqrt(DH)) + live_ref[:keys, :1]
    row = start + lax.broadcasted_iota(jnp.int32, (1, WIDE_BLOCK), 1)
    key_pos = start + lax.broadcasted_iota(jnp.int32, (WIDE_BLOCK, 1), 0)
    edge = jnp.where(key_pos <= row, scores[start:], -1e30)
    return jnp.concatenate([scores[:start], edge], axis=0) if start else edge


def split_blocks(block_ref, *refs):
    shards, slots, _ = block_ref.shape
    for shard in range(shards):
        for which, ref in enumerate(refs):
            ref[shard * slots : (shard + 1) * slots] = block_ref[
                shard, :, which * DH : (which + 1) * DH
            ]


def forward_kernel(
    count_ref, block_ref, attended_ref, stat_ref, live_ref, query_ref, key_ref, value_ref
):
    mark_live(count_ref, live_ref, block_ref.shape[1])
    split_blocks(block_ref, query_ref, key_ref, value_ref)
    value_flip = value_ref[...].T
    for start in range(0, query_ref.shape[0], WIDE_BLOCK):
        rows = slice(start, start + WIDE_BLOCK)
        keys = start + WIDE_BLOCK
        scores = masked_scores(start, keys, key_ref, query_ref[rows], live_ref)
        peak = jnp.max(scores, axis=0, keepdims=True)
        weights = jnp.exp(scores - peak)
        inverse = 1.0 / jnp.sum(weights, axis=0, keepdims=True)
        attended = dot(value_flip[:, :keys], (weights * inverse).astype(BF16))
        attended_ref[rows] = attended.T.astype(BF16)
        stat_ref[0:1, rows] = peak
        stat_ref[1:2, rows] = inverse


def attention_cost(keys, dots):
    return pl.CostEstimate(
        flops=dots * keys * keys * DH, bytes_accessed=16 * keys * DH, transcendentals=keys * keys // 2
    )


def forward(counts, blocks):
    keys = blocks.shape[0] * blocks.shape[1]
    return pl.pallas_call(
        forward_kernel,
        out_shape=[
            jax.ShapeDtypeStruct((keys, DH), BF16),
            jax.ShapeDtypeStruct((8, keys), F32),
        ],
        in_specs=[SMEM_SPEC, pl.BlockSpec()],
        scratch_shapes=[pltpu.VMEM((keys, DH), F32)] + [pltpu.VMEM((keys, DH), BF16)] * 3,
        compiler_params=params(32 * 1024 * 1024),
        cost_estimate=attention_cost(keys, 2),
    )(counts, blocks)


def backward_kernel(
    count_ref,
    block_ref,
    attended_ref,
    stat_ref,
    grads_ref,
    out_ref,
    live_ref,
    query_ref,
    key_ref,
    value_ref,
    grad_ref,
    query_total,
    key_total,
    value_total,
):
    seq_count, slots, _ = out_ref.shape
    scale = 1.0 / math.sqrt(DH)
    mark_live(count_ref, live_ref, slots)
    split_blocks(block_ref, query_ref, key_ref, value_ref)
    for shard in range(seq_count):
        grad_ref[shard * slots : (shard + 1) * slots] = grads_ref[shard, :slots]
    key_flip = key_ref[...].T
    for start in range(0, query_ref.shape[0], WIDE_BLOCK):
        rows = slice(start, start + WIDE_BLOCK)
        keys = start + WIDE_BLOCK
        query = query_ref[rows]
        grad = grad_ref[rows]
        scores = masked_scores(start, keys, key_ref, query, live_ref)
        probs = jnp.exp(scores - stat_ref[0:1, rows]) * stat_ref[1:2, rows]
        probs_low = probs.astype(BF16)
        product = grad.astype(F32) * attended_ref[rows].astype(F32)
        row_dot = jnp.sum(product.T, axis=0, keepdims=True)
        grad_probs = dot_cols(value_ref[:keys], grad)
        grad_scores = (probs * (grad_probs - row_dot)).astype(BF16)
        query_total[rows] = (dot(key_flip[:, :keys], grad_scores) * scale).T.astype(BF16)
        key_part = dot(grad_scores, query)
        value_part = dot(probs_low, grad)
        if start:
            key_total[:start] += key_part[:start]
            value_total[:start] += value_part[:start]
        key_total[rows] = key_part[start:]
        value_total[rows] = value_part[start:]
    for shard in range(seq_count):
        here = slice(shard * slots, (shard + 1) * slots)
        out_ref[shard, :, :DH] = query_total[here]
        out_ref[shard, :, DH : 2 * DH] = (key_total[here] * scale).astype(BF16)
        out_ref[shard, :, 2 * DH :] = value_total[here].astype(BF16)


def backward(counts, blocks, attended, stats, grads):
    keys = attended.shape[0]
    return pl.pallas_call(
        backward_kernel,
        in_specs=[SMEM_SPEC] + [pl.BlockSpec()] * 4,
        out_shape=jax.ShapeDtypeStruct(blocks.shape, BF16),
        scratch_shapes=[pltpu.VMEM((keys, DH), F32)]
        + [pltpu.VMEM((keys, DH), BF16)] * 5
        + [pltpu.VMEM((keys, DH), F32)] * 2,
        compiler_params=params(VMEM_MOST),
        cost_estimate=attention_cost(keys, 5),
    )(counts, blocks, attended, stats, grads)


def on_device_whole_heads(
    projections,
    output_gradient,
    output_projection_weight,
    kept_token_indices,
    surviving_token_count,
):
    tok_dev = projections.shape[0]
    slots = kept_token_indices.shape[1]
    seq_count = lax.axis_size("seq")
    head_count = lax.axis_size("head")
    index = kept_token_indices
    place = jnp.stack([lax.axis_index("seq"), lax.axis_index("head")]).astype(jnp.int32)
    seq_bits = [1 << bit for bit in reversed(range(seq_count.bit_length() - 1))]
    head_bits = [1 << bit for bit in reversed(range(head_count.bit_length() - 1))]

    def swap(blocks):
        return lax.all_to_all(blocks, "seq", split_axis=0, concat_axis=0, tiled=True)

    packed = pack_whole(index, projections.transpose(1, 0, 2))
    packed, grad_index = lax.optimization_barrier((packed, index))
    arrived = swap(packed)
    grad_blocks = gather_blocks(pack_grad(grad_index, output_gradient), "head", head_bits)
    grads = swap(grad_swap(place, grad_blocks, output_projection_weight, seq_count))
    attended, stats = forward(surviving_token_count, arrived)

    near, last = seq_bits[-2], seq_bits[-1]
    held = {bit: exchange(attended, "seq", bit) for bit in seq_bits}
    held[near ^ last] = exchange(held[near], "seq", last)
    back = backward(surviving_token_count, arrived, attended, stats, grads)
    back, held = lax.optimization_barrier((back, held))
    gathered = gather_blocks(attended, "seq", seq_bits, {0: attended, **held})
    home = swap(back)
    pieces = gather_blocks(grads[:, slots:], "head", head_bits)
    flip = flip_rows(place, pieces, slots)
    late = seq_count - 2
    weight_grad = weight_part(place, flip, gathered[:late], 0, seq_count, 1)
    projection_grad = unpack_whole(index, home, tok_dev)
    weight_grad = weight_part(place, flip, gathered[late:], late, seq_count, 28, weight_grad)
    projection_grad = projection_grad.transpose(1, 0, 2)
    return (projection_grad, weight_grad)


def on_device(projections, output_gradient, weight, index, counts):
    heads = projections.shape[2] // DH
    seq_count, head_count = lax.axis_size("seq"), lax.axis_size("head")
    width = output_gradient.shape[1] * head_count // seq_count
    whole = seq_count == heads and seq_count % 2 == 0 and width % DH == 0
    powers = seq_count & (seq_count - 1) == 0 and head_count & (head_count - 1) == 0
    body = on_device_whole_heads if whole and powers else on_device_split_heads
    return body(projections, output_gradient, weight, index, counts)


def solution(mesh):
    return jax.shard_map(
        on_device,
        mesh=mesh,
        in_specs=(P("seq", None, "head"), P("seq", "head"), P(None, "head"), P("seq", None), P()),
        out_specs=(P("seq", None, "head"), P("seq", "head")),
        check_vma=False,
    )
```

```python
import functools
import math

import jax
import jax.numpy as jnp
from jax import lax
from jax.experimental import pallas as pl
from jax.experimental.pallas import tpu as pltpu
from jax.sharding import PartitionSpec as P

DH = 128
QUERY_BLOCK = 256
WIDE_BLOCK = 512
VMEM_BYTES = 20 * 1024 * 1024
VMEM_MOST = 62 * 1024 * 1024
F32 = jnp.float32
BF16 = jnp.bfloat16


def params(limit=VMEM_BYTES):
    return pltpu.CompilerParams(vmem_limit_bytes=limit)


def dot(left, right):
    return jnp.dot(left, right, preferred_element_type=F32)


def dot_rows(left, right):
    return lax.dot_general(left, right, (((0,), (0,)), ((), ())), preferred_element_type=F32)


def dot_cols(left, right):
    return lax.dot_general(left, right, (((1,), (1,)), ((), ())), preferred_element_type=F32)


def token_selector(index_ref, tokens):
    slots = index_ref.shape[1]
    token = lax.broadcasted_iota(jnp.int32, (tokens, slots), 0)
    return jnp.where(token == index_ref[...], 1.0, 0.0).astype(BF16)


def pack_grad_kernel(index_ref, grad_ref, out_ref):
    selector = token_selector(index_ref, grad_ref.shape[0])
    out_ref[...] = dot_rows(selector, grad_ref[...]).astype(BF16)


def pack_grad(index, grad):
    slots = index.shape[1]
    return pl.pallas_call(
        pack_grad_kernel,
        out_shape=jax.ShapeDtypeStruct((slots, grad.shape[1]), BF16),
        compiler_params=params(),
    )(index, grad)


def pack_heads_kernel(index_ref, proj_ref, out_ref):
    selector = token_selector(index_ref, proj_ref.shape[1])
    for which in range(3):
        rows = dot_rows(selector, proj_ref[which]).astype(BF16)
        for head in range(out_ref.shape[0]):
            out_ref[head, :, which * DH : (which + 1) * DH] = rows[:, head * DH : (head + 1) * DH]


def pack_heads(index, proj):
    slots = index.shape[1]
    _, tokens, width = proj.shape
    heads = width // DH
    step = 2
    return pl.pallas_call(
        pack_heads_kernel,
        grid=(heads // step,),
        in_specs=[
            pl.BlockSpec((1, slots), lambda i: (0, 0)),
            pl.BlockSpec((3, tokens, step * DH), lambda i: (0, 0, i)),
        ],
        out_specs=pl.BlockSpec((step, slots, 3 * DH), lambda i: (i, 0, 0)),
        out_shape=jax.ShapeDtypeStruct((heads, slots, 3 * DH), BF16),
        compiler_params=params(),
    )(index, proj)


def unpack_heads_kernel(index_ref, rows_ref, out_ref):
    selector = token_selector(index_ref, out_ref.shape[1])
    for head in range(rows_ref.shape[0]):
        tokens = dot(selector, rows_ref[head]).astype(BF16)
        for which in range(3):
            out_ref[which, :, head * DH : (head + 1) * DH] = tokens[
                :, which * DH : (which + 1) * DH
            ]


def unpack_heads(index, rows, tokens):
    heads, slots, _ = rows.shape
    step = 2
    return pl.pallas_call(
        unpack_heads_kernel,
        grid=(heads // step,),
        in_specs=[
            pl.BlockSpec((1, slots), lambda i: (0, 0)),
            pl.BlockSpec((step, slots, 3 * DH), lambda i: (i, 0, 0)),
        ],
        out_specs=pl.BlockSpec((3, tokens, step * DH), lambda i: (0, 0, i)),
        out_shape=jax.ShapeDtypeStruct((3, tokens, heads * DH), BF16),
        compiler_params=params(),
    )(index, rows)


def grad_attn_kernel(rows_ref, weight_ref, out_ref):
    product = dot(rows_ref[...], weight_ref[...]).astype(BF16)
    for head in range(out_ref.shape[0]):
        out_ref[head] = product[:, head * DH : (head + 1) * DH]


def grad_attn_heads(rows, weight):
    slots, depth = rows.shape
    heads = weight.shape[1] // DH
    step = 2
    return pl.pallas_call(
        grad_attn_kernel,
        grid=(heads // step,),
        in_specs=[
            pl.BlockSpec((slots, depth), lambda i: (0, 0)),
            pl.BlockSpec((depth, step * DH), lambda i: (0, i)),
        ],
        out_specs=pl.BlockSpec((step, slots, DH), lambda i: (i, 0, 0)),
        out_shape=jax.ShapeDtypeStruct((heads, slots, DH), BF16),
        compiler_params=params(),
    )(rows, weight)


def weight_grad_kernel(rows_ref, attended_ref, out_ref):
    attended = jnp.concatenate([attended_ref[head] for head in range(attended_ref.shape[0])], axis=1)
    out_ref[...] = dot_rows(rows_ref[...], attended)


def weight_grad_heads(rows, attended):
    total, width = rows.shape
    heads = attended.shape[0]
    step = 2
    return pl.pallas_call(
        weight_grad_kernel,
        grid=(heads // step,),
        in_specs=[
            pl.BlockSpec((total, width), lambda i: (0, 0)),
            pl.BlockSpec((step, total, DH), lambda i: (i, 0, 0)),
        ],
        out_specs=pl.BlockSpec((width, step * DH), lambda i: (0, i)),
        out_shape=jax.ShapeDtypeStruct((width, heads * DH), F32),
        compiler_params=params(),
    )(rows, attended)


def attention_kernel(
    slots,
    part_rows,
    part_ref,
    live_ref,
    query_ref,
    grad_ref,
    key_ref,
    value_ref,
    attended_ref,
    query_grad_ref,
    key_grad_ref,
    value_grad_ref,
    key_total,
    value_total,
):
    scale = 1.0 / math.sqrt(DH)
    rows_total = query_ref.shape[0]
    keys_total = key_ref.shape[0]
    quarters = slots // part_rows
    key_flip = key_ref[...].T
    value_flip = value_ref[...].T
    for start in range(0, rows_total, QUERY_BLOCK):
        rows = slice(start, start + QUERY_BLOCK)
        last = start + QUERY_BLOCK - 1
        last_pos = last // part_rows * slots + (quarters - 1) * part_rows + last % part_rows
        first_pos = start // part_rows * slots + start % part_rows
        keys = min(-(-(last_pos + 1) // 128) * 128, keys_total)
        clear = first_pos // 128 * 128
        query = query_ref[rows]
        grad = grad_ref[rows]
        row = start + lax.broadcasted_iota(jnp.int32, (1, QUERY_BLOCK), 1)
        if quarters > 1:
            shard = row // part_rows
            row = shard * slots + part_ref[0] * part_rows + row - shard * part_rows
        scores = dot_cols(key_ref[:keys], query) * scale + live_ref[:keys, :1]
        key_pos = clear + lax.broadcasted_iota(jnp.int32, (keys - clear, 1), 0)
        edge = jnp.where(key_pos <= row, scores[clear:], -1e30)
        scores = jnp.concatenate([scores[:clear], edge], axis=0) if clear else edge
        peak = jnp.max(scores, axis=0, keepdims=True)
        weights = jnp.exp(scores - peak)
        probs = weights * (1.0 / jnp.sum(weights, axis=0, keepdims=True))
        probs_low = probs.astype(BF16)
        attended = dot(value_flip[:, :keys], probs_low)
        attended_ref[rows] = attended.T.astype(BF16)
        row_dot = jnp.sum(grad.T.astype(F32) * attended, axis=0, keepdims=True)
        grad_probs = dot_cols(value_ref[:keys], grad)
        grad_scores = (probs * (grad_probs - row_dot)).astype(BF16)
        query_grad = dot(key_flip[:, :keys], grad_scores) * scale
        query_grad_ref[rows] = query_grad.T.astype(BF16)
        key_part = dot(grad_scores, query)
        value_part = dot(probs_low, grad)
        prev = start - 1
        reached = 0
        if start:
            prev_pos = prev // part_rows * slots + (quarters - 1) * part_rows + prev % part_rows
            reached = min(-(-(prev_pos + 1) // 128) * 128, keys_total)
        if reached:
            key_total[:reached] += key_part[:reached]
            value_total[:reached] += value_part[:reached]
        if keys > reached:
            key_total[reached:keys] = key_part[reached:]
            value_total[reached:keys] = value_part[reached:]
    key_grad_ref[...] = (key_total[...] * scale).astype(key_grad_ref.dtype)
    value_grad_ref[...] = value_total[...].astype(value_grad_ref.dtype)


def attention(part, live, query, grad, key, value, slots, part_rows, key_type):
    rows, keys = query.shape[0], key.shape[0]
    vmem = pl.BlockSpec(memory_space=pltpu.VMEM)
    return pl.pallas_call(
        functools.partial(attention_kernel, slots, part_rows),
        in_specs=[pl.BlockSpec(memory_space=pltpu.SMEM)] + [vmem] * 5,
        out_specs=[vmem] * 4,
        out_shape=[
            jax.ShapeDtypeStruct((rows, DH), BF16),
            jax.ShapeDtypeStruct((rows, DH), BF16),
            jax.ShapeDtypeStruct((keys, DH), key_type),
            jax.ShapeDtypeStruct((keys, DH), key_type),
        ],
        scratch_shapes=[pltpu.VMEM((keys, DH), F32)] * 2,
        compiler_params=params(),
    )(part, live, query, grad, key, value)


def on_device_split_heads(
    projections,
    output_gradient,
    output_projection_weight,
    kept_token_indices,
    surviving_token_count,
):
    tok_dev = projections.shape[0]
    group_width = projections.shape[2]
    slots = kept_token_indices.shape[1]
    heads = group_width // DH
    seq_count = lax.axis_size("seq")
    head_count = lax.axis_size("head")
    quarters = seq_count // heads
    part_rows = slots // quarters
    part = (lax.axis_index("seq") % quarters).astype(jnp.int32).reshape(1)
    index = kept_token_indices
    keys = seq_count * slots

    grad_local = pack_grad(index, output_gradient)
    grad_rows = lax.all_gather(grad_local, "head", axis=1, tiled=True)
    packed = pack_heads(index, projections.transpose(1, 0, 2))

    position = jnp.arange(slots, dtype=jnp.int32)
    live = position[None, :] < surviving_token_count[:, None]
    live = jnp.where(live, 0.0, -1e30).astype(F32).reshape(keys, 1)
    live = jnp.broadcast_to(live, (keys, DH))

    def swap(blocks):
        return lax.all_to_all(blocks, "seq", split_axis=0, concat_axis=0, tiled=True)

    if quarters == 1:
        arrived = swap(packed).reshape(keys, 3 * DH)
        query, key, value = (arrived[:, n * DH : (n + 1) * DH] for n in range(3))
    else:
        query = swap(packed[:, :, :DH].reshape(seq_count, part_rows, DH))
        query = query.reshape(seq_count * part_rows, DH)
        sides = jnp.broadcast_to(packed[:, None, :, DH:], (heads, quarters, slots, 2 * DH))
        sides = swap(sides.reshape(seq_count, slots, 2 * DH)).reshape(keys, 2 * DH)
        key, value = sides[:, :DH], sides[:, DH:]

    grad_heads = grad_attn_heads(grad_rows, output_projection_weight)
    grad_in = swap(grad_heads.reshape(seq_count, part_rows, DH)).reshape(-1, DH)

    width = grad_rows.shape[1] // seq_count
    piece = slots // head_count
    mine = lax.dynamic_slice_in_dim(grad_rows, lax.axis_index("head") * piece, piece, 0)
    mine = swap(mine.reshape(piece, seq_count, width).transpose(1, 0, 2))
    all_rows = lax.all_gather(mine, "head", axis=1, tiled=True)

    key_type = BF16 if quarters == 1 else F32
    attended, query_grad, key_grad, value_grad = attention(
        part, live, query, grad_in, key, value, slots, part_rows, key_type
    )

    gathered = lax.all_gather(attended, "seq", axis=0).reshape(heads, keys, DH)
    all_rows = all_rows.reshape(seq_count, quarters, part_rows, width).transpose(1, 0, 2, 3)
    weight_grad = weight_grad_heads(all_rows.reshape(keys, width), gathered)

    if quarters == 1:
        back = jnp.concatenate([query_grad, key_grad, value_grad], axis=1)
        home = swap(back.reshape(seq_count, slots, 3 * DH))
    else:
        query_home = swap(query_grad.reshape(seq_count, part_rows, DH)).reshape(heads, slots, DH)
        back = jnp.concatenate([key_grad, value_grad], axis=1)
        key_home = swap(back.reshape(seq_count, slots, 2 * DH))
        key_home = jnp.sum(key_home.reshape(heads, quarters, slots, 2 * DH), axis=1)
        home = jnp.concatenate([query_home, key_home.astype(BF16)], axis=2)
    projection_grad = unpack_heads(index, home, tok_dev).transpose(1, 0, 2)
    return (projection_grad, weight_grad)


def pack_whole_kernel(index_ref, proj_ref, out_ref, loaded, packed, arrive, leave):
    parts = proj_ref.shape[0]
    copies = [
        pltpu.make_async_copy(proj_ref.at[which], loaded.at[which], arrive.at[which])
        for which in range(parts)
    ]
    for copy in copies:
        copy.start()
    token = lax.broadcasted_iota(jnp.int32, (loaded.shape[1], index_ref.shape[1]), 0)
    selector = jnp.where(token == index_ref[...], 1.0, 0.0).T.astype(BF16)
    away = []
    for which, copy in enumerate(copies):
        copy.wait()
        rows = dot(selector, loaded[which]).astype(BF16)
        for head in range(out_ref.shape[0]):
            packed[which, head] = rows[:, head * DH : (head + 1) * DH]
        away.append(
            pltpu.make_async_copy(
                packed.at[which],
                out_ref.at[:, :, which * DH : (which + 1) * DH],
                leave.at[which],
            )
        )
        away[-1].start()
    for copy in away:
        copy.wait()


def pack_whole(index, proj):
    slots = index.shape[1]
    parts, tokens, width = proj.shape
    heads = width // DH
    return pl.pallas_call(
        pack_whole_kernel,
        in_specs=[pl.BlockSpec(), pl.BlockSpec(memory_space=pltpu.HBM)],
        out_specs=pl.BlockSpec(memory_space=pltpu.HBM),
        out_shape=jax.ShapeDtypeStruct((heads, slots, parts * DH), BF16),
        scratch_shapes=[
            pltpu.VMEM(proj.shape, BF16),
            pltpu.VMEM((parts, heads, slots, DH), BF16),
            pltpu.SemaphoreType.DMA((parts,)),
            pltpu.SemaphoreType.DMA((parts,)),
        ],
        compiler_params=params(VMEM_MOST),
        cost_estimate=pl.CostEstimate(
            flops=2 * slots * tokens * parts * width,
            bytes_accessed=8 * tokens * width,
            transcendentals=0,
        ),
    )(index, proj)


def unpack_whole_kernel(index_ref, rows_ref, out_ref, tokens_ref, leave):
    selector = token_selector(index_ref, out_ref.shape[1])
    away = []
    for pair in range(rows_ref.shape[0] // 2):
        for side in range(2):
            tokens = dot(selector, rows_ref[2 * pair + side]).astype(BF16)
            for which in range(out_ref.shape[0]):
                tokens_ref[pair, which, :, side * DH : (side + 1) * DH] = tokens[
                    :, which * DH : (which + 1) * DH
                ]
        columns = pl.ds(pair * 2 * DH, 2 * DH)
        away.append(
            pltpu.make_async_copy(tokens_ref.at[pair], out_ref.at[:, :, columns], leave.at[pair])
        )
        away[-1].start()
    for copy in away:
        copy.wait()


def unpack_whole(index, rows, tokens):
    heads, slots, width = rows.shape
    parts = width // DH
    return pl.pallas_call(
        unpack_whole_kernel,
        in_specs=[VMEM_SPEC] * 2,
        out_specs=pl.BlockSpec(memory_space=pl.ANY),
        out_shape=jax.ShapeDtypeStruct((parts, tokens, heads * DH), BF16),
        scratch_shapes=[
            pltpu.VMEM((heads // 2, parts, tokens, 2 * DH), BF16),
            pltpu.SemaphoreType.DMA((heads // 2,)),
        ],
        compiler_params=params(),
    )(index, rows)


def exchange(block, axis, bit):
    return lax.ppermute(block, axis, [(i, i ^ bit) for i in range(lax.axis_size(axis))])


def gather_blocks(block, axis, bits, held=None):
    held = {0: block} if held is None else dict(held)
    reached = [0]
    for bit in bits:
        for step in list(reached):
            if step ^ bit not in held:
                held[step ^ bit] = exchange(held[step], axis, bit)
            reached.append(step ^ bit)
    return [held[step] for step in range(lax.axis_size(axis))]


SMEM_SPEC = pl.BlockSpec(memory_space=pltpu.SMEM)
VMEM_SPEC = pl.BlockSpec(memory_space=pltpu.VMEM)


def grad_swap_kernel(count, place_ref, *refs):
    row_refs, weight_ref, out_ref, total = refs[:count], refs[count], refs[count + 1], refs[count + 2]
    mine = place_ref[1]
    seq_count, height, _ = out_ref.shape
    slots, depth = row_refs[0].shape
    piece = slots // count
    chunks = (height - slots) // piece
    per_block = depth // (chunks * DH)
    for step in range(count):

        @pl.when(pl.program_id(0) == step)
        def _(step=step):
            part = dot(row_refs[step][...], weight_ref[...])
            total[...] = part if step == 0 else total[...] + part
            share = row_refs[step][pl.ds(pl.multiple_of(mine * piece, piece), piece), :]
            for chunk in range(per_block * chunks):
                partner = (mine ^ step) * per_block + chunk // chunks
                start = slots + chunk % chunks * piece
                out_ref[partner, start : start + piece, :] = share[:, chunk * DH : (chunk + 1) * DH]

    @pl.when(pl.program_id(0) == count - 1)
    def _():
        for head in range(seq_count):
            out_ref[head, :slots, :] = total[:, head * DH : (head + 1) * DH].astype(BF16)


def grad_swap(place, blocks, weight, seq_count):
    count = len(blocks)
    slots, depth = blocks[0].shape
    columns = weight.shape[1]
    height = slots + slots // count * (count * depth // seq_count // DH)
    return pl.pallas_call(
        functools.partial(grad_swap_kernel, count),
        grid_spec=pltpu.PrefetchScalarGridSpec(
            num_scalar_prefetch=1,
            grid=(count,),
            in_specs=[pl.BlockSpec((slots, depth), lambda i, place: (0, 0))] * count
            + [pl.BlockSpec((depth, columns), lambda i, place: (place[1] ^ i, 0))],
            out_specs=pl.BlockSpec((seq_count, height, DH), lambda i, place: (0, 0, 0)),
            scratch_shapes=[pltpu.VMEM((slots, columns), F32)],
        ),
        out_shape=jax.ShapeDtypeStruct((seq_count, height, DH), BF16),
        compiler_params=params(),
        cost_estimate=pl.CostEstimate(
            flops=2 * slots * count * depth * columns,
            bytes_accessed=2 * count * depth * columns,
            transcendentals=0,
        ),
    )(place, *blocks, weight)


def flip_rows_kernel(place_ref, *refs):
    piece_refs, out_ref, rows = refs[:-2], refs[-2], refs[-1]
    count = len(piece_refs)
    chunks = rows.shape[1] // DH
    shards, height, _ = piece_refs[0].shape
    piece = height // chunks
    for part in range(count):
        for shard in range(shards):
            start = shard * piece * count + (place_ref[1] ^ part) * piece
            here = pl.ds(pl.multiple_of(start, piece), piece)
            for chunk in range(chunks):
                rows[here, chunk * DH : (chunk + 1) * DH] = piece_refs[part][
                    shard, chunk * piece : (chunk + 1) * piece, :
                ]
    out_ref[...] = rows[...].T


def flip_rows(place, pieces, slots):
    shards, height, _ = pieces[0].shape
    width = height // (slots // len(pieces)) * DH
    keys = shards * slots
    return pl.pallas_call(
        flip_rows_kernel,
        in_specs=[SMEM_SPEC] + [pl.BlockSpec()] * len(pieces),
        out_specs=VMEM_SPEC,
        out_shape=jax.ShapeDtypeStruct((width, keys), BF16),
        scratch_shapes=[pltpu.VMEM((keys, width), BF16)],
        compiler_params=params(),
        cost_estimate=pl.CostEstimate(flops=0, bytes_accessed=4 * keys * width, transcendentals=0),
    )(place, *pieces)


def weight_part_kernel(first, count, place_ref, flip_ref, *refs):
    out_ref, product_ref, leave = refs[-3:]
    away = []
    for step in range(0, count, 2):
        both = jnp.concatenate([ref[...] for ref in refs[step : step + 2]], axis=1)
        product = dot(flip_ref[...], both)
        head = place_ref[0] ^ (first + step)
        for side in range(2):
            column = pl.multiple_of((head ^ side) % 2 * DH, DH)
            product_ref[step // 2, :, pl.ds(column, DH)] = product[:, side * DH : (side + 1) * DH]
        columns = pl.ds(pl.multiple_of(head // 2 * (2 * DH), 2 * DH), 2 * DH)
        away.append(
            pltpu.make_async_copy(
                product_ref.at[step // 2], out_ref.at[:, columns], leave.at[step // 2]
            )
        )
        away[-1].start()
    for copy in away:
        copy.wait()


def weight_part(place, flip, attended, first, heads, weight, before=None):
    count = len(attended)
    width, keys = flip.shape
    more = [] if before is None else [before]
    return pl.pallas_call(
        functools.partial(weight_part_kernel, first, count),
        in_specs=[SMEM_SPEC]
        + [VMEM_SPEC] * (1 + count)
        + [pl.BlockSpec(memory_space=pl.ANY)] * len(more),
        out_specs=pl.BlockSpec(memory_space=pl.ANY),
        out_shape=jax.ShapeDtypeStruct((width, heads * DH), F32),
        scratch_shapes=[
            pltpu.VMEM((count // 2, width, 2 * DH), F32),
            pltpu.SemaphoreType.DMA((count // 2,)),
        ],
        input_output_aliases={2 + count: 0} if more else {},
        compiler_params=params(),
        cost_estimate=pl.CostEstimate(
            flops=weight * 2 * keys * width * count * DH,
            bytes_accessed=8 * keys * DH * count,
            transcendentals=0,
        ),
    )(place, flip, *attended, *more)


def mark_live(count_ref, live_ref, slots):
    for shard in range(live_ref.shape[0] // slots):
        inside = lax.broadcasted_iota(jnp.int32, (slots, live_ref.shape[1]), 0)
        live_ref[shard * slots : (shard + 1) * slots] = jnp.where(
            inside < count_ref[shard], 0.0, -1e30
        )


def masked_scores(start, keys, key_ref, query, live_ref):
    scores = dot_cols(key_ref[:keys], query) * (1.0 / math.sqrt(DH)) + live_ref[:keys, :1]
    row = start + lax.broadcasted_iota(jnp.int32, (1, keys - start), 1)
    key_pos = start + lax.broadcasted_iota(jnp.int32, (keys - start, 1), 0)
    edge = jnp.where(key_pos <= row, scores[start:], -1e30)
    return jnp.concatenate([scores[:start], edge], axis=0) if start else edge


def split_blocks(block_ref, *refs):
    shards, slots, _ = block_ref.shape
    for shard in range(shards):
        for which, ref in enumerate(refs):
            ref[shard * slots : (shard + 1) * slots] = block_ref[
                shard, :, which * DH : (which + 1) * DH
            ]


def forward_kernel(
    count_ref, block_ref, attended_ref, stat_ref, live_ref, query_ref, key_ref, value_ref
):
    mark_live(count_ref, live_ref, block_ref.shape[1])
    split_blocks(block_ref, query_ref, key_ref, value_ref)
    value_flip = value_ref[...].T
    for start in range(0, query_ref.shape[0], WIDE_BLOCK):
        rows = slice(start, start + WIDE_BLOCK)
        keys = start + WIDE_BLOCK
        scores = masked_scores(start, keys, key_ref, query_ref[rows], live_ref)
        peak = jnp.max(scores, axis=0, keepdims=True)
        weights = jnp.exp(scores - peak)
        inverse = 1.0 / jnp.sum(weights, axis=0, keepdims=True)
        attended = dot(value_flip[:, :keys], (weights * inverse).astype(BF16))
        attended_ref[rows] = attended.T.astype(BF16)
        stat_ref[0:1, rows] = peak
        stat_ref[1:2, rows] = inverse


def attention_cost(keys, dots):
    return pl.CostEstimate(
        flops=dots * keys * keys * DH, bytes_accessed=16 * keys * DH, transcendentals=keys * keys // 2
    )


def forward(counts, blocks):
    keys = blocks.shape[0] * blocks.shape[1]
    return pl.pallas_call(
        forward_kernel,
        out_shape=[
            jax.ShapeDtypeStruct((keys, DH), BF16),
            jax.ShapeDtypeStruct((8, keys), F32),
        ],
        in_specs=[SMEM_SPEC, pl.BlockSpec()],
        scratch_shapes=[pltpu.VMEM((keys, DH), F32)] + [pltpu.VMEM((keys, DH), BF16)] * 3,
        compiler_params=params(32 * 1024 * 1024),
        cost_estimate=attention_cost(keys, 2),
    )(counts, blocks)


def backward_kernel(
    count_ref,
    block_ref,
    attended_ref,
    stat_ref,
    grads_ref,
    out_ref,
    live_ref,
    query_ref,
    key_ref,
    value_ref,
    grad_ref,
    query_total,
    key_total,
    value_total,
):
    seq_count, slots, _ = out_ref.shape
    scale = 1.0 / math.sqrt(DH)
    mark_live(count_ref, live_ref, slots)
    split_blocks(block_ref, query_ref, key_ref, value_ref)
    for shard in range(seq_count):
        grad_ref[shard * slots : (shard + 1) * slots] = grads_ref[shard, :slots]
    key_flip = key_ref[...].T
    for start in range(0, query_ref.shape[0], QUERY_BLOCK):
        rows = slice(start, start + QUERY_BLOCK)
        keys = start + QUERY_BLOCK
        query = query_ref[rows]
        grad = grad_ref[rows]
        scores = masked_scores(start, keys, key_ref, query, live_ref)
        probs = jnp.exp(scores - stat_ref[0:1, rows]) * stat_ref[1:2, rows]
        probs_low = probs.astype(BF16)
        product = grad.astype(F32) * attended_ref[rows].astype(F32)
        row_dot = jnp.sum(product.T, axis=0, keepdims=True)
        grad_probs = dot_cols(value_ref[:keys], grad)
        grad_scores = (probs * (grad_probs - row_dot)).astype(BF16)
        query_total[rows] = (dot(key_flip[:, :keys], grad_scores) * scale).T.astype(BF16)
        key_part = dot(grad_scores, query)
        value_part = dot(probs_low, grad)
        if start:
            key_total[:start] += key_part[:start]
            value_total[:start] += value_part[:start]
        key_total[rows] = key_part[start:]
        value_total[rows] = value_part[start:]
    for shard in range(seq_count):
        here = slice(shard * slots, (shard + 1) * slots)
        out_ref[shard, :, :DH] = query_total[here]
        out_ref[shard, :, DH : 2 * DH] = (key_total[here] * scale).astype(BF16)
        out_ref[shard, :, 2 * DH :] = value_total[here].astype(BF16)


def backward(counts, blocks, attended, stats, grads):
    keys = attended.shape[0]
    return pl.pallas_call(
        backward_kernel,
        in_specs=[SMEM_SPEC] + [pl.BlockSpec()] * 4,
        out_shape=jax.ShapeDtypeStruct(blocks.shape, BF16),
        scratch_shapes=[pltpu.VMEM((keys, DH), F32)]
        + [pltpu.VMEM((keys, DH), BF16)] * 5
        + [pltpu.VMEM((keys, DH), F32)] * 2,
        compiler_params=params(VMEM_MOST),
        cost_estimate=attention_cost(keys, 5),
    )(counts, blocks, attended, stats, grads)


def on_device_whole_heads(
    projections,
    output_gradient,
    output_projection_weight,
    kept_token_indices,
    surviving_token_count,
):
    tok_dev = projections.shape[0]
    slots = kept_token_indices.shape[1]
    seq_count = lax.axis_size("seq")
    head_count = lax.axis_size("head")
    index = kept_token_indices
    place = jnp.stack([lax.axis_index("seq"), lax.axis_index("head")]).astype(jnp.int32)
    seq_bits = [1 << bit for bit in reversed(range(seq_count.bit_length() - 1))]
    head_bits = [1 << bit for bit in reversed(range(head_count.bit_length() - 1))]

    def swap(blocks):
        return lax.all_to_all(blocks, "seq", split_axis=0, concat_axis=0, tiled=True)

    packed = pack_whole(index, projections.transpose(1, 0, 2))
    packed, grad_index = lax.optimization_barrier((packed, index))
    arrived = swap(packed)
    grad_blocks = gather_blocks(pack_grad(grad_index, output_gradient), "head", head_bits)
    grads = swap(grad_swap(place, grad_blocks, output_projection_weight, seq_count))
    attended, stats = forward(surviving_token_count, arrived)

    near, last = seq_bits[-2], seq_bits[-1]
    held = {bit: exchange(attended, "seq", bit) for bit in seq_bits}
    held[near ^ last] = exchange(held[near], "seq", last)
    back = backward(surviving_token_count, arrived, attended, stats, grads)
    back, held = lax.optimization_barrier((back, held))
    gathered = gather_blocks(attended, "seq", seq_bits, {0: attended, **held})
    home = swap(back)
    pieces = gather_blocks(grads[:, slots:], "head", head_bits)
    flip = flip_rows(place, pieces, slots)
    late = seq_count - 2
    weight_grad = weight_part(place, flip, gathered[:late], 0, seq_count, 1)
    projection_grad = unpack_whole(index, home, tok_dev)
    weight_grad = weight_part(place, flip, gathered[late:], late, seq_count, 28, weight_grad)
    projection_grad = projection_grad.transpose(1, 0, 2)
    return (projection_grad, weight_grad)


def on_device(projections, output_gradient, weight, index, counts):
    heads = projections.shape[2] // DH
    seq_count, head_count = lax.axis_size("seq"), lax.axis_size("head")
    width = output_gradient.shape[1] * head_count // seq_count
    whole = seq_count == heads and seq_count % 2 == 0 and width % DH == 0
    powers = seq_count & (seq_count - 1) == 0 and head_count & (head_count - 1) == 0
    body = on_device_whole_heads if whole and powers else on_device_split_heads
    return body(projections, output_gradient, weight, index, counts)


def solution(mesh):
    return jax.shard_map(
        on_device,
        mesh=mesh,
        in_specs=(P("seq", None, "head"), P("seq", "head"), P(None, "head"), P("seq", None), P()),
        out_specs=(P("seq", None, "head"), P("seq", "head")),
        check_vma=False,
    )
```
